32 devices in a mesh: grp: 4 (over z), blk: 8 (over y, x, core).
Axes of the slice: x: 2, y: 2, z: 4, core: 2. Of those that a mesh axis runs over, the one named last changes fastest.
Arguments:
- tile_values: bfloat16 [256, 320, 128], P(('grp', 'blk'))
- tile_paper: int32 [256], P(('grp', 'blk')), may hold values from 0 to 1
- tile_author: int32 [256], P(('grp', 'blk')), may hold values from 0 to 1
- tile_count: int32 [32], P(('grp', 'blk')), may hold values from 2 to 8, as said below
- seed_class: int32 [20480], P(('grp', 'blk')), may hold values from 0 to 152
- train_mask: int32 [20480], P(('grp', 'blk')), may hold values from 0 to 1
- class_prior: float32 [256], replicated, may hold values from 0.02 to 0.2
- class_target: float32 [256], replicated, may hold values from 0.5 to 2
Outputs:
- paper_scores: float32 [20480, 256], P(('grp', 'blk'))
- author_scores: float32 [8192, 256], P(('grp', 'blk'))
The draws below stay inside these ranges and needn't reach their ends.
Inputs may be any that keep to these rules, and one draw needn't show every extreme that they name: The first tile_count[d] slots of device d are live, the others empty; some device has all 8 live.
All inputs are finite; a program needn't handle non-finite values.
Results may differ from the reference program's by a relative error of at most 0.0012.
Values may be sent and summed in bfloat16 or wider, within the bound.
No kernel may reach another device: no remote copies, remote signals or barrier semaphores. Data moves between devices by JAX's collectives and lax.ppermute only.
A program may use at most 64 MiB of HBM per device.

```python
import math
import jax
import jax.numpy as jnp
from jax import lax

CLASSES = 256
TP = 320
TA = 128
PT_DEV = 2
AT_DEV = 2
SLOT_PEER = 1
ITERS = 4
ROUNDS = 2
SLOTS = 8
PAPERS = 20480
AUTHORS = 8192
N_GRP = 4
N_BLK = 8
DEVICES = 32


def draw_tile_values(key, part):
    key_value, key_scale = jax.random.split(key)
    row_total = DEVICES * SLOTS
    base_values = jax.random.uniform(key_value, (row_total, TP, TA), jnp.float32, 0.2, 1.0)
    row_scale = jnp.exp(jax.random.uniform(key_scale, (row_total, TP, 1), jnp.float32, 0.0, jnp.log(10.0)))
    device_ramp = 1.0 + 2.0 * (jnp.arange(row_total) // SLOTS).astype(jnp.float32) / max(DEVICES - 1, 1)
    return (base_values * row_scale * device_ramp[:, None, None] * (16.0 / TA)).astype(jnp.bfloat16)


def draw_tile_count(key, part):
    lowest = max(SLOTS // 4, 1)
    counts = jax.random.randint(key, (DEVICES,), lowest, SLOTS + 1)
    return counts.at[0].set(SLOTS).at[1].set(lowest).astype(jnp.int32)


def draw_seed_class(key, part):
    class_total = min(153, CLASSES)
    group_width = SLOTS // SLOT_PEER
    group_total = DEVICES // group_width
    device_papers = PT_DEV * TP
    key_center, key_offset, key_inside = jax.random.split(jax.random.fold_in(key, 11), 3)
    group_center = jax.random.randint(key_center, (group_total,), 0, class_total)
    device_offset = jax.random.randint(key_offset, (DEVICES,), 0, max(class_total // 8, 1))
    inside = jax.random.randint(key_inside, (DEVICES, device_papers), 0, max(class_total // 16, 2))
    device_group = jnp.arange(DEVICES) // group_width
    band_start = group_center[device_group] + device_offset
    classes = (band_start[:, None] + inside) % class_total
    flattened = classes.reshape(DEVICES * device_papers)
    return flattened.at[0].set(class_total - 1).at[1].set(0).astype(jnp.int32)


def draw_train_mask(key, part):
    device_papers = PT_DEV * TP
    key_level, key_value = jax.random.split(jax.random.fold_in(key, 23))
    levels = jax.random.randint(key_level, (DEVICES,), 0, 5).at[0].set(4).at[1].set(1)
    picks = jax.random.randint(key_value, (DEVICES, device_papers), 0, 4)
    return (picks < levels[:, None]).astype(jnp.int32).reshape(DEVICES * device_papers)


def set_ends(array, key, least, high):
    longest = array.shape.index(max(array.shape))
    spots = []
    for shift in (0, 1):
        where = [jax.random.randint(jax.random.fold_in(key, axis), (), 0, length) for axis, length in enumerate(array.shape)]
        where[longest] = (where[longest] + shift) % array.shape[longest]
        spots.append(tuple(where))
    return array.at[spots[0]].set(least).at[spots[1]].set(high)


def setup_inputs(seed: int = 0) -> dict:
    streams_of = jax.random.split(jax.random.key(seed), 9)
    return {
        "tile_values": draw_tile_values(jax.random.fold_in(streams_of[8], 71), 0),
        "tile_paper": set_ends(jax.random.randint(streams_of[1], (DEVICES * SLOTS,), 0, PT_DEV), jax.random.fold_in(streams_of[1], 1), 0, PT_DEV - 1).astype(jnp.int32),
        "tile_author": set_ends(jax.random.randint(streams_of[2], (DEVICES * SLOTS,), 0, AT_DEV), jax.random.fold_in(streams_of[2], 1), 0, AT_DEV - 1).astype(jnp.int32),
        "tile_count": draw_tile_count(jax.random.fold_in(streams_of[8], 71), 0),
        "seed_class": draw_seed_class(jax.random.fold_in(streams_of[8], 71), 0),
        "train_mask": draw_train_mask(jax.random.fold_in(streams_of[8], 71), 0),
        "class_prior": jnp.clip(jnp.exp(jax.random.uniform(streams_of[6], (CLASSES,), jnp.float32, math.log(0.02), math.log(0.2))), 0.02, 0.2),
        "class_target": jnp.clip(jnp.exp(jax.random.uniform(streams_of[7], (CLASSES,), jnp.float32, math.log(0.5), math.log(2.0))), 0.5, 2.0),
    }


keep_share = 0.8


def class_balancer(label_masses, class_prior, class_target):
    kernel = label_masses + class_prior[None, :]
    scale_rows = jnp.ones((kernel.shape[0],), jnp.float32)
    scale_cols = jnp.ones((kernel.shape[1],), jnp.float32)
    for iteration in range(ITERS):
        column = jnp.sum(scale_rows[:, None] * kernel, axis=0)
        scale_cols = class_target / column
        scale_rows = 1.0 / jnp.sum(kernel * scale_cols[None, :], axis=1)
    return scale_rows[:, None] * kernel * scale_cols[None, :]


def reference(tile_values, tile_paper, tile_author, tile_count, seed_class, train_mask, class_prior, class_target):
    slot_count = SLOT_PEER * N_BLK
    high = lax.Precision.HIGHEST
    seed_rows = ((seed_class[:, None] == jnp.arange(CLASSES)[None, :]) & (train_mask[:, None] == 1)).astype(jnp.float32)
    labels = seed_rows.astype(jnp.bfloat16)
    tiles_all = tile_values.reshape(N_GRP, N_BLK, slot_count, TP, TA)
    paper_index = tile_paper.reshape(N_GRP, N_BLK, slot_count)
    author_index = tile_author.reshape(N_GRP, N_BLK, slot_count)
    live_slots = (jnp.arange(slot_count)[None, :] < tile_count[:, None]).astype(jnp.float32).reshape(N_GRP, N_BLK, slot_count)
    target_index = ((jnp.arange(slot_count) // SLOT_PEER)[None, None, :] * AT_DEV + author_index).astype(jnp.int32)
    updated = seed_rows
    author_share = jnp.zeros((AUTHORS, CLASSES), jnp.float32)
    for repeat in range(ROUNDS):
        label_tiles = labels.reshape(N_GRP, N_BLK, PT_DEV, TP, CLASSES)

        def forward(operands):
            tiles_group, label_group, paper_group, target_group, live_group = operands
            chosen = jax.vmap(lambda lookup_table, index_array: lookup_table[index_array])(label_group, paper_group)
            partial_value = jnp.einsum("bspa,bspc->bsac", tiles_group.astype(jnp.float32), chosen.astype(jnp.float32), precision=high)
            parcel = (partial_value * live_group[:, :, None, None]).astype(jnp.bfloat16)
            onehot = (target_group[:, :, None] == jnp.arange(N_BLK * AT_DEV)[None, None, :]).astype(jnp.float32)
            return jnp.einsum("bsk,bsac->kac", onehot, parcel.astype(jnp.float32), precision=high)

        author_mass = lax.map(forward, (tiles_all, label_tiles, paper_index, target_index, live_slots))
        author_mass = author_mass.reshape(AUTHORS, CLASSES)
        author_share = class_balancer(author_mass, class_prior, class_target)
        author_class_labels = author_share.astype(jnp.bfloat16).reshape(N_GRP, N_BLK * AT_DEV, TA, CLASSES)

        def backward(operands):
            tiles_group, authors_group, paper_group, target_group, live_group = operands
            returned = authors_group[target_group]
            products = jnp.einsum("bspa,bsac->bspc", tiles_group.astype(jnp.float32), returned.astype(jnp.float32), precision=high)
            onehot = (paper_group[:, :, None] == jnp.arange(PT_DEV)[None, None, :]).astype(jnp.float32) * live_group[:, :, None]
            return jnp.einsum("bsq,bspc->bqpc", onehot, products, precision=high)

        paper_mass = lax.map(backward, (tiles_all, author_class_labels, paper_index, target_index, live_slots))
        paper_mass = paper_mass.reshape(PAPERS, CLASSES)
        paper_share = class_balancer(paper_mass, class_prior, class_target)
        updated = keep_share * paper_share + (1.0 - keep_share) * seed_rows
        labels = updated.astype(jnp.bfloat16)
    return CLASSES * updated, CLASSES * author_share
```

```python
import jax
import jax.numpy as jnp
from jax import lax
from jax.sharding import PartitionSpec as P

AT_DEV = 2
ITERS = 4
ROUNDS = 2


keep_share = 0.8


def total(local_mass):
    devices = lax.axis_size(("grp", "blk"))
    sent = jnp.broadcast_to(local_mass[None, :], (devices, local_mass.shape[0]))
    parts = lax.all_to_all(sent, ("grp", "blk"), split_axis=0, concat_axis=0, tiled=True)
    return jnp.sum(parts, axis=0)


def class_balancer(label_masses, class_prior, class_target):
    kernel = label_masses + class_prior[None, :]
    scale_rows = None
    scale_cols = None
    for iteration in range(ITERS):
        if scale_rows is None:
            local_mass = jnp.sum(kernel, axis=0)
        else:
            local_mass = jnp.sum(scale_rows[:, None] * kernel, axis=0)
        column = total(local_mass)
        scale_cols = class_target / column
        scale_rows = 1.0 / jnp.sum(kernel * scale_cols[None, :], axis=1)
    return scale_rows[:, None] * kernel * scale_cols[None, :]


def on_device(
    tile_values,
    tile_paper,
    tile_author,
    tile_count,
    seed_class,
    train_mask,
    class_prior,
    class_target,
):
    high = lax.Precision.HIGHEST
    slot_count = tile_values.shape[0]
    tile_rows = tile_values.shape[1]
    tile_cols = tile_values.shape[2]
    classes = class_prior.shape[0]
    paper_rows = seed_class.shape[0]
    paper_tiles = paper_rows // tile_rows
    author_tiles = AT_DEV
    live_slots = (jnp.arange(slot_count) < tile_count[0]).astype(jnp.float32)
    seed_rows = (
        (seed_class[:, None] == jnp.arange(classes)[None, :]) & (train_mask[:, None] == 1)
    ).astype(jnp.float32)
    labels = seed_rows.astype(jnp.bfloat16).reshape(paper_tiles, tile_rows, classes)
    paper_pick = (tile_paper[:, None] == jnp.arange(paper_tiles)[None, :]).astype(
        jnp.float32
    ) * live_slots[:, None]
    author_pick = (tile_author[:, None] == jnp.arange(author_tiles)[None, :]).astype(jnp.bfloat16)
    updated = seed_rows
    author_share = jnp.zeros((author_tiles * tile_cols, classes), jnp.float32)
    for repeat in range(ROUNDS):
        chosen = labels[tile_paper]
        partial_value = jnp.einsum(
            "spa,spc->sac", tile_values, chosen, preferred_element_type=jnp.float32
        )
        parcel = (partial_value * live_slots[:, None, None]).astype(jnp.bfloat16)
        received_mass, received_selection = (
            lax.all_to_all(parcel, "blk", split_axis=0, concat_axis=0, tiled=True),
            lax.all_to_all(author_pick, "blk", split_axis=0, concat_axis=0, tiled=True),
        )
        author_mass = jnp.einsum(
            "ib,iey->bey", received_selection, received_mass, preferred_element_type=jnp.float32
        )
        author_mass = author_mass.reshape(author_tiles * tile_cols, classes)
        author_share = class_balancer(author_mass, class_prior, class_target)
        author_class_labels = author_share.astype(jnp.bfloat16).reshape(
            author_tiles, tile_cols, classes
        )
        picked = jnp.einsum(
            "ih,hlp->ilp",
            received_selection,
            author_class_labels,
            preferred_element_type=jnp.float32,
        ).astype(jnp.bfloat16)
        returned = lax.all_to_all(picked, "blk", split_axis=0, concat_axis=0, tiled=True)
        products = jnp.einsum(
            "spa,sac->spc", tile_values, returned, preferred_element_type=jnp.float32
        )
        paper_mass = jnp.einsum("sq,spc->qpc", paper_pick, products, precision=high)
        paper_mass = paper_mass.reshape(paper_rows, classes)
        paper_share = class_balancer(paper_mass, class_prior, class_target)
        updated = keep_share * paper_share + (1.0 - keep_share) * seed_rows
        labels = updated.astype(jnp.bfloat16).reshape(paper_tiles, tile_rows, classes)
    return (classes * updated, classes * author_share)


def solution(mesh):
    placed = (
        P(("grp", "blk"), None, None),
        P(("grp", "blk")),
        P(("grp", "blk")),
        P(("grp", "blk")),
        P(("grp", "blk")),
        P(("grp", "blk")),
        P(),
        P(),
    )
    return jax.shard_map(
        on_device,
        mesh=mesh,
        in_specs=placed,
        out_specs=(P(("grp", "blk"), None), P(("grp", "blk"), None)),
        check_vma=False,
    )
```

```python
import jax
import jax.numpy as jnp
from jax import lax
from jax.sharding import PartitionSpec as P

AT_DEV = 2
ITERS = 4
ROUNDS = 2


keep_share = 0.8


def axis_total(value, axis):
    size = lax.axis_size(axis)
    parts = [value]
    for shift in range(1, size):
        pairs = [(i, (i + shift) % size) for i in range(size)]
        parts.append(lax.ppermute(value, axis, pairs))
    while len(parts) > 1:
        half = len(parts) // 2
        parts = [parts[i] + parts[i + half] for i in range(half)] + parts[2 * half :]
    return parts[0]


def total(local_mass):
    return axis_total(axis_total(local_mass, "blk"), "grp")


def class_balancer(label_masses, class_prior, class_target):
    kernel = label_masses + class_prior[None, :]
    scale_rows = None
    scale_cols = None
    for iteration in range(ITERS):
        if scale_rows is None:
            local_mass = jnp.sum(kernel, axis=0)
        else:
            local_mass = jnp.sum(scale_rows[:, None] * kernel, axis=0)
        column = total(local_mass)
        scale_cols = class_target / column
        scale_rows = 1.0 / jnp.sum(kernel * scale_cols[None, :], axis=1)
    return scale_rows[:, None] * kernel * scale_cols[None, :]


def on_device(
    tile_values,
    tile_paper,
    tile_author,
    tile_count,
    seed_class,
    train_mask,
    class_prior,
    class_target,
):
    high = lax.Precision.HIGHEST
    slot_count = tile_values.shape[0]
    tile_rows = tile_values.shape[1]
    tile_cols = tile_values.shape[2]
    classes = class_prior.shape[0]
    paper_rows = seed_class.shape[0]
    paper_tiles = paper_rows // tile_rows
    author_tiles = AT_DEV
    live_slots = (jnp.arange(slot_count) < tile_count[0]).astype(jnp.float32)
    seed_rows = (
        (seed_class[:, None] == jnp.arange(classes)[None, :]) & (train_mask[:, None] == 1)
    ).astype(jnp.float32)
    labels = seed_rows.astype(jnp.bfloat16).reshape(paper_tiles, tile_rows, classes)
    paper_pick = (tile_paper[:, None] == jnp.arange(paper_tiles)[None, :]).astype(
        jnp.float32
    ) * live_slots[:, None]
    author_pick = (tile_author[:, None] == jnp.arange(author_tiles)[None, :]).astype(jnp.bfloat16)
    updated = seed_rows
    author_share = jnp.zeros((author_tiles * tile_cols, classes), jnp.float32)
    for repeat in range(ROUNDS):
        chosen = labels[tile_paper]
        partial_value = jnp.einsum(
            "spa,spc->sac", tile_values, chosen, preferred_element_type=jnp.float32
        )
        parcel = (partial_value * live_slots[:, None, None]).astype(jnp.bfloat16)
        received_mass, received_selection = (
            lax.all_to_all(parcel, "blk", split_axis=0, concat_axis=0, tiled=True),
            lax.all_to_all(author_pick, "blk", split_axis=0, concat_axis=0, tiled=True),
        )
        author_mass = jnp.einsum(
            "ib,iey->bey", received_selection, received_mass, preferred_element_type=jnp.float32
        )
        author_mass = author_mass.reshape(author_tiles * tile_cols, classes)
        author_share = class_balancer(author_mass, class_prior, class_target)
        author_class_labels = author_share.astype(jnp.bfloat16).reshape(
            author_tiles, tile_cols, classes
        )
        picked = jnp.einsum(
            "ih,hlp->ilp",
            received_selection,
            author_class_labels,
            preferred_element_type=jnp.float32,
        ).astype(jnp.bfloat16)
        returned = lax.all_to_all(picked, "blk", split_axis=0, concat_axis=0, tiled=True)
        products = jnp.einsum(
            "spa,sac->spc", tile_values, returned, preferred_element_type=jnp.float32
        )
        paper_mass = jnp.einsum("sq,spc->qpc", paper_pick, products, precision=high)
        paper_mass = paper_mass.reshape(paper_rows, classes)
        paper_share = class_balancer(paper_mass, class_prior, class_target)
        updated = keep_share * paper_share + (1.0 - keep_share) * seed_rows
        labels = updated.astype(jnp.bfloat16).reshape(paper_tiles, tile_rows, classes)
    return (classes * updated, classes * author_share)


def solution(mesh):
    placed = (
        P(("grp", "blk"), None, None),
        P(("grp", "blk")),
        P(("grp", "blk")),
        P(("grp", "blk")),
        P(("grp", "blk")),
        P(("grp", "blk")),
        P(),
        P(),
    )
    return jax.shard_map(
        on_device,
        mesh=mesh,
        in_specs=placed,
        out_specs=(P(("grp", "blk"), None), P(("grp", "blk"), None)),
        check_vma=False,
    )
```

```python
import jax
import jax.numpy as jnp
from jax import lax
from jax.sharding import PartitionSpec as P

AT_DEV = 2
ITERS = 4
ROUNDS = 2


keep_share = 0.8


def total(value):
    for axis in ("blk", "grp"):
        size = lax.axis_size(axis)
        step = 1
        while step < size:
            pairs = [(i, i ^ step) for i in range(size)]
            value = value + lax.ppermute(value, axis, pairs)
            step *= 2
    return value


def class_balancer(label_masses, class_prior, class_target):
    kernel = label_masses + class_prior[None, :]
    scale_rows = None
    scale_cols = None
    for iteration in range(ITERS):
        if scale_rows is None:
            local_mass = jnp.sum(kernel, axis=0)
        else:
            local_mass = jnp.sum(scale_rows[:, None] * kernel, axis=0)
        column = total(local_mass)
        scale_cols = class_target / column
        scale_rows = 1.0 / jnp.sum(kernel * scale_cols[None, :], axis=1)
    return scale_rows[:, None] * kernel * scale_cols[None, :]


def on_device(
    tile_values,
    tile_paper,
    tile_author,
    tile_count,
    seed_class,
    train_mask,
    class_prior,
    class_target,
):
    high = lax.Precision.HIGHEST
    slot_count = tile_values.shape[0]
    tile_rows = tile_values.shape[1]
    tile_cols = tile_values.shape[2]
    classes = class_prior.shape[0]
    paper_rows = seed_class.shape[0]
    paper_tiles = paper_rows // tile_rows
    author_tiles = AT_DEV
    live_slots = (jnp.arange(slot_count) < tile_count[0]).astype(jnp.float32)
    seed_rows = (
        (seed_class[:, None] == jnp.arange(classes)[None, :]) & (train_mask[:, None] == 1)
    ).astype(jnp.float32)
    labels = seed_rows.astype(jnp.bfloat16).reshape(paper_tiles, tile_rows, classes)
    paper_pick = (tile_paper[:, None] == jnp.arange(paper_tiles)[None, :]).astype(
        jnp.float32
    ) * live_slots[:, None]
    author_pick = (tile_author[:, None] == jnp.arange(author_tiles)[None, :]).astype(jnp.bfloat16)
    updated = seed_rows
    author_share = jnp.zeros((author_tiles * tile_cols, classes), jnp.float32)
    for repeat in range(ROUNDS):
        chosen = labels[tile_paper]
        partial_value = jnp.einsum(
            "spa,spc->sac", tile_values, chosen, preferred_element_type=jnp.float32
        )
        parcel = (partial_value * live_slots[:, None, None]).astype(jnp.bfloat16)
        received_mass, received_selection = (
            lax.all_to_all(parcel, "blk", split_axis=0, concat_axis=0, tiled=True),
            lax.all_to_all(author_pick, "blk", split_axis=0, concat_axis=0, tiled=True),
        )
        author_mass = jnp.einsum(
            "ib,iey->bey", received_selection, received_mass, preferred_element_type=jnp.float32
        )
        author_mass = author_mass.reshape(author_tiles * tile_cols, classes)
        author_share = class_balancer(author_mass, class_prior, class_target)
        author_class_labels = author_share.astype(jnp.bfloat16).reshape(
            author_tiles, tile_cols, classes
        )
        picked = jnp.einsum(
            "ih,hlp->ilp",
            received_selection,
            author_class_labels,
            preferred_element_type=jnp.float32,
        ).astype(jnp.bfloat16)
        returned = lax.all_to_all(picked, "blk", split_axis=0, concat_axis=0, tiled=True)
        products = jnp.einsum(
            "spa,sac->spc", tile_values, returned, preferred_element_type=jnp.float32
        )
        paper_mass = jnp.einsum("sq,spc->qpc", paper_pick, products, precision=high)
        paper_mass = paper_mass.reshape(paper_rows, classes)
        paper_share = class_balancer(paper_mass, class_prior, class_target)
        updated = keep_share * paper_share + (1.0 - keep_share) * seed_rows
        labels = updated.astype(jnp.bfloat16).reshape(paper_tiles, tile_rows, classes)
    return (classes * updated, classes * author_share)


def solution(mesh):
    placed = (
        P(("grp", "blk"), None, None),
        P(("grp", "blk")),
        P(("grp", "blk")),
        P(("grp", "blk")),
        P(("grp", "blk")),
        P(("grp", "blk")),
        P(),
        P(),
    )
    return jax.shard_map(
        on_device,
        mesh=mesh,
        in_specs=placed,
        out_specs=(P(("grp", "blk"), None), P(("grp", "blk"), None)),
        check_vma=False,
    )
```

```python
import jax
import jax.numpy as jnp
from jax import lax
from jax.sharding import PartitionSpec as P

AT_DEV = 2
ITERS = 4
ROUNDS = 2


keep_share = 0.8


def total(local_mass):
    groups = lax.axis_size("grp")
    blocks = lax.axis_size("blk")
    pairs = [(i, i ^ 1) for i in range(blocks)]
    value = local_mass + lax.ppermute(local_mass, "blk", pairs)
    peers = [[g * blocks + b for g in range(groups) for b in range(p, blocks, 2)] for p in range(2)]
    sent = jnp.broadcast_to(value[None, :], (len(peers[0]), value.shape[0]))
    parts = lax.all_to_all(
        sent,
        ("grp", "blk"),
        split_axis=0,
        concat_axis=0,
        axis_index_groups=peers,
        tiled=True,
    )
    return jnp.sum(parts, axis=0)


def class_balancer(label_masses, class_prior, class_target):
    kernel = label_masses + class_prior[None, :]
    scale_rows = None
    scale_cols = None
    for iteration in range(ITERS):
        if scale_rows is None:
            local_mass = jnp.sum(kernel, axis=0)
        else:
            local_mass = jnp.sum(scale_rows[:, None] * kernel, axis=0)
        column = total(local_mass)
        scale_cols = class_target / column
        scale_rows = 1.0 / jnp.sum(kernel * scale_cols[None, :], axis=1)
    return scale_rows[:, None] * kernel * scale_cols[None, :]


def on_device(
    tile_values,
    tile_paper,
    tile_author,
    tile_count,
    seed_class,
    train_mask,
    class_prior,
    class_target,
):
    high = lax.Precision.HIGHEST
    slot_count = tile_values.shape[0]
    tile_rows = tile_values.shape[1]
    tile_cols = tile_values.shape[2]
    classes = class_prior.shape[0]
    paper_rows = seed_class.shape[0]
    paper_tiles = paper_rows // tile_rows
    author_tiles = AT_DEV
    live_slots = (jnp.arange(slot_count) < tile_count[0]).astype(jnp.float32)
    seed_rows = (
        (seed_class[:, None] == jnp.arange(classes)[None, :]) & (train_mask[:, None] == 1)
    ).astype(jnp.float32)
    labels = seed_rows.astype(jnp.bfloat16).reshape(paper_tiles, tile_rows, classes)
    paper_pick = (tile_paper[:, None] == jnp.arange(paper_tiles)[None, :]).astype(
        jnp.float32
    ) * live_slots[:, None]
    author_pick = (tile_author[:, None] == jnp.arange(author_tiles)[None, :]).astype(jnp.bfloat16)
    updated = seed_rows
    author_share = jnp.zeros((author_tiles * tile_cols, classes), jnp.float32)
    for repeat in range(ROUNDS):
        chosen = labels[tile_paper]
        partial_value = jnp.einsum(
            "spa,spc->sac", tile_values, chosen, preferred_element_type=jnp.float32
        )
        parcel = (partial_value * live_slots[:, None, None]).astype(jnp.bfloat16)
        received_mass, received_selection = (
            lax.all_to_all(parcel, "blk", split_axis=0, concat_axis=0, tiled=True),
            lax.all_to_all(author_pick, "blk", split_axis=0, concat_axis=0, tiled=True),
        )
        author_mass = jnp.einsum(
            "ib,iey->bey", received_selection, received_mass, preferred_element_type=jnp.float32
        )
        author_mass = author_mass.reshape(author_tiles * tile_cols, classes)
        author_share = class_balancer(author_mass, class_prior, class_target)
        author_class_labels = author_share.astype(jnp.bfloat16).reshape(
            author_tiles, tile_cols, classes
        )
        picked = jnp.einsum(
            "ih,hlp->ilp",
            received_selection,
            author_class_labels,
            preferred_element_type=jnp.float32,
        ).astype(jnp.bfloat16)
        returned = lax.all_to_all(picked, "blk", split_axis=0, concat_axis=0, tiled=True)
        products = jnp.einsum(
            "spa,sac->spc", tile_values, returned, preferred_element_type=jnp.float32
        )
        paper_mass = jnp.einsum("sq,spc->qpc", paper_pick, products, precision=high)
        paper_mass = paper_mass.reshape(paper_rows, classes)
        paper_share = class_balancer(paper_mass, class_prior, class_target)
        updated = keep_share * paper_share + (1.0 - keep_share) * seed_rows
        labels = updated.astype(jnp.bfloat16).reshape(paper_tiles, tile_rows, classes)
    return (classes * updated, classes * author_share)


def solution(mesh):
    placed = (
        P(("grp", "blk"), None, None),
        P(("grp", "blk")),
        P(("grp", "blk")),
        P(("grp", "blk")),
        P(("grp", "blk")),
        P(("grp", "blk")),
        P(),
        P(),
    )
    return jax.shard_map(
        on_device,
        mesh=mesh,
        in_specs=placed,
        out_specs=(P(("grp", "blk"), None), P(("grp", "blk"), None)),
        check_vma=False,
    )
```

```python
import jax
import jax.numpy as jnp
from jax import lax
from jax.sharding import PartitionSpec as P

AT_DEV = 2
ITERS = 4
ROUNDS = 2


keep_share = 0.8


def total(local_mass):
    parts = lax.all_gather(local_mass, ("grp", "blk"))
    return jnp.sum(parts, axis=0)


def class_balancer(label_masses, class_prior, class_target):
    kernel = label_masses + class_prior[None, :]
    scale_rows = None
    scale_cols = None
    for iteration in range(ITERS):
        if scale_rows is None:
            local_mass = jnp.sum(kernel, axis=0)
        else:
            local_mass = jnp.sum(scale_rows[:, None] * kernel, axis=0)
        column = total(local_mass)
        scale_cols = class_target / column
        scale_rows = 1.0 / jnp.sum(kernel * scale_cols[None, :], axis=1)
    return scale_rows[:, None] * kernel * scale_cols[None, :]


def on_device(
    tile_values,
    tile_paper,
    tile_author,
    tile_count,
    seed_class,
    train_mask,
    class_prior,
    class_target,
):
    high = lax.Precision.HIGHEST
    slot_count = tile_values.shape[0]
    tile_rows = tile_values.shape[1]
    tile_cols = tile_values.shape[2]
    classes = class_prior.shape[0]
    paper_rows = seed_class.shape[0]
    paper_tiles = paper_rows // tile_rows
    author_tiles = AT_DEV
    live_slots = (jnp.arange(slot_count) < tile_count[0]).astype(jnp.float32)
    seed_rows = (
        (seed_class[:, None] == jnp.arange(classes)[None, :]) & (train_mask[:, None] == 1)
    ).astype(jnp.float32)
    labels = seed_rows.astype(jnp.bfloat16).reshape(paper_tiles, tile_rows, classes)
    paper_pick = (tile_paper[:, None] == jnp.arange(paper_tiles)[None, :]).astype(
        jnp.float32
    ) * live_slots[:, None]
    author_pick = (tile_author[:, None] == jnp.arange(author_tiles)[None, :]).astype(jnp.bfloat16)
    updated = seed_rows
    author_share = jnp.zeros((author_tiles * tile_cols, classes), jnp.float32)
    for repeat in range(ROUNDS):
        chosen = labels[tile_paper]
        partial_value = jnp.einsum(
            "spa,spc->sac", tile_values, chosen, preferred_element_type=jnp.float32
        )
        parcel = (partial_value * live_slots[:, None, None]).astype(jnp.bfloat16)
        received_mass, received_selection = (
            lax.all_to_all(parcel, "blk", split_axis=0, concat_axis=0, tiled=True),
            lax.all_to_all(author_pick, "blk", split_axis=0, concat_axis=0, tiled=True),
        )
        author_mass = jnp.einsum(
            "ib,iey->bey", received_selection, received_mass, preferred_element_type=jnp.float32
        )
        author_mass = author_mass.reshape(author_tiles * tile_cols, classes)
        author_share = class_balancer(author_mass, class_prior, class_target)
        author_class_labels = author_share.astype(jnp.bfloat16).reshape(
            author_tiles, tile_cols, classes
        )
        picked = jnp.einsum(
            "ih,hlp->ilp",
            received_selection,
            author_class_labels,
            preferred_element_type=jnp.float32,
        ).astype(jnp.bfloat16)
        returned = lax.all_to_all(picked, "blk", split_axis=0, concat_axis=0, tiled=True)
        products = jnp.einsum(
            "spa,sac->spc", tile_values, returned, preferred_element_type=jnp.float32
        )
        paper_mass = jnp.einsum("sq,spc->qpc", paper_pick, products, precision=high)
        paper_mass = paper_mass.reshape(paper_rows, classes)
        paper_share = class_balancer(paper_mass, class_prior, class_target)
        updated = keep_share * paper_share + (1.0 - keep_share) * seed_rows
        labels = updated.astype(jnp.bfloat16).reshape(paper_tiles, tile_rows, classes)
    return (classes * updated, classes * author_share)


def solution(mesh):
    placed = (
        P(("grp", "blk"), None, None),
        P(("grp", "blk")),
        P(("grp", "blk")),
        P(("grp", "blk")),
        P(("grp", "blk")),
        P(("grp", "blk")),
        P(),
        P(),
    )
    return jax.shard_map(
        on_device,
        mesh=mesh,
        in_specs=placed,
        out_specs=(P(("grp", "blk"), None), P(("grp", "blk"), None)),
        check_vma=False,
    )
```

```python
import functools

import jax
import jax.numpy as jnp
from jax import lax
from jax.experimental import pallas as pl
from jax.experimental.pallas import tpu as pltpu
from jax.sharding import PartitionSpec as P

AT_DEV = 2
ITERS = 4
ROUNDS = 2
LANES = 128
META = 16

keep_share = 0.8

AXES = ("grp", "blk")
VMEM = pl.BlockSpec(memory_space=pltpu.VMEM)
SMEM = pl.BlockSpec(memory_space=pltpu.SMEM)
ANY = pl.BlockSpec(memory_space=pl.ANY)


def call(kernel, out_shape, in_specs, scratch_shapes=()):
    out_specs = jax.tree.map(lambda _: VMEM, out_shape)
    return pl.pallas_call(
        kernel,
        out_shape=out_shape,
        in_specs=in_specs,
        out_specs=out_specs,
        scratch_shapes=list(scratch_shapes),
        compiler_params=pltpu.CompilerParams(vmem_limit_bytes=48 * 1024 * 1024),
    )


def col_scale(parts_ref, target_ref):
    return target_ref[...] / jnp.sum(parts_ref[...], axis=0)


def row_scale(kernel, scale_cols):
    return 1.0 / jnp.sum(kernel * scale_cols, axis=1, keepdims=True)


def spread(value, parts_ref):
    parts_ref[...] = jnp.broadcast_to(value[None], parts_ref.shape)


def pack_kernel(slots, rows, tile_paper, tile_author, tile_count, tiles, codes, out):
    line = lax.broadcasted_iota(jnp.int32, (META, LANES), 0)
    code_rows = -(-rows // LANES)
    for slot in range(slots):
        out[slot, :rows, :] = tiles[slot]
        paper = tile_paper[slot]
        live = slot < tile_count[0]
        block = codes[paper]
        for author in range(AT_DEV):
            chosen = jnp.where(live & (tile_author[slot] == author), 1.0, 0.0)
            block = jnp.where(line == code_rows + author, chosen, block)
        block = jnp.where(line == code_rows + AT_DEV, paper.astype(jnp.float32), block)
        out[slot, rows:, :] = block.astype(jnp.bfloat16)


def finish_mass(mass, class_prior, full, half, parts):
    kernel = mass + class_prior[...]
    full[...] = kernel
    half[...] = kernel.astype(jnp.bfloat16)
    spread(jnp.sum(kernel, axis=0, keepdims=True), parts)


def first_author_kernel(slots, rows, packed, class_prior, full, half, parts):
    classes = full.shape[1]
    code_rows = -(-rows // LANES)
    totals = [jnp.zeros((classes, LANES), jnp.float32) for _ in range(AT_DEV)]
    class_line = lax.broadcasted_iota(jnp.int32, (classes, rows), 0).astype(jnp.float32)
    for slot in range(slots):
        meta = packed[slot, rows:, :].astype(jnp.float32)
        codes = jnp.concatenate([meta[i : i + 1] for i in range(code_rows)], axis=1)[:, :rows]
        seeds = jnp.where(class_line == codes, 1.0, 0.0).astype(jnp.bfloat16)
        parcel = jnp.dot(seeds, packed[slot, :rows, :], preferred_element_type=jnp.float32)
        parcel = parcel.astype(jnp.bfloat16).astype(jnp.float32)
        for author in range(AT_DEV):
            chosen = meta[code_rows + author : code_rows + author + 1]
            totals[author] = totals[author] + parcel * chosen
    mass = jnp.concatenate([total.T for total in totals], axis=0)
    finish_mass(mass, class_prior, full, half, parts)


def author_kernel(
    slots, rows, paper, packed, gathered, seeds, summed, class_prior, class_target,
    full, half, parts, shares_in, seeds_in, arrived,
):
    classes = full.shape[1]
    code_rows = -(-rows // LANES)
    copies = []
    for slot in range(slots):
        start = pl.multiple_of((slot * (gathered.shape[0] // slots // rows) + paper[slot]) * rows, rows)
        pair = (
            pltpu.make_async_copy(
                gathered.at[pl.ds(start, rows)], shares_in.at[slot], arrived.at[0, slot]
            ),
            pltpu.make_async_copy(
                seeds.at[pl.ds(start, rows)], seeds_in.at[slot], arrived.at[1, slot]
            ),
        )
        for copy in pair:
            copy.start()
        copies.append(pair)
    scale_cols = col_scale(summed, class_target)
    totals = [jnp.zeros((LANES, classes), jnp.float32) for _ in range(AT_DEV)]
    lane = lax.broadcasted_iota(jnp.int32, (rows, classes), 1).astype(jnp.float32)
    for slot in range(slots):
        for copy in copies[slot]:
            copy.wait()
        kernel = shares_in[slot].astype(jnp.float32) * scale_cols
        share = kernel * (keep_share / jnp.sum(kernel, axis=1, keepdims=True))
        code = seeds_in[slot].astype(jnp.float32)
        code = jnp.concatenate([code] * (classes // LANES), axis=1)
        labels = share + jnp.where(code == lane, 1.0 - keep_share, 0.0)
        parcel = lax.dot_general(
            packed[slot, :rows, :],
            labels.astype(jnp.bfloat16),
            (((0,), (0,)), ((), ())),
            preferred_element_type=jnp.float32,
        )
        parcel = parcel.astype(jnp.bfloat16).astype(jnp.float32)
        meta = packed[slot, rows:, :].astype(jnp.float32)
        for author in range(AT_DEV):
            chosen = meta[code_rows + author : code_rows + author + 1, :1]
            totals[author] = totals[author] + parcel * chosen
    finish_mass(jnp.concatenate(totals, axis=0), class_prior, full, half, parts)


def paper_kernel(
    slots, tile_paper, tile_author, tile_count, tiles, gathered, own, summed, class_prior,
    class_target, full, half, parts, scores, mass, shares_in, arrived,
):
    columns = tiles.shape[2]
    copies = []
    for slot in range(slots):
        start = pl.multiple_of((slot * AT_DEV + tile_author[slot]) * columns, columns)
        copy = pltpu.make_async_copy(
            gathered.at[pl.ds(start, columns)], shares_in.at[slot], arrived.at[slot]
        )
        copy.start()
        copies.append(copy)
    scale_cols = col_scale(summed, class_target)
    mass[...] = jnp.zeros_like(mass)
    scaled = own[...] * scale_cols
    scores[...] = scaled * (full.shape[1] / jnp.sum(scaled, axis=1, keepdims=True))
    for slot in range(slots):
        copies[slot].wait()

        @pl.when(slot < tile_count[0])
        def _():
            kernel = shares_in[slot].astype(jnp.float32) * scale_cols
            labels = kernel * (1.0 / jnp.sum(kernel, axis=1, keepdims=True))
            mass[tile_paper[slot]] += jnp.dot(
                tiles[slot], labels.astype(jnp.bfloat16), preferred_element_type=jnp.float32
            )

    finish_mass(mass[...].reshape(full.shape), class_prior, full, half, parts)


def balance_kernel(kernel_ref, summed, class_target, parts):
    kernel = kernel_ref[...]
    scale_rows = row_scale(kernel, col_scale(summed, class_target))
    spread(jnp.sum(scale_rows * kernel, axis=0, keepdims=True), parts)


def final_kernel(kernel_ref, summed, class_target, seeds, out):
    classes = out.shape[1]
    scaled = kernel_ref[...] * col_scale(summed, class_target)
    share = scaled * (1.0 / jnp.sum(scaled, axis=1, keepdims=True))
    code = seeds[...].astype(jnp.float32)
    code = jnp.concatenate([code] * (classes // LANES), axis=1)
    lane = lax.broadcasted_iota(jnp.int32, out.shape, 1).astype(jnp.float32)
    updated = keep_share * share + jnp.where(code == lane, 1.0 - keep_share, 0.0)
    out[...] = classes * updated


def exchange(parts):
    return lax.all_to_all(parts, AXES, split_axis=0, concat_axis=0, tiled=True)


def on_device(
    tile_values,
    tile_paper,
    tile_author,
    tile_count,
    seed_class,
    train_mask,
    class_prior,
    class_target,
):
    f32 = jnp.float32
    bf16 = jnp.bfloat16
    shape = jax.ShapeDtypeStruct
    slots, rows, columns = tile_values.shape
    classes = class_prior.shape[0]
    papers = seed_class.shape[0]
    authors = AT_DEV * columns
    paper_tiles = papers // rows
    devices = lax.axis_size(AXES)
    code_rows = -(-rows // LANES)
    prior = class_prior.reshape(1, classes)
    target = class_target.reshape(1, classes)
    parts = shape((devices, 1, classes), f32)

    code = jnp.where(train_mask == 1, seed_class, -1).astype(f32)
    code_lines = jnp.pad(code.reshape(paper_tiles, rows), ((0, 0), (0, code_rows * LANES - rows)))
    code_lines = code_lines.reshape(paper_tiles, code_rows, LANES)
    code_lines = jnp.pad(code_lines, ((0, 0), (0, META - code_rows), (0, 0)))
    seed_codes = jnp.broadcast_to(code.astype(bf16)[:, None], (papers, LANES))
    seed_codes = lax.optimization_barrier(seed_codes)

    packed = call(
        functools.partial(pack_kernel, slots, rows),
        shape((slots, rows + META, columns), bf16),
        [SMEM, SMEM, SMEM, VMEM, VMEM],
    )(tile_paper, tile_author, tile_count, tile_values, code_lines)
    packed = lax.all_to_all(packed, "blk", split_axis=0, concat_axis=0, tiled=True)
    paper_of = packed[:, rows + code_rows + AT_DEV, 0].astype(jnp.int32)
    seeds_all = lax.all_gather(seed_codes, "blk", tiled=True)

    author_out = (shape((authors, classes), f32), shape((authors, classes), bf16), parts)
    paper_out = (
        shape((papers, classes), f32),
        shape((papers, classes), bf16),
        parts,
        shape((authors, classes), f32),
    )

    def balance(kernel, summed):
        for _ in range(ITERS - 1):
            summed = exchange(call(balance_kernel, parts, [VMEM] * 3)(kernel, summed, target))
        return summed

    for repeat in range(ROUNDS):
        if repeat == 0:
            own, half, local = call(
                functools.partial(first_author_kernel, slots, rows), author_out, [VMEM] * 2
            )(packed, prior)
        else:
            own, half, local = call(
                functools.partial(author_kernel, slots, rows),
                author_out,
                [SMEM, VMEM, ANY, ANY, VMEM, VMEM, VMEM],
                [
                    pltpu.VMEM((slots, rows, classes), bf16),
                    pltpu.VMEM((slots, rows, LANES), bf16),
                    pltpu.SemaphoreType.DMA((2, slots)),
                ],
            )(paper_of, packed, gathered, seeds_all, summed, prior, target)
        gathered = lax.all_gather(half, "blk", tiled=True)
        summed = balance(own, exchange(local))
        kernel, half, local, author_scores = call(
            functools.partial(paper_kernel, slots),
            paper_out,
            [SMEM, SMEM, SMEM, VMEM, ANY, VMEM, VMEM, VMEM, VMEM],
            [
                pltpu.VMEM((paper_tiles, rows, classes), f32),
                pltpu.VMEM((slots, columns, classes), bf16),
                pltpu.SemaphoreType.DMA((slots,)),
            ],
        )(tile_paper, tile_author, tile_count, tile_values, gathered, own, summed, prior, target)
        if repeat + 1 < ROUNDS:
            gathered = lax.all_gather(half, "blk", tiled=True)
        summed = balance(kernel, exchange(local))
    paper_scores = call(final_kernel, shape((papers, classes), f32), [VMEM] * 4)(
        kernel, summed, target, seed_codes
    )
    return paper_scores, author_scores


def solution(mesh):
    placed = (
        P(("grp", "blk"), None, None),
        P(("grp", "blk")),
        P(("grp", "blk")),
        P(("grp", "blk")),
        P(("grp", "blk")),
        P(("grp", "blk")),
        P(),
        P(),
    )
    return jax.shard_map(
        on_device,
        mesh=mesh,
        in_specs=placed,
        out_specs=(P(("grp", "blk"), None), P(("grp", "blk"), None)),
        check_vma=False,
    )
```

```python
import functools

import jax
import jax.numpy as jnp
from jax import lax
from jax.experimental import pallas as pl
from jax.experimental.pallas import tpu as pltpu
from jax.sharding import PartitionSpec as P

AT_DEV = 2
ITERS = 4
ROUNDS = 2
LANES = 128
META = 16

keep_share = 0.8

AXES = ("grp", "blk")
VMEM = pl.BlockSpec(memory_space=pltpu.VMEM)
SMEM = pl.BlockSpec(memory_space=pltpu.SMEM)
HBM = pl.BlockSpec(memory_space=pltpu.HBM)


def call(kernel, out_shape, in_specs, scratch_shapes=()):
    out_specs = jax.tree.map(lambda _: VMEM, out_shape)
    return pl.pallas_call(
        kernel,
        out_shape=out_shape,
        in_specs=in_specs,
        out_specs=out_specs,
        scratch_shapes=list(scratch_shapes),
        compiler_params=pltpu.CompilerParams(vmem_limit_bytes=48 * 1024 * 1024),
    )


def col_scale(parts_ref, target_ref):
    return target_ref[...] / jnp.sum(parts_ref[...], axis=0)


def row_scale(kernel, scale_cols):
    return 1.0 / jnp.sum(kernel * scale_cols, axis=1, keepdims=True)


def spread(value, parts_ref):
    parts_ref[...] = jnp.broadcast_to(value[None], parts_ref.shape)


def split(value):
    high = value.astype(jnp.bfloat16)
    return high, (value - high.astype(jnp.float32)).astype(jnp.bfloat16)


def scale_block(scale_cols):
    wide = jnp.broadcast_to(scale_cols, (LANES, scale_cols.shape[1])).T
    return jnp.concatenate(split(wide), axis=1)


def row_sums(half, block):
    sums = jnp.dot(half, block, preferred_element_type=jnp.float32)
    return sums[:, :LANES] + sums[:, LANES:]


def across(column, classes):
    return jnp.concatenate([column] * (classes // LANES), axis=1)


def dot_rows(left, right):
    return lax.dot_general(
        left, right, (((1,), (1,)), ((), ())), preferred_element_type=jnp.float32
    )


def code_line(lines, rows):
    count = -(-rows // LANES)
    return jnp.concatenate([lines[i : i + 1] for i in range(count)], axis=1)[:, :rows]


def code_column(line, eye):
    wide = jnp.broadcast_to(line, (LANES, line.shape[1])).astype(jnp.bfloat16)
    return dot_rows(eye, wide)


def identity(rows):
    line = lax.broadcasted_iota(jnp.int32, (rows, rows), 0)
    lane = lax.broadcasted_iota(jnp.int32, (rows, rows), 1)
    return jnp.where(line == lane, 1.0, 0.0).astype(jnp.bfloat16)


def seeds_of(line, classes):
    class_line = lax.broadcasted_iota(jnp.int32, (classes, line.shape[1]), 0)
    return jnp.where(class_line.astype(jnp.float32) == line, 1.0, 0.0).astype(jnp.bfloat16)


def pack_kernel(rows, papers_in, authors_in, count_in, tiles, codes, *rest):
    *outs, tile_paper, tile_author, tile_count, arrived, ready = rest
    slots = len(outs)
    me = lax.axis_index("blk")
    scalars = [
        pltpu.make_async_copy(source, target, ready.at[i])
        for i, (source, target) in enumerate(
            zip((papers_in, authors_in, count_in), (tile_paper, tile_author, tile_count))
        )
    ]
    for copy in scalars:
        copy.start()
    copies = []
    for shift, out in enumerate(outs):
        slot = lax.rem(me + shift, slots)
        copy = pltpu.make_async_copy(tiles.at[slot], out.at[pl.ds(0, rows)], arrived.at[shift])
        copy.start()
        copies.append(copy)
    for copy in scalars:
        copy.wait()
    line = lax.broadcasted_iota(jnp.int32, (META, LANES), 0)
    code_rows = -(-rows // LANES)
    for shift, out in enumerate(outs):
        slot = lax.rem(me + shift, slots)
        paper = tile_paper[slot]
        live = slot < tile_count[0]
        block = codes[paper]
        for author in range(AT_DEV):
            chosen = jnp.where(live & (tile_author[slot] == author), 1.0, 0.0)
            block = jnp.where(line == code_rows + author, chosen, block)
        block = jnp.where(line == code_rows + AT_DEV, paper.astype(jnp.float32), block)
        out[rows:, :] = block.astype(jnp.bfloat16)
    for copy in copies:
        copy.wait()


def first_sum_kernel(authors, tile_paper, tile_count, tiles, codes, class_prior, parts):
    slots, rows, columns = tiles.shape
    classes = parts.shape[2]
    ones = jnp.ones((8, columns), jnp.bfloat16)
    total = authors * class_prior[...]
    for paper in range(codes.shape[0]):
        weight = jnp.zeros((rows, columns), jnp.float32)
        for slot in range(slots):
            chosen = (slot < tile_count[0]) & (tile_paper[slot] == paper)
            weight = weight + jnp.where(chosen, tiles[slot].astype(jnp.float32), 0.0)
        high, low = split(weight)
        high, low = split(dot_rows(ones, high) + dot_rows(ones, low))
        seeds = seeds_of(code_line(codes[paper], rows), classes)
        total = total + (dot_rows(high, seeds) + dot_rows(low, seeds))[:1]
    spread(total, parts)


def next_sum(kernel, summed, class_target, parts):
    scale_rows = row_scale(kernel, col_scale(summed, class_target))
    spread(jnp.sum(scale_rows * kernel, axis=0, keepdims=True), parts)


def first_author_kernel(rows, summed, class_prior, class_target, *rest):
    *packed, full, parts = rest
    classes = full.shape[1]
    code_rows = -(-rows // LANES)
    totals = [jnp.zeros((classes, LANES), jnp.float32) for _ in range(AT_DEV)]
    for one in packed:
        meta = one[rows:, :].astype(jnp.float32)
        seeds = seeds_of(code_line(meta, rows), classes)
        parcel = jnp.dot(seeds, one[:rows, :], preferred_element_type=jnp.float32)
        parcel = parcel.astype(jnp.bfloat16).astype(jnp.float32)
        for author in range(AT_DEV):
            chosen = meta[code_rows + author : code_rows + author + 1]
            totals[author] = totals[author] + parcel * chosen
    kernel = jnp.concatenate([total.T for total in totals], axis=0) + class_prior[...]
    full[...] = kernel
    next_sum(kernel, summed, class_target, parts)


def author_kernel(
    rows, paper, gathered, summed, class_prior, class_target, *rest
):
    *packed, full, parts, shares_in, arrived = rest
    slots = len(packed)
    classes = full.shape[1]
    code_rows = -(-rows // LANES)
    paper_tiles = gathered.shape[0] // slots // rows
    me = lax.axis_index("blk")
    copies = []
    for shift in range(slots):
        source = lax.rem(me + slots - shift, slots)
        start = pl.multiple_of((source * paper_tiles + paper[shift]) * rows, rows)
        copy = pltpu.make_async_copy(
            gathered.at[pl.ds(start, rows)], shares_in.at[shift], arrived.at[shift]
        )
        copy.start()
        copies.append(copy)
    scale_cols = col_scale(summed, class_target)
    block = scale_block(scale_cols)
    eye = identity(rows)
    totals = [jnp.zeros((LANES, classes), jnp.float32) for _ in range(AT_DEV)]
    lane = lax.broadcasted_iota(jnp.int32, (rows, classes), 1).astype(jnp.float32)
    for shift, one in enumerate(packed):
        meta = one[rows:, :].astype(jnp.float32)
        code = across(code_column(code_line(meta, rows), eye), classes)
        copies[shift].wait()
        half = shares_in[shift]
        scale_rows = across(keep_share / row_sums(half, block), classes)
        share = half.astype(jnp.float32) * scale_cols * scale_rows
        labels = share + jnp.where(code == lane, 1.0 - keep_share, 0.0)
        parcel = lax.dot_general(
            one[:rows, :],
            labels.astype(jnp.bfloat16),
            (((0,), (0,)), ((), ())),
            preferred_element_type=jnp.float32,
        )
        parcel = parcel.astype(jnp.bfloat16).astype(jnp.float32)
        for author in range(AT_DEV):
            chosen = meta[code_rows + author : code_rows + author + 1, :1]
            totals[author] = totals[author] + parcel * chosen
    kernel = jnp.concatenate(totals, axis=0) + class_prior[...]
    full[...] = kernel
    spread(jnp.sum(kernel, axis=0, keepdims=True), parts)


def paper_kernel(
    tile_paper, tile_author, tile_count, tiles, gathered, own, summed, class_prior,
    class_target, full, half, parts, scores, shares_in, arrived,
):
    slots, rows, columns = tiles.shape
    classes = full.shape[1]
    copies = []
    for slot in range(slots):
        start = pl.multiple_of((slot * AT_DEV + tile_author[slot]) * columns, columns)
        copy = pltpu.make_async_copy(
            gathered.at[pl.ds(start, columns)], shares_in.at[slot], arrived.at[slot]
        )
        copy.start()
        copies.append(copy)
    scale_cols = col_scale(summed, class_target)
    block = scale_block(scale_cols)
    scaled = own[...] * scale_cols
    scores[...] = scaled * (classes / jnp.sum(scaled, axis=1, keepdims=True))
    wide = jnp.concatenate([tiles[slot] for slot in range(slots)], axis=1)
    labels = []
    for slot in range(slots):
        copies[slot].wait()
        kernel = shares_in[slot]
        high, low = split(kernel)
        sums = row_sums(high, block) + jnp.dot(
            low, block[:, :LANES], preferred_element_type=jnp.float32
        )
        share = kernel * scale_cols * across(1.0 / sums, classes)
        labels.append(share.astype(jnp.bfloat16))
    column = jnp.zeros((1, classes), jnp.float32)
    for paper in range(full.shape[0] // rows):
        chosen = []
        for slot in range(slots):
            keep = (slot < tile_count[0]) & (tile_paper[slot] == paper)
            chosen.append(jnp.where(keep, labels[slot], jnp.zeros_like(labels[slot])))
        mass = jnp.dot(wide, jnp.concatenate(chosen, axis=0), preferred_element_type=jnp.float32)
        kernel = mass + class_prior[...]
        full[paper * rows : (paper + 1) * rows, :] = kernel
        half[paper * rows : (paper + 1) * rows, :] = kernel.astype(jnp.bfloat16)
        column = column + jnp.sum(kernel, axis=0, keepdims=True)
    spread(column, parts)


def balance_kernel(kernel_ref, summed, class_target, parts):
    next_sum(kernel_ref[...], summed, class_target, parts)


def final_kernel(rows, kernel_ref, summed, class_target, codes, out):
    classes = out.shape[1]
    scale_cols = col_scale(summed, class_target)
    eye = identity(rows)
    lane = lax.broadcasted_iota(jnp.int32, (rows, classes), 1).astype(jnp.float32)
    for paper in range(codes.shape[0]):
        part = slice(paper * rows, (paper + 1) * rows)
        scaled = kernel_ref[part, :] * scale_cols
        share = scaled * (1.0 / jnp.sum(scaled, axis=1, keepdims=True))
        code = across(code_column(code_line(codes[paper], rows), eye), classes)
        updated = keep_share * share + jnp.where(code == lane, 1.0 - keep_share, 0.0)
        out[part, :] = classes * updated


def exchange(parts):
    return lax.all_to_all(parts, AXES, split_axis=0, concat_axis=0, tiled=True)


def on_device(
    tile_values,
    tile_paper,
    tile_author,
    tile_count,
    seed_class,
    train_mask,
    class_prior,
    class_target,
):
    f32 = jnp.float32
    bf16 = jnp.bfloat16
    i32 = jnp.int32
    shape = jax.ShapeDtypeStruct
    slots, rows, columns = tile_values.shape
    classes = class_prior.shape[0]
    papers = seed_class.shape[0]
    authors = AT_DEV * columns
    paper_tiles = papers // rows
    devices = lax.axis_size(AXES)
    code_rows = -(-rows // LANES)
    prior = class_prior.reshape(1, classes)
    target = class_target.reshape(1, classes)
    parts = shape((devices, 1, classes), f32)

    code = jnp.where(train_mask == 1, seed_class, -1).astype(f32)
    codes = jnp.pad(code.reshape(paper_tiles, rows), ((0, 0), (0, code_rows * LANES - rows)))
    codes = codes.reshape(paper_tiles, code_rows, LANES)
    codes = jnp.pad(codes, ((0, 0), (0, META - code_rows), (0, 0)))

    packed = call(
        functools.partial(pack_kernel, rows),
        (shape((rows + META, columns), bf16),) * slots,
        [HBM, HBM, HBM, HBM, VMEM],
        [
            pltpu.SMEM((slots,), i32),
            pltpu.SMEM((slots,), i32),
            pltpu.SMEM((1,), i32),
            pltpu.SemaphoreType.DMA((slots,)),
            pltpu.SemaphoreType.DMA((3,)),
        ],
    )(tile_paper, tile_author, tile_count, tile_values, codes)
    packed = [
        lax.ppermute(one, "blk", [(i, (i + shift) % slots) for i in range(slots)]) if shift else one
        for shift, one in enumerate(packed)
    ]
    local = call(
        functools.partial(first_sum_kernel, authors), parts, [SMEM, SMEM, VMEM, VMEM, VMEM]
    )(tile_paper, tile_count, tile_values, codes, prior)
    summed = exchange(local)
    paper_of = jnp.stack([one[rows + code_rows + AT_DEV, 0] for one in packed]).astype(i32)
    paper_of, *packed = lax.optimization_barrier((paper_of, *packed))

    author_out = (shape((authors, classes), f32), parts)
    paper_out = (
        shape((papers, classes), f32),
        shape((papers, classes), bf16),
        parts,
        shape((authors, classes), f32),
    )

    def balance(kernel, summed, count):
        for _ in range(count):
            summed = exchange(call(balance_kernel, parts, [VMEM] * 3)(kernel, summed, target))
        return summed

    for repeat in range(ROUNDS):
        if repeat == 0:
            own, local = call(
                functools.partial(first_author_kernel, rows), author_out, [VMEM] * (3 + slots)
            )(summed, prior, target, *packed)
            left = ITERS - 2
        else:
            own, local = call(
                functools.partial(author_kernel, rows),
                author_out,
                [SMEM, HBM] + [VMEM] * (3 + slots),
                [
                    pltpu.VMEM((slots, rows, classes), bf16),
                    pltpu.SemaphoreType.DMA((slots,)),
                ],
            )(paper_of, gathered, summed, prior, target, *packed)
            left = ITERS - 1
        gathered = lax.all_gather(own, "blk", tiled=True)
        summed = balance(own, exchange(local), left)
        kernel, half, local, author_scores = call(
            paper_kernel,
            paper_out,
            [SMEM, SMEM, SMEM, VMEM, HBM, VMEM, VMEM, VMEM, VMEM],
            [
                pltpu.VMEM((slots, columns, classes), f32),
                pltpu.SemaphoreType.DMA((slots,)),
            ],
        )(tile_paper, tile_author, tile_count, tile_values, gathered, own, summed, prior, target)
        if repeat + 1 < ROUNDS:
            gathered = lax.all_gather(half, "blk", tiled=True)
        summed = balance(kernel, exchange(local), ITERS - 1)
    paper_scores = call(
        functools.partial(final_kernel, rows), shape((papers, classes), f32), [VMEM] * 4
    )(kernel, summed, target, codes)
    return paper_scores, author_scores


def solution(mesh):
    placed = (
        P(("grp", "blk"), None, None),
        P(("grp", "blk")),
        P(("grp", "blk")),
        P(("grp", "blk")),
        P(("grp", "blk")),
        P(("grp", "blk")),
        P(),
        P(),
    )
    return jax.shard_map(
        on_device,
        mesh=mesh,
        in_specs=placed,
        out_specs=(P(("grp", "blk"), None), P(("grp", "blk"), None)),
        check_vma=False,
    )
```

```python
import functools

import jax
import jax.numpy as jnp
from jax import lax
from jax.experimental import pallas as pl
from jax.experimental.pallas import tpu as pltpu
from jax.sharding import PartitionSpec as P

AT_DEV = 2
ITERS = 4
ROUNDS = 2
LANES = 128
META = 16

keep_share = 0.8

AXES = ("grp", "blk")
VMEM = pl.BlockSpec(memory_space=pltpu.VMEM)
SMEM = pl.BlockSpec(memory_space=pltpu.SMEM)
HBM = pl.BlockSpec(memory_space=pltpu.HBM)


def call(kernel, out_shape, in_specs, scratch_shapes=(), out_specs=None):
    if out_specs is None:
        out_specs = jax.tree.map(lambda _: VMEM, out_shape)
    return pl.pallas_call(
        kernel,
        out_shape=out_shape,
        in_specs=in_specs,
        out_specs=out_specs,
        scratch_shapes=list(scratch_shapes),
        compiler_params=pltpu.CompilerParams(vmem_limit_bytes=48 * 1024 * 1024),
    )


def col_scale(parts_ref, target_ref):
    return target_ref[...] / jnp.sum(parts_ref[...], axis=0)


def row_scale(kernel, scale_cols):
    return 1.0 / jnp.sum(kernel * scale_cols, axis=1, keepdims=True)


def spread(value, parts_ref):
    parts_ref[...] = jnp.broadcast_to(value[None], parts_ref.shape)


def split(value):
    high = value.astype(jnp.bfloat16)
    return high, (value - high.astype(jnp.float32)).astype(jnp.bfloat16)


def scale_block(scale_cols):
    wide = jnp.broadcast_to(scale_cols, (LANES, scale_cols.shape[1])).T
    return jnp.concatenate(split(wide), axis=1)


def row_sums(half, block):
    sums = jnp.dot(half, block, preferred_element_type=jnp.float32)
    return sums[:, :LANES] + sums[:, LANES:]


def across(column, classes):
    return jnp.concatenate([column] * (classes // LANES), axis=1)


def dot_rows(left, right):
    return lax.dot_general(
        left, right, (((1,), (1,)), ((), ())), preferred_element_type=jnp.float32
    )


def code_lines(seed_class, train_mask, rows):
    code = jnp.where(train_mask[...] == 1, seed_class[...], -1).astype(jnp.float32)
    line = jnp.concatenate([code[i : i + 1] for i in range(code.shape[0])], axis=1)
    papers = line.shape[1]
    wide = jnp.broadcast_to(line, (8, papers))
    lines = []
    for start in range(0, papers, rows):
        lines.append((pltpu.roll(wide, papers - start, 1) if start else wide)[:1, :rows])
    return lines


def meta_line(meta, rows):
    count = -(-rows // LANES)
    return jnp.concatenate([meta[i : i + 1] for i in range(count)], axis=1)[:, :rows]


def code_column(line, eye):
    wide = jnp.broadcast_to(line, (LANES, line.shape[1])).astype(jnp.bfloat16)
    return dot_rows(eye, wide)


def identity(rows):
    line = lax.broadcasted_iota(jnp.int32, (rows, rows), 0)
    lane = lax.broadcasted_iota(jnp.int32, (rows, rows), 1)
    return jnp.where(line == lane, 1.0, 0.0).astype(jnp.bfloat16)


def seeds_of(line, classes):
    class_line = lax.broadcasted_iota(jnp.int32, (classes, line.shape[1]), 0)
    return jnp.where(class_line.astype(jnp.float32) == line, 1.0, 0.0).astype(jnp.bfloat16)


def pack_kernel(rows, tile_count, *refs):
    count = 7
    ins, places, outs = refs[:count], refs[count : 2 * count], refs[2 * count : -2]
    ready, arrived = refs[-2:]
    tile_paper, tile_author, seed_class, train_mask = places[:4]
    tiles = ins[-1]
    slots = len(outs)
    me = lax.axis_index("blk")
    moves = [
        pltpu.make_async_copy(source, place, ready.at[i])
        for i, (source, place) in enumerate(zip(ins, places))
    ]
    for copy in moves:
        copy.start()
    copies = []
    for shift, out in enumerate(outs):
        slot = lax.rem(me + shift, slots)
        copy = pltpu.make_async_copy(tiles.at[slot], out.at[pl.ds(0, rows)], arrived.at[shift])
        copy.start()
        copies.append(copy)
    for copy in moves[:4]:
        copy.wait()
    line = lax.broadcasted_iota(jnp.int32, (META, LANES), 0)
    code_rows = -(-rows // LANES)
    blocks = []
    for codes in code_lines(seed_class, train_mask, rows):
        pad = jnp.full((1, code_rows * LANES - rows), -1.0, jnp.float32)
        codes = jnp.concatenate([codes, pad], axis=1)
        block = jnp.zeros((META, LANES), jnp.float32)
        for i in range(code_rows):
            block = jnp.where(line == i, codes[:, i * LANES : (i + 1) * LANES], block)
        blocks.append(block)
    for shift, out in enumerate(outs):
        slot = lax.rem(me + shift, slots)
        paper = tile_paper[slot]
        live = slot < tile_count[0]
        block = blocks[0]
        for i in range(1, len(blocks)):
            block = jnp.where(paper == i, blocks[i], block)
        for author in range(AT_DEV):
            chosen = jnp.where(live & (tile_author[slot] == author), 1.0, 0.0)
            block = jnp.where(line == code_rows + author, chosen, block)
        block = jnp.where(line == code_rows + AT_DEV, paper.astype(jnp.float32), block)
        out[rows:, :] = block.astype(jnp.bfloat16)
    for copy in moves[4:] + copies:
        copy.wait()


def first_sum_kernel(
    authors, tile_paper, tile_count, tiles, seed_class, train_mask, class_prior, parts
):
    slots, rows, columns = tiles.shape
    classes = parts.shape[2]
    ones = jnp.ones((8, columns), jnp.bfloat16)
    total = authors * class_prior[...]
    for paper, codes in enumerate(code_lines(seed_class, train_mask, rows)):
        weight = jnp.zeros((rows, columns), jnp.float32)
        for slot in range(slots):
            chosen = (slot < tile_count[0]) & (tile_paper[slot] == paper)
            weight = weight + jnp.where(chosen, tiles[slot].astype(jnp.float32), 0.0)
        high, low = split(weight)
        high, low = split(dot_rows(ones, high) + dot_rows(ones, low))
        seeds = seeds_of(codes, classes)
        total = total + (dot_rows(high, seeds) + dot_rows(low, seeds))[:1]
    spread(total, parts)


def next_sum(kernel, summed, class_target, parts):
    scale_rows = row_scale(kernel, col_scale(summed, class_target))
    spread(jnp.sum(scale_rows * kernel, axis=0, keepdims=True), parts)


def first_author_kernel(rows, summed, class_prior, class_target, *rest):
    *packed, full, sent, parts = rest
    classes = full.shape[1]
    code_rows = -(-rows // LANES)
    totals = [jnp.zeros((classes, LANES), jnp.float32) for _ in range(AT_DEV)]
    for one in packed:
        meta = one[rows:, :].astype(jnp.float32)
        seeds = seeds_of(meta_line(meta, rows), classes)
        parcel = jnp.dot(seeds, one[:rows, :], preferred_element_type=jnp.float32)
        parcel = parcel.astype(jnp.bfloat16).astype(jnp.float32)
        for author in range(AT_DEV):
            chosen = meta[code_rows + author : code_rows + author + 1]
            totals[author] = totals[author] + parcel * chosen
    kernel = jnp.concatenate([total.T for total in totals], axis=0) + class_prior[...]
    full[...] = kernel
    sent[...] = kernel
    next_sum(kernel, summed, class_target, parts)


def author_kernel(rows, gathered, summed, class_prior, class_target, *rest):
    *packed, full, sent, parts, shares_in, arrived = rest
    slots = len(packed)
    classes = full.shape[1]
    code_rows = -(-rows // LANES)
    paper_tiles = gathered.shape[0] // slots // rows
    me = lax.axis_index("blk")
    metas = [one[rows:, :].astype(jnp.float32) for one in packed]
    copies = []
    for shift in range(slots):
        source = lax.rem(me + slots - shift, slots)
        at = code_rows + AT_DEV
        paper = jnp.max(metas[shift][at : at + 1]).astype(jnp.int32)
        start = pl.multiple_of((source * paper_tiles + paper) * rows, rows)
        copy = pltpu.make_async_copy(
            gathered.at[pl.ds(start, rows)], shares_in.at[shift], arrived.at[shift]
        )
        copy.start()
        copies.append(copy)
    scale_cols = col_scale(summed, class_target)
    block = scale_block(scale_cols)
    eye = identity(rows)
    codes = [code_column(meta_line(meta, rows), eye) for meta in metas]
    totals = [jnp.zeros((LANES, classes), jnp.float32) for _ in range(AT_DEV)]
    lane = lax.broadcasted_iota(jnp.int32, (rows, classes), 1).astype(jnp.float32)
    for copy in copies:
        copy.wait()
    for shift, one in enumerate(packed):
        half = shares_in[shift]
        scale_rows = across(keep_share / row_sums(half, block), classes)
        share = half.astype(jnp.float32) * scale_cols * scale_rows
        labels = share + jnp.where(across(codes[shift], classes) == lane, 1.0 - keep_share, 0.0)
        parcel = lax.dot_general(
            one[:rows, :],
            labels.astype(jnp.bfloat16),
            (((0,), (0,)), ((), ())),
            preferred_element_type=jnp.float32,
        )
        parcel = parcel.astype(jnp.bfloat16).astype(jnp.float32)
        for author in range(AT_DEV):
            at = code_rows + author
            totals[author] = totals[author] + parcel * metas[shift][at : at + 1, :1]
    kernel = jnp.concatenate(totals, axis=0) + class_prior[...]
    full[...] = kernel
    sent[...] = kernel
    spread(jnp.sum(kernel, axis=0, keepdims=True), parts)


def paper_kernel(
    tile_paper, tile_author, tile_count, tiles, gathered, summed, class_prior, class_target,
    full, half, parts, shares_in, arrived,
):
    slots, rows, columns = tiles.shape
    classes = full.shape[1]
    copies = []
    for slot in range(slots):
        start = pl.multiple_of((slot * AT_DEV + tile_author[slot]) * columns, columns)
        copy = pltpu.make_async_copy(
            gathered.at[pl.ds(start, columns)], shares_in.at[slot], arrived.at[slot]
        )
        copy.start()
        copies.append(copy)
    scale_cols = col_scale(summed, class_target)
    block = scale_block(scale_cols)
    wide = jnp.concatenate([tiles[slot] for slot in range(slots)], axis=1)
    labels = []
    for copy in copies:
        copy.wait()
    for slot in range(slots):
        kernel = shares_in[slot]
        high, low = split(kernel)
        sums = row_sums(high, block) + jnp.dot(
            low, block[:, :LANES], preferred_element_type=jnp.float32
        )
        share = kernel * scale_cols * across(1.0 / sums, classes)
        labels.append(share.astype(jnp.bfloat16))
    column = jnp.zeros((1, classes), jnp.float32)
    for paper in range(full.shape[0] // rows):
        chosen = []
        for slot in range(slots):
            keep = (slot < tile_count[0]) & (tile_paper[slot] == paper)
            chosen.append(jnp.where(keep, labels[slot], jnp.zeros_like(labels[slot])))
        mass = jnp.dot(wide, jnp.concatenate(chosen, axis=0), preferred_element_type=jnp.float32)
        kernel = mass + class_prior[...]
        full[paper * rows : (paper + 1) * rows, :] = kernel
        half[paper * rows : (paper + 1) * rows, :] = kernel.astype(jnp.bfloat16)
        column = column + jnp.sum(kernel, axis=0, keepdims=True)
    spread(column, parts)


def balance_kernel(kernel_ref, summed, class_target, parts):
    next_sum(kernel_ref[...], summed, class_target, parts)


def final_kernel(
    rows, kernel_ref, summed, own, author_summed, class_target, seed_class, train_mask, out, scores
):
    classes = out.shape[1]
    scaled = own[...] * col_scale(author_summed, class_target)
    scores[...] = scaled * (classes / jnp.sum(scaled, axis=1, keepdims=True))
    scale_cols = col_scale(summed, class_target)
    eye = identity(rows)
    lane = lax.broadcasted_iota(jnp.int32, (rows, classes), 1).astype(jnp.float32)
    for paper, line in enumerate(code_lines(seed_class, train_mask, rows)):
        part = slice(paper * rows, (paper + 1) * rows)
        scaled = kernel_ref[part, :] * scale_cols
        share = scaled * (1.0 / jnp.sum(scaled, axis=1, keepdims=True))
        code = across(code_column(line, eye), classes)
        updated = keep_share * share + jnp.where(code == lane, 1.0 - keep_share, 0.0)
        out[part, :] = classes * updated


def in_hbm(value):
    return pltpu.with_memory_space_constraint(value, pltpu.HBM)


def exchange(parts):
    return lax.all_to_all(parts, AXES, split_axis=0, concat_axis=0, tiled=True)


def on_device(
    tile_values,
    tile_paper,
    tile_author,
    tile_count,
    seed_class,
    train_mask,
    class_prior,
    class_target,
):
    f32 = jnp.float32
    bf16 = jnp.bfloat16
    shape = jax.ShapeDtypeStruct
    slots, rows, columns = tile_values.shape
    classes = class_prior.shape[0]
    papers = seed_class.shape[0]
    authors = AT_DEV * columns
    paper_tiles = papers // rows
    devices = lax.axis_size(AXES)
    prior = class_prior.reshape(1, classes)
    target = class_target.reshape(1, classes)
    seed_class = seed_class.reshape(papers // LANES, LANES)
    train_mask = train_mask.reshape(papers // LANES, LANES)
    parts = shape((devices, 1, classes), f32)

    inputs = (
        tile_paper, tile_author, seed_class, train_mask, prior, target, tile_values,
    )
    places = (SMEM, SMEM, VMEM, VMEM, VMEM, VMEM, VMEM)
    moved = call(
        functools.partial(pack_kernel, rows),
        tuple(shape(one.shape, one.dtype) for one in inputs)
        + (shape((rows + META, columns), bf16),) * slots,
        [SMEM] + [HBM] * len(inputs),
        [pltpu.SemaphoreType.DMA((len(inputs),)), pltpu.SemaphoreType.DMA((slots,))],
        places + (VMEM,) * slots,
    )(tile_count, *(in_hbm(one) for one in inputs))
    packed = moved[len(inputs) :]
    tile_paper, tile_author, seed_class, train_mask, prior, target, tile_values = (
        moved[: len(inputs)]
    )
    packed = [
        lax.ppermute(one, "blk", [(i, (i + shift) % slots) for i in range(slots)]) if shift else one
        for shift, one in enumerate(packed)
    ]
    local = call(
        functools.partial(first_sum_kernel, authors), parts, [SMEM, SMEM] + [VMEM] * 4
    )(tile_paper, tile_count, tile_values, seed_class, train_mask, prior)
    summed = exchange(local)

    author_out = (shape((authors, classes), f32), shape((authors, classes), f32), parts)
    paper_out = (shape((papers, classes), f32), shape((papers, classes), bf16), parts)

    def balance(kernel, summed, count):
        for _ in range(count):
            summed = exchange(call(balance_kernel, parts, [VMEM] * 3)(kernel, summed, target))
        return summed

    for repeat in range(ROUNDS):
        if repeat == 0:
            own, sent, local = call(
                functools.partial(first_author_kernel, rows), author_out, [VMEM] * (3 + slots)
            )(summed, prior, target, *packed)
            left = ITERS - 2
        else:
            own, sent, local = call(
                functools.partial(author_kernel, rows),
                author_out,
                [HBM] + [VMEM] * (3 + slots),
                [
                    pltpu.VMEM((slots, rows, classes), bf16),
                    pltpu.SemaphoreType.DMA((slots,)),
                ],
            )(in_hbm(gathered), summed, prior, target, *packed)
            left = ITERS - 1
        gathered = lax.all_gather(sent, "blk", tiled=True)
        author_summed = balance(own, exchange(local), left)
        kernel, half, local = call(
            paper_kernel,
            paper_out,
            [SMEM, SMEM, SMEM, VMEM, HBM, VMEM, VMEM, VMEM],
            [
                pltpu.VMEM((slots, columns, classes), f32),
                pltpu.SemaphoreType.DMA((slots,)),
            ],
        )(
            tile_paper, tile_author, tile_count, tile_values, in_hbm(gathered), author_summed,
            prior, target,
        )
        if repeat + 1 < ROUNDS:
            gathered = lax.all_gather(half, "blk", tiled=True)
        summed = balance(kernel, exchange(local), ITERS - 1)
    return call(
        functools.partial(final_kernel, rows),
        (shape((papers, classes), f32), shape((authors, classes), f32)),
        [VMEM] * 7,
    )(kernel, summed, own, author_summed, target, seed_class, train_mask)


def solution(mesh):
    placed = (
        P(("grp", "blk"), None, None),
        P(("grp", "blk")),
        P(("grp", "blk")),
        P(("grp", "blk")),
        P(("grp", "blk")),
        P(("grp", "blk")),
        P(),
        P(),
    )
    return jax.shard_map(
        on_device,
        mesh=mesh,
        in_specs=placed,
        out_specs=(P(("grp", "blk"), None), P(("grp", "blk"), None)),
        check_vma=False,
    )
```

```python
import functools

import jax
import jax.numpy as jnp
from jax import lax
from jax.experimental import pallas as pl
from jax.experimental.pallas import tpu as pltpu
from jax.sharding import PartitionSpec as P

AT_DEV = 2
ITERS = 4
ROUNDS = 2
LANES = 128
META = 16

keep_share = 0.8

AXES = ("grp", "blk")
VMEM = pl.BlockSpec(memory_space=pltpu.VMEM)
SMEM = pl.BlockSpec(memory_space=pltpu.SMEM)
HBM = pl.BlockSpec(memory_space=pltpu.HBM)


def call(kernel, out_shape, in_specs, scratch_shapes=(), out_specs=None):
    if out_specs is None:
        out_specs = jax.tree.map(lambda _: VMEM, out_shape)
    return pl.pallas_call(
        kernel,
        out_shape=out_shape,
        in_specs=in_specs,
        out_specs=out_specs,
        scratch_shapes=list(scratch_shapes),
        compiler_params=pltpu.CompilerParams(vmem_limit_bytes=48 * 1024 * 1024),
    )


def col_scale(parts_ref, target_ref):
    return target_ref[...] / jnp.sum(parts_ref[...], axis=0)


def row_scale(kernel, scale_cols):
    return 1.0 / jnp.sum(kernel * scale_cols, axis=1, keepdims=True)


def spread(value, parts_ref):
    parts_ref[...] = jnp.broadcast_to(value[None], parts_ref.shape)


def split(value):
    high = value.astype(jnp.bfloat16)
    return high, (value - high.astype(jnp.float32)).astype(jnp.bfloat16)


def scale_block(scale_cols):
    wide = jnp.broadcast_to(scale_cols, (LANES, scale_cols.shape[1])).T
    return jnp.concatenate(split(wide), axis=1)


def row_sums(half, block):
    sums = jnp.dot(half, block, preferred_element_type=jnp.float32)
    return sums[:, :LANES] + sums[:, LANES:]


def across(column, classes):
    return jnp.concatenate([column] * (classes // LANES), axis=1)


def dot_rows(left, right):
    return lax.dot_general(
        left, right, (((1,), (1,)), ((), ())), preferred_element_type=jnp.float32
    )


def code_lines(seed_class, train_mask, rows):
    code = jnp.where(train_mask[...] == 1, seed_class[...], -1).astype(jnp.float32)
    line = jnp.concatenate([code[i : i + 1] for i in range(code.shape[0])], axis=1)
    papers = line.shape[1]
    wide = jnp.broadcast_to(line, (8, papers))
    lines = []
    for start in range(0, papers, rows):
        lines.append((pltpu.roll(wide, papers - start, 1) if start else wide)[:1, :rows])
    return lines


def meta_line(meta, rows):
    count = -(-rows // LANES)
    return jnp.concatenate([meta[i : i + 1] for i in range(count)], axis=1)[:, :rows]


def code_column(line, eye):
    wide = jnp.broadcast_to(line, (LANES, line.shape[1])).astype(jnp.bfloat16)
    return dot_rows(eye, wide)


def identity(rows):
    line = lax.broadcasted_iota(jnp.int32, (rows, rows), 0)
    lane = lax.broadcasted_iota(jnp.int32, (rows, rows), 1)
    return jnp.where(line == lane, 1.0, 0.0).astype(jnp.bfloat16)


def seeds_of(line, classes):
    class_line = lax.broadcasted_iota(jnp.int32, (classes, line.shape[1]), 0)
    return jnp.where(class_line.astype(jnp.float32) == line, 1.0, 0.0).astype(jnp.bfloat16)


def pack_kernel(rows, tile_count, *refs):
    count = 7
    ins, places = refs[:count], refs[count : 2 * count]
    keep, swap, ready, arrived = refs[2 * count :]
    tile_paper, tile_author, seed_class, train_mask = places[:4]
    tiles = ins[-1]
    pairs = keep.shape[0]
    me = lax.axis_index("blk")
    pair, side = lax.div(me, 2), lax.rem(me, 2)
    moves = [
        pltpu.make_async_copy(source, place, ready.at[i])
        for i, (source, place) in enumerate(zip(ins, places))
    ]
    for copy in moves:
        copy.start()
    outs = []
    copies = []
    for k in range(pairs):
        for way, (out, to) in enumerate(((keep, side), (swap, 1 - side))):
            slot = 2 * lax.bitwise_xor(pair, k) + to
            copy = pltpu.make_async_copy(
                tiles.at[slot], out.at[k, pl.ds(0, rows)], arrived.at[way, k]
            )
            copy.start()
            copies.append(copy)
            outs.append((out, k, slot))
    for copy in moves[:4]:
        copy.wait()
    line = lax.broadcasted_iota(jnp.int32, (META, LANES), 0)
    code_rows = -(-rows // LANES)
    blocks = []
    for codes in code_lines(seed_class, train_mask, rows):
        pad = jnp.full((1, code_rows * LANES - rows), -1.0, jnp.float32)
        codes = jnp.concatenate([codes, pad], axis=1)
        block = jnp.zeros((META, LANES), jnp.float32)
        for i in range(code_rows):
            block = jnp.where(line == i, codes[:, i * LANES : (i + 1) * LANES], block)
        blocks.append(block)
    for out, k, slot in outs:
        paper = tile_paper[slot]
        live = slot < tile_count[0]
        block = blocks[0]
        for i in range(1, len(blocks)):
            block = jnp.where(paper == i, blocks[i], block)
        for author in range(AT_DEV):
            chosen = jnp.where(live & (tile_author[slot] == author), 1.0, 0.0)
            block = jnp.where(line == code_rows + author, chosen, block)
        block = jnp.where(line == code_rows + AT_DEV, paper.astype(jnp.float32), block)
        out[k, rows:, :] = block.astype(jnp.bfloat16)
    for copy in moves[4:] + copies:
        copy.wait()


def pair_kernel(keep, swapped, *outs):
    for k, out in enumerate(outs, 1):
        out[0] = keep[k]
        out[1] = swapped[k]


def slots_of(keep, swapped, *pairs):
    me = lax.axis_index("blk")
    pair, side = lax.div(me, 2), lax.rem(me, 2)
    held = [(keep, 0, me), (swapped, 0, 2 * pair + 1 - side)]
    for k, ref in enumerate(pairs, 1):
        other = 2 * lax.bitwise_xor(pair, k)
        held += [(ref, 0, other + side), (ref, 1, other + 1 - side)]
    return held


def first_sum_kernel(
    authors, tile_paper, tile_count, tiles, seed_class, train_mask, class_prior, parts
):
    slots, rows, columns = tiles.shape
    classes = parts.shape[2]
    ones = jnp.ones((8, columns), jnp.bfloat16)
    total = authors * class_prior[...]
    for paper, codes in enumerate(code_lines(seed_class, train_mask, rows)):
        weight = jnp.zeros((rows, columns), jnp.float32)
        for slot in range(slots):
            chosen = (slot < tile_count[0]) & (tile_paper[slot] == paper)
            weight = weight + jnp.where(chosen, tiles[slot].astype(jnp.float32), 0.0)
        high, low = split(weight)
        high, low = split(dot_rows(ones, high) + dot_rows(ones, low))
        seeds = seeds_of(codes, classes)
        total = total + (dot_rows(high, seeds) + dot_rows(low, seeds))[:1]
    spread(total, parts)


def next_sum(kernel, summed, class_target, parts):
    scale_rows = row_scale(kernel, col_scale(summed, class_target))
    spread(jnp.sum(scale_rows * kernel, axis=0, keepdims=True), parts)


def first_author_kernel(rows, summed, class_prior, class_target, *rest):
    *held, full, sent, parts = rest
    classes = full.shape[1]
    code_rows = -(-rows // LANES)
    totals = [jnp.zeros((classes, LANES), jnp.float32) for _ in range(AT_DEV)]
    for ref, place, _ in slots_of(*held):
        meta = ref[place, rows:, :].astype(jnp.float32)
        seeds = seeds_of(meta_line(meta, rows), classes)
        parcel = jnp.dot(seeds, ref[place, :rows, :], preferred_element_type=jnp.float32)
        parcel = parcel.astype(jnp.bfloat16).astype(jnp.float32)
        for author in range(AT_DEV):
            chosen = meta[code_rows + author : code_rows + author + 1]
            totals[author] = totals[author] + parcel * chosen
    kernel = jnp.concatenate([total.T for total in totals], axis=0) + class_prior[...]
    full[...] = kernel
    sent[...] = kernel
    next_sum(kernel, summed, class_target, parts)


def author_kernel(rows, gathered, summed, class_prior, class_target, *rest):
    *held, full, sent, parts, shares_in, arrived = rest
    held = slots_of(*held)
    slots = len(held)
    classes = full.shape[1]
    code_rows = -(-rows // LANES)
    paper_tiles = gathered.shape[0] // slots // rows
    metas = [ref[place, rows:, :].astype(jnp.float32) for ref, place, _ in held]
    copies = []
    for shift, (_, _, source) in enumerate(held):
        at = code_rows + AT_DEV
        paper = jnp.max(metas[shift][at : at + 1]).astype(jnp.int32)
        start = pl.multiple_of((source * paper_tiles + paper) * rows, rows)
        copy = pltpu.make_async_copy(
            gathered.at[pl.ds(start, rows)], shares_in.at[shift], arrived.at[shift]
        )
        copy.start()
        copies.append(copy)
    scale_cols = col_scale(summed, class_target)
    block = scale_block(scale_cols)
    eye = identity(rows)
    codes = [code_column(meta_line(meta, rows), eye) for meta in metas]
    totals = [jnp.zeros((LANES, classes), jnp.float32) for _ in range(AT_DEV)]
    lane = lax.broadcasted_iota(jnp.int32, (rows, classes), 1).astype(jnp.float32)
    for copy in copies:
        copy.wait()
    for shift, (ref, place, _) in enumerate(held):
        half = shares_in[shift]
        scale_rows = across(keep_share / row_sums(half, block), classes)
        share = half.astype(jnp.float32) * scale_cols * scale_rows
        labels = share + jnp.where(across(codes[shift], classes) == lane, 1.0 - keep_share, 0.0)
        parcel = lax.dot_general(
            ref[place, :rows, :],
            labels.astype(jnp.bfloat16),
            (((0,), (0,)), ((), ())),
            preferred_element_type=jnp.float32,
        )
        parcel = parcel.astype(jnp.bfloat16).astype(jnp.float32)
        for author in range(AT_DEV):
            at = code_rows + author
            totals[author] = totals[author] + parcel * metas[shift][at : at + 1, :1]
    kernel = jnp.concatenate(totals, axis=0) + class_prior[...]
    full[...] = kernel
    sent[...] = kernel
    spread(jnp.sum(kernel, axis=0, keepdims=True), parts)


def paper_kernel(
    tile_paper, tile_author, tile_count, tiles, gathered, summed, class_prior, class_target,
    full, parts, *rest,
):
    *half, shares_in, arrived = rest
    slots, rows, columns = tiles.shape
    classes = full.shape[1]
    copies = []
    for slot in range(slots):
        start = pl.multiple_of((slot * AT_DEV + tile_author[slot]) * columns, columns)
        copy = pltpu.make_async_copy(
            gathered.at[pl.ds(start, columns)], shares_in.at[slot], arrived.at[slot]
        )
        copy.start()
        copies.append(copy)
    scale_cols = col_scale(summed, class_target)
    block = scale_block(scale_cols)
    wide = jnp.concatenate([tiles[slot] for slot in range(slots)], axis=1)
    labels = []
    for copy in copies:
        copy.wait()
    for slot in range(slots):
        kernel = shares_in[slot]
        high, low = split(kernel)
        sums = row_sums(high, block) + jnp.dot(
            low, block[:, :LANES], preferred_element_type=jnp.float32
        )
        share = kernel * scale_cols * across(1.0 / sums, classes)
        labels.append(share.astype(jnp.bfloat16))
    column = jnp.zeros((1, classes), jnp.float32)
    for paper in range(full.shape[0] // rows):
        chosen = []
        for slot in range(slots):
            keep = (slot < tile_count[0]) & (tile_paper[slot] == paper)
            chosen.append(jnp.where(keep, labels[slot], jnp.zeros_like(labels[slot])))
        mass = jnp.dot(wide, jnp.concatenate(chosen, axis=0), preferred_element_type=jnp.float32)
        kernel = mass + class_prior[...]
        full[paper * rows : (paper + 1) * rows, :] = kernel
        for out in half:
            out[paper * rows : (paper + 1) * rows, :] = kernel.astype(jnp.bfloat16)
        column = column + jnp.sum(kernel, axis=0, keepdims=True)
    spread(column, parts)


def balance_kernel(kernel_ref, summed, class_target, parts):
    next_sum(kernel_ref[...], summed, class_target, parts)


def final_kernel(
    rows, kernel_ref, summed, own, author_summed, class_target, seed_class, train_mask, out, scores
):
    classes = out.shape[1]
    scaled = own[...] * col_scale(author_summed, class_target)
    scores[...] = scaled * (classes / jnp.sum(scaled, axis=1, keepdims=True))
    scale_cols = col_scale(summed, class_target)
    eye = identity(rows)
    lane = lax.broadcasted_iota(jnp.int32, (rows, classes), 1).astype(jnp.float32)
    for paper, line in enumerate(code_lines(seed_class, train_mask, rows)):
        part = slice(paper * rows, (paper + 1) * rows)
        scaled = kernel_ref[part, :] * scale_cols
        share = scaled * (1.0 / jnp.sum(scaled, axis=1, keepdims=True))
        code = across(code_column(line, eye), classes)
        updated = keep_share * share + jnp.where(code == lane, 1.0 - keep_share, 0.0)
        out[part, :] = classes * updated


def in_hbm(value):
    return pltpu.with_memory_space_constraint(value, pltpu.HBM)


def exchange(parts):
    return lax.all_to_all(parts, AXES, split_axis=0, concat_axis=0, tiled=True)


def on_device(
    tile_values,
    tile_paper,
    tile_author,
    tile_count,
    seed_class,
    train_mask,
    class_prior,
    class_target,
):
    f32 = jnp.float32
    bf16 = jnp.bfloat16
    shape = jax.ShapeDtypeStruct
    slots, rows, columns = tile_values.shape
    classes = class_prior.shape[0]
    papers = seed_class.shape[0]
    authors = AT_DEV * columns
    paper_tiles = papers // rows
    devices = lax.axis_size(AXES)
    prior = class_prior.reshape(1, classes)
    target = class_target.reshape(1, classes)
    seed_class = seed_class.reshape(papers // LANES, LANES)
    train_mask = train_mask.reshape(papers // LANES, LANES)
    parts = shape((devices, 1, classes), f32)

    inputs = (
        tile_paper, tile_author, seed_class, train_mask, prior, target, tile_values,
    )
    places = (SMEM, SMEM, VMEM, VMEM, VMEM, VMEM, VMEM)
    blocks = lax.axis_size("blk")
    load = shape((blocks // 2, rows + META, columns), bf16)
    moved = call(
        functools.partial(pack_kernel, rows),
        tuple(shape(one.shape, one.dtype) for one in inputs) + (load, load),
        [SMEM] + [HBM] * len(inputs),
        [pltpu.SemaphoreType.DMA((len(inputs),)), pltpu.SemaphoreType.DMA((2, blocks // 2))],
        places + (VMEM, VMEM),
    )(tile_count, *(in_hbm(one) for one in inputs))
    tile_paper, tile_author, seed_class, train_mask, prior, target, tile_values, keep, swap = moved
    swapped = lax.ppermute(swap, "blk", [(i, i ^ 1) for i in range(blocks)])
    local = call(
        functools.partial(first_sum_kernel, authors), parts, [SMEM, SMEM] + [VMEM] * 4
    )(tile_paper, tile_count, tile_values, seed_class, train_mask, prior)
    both = shape((2, rows + META, columns), bf16)
    pairs = call(pair_kernel, (both,) * (blocks // 2 - 1), [VMEM] * 2)(keep, swapped)
    local, *pairs = lax.optimization_barrier((local, *pairs))
    held = [keep, swapped] + [
        lax.ppermute(one, "blk", [(i, i ^ (2 * k)) for i in range(blocks)])
        for k, one in enumerate(pairs, 1)
    ]
    summed = exchange(local)

    author_out = (shape((authors, classes), f32), shape((authors, classes), f32), parts)
    paper_out = (shape((papers, classes), f32), parts, shape((papers, classes), bf16))

    def balance(kernel, summed, count):
        for _ in range(count):
            summed = exchange(call(balance_kernel, parts, [VMEM] * 3)(kernel, summed, target))
        return summed

    for repeat in range(ROUNDS):
        if repeat == 0:
            own, sent, local = call(
                functools.partial(first_author_kernel, rows), author_out, [VMEM] * (3 + len(held))
            )(summed, prior, target, *held)
            left = ITERS - 2
        else:
            own, sent, local = call(
                functools.partial(author_kernel, rows),
                author_out,
                [HBM] + [VMEM] * (3 + len(held)),
                [
                    pltpu.VMEM((slots, rows, classes), bf16),
                    pltpu.SemaphoreType.DMA((slots,)),
                ],
            )(in_hbm(gathered), summed, prior, target, *held)
            left = ITERS - 1
        gathered = lax.all_gather(sent, "blk", tiled=True)
        author_summed = balance(own, exchange(local), left)
        last = repeat + 1 == ROUNDS
        kernel, local, *half = call(
            paper_kernel,
            paper_out[:2] if last else paper_out,
            [SMEM, SMEM, SMEM, VMEM, HBM, VMEM, VMEM, VMEM],
            [
                pltpu.VMEM((slots, columns, classes), f32),
                pltpu.SemaphoreType.DMA((slots,)),
            ],
        )(
            tile_paper, tile_author, tile_count, tile_values, in_hbm(gathered), author_summed,
            prior, target,
        )
        if not last:
            gathered = lax.all_gather(half[0], "blk", tiled=True)
        summed = balance(kernel, exchange(local), ITERS - 1)
    return call(
        functools.partial(final_kernel, rows),
        (shape((papers, classes), f32), shape((authors, classes), f32)),
        [VMEM] * 7,
    )(kernel, summed, own, author_summed, target, seed_class, train_mask)


def solution(mesh):
    placed = (
        P(("grp", "blk"), None, None),
        P(("grp", "blk")),
        P(("grp", "blk")),
        P(("grp", "blk")),
        P(("grp", "blk")),
        P(("grp", "blk")),
        P(),
        P(),
    )
    return jax.shard_map(
        on_device,
        mesh=mesh,
        in_specs=placed,
        out_specs=(P(("grp", "blk"), None), P(("grp", "blk"), None)),
        check_vma=False,
    )
```

```python
import functools

import jax
import jax.numpy as jnp
from jax import lax
from jax.experimental import pallas as pl
from jax.experimental.pallas import tpu as pltpu
from jax.sharding import PartitionSpec as P

AT_DEV = 2
ITERS = 4
ROUNDS = 2
LANES = 128
META = 16

keep_share = 0.8

AXES = ("grp", "blk")
VMEM = pl.BlockSpec(memory_space=pltpu.VMEM)
SMEM = pl.BlockSpec(memory_space=pltpu.SMEM)
HBM = pl.BlockSpec(memory_space=pltpu.HBM)


def call(kernel, out_shape, in_specs, scratch_shapes=(), out_specs=None):
    if out_specs is None:
        out_specs = jax.tree.map(lambda _: VMEM, out_shape)
    return pl.pallas_call(
        kernel,
        out_shape=out_shape,
        in_specs=in_specs,
        out_specs=out_specs,
        scratch_shapes=list(scratch_shapes),
        compiler_params=pltpu.CompilerParams(vmem_limit_bytes=48 * 1024 * 1024),
    )


def col_scale(parts_ref, target_ref):
    return target_ref[...] / jnp.sum(parts_ref[...], axis=0)


def row_scale(kernel, scale_cols):
    return 1.0 / jnp.sum(kernel * scale_cols, axis=1, keepdims=True)


def spread(value, parts_ref):
    parts_ref[...] = jnp.broadcast_to(value[None], parts_ref.shape)


def split(value):
    high = value.astype(jnp.bfloat16)
    return high, (value - high.astype(jnp.float32)).astype(jnp.bfloat16)


def scale_block(scale_cols):
    wide = jnp.broadcast_to(scale_cols, (LANES, scale_cols.shape[1])).T
    return jnp.concatenate(split(wide), axis=1)


def row_sums(half, block):
    sums = jnp.dot(half, block, preferred_element_type=jnp.float32)
    return sums[:, :LANES] + sums[:, LANES:]


def across(column, classes):
    return jnp.concatenate([column] * (classes // LANES), axis=1)


def dot_rows(left, right):
    return lax.dot_general(
        left, right, (((1,), (1,)), ((), ())), preferred_element_type=jnp.float32
    )


def code_lines(seed_class, train_mask, rows):
    code = jnp.where(train_mask[...] == 1, seed_class[...], -1).astype(jnp.float32)
    line = jnp.concatenate([code[i : i + 1] for i in range(code.shape[0])], axis=1)
    papers = line.shape[1]
    wide = jnp.broadcast_to(line, (8, papers))
    lines = []
    for start in range(0, papers, rows):
        lines.append((pltpu.roll(wide, papers - start, 1) if start else wide)[:1, :rows])
    return lines


def meta_line(meta, rows):
    count = -(-rows // LANES)
    return jnp.concatenate([meta[i : i + 1] for i in range(count)], axis=1)[:, :rows]


def code_column(line, eye):
    wide = jnp.broadcast_to(line, (LANES, line.shape[1])).astype(jnp.bfloat16)
    return dot_rows(eye, wide)


def identity(rows):
    line = lax.broadcasted_iota(jnp.int32, (rows, rows), 0)
    lane = lax.broadcasted_iota(jnp.int32, (rows, rows), 1)
    return jnp.where(line == lane, 1.0, 0.0).astype(jnp.bfloat16)


def seeds_of(line, classes):
    class_line = lax.broadcasted_iota(jnp.int32, (classes, line.shape[1]), 0)
    return jnp.where(class_line.astype(jnp.float32) == line, 1.0, 0.0).astype(jnp.bfloat16)


def pack_kernel(rows, tile_count, *refs):
    count = 7
    ins, places = refs[:count], refs[count : 2 * count]
    keep, swap, ready, arrived = refs[2 * count :]
    tile_paper, tile_author, seed_class, train_mask = places[:4]
    tiles = ins[-1]
    pairs = keep.shape[0]
    me = lax.axis_index("blk")
    pair, side = lax.div(me, 2), lax.rem(me, 2)
    moves = [
        pltpu.make_async_copy(source, place, ready.at[i])
        for i, (source, place) in enumerate(zip(ins, places))
    ]
    for copy in moves:
        copy.start()
    outs = []
    copies = []
    for k in range(pairs):
        for way, (out, to) in enumerate(((keep, side), (swap, 1 - side))):
            slot = 2 * lax.bitwise_xor(pair, k) + to
            copy = pltpu.make_async_copy(
                tiles.at[slot], out.at[k, pl.ds(0, rows)], arrived.at[way, k]
            )
            copy.start()
            copies.append(copy)
            outs.append((out, k, slot))
    for copy in moves[:4]:
        copy.wait()
    line = lax.broadcasted_iota(jnp.int32, (META, LANES), 0)
    code_rows = -(-rows // LANES)
    blocks = []
    for codes in code_lines(seed_class, train_mask, rows):
        pad = jnp.full((1, code_rows * LANES - rows), -1.0, jnp.float32)
        codes = jnp.concatenate([codes, pad], axis=1)
        block = jnp.zeros((META, LANES), jnp.float32)
        for i in range(code_rows):
            block = jnp.where(line == i, codes[:, i * LANES : (i + 1) * LANES], block)
        blocks.append(block)
    for out, k, slot in outs:
        paper = tile_paper[slot]
        live = slot < tile_count[0]
        block = blocks[0]
        for i in range(1, len(blocks)):
            block = jnp.where(paper == i, blocks[i], block)
        for author in range(AT_DEV):
            chosen = jnp.where(live & (tile_author[slot] == author), 1.0, 0.0)
            block = jnp.where(line == code_rows + author, chosen, block)
        block = jnp.where(line == code_rows + AT_DEV, paper.astype(jnp.float32), block)
        out[k, rows:, :] = block.astype(jnp.bfloat16)
    for copy in moves[4:] + copies:
        copy.wait()


def pair_kernel(keep, swapped, *outs):
    for k, out in enumerate(outs, 1):
        out[0] = keep[k]
        out[1] = swapped[k]


def sources(count):
    me = lax.axis_index("blk")
    pair, side = lax.div(me, 2), lax.rem(me, 2)
    pairs = [2 * lax.bitwise_xor(pair, k) for k in range(count // 2)]
    return [other + side for other in pairs] + [other + 1 - side for other in pairs]


def slots_of(keep, swapped, *pairs):
    return [(keep, 0), *((ref, 0) for ref in pairs), (swapped, 0), *((ref, 1) for ref in pairs)]


def first_sum_kernel(
    authors, tile_paper, tile_count, tiles, seed_class, train_mask, class_prior, parts
):
    slots, rows, columns = tiles.shape
    classes = parts.shape[2]
    ones = jnp.ones((8, columns), jnp.bfloat16)
    total = authors * class_prior[...]
    for paper, codes in enumerate(code_lines(seed_class, train_mask, rows)):
        weight = jnp.zeros((rows, columns), jnp.float32)
        for slot in range(slots):
            chosen = (slot < tile_count[0]) & (tile_paper[slot] == paper)
            weight = weight + jnp.where(chosen, tiles[slot].astype(jnp.float32), 0.0)
        high, low = split(weight)
        high, low = split(dot_rows(ones, high) + dot_rows(ones, low))
        seeds = seeds_of(codes, classes)
        total = total + (dot_rows(high, seeds) + dot_rows(low, seeds))[:1]
    spread(total, parts)


def next_sum(kernel, summed, class_target, parts):
    scale_rows = row_scale(kernel, col_scale(summed, class_target))
    spread(jnp.sum(scale_rows * kernel, axis=0, keepdims=True), parts)


def first_author_kernel(rows, summed, class_prior, class_target, *rest):
    *held, full, parts = rest
    classes = full.shape[1]
    code_rows = -(-rows // LANES)
    totals = [jnp.zeros((classes, LANES), jnp.float32) for _ in range(AT_DEV)]
    for ref, place in slots_of(*held):
        meta = ref[place, rows:, :].astype(jnp.float32)
        seeds = seeds_of(meta_line(meta, rows), classes)
        parcel = jnp.dot(seeds, ref[place, :rows, :], preferred_element_type=jnp.float32)
        parcel = parcel.astype(jnp.bfloat16).astype(jnp.float32)
        for author in range(AT_DEV):
            chosen = meta[code_rows + author : code_rows + author + 1]
            totals[author] = totals[author] + parcel * chosen
    kernel = jnp.concatenate([total.T for total in totals], axis=0) + class_prior[...]
    full[...] = kernel
    next_sum(kernel, summed, class_target, parts)


def author_kernel(rows, blocks, summed, class_prior, class_target, *rest):
    *rest, full, parts = rest
    kernels, held = rest[:blocks], slots_of(*rest[blocks:])
    classes = full.shape[1]
    code_rows = -(-rows // LANES)
    metas = [ref[place, rows:, :].astype(jnp.float32) for ref, place in held]
    at = code_rows + AT_DEV
    papers = [jnp.max(meta[at : at + 1]).astype(jnp.int32) for meta in metas]
    scale_cols = col_scale(summed, class_target)
    block = scale_block(scale_cols)
    eye = identity(rows)
    codes = [code_column(meta_line(meta, rows), eye) for meta in metas]
    totals = [jnp.zeros((LANES, classes), jnp.float32) for _ in range(AT_DEV)]
    lane = lax.broadcasted_iota(jnp.int32, (rows, classes), 1).astype(jnp.float32)
    for shift, (ref, place) in enumerate(held):
        half = kernels[shift][pl.ds(pl.multiple_of(papers[shift] * rows, rows), rows), :]
        scale_rows = across(keep_share / row_sums(half, block), classes)
        share = half.astype(jnp.float32) * scale_cols * scale_rows
        labels = share + jnp.where(across(codes[shift], classes) == lane, 1.0 - keep_share, 0.0)
        parcel = lax.dot_general(
            ref[place, :rows, :],
            labels.astype(jnp.bfloat16),
            (((0,), (0,)), ((), ())),
            preferred_element_type=jnp.float32,
        )
        parcel = parcel.astype(jnp.bfloat16).astype(jnp.float32)
        for author in range(AT_DEV):
            at = code_rows + author
            totals[author] = totals[author] + parcel * metas[shift][at : at + 1, :1]
    kernel = jnp.concatenate(totals, axis=0) + class_prior[...]
    full[...] = kernel
    spread(jnp.sum(kernel, axis=0, keepdims=True), parts)


def paper_kernel(
    blocks, tile_paper, tile_author, tile_count, tiles, summed, class_prior, class_target, *rest
):
    kernels, (full, parts, *half) = rest[:blocks], rest[blocks:]
    _, rows, columns = tiles.shape
    classes = full.shape[1]
    scale_cols = col_scale(summed, class_target)
    block = scale_block(scale_cols)
    slots = sources(blocks)
    wide = jnp.concatenate([tiles[slot] for slot in slots], axis=1)
    labels = []
    for ref, slot in zip(kernels, slots):
        start = pl.multiple_of(tile_author[slot] * columns, columns)
        kernel = ref[pl.ds(start, columns), :]
        high, low = split(kernel)
        sums = row_sums(high, block) + jnp.dot(
            low, block[:, :LANES], preferred_element_type=jnp.float32
        )
        share = kernel * scale_cols * across(1.0 / sums, classes)
        labels.append(share.astype(jnp.bfloat16))
    column = jnp.zeros((1, classes), jnp.float32)
    for paper in range(full.shape[0] // rows):
        chosen = []
        for one, slot in zip(labels, slots):
            keep = (slot < tile_count[0]) & (tile_paper[slot] == paper)
            chosen.append(jnp.where(keep, one, jnp.zeros_like(one)))
        mass = jnp.dot(wide, jnp.concatenate(chosen, axis=0), preferred_element_type=jnp.float32)
        kernel = mass + class_prior[...]
        full[paper * rows : (paper + 1) * rows, :] = kernel
        for out in half:
            out[paper * rows : (paper + 1) * rows, :] = kernel.astype(jnp.bfloat16)
        column = column + jnp.sum(kernel, axis=0, keepdims=True)
    spread(column, parts)


def balance_kernel(kernel_ref, summed, class_target, parts):
    next_sum(kernel_ref[...], summed, class_target, parts)


def final_kernel(
    rows, kernel_ref, summed, own, author_summed, class_target, seed_class, train_mask, out, scores
):
    classes = out.shape[1]
    scaled = own[...] * col_scale(author_summed, class_target)
    scores[...] = scaled * (classes / jnp.sum(scaled, axis=1, keepdims=True))
    scale_cols = col_scale(summed, class_target)
    eye = identity(rows)
    lane = lax.broadcasted_iota(jnp.int32, (rows, classes), 1).astype(jnp.float32)
    for paper, line in enumerate(code_lines(seed_class, train_mask, rows)):
        part = slice(paper * rows, (paper + 1) * rows)
        scaled = kernel_ref[part, :] * scale_cols
        share = scaled * (1.0 / jnp.sum(scaled, axis=1, keepdims=True))
        code = across(code_column(line, eye), classes)
        updated = keep_share * share + jnp.where(code == lane, 1.0 - keep_share, 0.0)
        out[part, :] = classes * updated


def in_hbm(value):
    return pltpu.with_memory_space_constraint(value, pltpu.HBM)


def exchange(parts):
    return lax.all_to_all(parts, AXES, split_axis=0, concat_axis=0, tiled=True)


def on_device(
    tile_values,
    tile_paper,
    tile_author,
    tile_count,
    seed_class,
    train_mask,
    class_prior,
    class_target,
):
    f32 = jnp.float32
    bf16 = jnp.bfloat16
    shape = jax.ShapeDtypeStruct
    slots, rows, columns = tile_values.shape
    classes = class_prior.shape[0]
    papers = seed_class.shape[0]
    authors = AT_DEV * columns
    paper_tiles = papers // rows
    devices = lax.axis_size(AXES)
    prior = class_prior.reshape(1, classes)
    target = class_target.reshape(1, classes)
    seed_class = seed_class.reshape(papers // LANES, LANES)
    train_mask = train_mask.reshape(papers // LANES, LANES)
    parts = shape((devices, 1, classes), f32)

    inputs = (
        tile_paper, tile_author, seed_class, train_mask, prior, target, tile_values,
    )
    places = (SMEM, SMEM, VMEM, VMEM, VMEM, VMEM, VMEM)
    blocks = lax.axis_size("blk")
    load = shape((blocks // 2, rows + META, columns), bf16)
    moved = call(
        functools.partial(pack_kernel, rows),
        tuple(shape(one.shape, one.dtype) for one in inputs) + (load, load),
        [SMEM] + [HBM] * len(inputs),
        [pltpu.SemaphoreType.DMA((len(inputs),)), pltpu.SemaphoreType.DMA((2, blocks // 2))],
        places + (VMEM, VMEM),
    )(tile_count, *(in_hbm(one) for one in inputs))
    tile_paper, tile_author, seed_class, train_mask, prior, target, tile_values, keep, swap = moved
    swapped = lax.ppermute(swap, "blk", [(i, i ^ 1) for i in range(blocks)])
    local = call(
        functools.partial(first_sum_kernel, authors), parts, [SMEM, SMEM] + [VMEM] * 4
    )(tile_paper, tile_count, tile_values, seed_class, train_mask, prior)
    both = shape((2, rows + META, columns), bf16)
    pairs = call(pair_kernel, (both,) * (blocks // 2 - 1), [VMEM] * 2)(keep, swapped)
    local, *pairs = lax.optimization_barrier((local, *pairs))
    held = [keep, swapped] + [
        lax.ppermute(one, "blk", [(i, i ^ (2 * k)) for i in range(blocks)])
        for k, one in enumerate(pairs, 1)
    ]
    summed = exchange(local)

    author_out = (shape((authors, classes), f32), parts)
    paper_out = (shape((papers, classes), f32), parts, shape((papers, classes), bf16))

    def across_pairs(value, k):
        return lax.ppermute(value, "blk", [(i, i ^ (2 * k)) for i in range(blocks)])

    def to_other(value):
        return lax.ppermute(value, "blk", [(i, i ^ 1) for i in range(blocks)])

    def balance(kernel, sent, local, count):
        here = [sent] + [across_pairs(sent, k) for k in range(1, blocks // 2)]
        there = [to_other(sent)]
        for step in range(count):
            if step + 1 == count:
                local, *here = lax.optimization_barrier((local, *here))
                there += [to_other(one) for one in here[1:]]
            summed = exchange(local)
            if step + 1 < count:
                local = call(balance_kernel, parts, [VMEM] * 3)(kernel, summed, target)
        return summed, here + there

    def last_balance(kernel, local):
        for step in range(ITERS):
            summed = exchange(local)
            if step + 1 < ITERS:
                local = call(balance_kernel, parts, [VMEM] * 3)(kernel, summed, target)
        return summed

    for repeat in range(ROUNDS):
        if repeat == 0:
            own, local = call(
                functools.partial(first_author_kernel, rows), author_out, [VMEM] * (3 + len(held))
            )(summed, prior, target, *held)
            left = ITERS - 1
        else:
            own, local = call(
                functools.partial(author_kernel, rows, blocks),
                author_out,
                [VMEM] * (3 + blocks + len(held)),
            )(summed, prior, target, *kernels, *held)
            left = ITERS
        author_summed, kernels = balance(own, own, local, left)
        last = repeat + 1 == ROUNDS
        kernel, local, *half = call(
            functools.partial(paper_kernel, blocks),
            paper_out[:2] if last else paper_out,
            [SMEM, SMEM, SMEM] + [VMEM] * (4 + blocks),
        )(
            tile_paper, tile_author, tile_count, tile_values, author_summed, prior, target, *kernels
        )
        if last:
            summed = last_balance(kernel, local)
        else:
            summed, kernels = balance(kernel, half[0], local, ITERS)
    return call(
        functools.partial(final_kernel, rows),
        (shape((papers, classes), f32), shape((authors, classes), f32)),
        [VMEM] * 7,
    )(kernel, summed, own, author_summed, target, seed_class, train_mask)


def solution(mesh):
    placed = (
        P(("grp", "blk"), None, None),
        P(("grp", "blk")),
        P(("grp", "blk")),
        P(("grp", "blk")),
        P(("grp", "blk")),
        P(("grp", "blk")),
        P(),
        P(),
    )
    return jax.shard_map(
        on_device,
        mesh=mesh,
        in_specs=placed,
        out_specs=(P(("grp", "blk"), None), P(("grp", "blk"), None)),
        check_vma=False,
    )
```

```python
import functools

import jax
import jax.numpy as jnp
from jax import lax
from jax.experimental import pallas as pl
from jax.experimental.pallas import tpu as pltpu
from jax.sharding import PartitionSpec as P

AT_DEV = 2
ITERS = 4
ROUNDS = 2
LANES = 128
META = 16

keep_share = 0.8

AXES = ("grp", "blk")
VMEM = pl.BlockSpec(memory_space=pltpu.VMEM)
SMEM = pl.BlockSpec(memory_space=pltpu.SMEM)
HBM = pl.BlockSpec(memory_space=pltpu.HBM)


def call(kernel, out_shape, in_specs, scratch_shapes=(), out_specs=None):
    if out_specs is None:
        out_specs = jax.tree.map(lambda _: VMEM, out_shape)
    return pl.pallas_call(
        kernel,
        out_shape=out_shape,
        in_specs=in_specs,
        out_specs=out_specs,
        scratch_shapes=list(scratch_shapes),
        compiler_params=pltpu.CompilerParams(vmem_limit_bytes=48 * 1024 * 1024),
    )


def col_scale(parts_ref, target_ref):
    return target_ref[...] / jnp.sum(parts_ref[...], axis=0)


def row_scale(kernel, scale_cols):
    return 1.0 / jnp.sum(kernel * scale_cols, axis=1, keepdims=True)


def spread(value, parts_ref):
    parts_ref[...] = jnp.broadcast_to(value[None], parts_ref.shape)


def split(value):
    high = value.astype(jnp.bfloat16)
    return high, (value - high.astype(jnp.float32)).astype(jnp.bfloat16)


def scale_block(scale_cols):
    wide = jnp.broadcast_to(scale_cols, (LANES, scale_cols.shape[1])).T
    return jnp.concatenate(split(wide), axis=1)


def row_sums(half, block):
    sums = jnp.dot(half, block, preferred_element_type=jnp.float32)
    return sums[:, :LANES] + sums[:, LANES:]


def across(column, classes):
    return jnp.concatenate([column] * (classes // LANES), axis=1)


def dot_rows(left, right):
    return lax.dot_general(
        left, right, (((1,), (1,)), ((), ())), preferred_element_type=jnp.float32
    )


def code_lines(seed_class, train_mask, rows):
    code = jnp.where(train_mask[...] == 1, seed_class[...], -1).astype(jnp.float32)
    line = jnp.concatenate([code[i : i + 1] for i in range(code.shape[0])], axis=1)
    papers = line.shape[1]
    wide = jnp.broadcast_to(line, (8, papers))
    lines = []
    for start in range(0, papers, rows):
        lines.append((pltpu.roll(wide, papers - start, 1) if start else wide)[:1, :rows])
    return lines


def meta_line(meta, rows):
    count = -(-rows // LANES)
    return jnp.concatenate([meta[i : i + 1] for i in range(count)], axis=1)[:, :rows]


def code_column(line, eye):
    wide = jnp.broadcast_to(line, (LANES, line.shape[1])).astype(jnp.bfloat16)
    return dot_rows(eye, wide)


def identity(rows):
    line = lax.broadcasted_iota(jnp.int32, (rows, rows), 0)
    lane = lax.broadcasted_iota(jnp.int32, (rows, rows), 1)
    return jnp.where(line == lane, 1.0, 0.0).astype(jnp.bfloat16)


def seeds_of(line, classes):
    class_line = lax.broadcasted_iota(jnp.int32, (classes, line.shape[1]), 0)
    return jnp.where(class_line.astype(jnp.float32) == line, 1.0, 0.0).astype(jnp.bfloat16)


def pack_kernel(rows, tile_count, *refs):
    count = 7
    ins, places = refs[:count], refs[count : 2 * count]
    keep, swap, ready, arrived = refs[2 * count :]
    tile_paper, tile_author, seed_class, train_mask = places[:4]
    tiles = ins[-1]
    pairs = keep.shape[0]
    me = lax.axis_index("blk")
    pair, side = lax.div(me, 2), lax.rem(me, 2)
    moves = [
        pltpu.make_async_copy(source, place, ready.at[i])
        for i, (source, place) in enumerate(zip(ins, places))
    ]
    for copy in moves:
        copy.start()
    outs = []
    copies = []
    for k in range(pairs):
        for way, (out, to) in enumerate(((keep, side), (swap, 1 - side))):
            slot = 2 * lax.bitwise_xor(pair, k) + to
            copy = pltpu.make_async_copy(
                tiles.at[slot], out.at[k, pl.ds(0, rows)], arrived.at[way, k]
            )
            copy.start()
            copies.append(copy)
            outs.append((out, k, slot))
    for copy in moves[:4]:
        copy.wait()
    line = lax.broadcasted_iota(jnp.int32, (META, LANES), 0)
    code_rows = -(-rows // LANES)
    blocks = []
    for codes in code_lines(seed_class, train_mask, rows):
        pad = jnp.full((1, code_rows * LANES - rows), -1.0, jnp.float32)
        codes = jnp.concatenate([codes, pad], axis=1)
        block = jnp.zeros((META, LANES), jnp.float32)
        for i in range(code_rows):
            block = jnp.where(line == i, codes[:, i * LANES : (i + 1) * LANES], block)
        blocks.append(block)
    for out, k, slot in outs:
        paper = tile_paper[slot]
        live = slot < tile_count[0]
        block = blocks[0]
        for i in range(1, len(blocks)):
            block = jnp.where(paper == i, blocks[i], block)
        for author in range(AT_DEV):
            chosen = jnp.where(live & (tile_author[slot] == author), 1.0, 0.0)
            block = jnp.where(line == code_rows + author, chosen, block)
        block = jnp.where(line == code_rows + AT_DEV, paper.astype(jnp.float32), block)
        out[k, rows:, :] = block.astype(jnp.bfloat16)
    for copy in moves[4:] + copies:
        copy.wait()


def pair_kernel(keep, swapped, *outs):
    for k, out in enumerate(outs, 1):
        out[0] = keep[k]
        out[1] = swapped[k]


def sources(count):
    me = lax.axis_index("blk")
    pair, side = lax.div(me, 2), lax.rem(me, 2)
    pairs = [2 * lax.bitwise_xor(pair, k) for k in range(count // 2)]
    return [other + side for other in pairs] + [other + 1 - side for other in pairs]


def slots_of(keep, swapped, *pairs):
    return [(keep, 0), *((ref, 0) for ref in pairs), (swapped, 0), *((ref, 1) for ref in pairs)]


def first_sum_kernel(
    authors, tile_paper, tile_count, tiles, seed_class, train_mask, class_prior, parts
):
    slots, rows, columns = tiles.shape
    classes = parts.shape[2]
    ones = jnp.ones((8, columns), jnp.bfloat16)
    total = authors * class_prior[...]
    for paper, codes in enumerate(code_lines(seed_class, train_mask, rows)):
        weight = jnp.zeros((rows, columns), jnp.float32)
        for slot in range(slots):
            chosen = (slot < tile_count[0]) & (tile_paper[slot] == paper)
            weight = weight + jnp.where(chosen, tiles[slot].astype(jnp.float32), 0.0)
        high, low = split(weight)
        high, low = split(dot_rows(ones, high) + dot_rows(ones, low))
        seeds = seeds_of(codes, classes)
        total = total + (dot_rows(high, seeds) + dot_rows(low, seeds))[:1]
    spread(total, parts)


def next_sum(kernel, summed, class_target, parts):
    scale_rows = row_scale(kernel, col_scale(summed, class_target))
    spread(jnp.sum(scale_rows * kernel, axis=0, keepdims=True), parts)


def first_author_kernel(rows, summed, class_prior, class_target, *rest):
    *held, full, parts = rest
    classes = full.shape[1]
    code_rows = -(-rows // LANES)
    totals = [jnp.zeros((classes, LANES), jnp.float32) for _ in range(AT_DEV)]
    for ref, place in slots_of(*held):
        meta = ref[place, rows:, :].astype(jnp.float32)
        seeds = seeds_of(meta_line(meta, rows), classes)
        parcel = jnp.dot(seeds, ref[place, :rows, :], preferred_element_type=jnp.float32)
        parcel = parcel.astype(jnp.bfloat16).astype(jnp.float32)
        for author in range(AT_DEV):
            chosen = meta[code_rows + author : code_rows + author + 1]
            totals[author] = totals[author] + parcel * chosen
    kernel = jnp.concatenate([total.T for total in totals], axis=0) + class_prior[...]
    full[...] = kernel
    next_sum(kernel, summed, class_target, parts)


def author_kernel(rows, blocks, summed, class_prior, class_target, *rest):
    *rest, full, parts = rest
    kernels, held = rest[:blocks], slots_of(*rest[blocks:])
    classes = full.shape[1]
    code_rows = -(-rows // LANES)
    metas = [ref[place, rows:, :].astype(jnp.float32) for ref, place in held]
    at = code_rows + AT_DEV
    papers = [jnp.max(meta[at : at + 1]).astype(jnp.int32) for meta in metas]
    scale_cols = col_scale(summed, class_target)
    block = scale_block(scale_cols)
    eye = identity(rows)
    codes = [code_column(meta_line(meta, rows), eye) for meta in metas]
    totals = [jnp.zeros((LANES, classes), jnp.float32) for _ in range(AT_DEV)]
    lane = lax.broadcasted_iota(jnp.int32, (rows, classes), 1).astype(jnp.float32)
    for shift, (ref, place) in enumerate(held):
        half = kernels[shift][pl.ds(pl.multiple_of(papers[shift] * rows, rows), rows), :]
        scale_rows = across(keep_share / row_sums(half, block), classes)
        share = half.astype(jnp.float32) * scale_cols * scale_rows
        labels = share + jnp.where(across(codes[shift], classes) == lane, 1.0 - keep_share, 0.0)
        parcel = lax.dot_general(
            ref[place, :rows, :],
            labels.astype(jnp.bfloat16),
            (((0,), (0,)), ((), ())),
            preferred_element_type=jnp.float32,
        )
        parcel = parcel.astype(jnp.bfloat16).astype(jnp.float32)
        for author in range(AT_DEV):
            at = code_rows + author
            totals[author] = totals[author] + parcel * metas[shift][at : at + 1, :1]
    kernel = jnp.concatenate(totals, axis=0) + class_prior[...]
    full[...] = kernel
    spread(jnp.sum(kernel, axis=0, keepdims=True), parts)


def paper_kernel(
    blocks, tile_paper, tile_author, tile_count, tiles, summed, class_prior, class_target, *rest
):
    kernels, (full, parts, *half) = rest[:blocks], rest[blocks:]
    _, rows, columns = tiles.shape
    classes = full.shape[1]
    scale_cols = col_scale(summed, class_target)
    block = scale_block(scale_cols)
    slots = sources(blocks)
    wide = jnp.concatenate([tiles[slot] for slot in slots], axis=1)
    labels = []
    for ref, slot in zip(kernels, slots):
        start = pl.multiple_of(tile_author[slot] * columns, columns)
        kernel = ref[pl.ds(start, columns), :]
        high, low = split(kernel)
        sums = row_sums(high, block) + jnp.dot(
            low, block[:, :LANES], preferred_element_type=jnp.float32
        )
        share = kernel * scale_cols * across(1.0 / sums, classes)
        labels.append(share.astype(jnp.bfloat16))
    column = jnp.zeros((1, classes), jnp.float32)
    for paper in range(full.shape[0] // rows):
        chosen = []
        for one, slot in zip(labels, slots):
            keep = (slot < tile_count[0]) & (tile_paper[slot] == paper)
            chosen.append(jnp.where(keep, one, jnp.zeros_like(one)))
        mass = jnp.dot(wide, jnp.concatenate(chosen, axis=0), preferred_element_type=jnp.float32)
        kernel = mass + class_prior[...]
        full[paper * rows : (paper + 1) * rows, :] = kernel
        for out in half:
            out[paper * rows : (paper + 1) * rows, :] = kernel.astype(jnp.bfloat16)
        column = column + jnp.sum(kernel, axis=0, keepdims=True)
    spread(column, parts)


def balance_kernel(kernel_ref, summed, class_target, parts):
    next_sum(kernel_ref[...], summed, class_target, parts)


def final_kernel(
    rows, kernel_ref, summed, own, author_summed, class_target, seed_class, train_mask, out, scores
):
    classes = out.shape[1]
    scaled = own[...] * col_scale(author_summed, class_target)
    scores[...] = scaled * (classes / jnp.sum(scaled, axis=1, keepdims=True))
    scale_cols = col_scale(summed, class_target)
    eye = identity(rows)
    lane = lax.broadcasted_iota(jnp.int32, (rows, classes), 1).astype(jnp.float32)
    for paper, line in enumerate(code_lines(seed_class, train_mask, rows)):
        part = slice(paper * rows, (paper + 1) * rows)
        scaled = kernel_ref[part, :] * scale_cols
        share = scaled * (1.0 / jnp.sum(scaled, axis=1, keepdims=True))
        code = across(code_column(line, eye), classes)
        updated = keep_share * share + jnp.where(code == lane, 1.0 - keep_share, 0.0)
        out[part, :] = classes * updated


def in_hbm(value):
    return pltpu.with_memory_space_constraint(value, pltpu.HBM)


def exchange(parts):
    return lax.all_to_all(parts, AXES, split_axis=0, concat_axis=0, tiled=True)


def on_device(
    tile_values,
    tile_paper,
    tile_author,
    tile_count,
    seed_class,
    train_mask,
    class_prior,
    class_target,
):
    f32 = jnp.float32
    bf16 = jnp.bfloat16
    shape = jax.ShapeDtypeStruct
    slots, rows, columns = tile_values.shape
    classes = class_prior.shape[0]
    papers = seed_class.shape[0]
    authors = AT_DEV * columns
    paper_tiles = papers // rows
    devices = lax.axis_size(AXES)
    prior = class_prior.reshape(1, classes)
    target = class_target.reshape(1, classes)
    seed_class = seed_class.reshape(papers // LANES, LANES)
    train_mask = train_mask.reshape(papers // LANES, LANES)
    parts = shape((devices, 1, classes), f32)

    inputs = (
        tile_paper, tile_author, seed_class, train_mask, prior, target, tile_values,
    )
    places = (SMEM, SMEM, VMEM, VMEM, VMEM, VMEM, VMEM)
    blocks = lax.axis_size("blk")
    load = shape((blocks // 2, rows + META, columns), bf16)
    moved = call(
        functools.partial(pack_kernel, rows),
        tuple(shape(one.shape, one.dtype) for one in inputs) + (load, load),
        [SMEM] + [HBM] * len(inputs),
        [pltpu.SemaphoreType.DMA((len(inputs),)), pltpu.SemaphoreType.DMA((2, blocks // 2))],
        places + (VMEM, VMEM),
    )(tile_count, *(in_hbm(one) for one in inputs))
    tile_paper, tile_author, seed_class, train_mask, prior, target, tile_values, keep, swap = moved
    swapped = lax.ppermute(swap, "blk", [(i, i ^ 1) for i in range(blocks)])
    local = call(
        functools.partial(first_sum_kernel, authors), parts, [SMEM, SMEM] + [VMEM] * 4
    )(tile_paper, tile_count, tile_values, seed_class, train_mask, prior)
    both = shape((2, rows + META, columns), bf16)
    pairs = call(pair_kernel, (both,) * (blocks // 2 - 1), [VMEM] * 2)(keep, swapped)
    local, *pairs = lax.optimization_barrier((local, *pairs))
    held = [keep, swapped] + [
        lax.ppermute(one, "blk", [(i, i ^ (2 * k)) for i in range(blocks)])
        for k, one in enumerate(pairs, 1)
    ]
    summed = exchange(local)

    author_out = (shape((authors, classes), f32), parts)
    paper_out = (shape((papers, classes), f32), parts, shape((papers, classes), bf16))

    def across_pairs(value, k):
        return lax.ppermute(value, "blk", [(i, i ^ (2 * k)) for i in range(blocks)])

    def to_other(value):
        return lax.ppermute(value, "blk", [(i, i ^ 1) for i in range(blocks)])

    def balance(kernel, sent, local, count):
        here, there = {0: sent}, {}
        for step in range(count):
            if step == 0:
                moves = [(here, k, across_pairs(sent, k)) for k in range(1, blocks // 2)][:2]
            elif step == 1:
                moves = [(there, 0, to_other(sent))]
                moves += [(here, k, across_pairs(sent, k)) for k in range(3, blocks // 2)]
            else:
                ready = [k for k in here if k not in there]
                if step + 1 < count:
                    ready = ready[:2]
                moves = [(there, k, to_other(here[k])) for k in ready]
            summed = exchange(local)
            summed, *moved = lax.optimization_barrier((summed, *(one for _, _, one in moves)))
            for (place, k, _), one in zip(moves, moved):
                place[k] = one
            if step + 1 < count:
                local = call(balance_kernel, parts, [VMEM] * 3)(kernel, summed, target)
                local, sent, *moved = lax.optimization_barrier((local, sent, *here.values()))
                here = dict(zip(here, moved))
        order = range(blocks // 2)
        return summed, [here[k] for k in order] + [there[k] for k in order]

    def last_balance(kernel, local):
        for step in range(ITERS):
            summed = exchange(local)
            if step + 1 < ITERS:
                local = call(balance_kernel, parts, [VMEM] * 3)(kernel, summed, target)
        return summed

    for repeat in range(ROUNDS):
        if repeat == 0:
            own, local = call(
                functools.partial(first_author_kernel, rows), author_out, [VMEM] * (3 + len(held))
            )(summed, prior, target, *held)
            left = ITERS - 1
        else:
            own, local = call(
                functools.partial(author_kernel, rows, blocks),
                author_out,
                [VMEM] * (3 + blocks + len(held)),
            )(summed, prior, target, *kernels, *held)
            left = ITERS
        author_summed, kernels = balance(own, own, local, left)
        last = repeat + 1 == ROUNDS
        kernel, local, *half = call(
            functools.partial(paper_kernel, blocks),
            paper_out[:2] if last else paper_out,
            [SMEM, SMEM, SMEM] + [VMEM] * (4 + blocks),
        )(
            tile_paper, tile_author, tile_count, tile_values, author_summed, prior, target, *kernels
        )
        if last:
            summed = last_balance(kernel, local)
        else:
            summed, kernels = balance(kernel, half[0], local, ITERS)
    return call(
        functools.partial(final_kernel, rows),
        (shape((papers, classes), f32), shape((authors, classes), f32)),
        [VMEM] * 7,
    )(kernel, summed, own, author_summed, target, seed_class, train_mask)


def solution(mesh):
    placed = (
        P(("grp", "blk"), None, None),
        P(("grp", "blk")),
        P(("grp", "blk")),
        P(("grp", "blk")),
        P(("grp", "blk")),
        P(("grp", "blk")),
        P(),
        P(),
    )
    return jax.shard_map(
        on_device,
        mesh=mesh,
        in_specs=placed,
        out_specs=(P(("grp", "blk"), None), P(("grp", "blk"), None)),
        check_vma=False,
    )
```

```python
import functools

import jax
import jax.numpy as jnp
from jax import lax
from jax.experimental import pallas as pl
from jax.experimental.pallas import tpu as pltpu
from jax.sharding import PartitionSpec as P

AT_DEV = 2
ITERS = 4
ROUNDS = 2
LANES = 128
META = 16

keep_share = 0.8

AXES = ("grp", "blk")
VMEM = pl.BlockSpec(memory_space=pltpu.VMEM)
SMEM = pl.BlockSpec(memory_space=pltpu.SMEM)
HBM = pl.BlockSpec(memory_space=pltpu.HBM)


def call(kernel, out_shape, in_specs, scratch_shapes=(), out_specs=None):
    if out_specs is None:
        out_specs = jax.tree.map(lambda _: VMEM, out_shape)
    return pl.pallas_call(
        kernel,
        out_shape=out_shape,
        in_specs=in_specs,
        out_specs=out_specs,
        scratch_shapes=list(scratch_shapes),
        compiler_params=pltpu.CompilerParams(vmem_limit_bytes=48 * 1024 * 1024),
    )


def col_scale(parts_ref, target_ref):
    return target_ref[...] / jnp.sum(parts_ref[...], axis=0)


def row_scale(kernel, scale_cols):
    return 1.0 / jnp.sum(kernel * scale_cols, axis=1, keepdims=True)


def spread(value, parts_ref):
    parts_ref[...] = jnp.broadcast_to(value[None], parts_ref.shape)


def split(value):
    high = value.astype(jnp.bfloat16)
    return high, (value - high.astype(jnp.float32)).astype(jnp.bfloat16)


def scale_block(scale_cols):
    wide = jnp.broadcast_to(scale_cols, (LANES, scale_cols.shape[1])).T
    return jnp.concatenate(split(wide), axis=1)


def row_sums(half, block):
    sums = jnp.dot(half, block, preferred_element_type=jnp.float32)
    return sums[:, :LANES] + sums[:, LANES:]


def across(column, classes):
    return jnp.concatenate([column] * (classes // LANES), axis=1)


def dot_rows(left, right):
    return lax.dot_general(
        left, right, (((1,), (1,)), ((), ())), preferred_element_type=jnp.float32
    )


def code_lines(seed_class, train_mask, rows):
    code = jnp.where(train_mask[...] == 1, seed_class[...], -1).astype(jnp.float32)
    line = jnp.concatenate([code[i : i + 1] for i in range(code.shape[0])], axis=1)
    papers = line.shape[1]
    wide = jnp.broadcast_to(line, (8, papers))
    lines = []
    for start in range(0, papers, rows):
        lines.append((pltpu.roll(wide, papers - start, 1) if start else wide)[:1, :rows])
    return lines


def meta_line(meta, rows):
    count = -(-rows // LANES)
    return jnp.concatenate([meta[i : i + 1] for i in range(count)], axis=1)[:, :rows]


def code_column(line, eye):
    wide = jnp.broadcast_to(line, (LANES, line.shape[1])).astype(jnp.bfloat16)
    return dot_rows(eye, wide)


def identity(rows):
    line = lax.broadcasted_iota(jnp.int32, (rows, rows), 0)
    lane = lax.broadcasted_iota(jnp.int32, (rows, rows), 1)
    return jnp.where(line == lane, 1.0, 0.0).astype(jnp.bfloat16)


def seeds_of(line, classes):
    class_line = lax.broadcasted_iota(jnp.int32, (classes, line.shape[1]), 0)
    return jnp.where(class_line.astype(jnp.float32) == line, 1.0, 0.0).astype(jnp.bfloat16)


def pack_kernel(rows, tile_count, *refs):
    count = 7
    ins, places = refs[:count], refs[count : 2 * count]
    keep, swap, ready, arrived = refs[2 * count :]
    tile_paper, tile_author, seed_class, train_mask = places[:4]
    tiles = ins[-1]
    pairs = keep.shape[0]
    me = lax.axis_index("blk")
    pair, side = lax.div(me, 2), lax.rem(me, 2)
    moves = [
        pltpu.make_async_copy(source, place, ready.at[i])
        for i, (source, place) in enumerate(zip(ins, places))
    ]
    for copy in moves:
        copy.start()
    outs = []
    copies = []
    for k in range(pairs):
        for way, (out, to) in enumerate(((keep, side), (swap, 1 - side))):
            slot = 2 * lax.bitwise_xor(pair, k) + to
            copy = pltpu.make_async_copy(
                tiles.at[slot], out.at[k, pl.ds(0, rows)], arrived.at[way, k]
            )
            copy.start()
            copies.append(copy)
            outs.append((out, k, slot))
    for copy in moves[:4]:
        copy.wait()
    line = lax.broadcasted_iota(jnp.int32, (META, LANES), 0)
    code_rows = -(-rows // LANES)
    blocks = []
    for codes in code_lines(seed_class, train_mask, rows):
        pad = jnp.full((1, code_rows * LANES - rows), -1.0, jnp.float32)
        codes = jnp.concatenate([codes, pad], axis=1)
        block = jnp.zeros((META, LANES), jnp.float32)
        for i in range(code_rows):
            block = jnp.where(line == i, codes[:, i * LANES : (i + 1) * LANES], block)
        blocks.append(block)
    for out, k, slot in outs:
        paper = tile_paper[slot]
        live = slot < tile_count[0]
        block = blocks[0]
        for i in range(1, len(blocks)):
            block = jnp.where(paper == i, blocks[i], block)
        for author in range(AT_DEV):
            chosen = jnp.where(live & (tile_author[slot] == author), 1.0, 0.0)
            block = jnp.where(line == code_rows + author, chosen, block)
        block = jnp.where(line == code_rows + AT_DEV, paper.astype(jnp.float32), block)
        out[k, rows:, :] = block.astype(jnp.bfloat16)
    for copy in moves[4:] + copies:
        copy.wait()


def pair_kernel(keep, swapped, *outs):
    for k, out in enumerate(outs, 1):
        out[0] = keep[k]
        out[1] = swapped[k]


def sources(count):
    me = lax.axis_index("blk")
    pair, side = lax.div(me, 2), lax.rem(me, 2)
    pairs = [2 * lax.bitwise_xor(pair, k) for k in range(count // 2)]
    return [other + side for other in pairs] + [other + 1 - side for other in pairs]


def slots_of(keep, swapped, *pairs):
    return [(keep, 0), *((ref, 0) for ref in pairs), (swapped, 0), *((ref, 1) for ref in pairs)]


def first_sum_kernel(
    authors, tile_paper, tile_count, tiles, seed_class, train_mask, class_prior, parts
):
    slots, rows, columns = tiles.shape
    classes = parts.shape[2]
    ones = jnp.ones((8, columns), jnp.bfloat16)
    total = authors * class_prior[...]
    for paper, codes in enumerate(code_lines(seed_class, train_mask, rows)):
        weight = jnp.zeros((rows, columns), jnp.float32)
        for slot in range(slots):
            chosen = (slot < tile_count[0]) & (tile_paper[slot] == paper)
            weight = weight + jnp.where(chosen, tiles[slot].astype(jnp.float32), 0.0)
        high, low = split(weight)
        high, low = split(dot_rows(ones, high) + dot_rows(ones, low))
        seeds = seeds_of(codes, classes)
        total = total + (dot_rows(high, seeds) + dot_rows(low, seeds))[:1]
    spread(total, parts)


def next_sum(kernel, summed, class_target, parts):
    scale_rows = row_scale(kernel, col_scale(summed, class_target))
    spread(jnp.sum(scale_rows * kernel, axis=0, keepdims=True), parts)


def first_author_kernel(rows, summed, class_prior, class_target, *rest):
    *held, full, parts = rest
    classes = full.shape[1]
    code_rows = -(-rows // LANES)
    totals = [jnp.zeros((classes, LANES), jnp.float32) for _ in range(AT_DEV)]
    for ref, place in slots_of(*held):
        meta = ref[place, rows:, :].astype(jnp.float32)
        seeds = seeds_of(meta_line(meta, rows), classes)
        parcel = jnp.dot(seeds, ref[place, :rows, :], preferred_element_type=jnp.float32)
        parcel = parcel.astype(jnp.bfloat16).astype(jnp.float32)
        for author in range(AT_DEV):
            chosen = meta[code_rows + author : code_rows + author + 1]
            totals[author] = totals[author] + parcel * chosen
    kernel = jnp.concatenate([total.T for total in totals], axis=0) + class_prior[...]
    full[...] = kernel
    next_sum(kernel, summed, class_target, parts)


def author_kernel(rows, blocks, summed, class_prior, class_target, *rest):
    *rest, full, parts = rest
    kernels, held = rest[:blocks], slots_of(*rest[blocks:])
    classes = full.shape[1]
    code_rows = -(-rows // LANES)
    metas = [ref[place, rows:, :].astype(jnp.float32) for ref, place in held]
    at = code_rows + AT_DEV
    papers = [jnp.max(meta[at : at + 1]).astype(jnp.int32) for meta in metas]
    scale_cols = col_scale(summed, class_target)
    block = scale_block(scale_cols)
    eye = identity(rows)
    codes = [code_column(meta_line(meta, rows), eye) for meta in metas]
    totals = [jnp.zeros((LANES, classes), jnp.float32) for _ in range(AT_DEV)]
    lane = lax.broadcasted_iota(jnp.int32, (rows, classes), 1).astype(jnp.float32)
    for shift, (ref, place) in enumerate(held):
        half = kernels[shift][pl.ds(pl.multiple_of(papers[shift] * rows, rows), rows), :]
        scale_rows = across(keep_share / row_sums(half, block), classes)
        share = half.astype(jnp.float32) * scale_cols * scale_rows
        labels = share + jnp.where(across(codes[shift], classes) == lane, 1.0 - keep_share, 0.0)
        parcel = lax.dot_general(
            ref[place, :rows, :],
            labels.astype(jnp.bfloat16),
            (((0,), (0,)), ((), ())),
            preferred_element_type=jnp.float32,
        )
        parcel = parcel.astype(jnp.bfloat16).astype(jnp.float32)
        for author in range(AT_DEV):
            at = code_rows + author
            totals[author] = totals[author] + parcel * metas[shift][at : at + 1, :1]
    kernel = jnp.concatenate(totals, axis=0) + class_prior[...]
    full[...] = kernel
    spread(jnp.sum(kernel, axis=0, keepdims=True), parts)


def paper_kernel(
    blocks, tile_paper, tile_author, tile_count, tiles, summed, class_prior, class_target, *rest
):
    kernels, (full, parts, *half) = rest[:blocks], rest[blocks:]
    _, rows, columns = tiles.shape
    classes = full.shape[1]
    scale_cols = col_scale(summed, class_target)
    block = scale_block(scale_cols)
    slots = sources(blocks)
    wide = jnp.concatenate([tiles[slot] for slot in slots], axis=1)
    labels = []
    for ref, slot in zip(kernels, slots):
        start = pl.multiple_of(tile_author[slot] * columns, columns)
        kernel = ref[pl.ds(start, columns), :]
        high, low = split(kernel)
        sums = row_sums(high, block) + jnp.dot(
            low, block[:, :LANES], preferred_element_type=jnp.float32
        )
        share = kernel * scale_cols * across(1.0 / sums, classes)
        labels.append(share.astype(jnp.bfloat16))
    column = jnp.zeros((1, classes), jnp.float32)
    for paper in range(full.shape[0] // rows):
        chosen = []
        for one, slot in zip(labels, slots):
            keep = (slot < tile_count[0]) & (tile_paper[slot] == paper)
            chosen.append(jnp.where(keep, one, jnp.zeros_like(one)))
        mass = jnp.dot(wide, jnp.concatenate(chosen, axis=0), preferred_element_type=jnp.float32)
        kernel = mass + class_prior[...]
        full[paper * rows : (paper + 1) * rows, :] = kernel
        for out in half:
            out[paper * rows : (paper + 1) * rows, :] = kernel.astype(jnp.bfloat16)
        column = column + jnp.sum(kernel, axis=0, keepdims=True)
    spread(column, parts)


def balance_kernel(kernel_ref, summed, class_target, parts):
    next_sum(kernel_ref[...], summed, class_target, parts)


def final_kernel(
    rows, kernel_ref, summed, own, author_summed, class_target, seed_class, train_mask,
    out, scores, out_made, scores_made, left,
):
    classes = out.shape[1]
    scaled = own[...] * col_scale(author_summed, class_target)
    scores_made[...] = scaled * (classes / jnp.sum(scaled, axis=1, keepdims=True))
    copies = [pltpu.make_async_copy(scores_made, scores, left.at[0])]
    copies[0].start()
    scale_cols = col_scale(summed, class_target)
    eye = identity(rows)
    lane = lax.broadcasted_iota(jnp.int32, (rows, classes), 1).astype(jnp.float32)
    for paper, line in enumerate(code_lines(seed_class, train_mask, rows)):
        part = pl.ds(paper * rows, rows)
        scaled = kernel_ref[part, :] * scale_cols
        share = scaled * (1.0 / jnp.sum(scaled, axis=1, keepdims=True))
        code = across(code_column(line, eye), classes)
        updated = keep_share * share + jnp.where(code == lane, 1.0 - keep_share, 0.0)
        out_made[part, :] = classes * updated
        copies.append(pltpu.make_async_copy(out_made.at[part], out.at[part], left.at[paper + 1]))
        copies[-1].start()
    for copy in copies:
        copy.wait()


def in_hbm(value):
    return pltpu.with_memory_space_constraint(value, pltpu.HBM)


def exchange(parts):
    groups, blocks = lax.axis_size("grp"), lax.axis_size("blk")
    planes = [i // 2 if i % 2 == 0 else groups - 1 - i // 2 for i in range(groups)]
    order = [plane * blocks + i for plane in planes for i in range(blocks)]
    return lax.all_to_all(
        parts, AXES, split_axis=0, concat_axis=0, axis_index_groups=[order], tiled=True
    )


def on_device(
    tile_values,
    tile_paper,
    tile_author,
    tile_count,
    seed_class,
    train_mask,
    class_prior,
    class_target,
):
    f32 = jnp.float32
    bf16 = jnp.bfloat16
    shape = jax.ShapeDtypeStruct
    slots, rows, columns = tile_values.shape
    classes = class_prior.shape[0]
    papers = seed_class.shape[0]
    authors = AT_DEV * columns
    paper_tiles = papers // rows
    devices = lax.axis_size(AXES)
    prior = class_prior.reshape(1, classes)
    target = class_target.reshape(1, classes)
    seed_class = seed_class.reshape(papers // LANES, LANES)
    train_mask = train_mask.reshape(papers // LANES, LANES)
    parts = shape((devices, 1, classes), f32)

    inputs = (
        tile_paper, tile_author, seed_class, train_mask, prior, target, tile_values,
    )
    places = (SMEM, SMEM, VMEM, VMEM, VMEM, VMEM, VMEM)
    blocks = lax.axis_size("blk")
    load = shape((blocks // 2, rows + META, columns), bf16)
    moved = call(
        functools.partial(pack_kernel, rows),
        tuple(shape(one.shape, one.dtype) for one in inputs) + (load, load),
        [SMEM] + [HBM] * len(inputs),
        [pltpu.SemaphoreType.DMA((len(inputs),)), pltpu.SemaphoreType.DMA((2, blocks // 2))],
        places + (VMEM, VMEM),
    )(tile_count, *(in_hbm(one) for one in inputs))
    tile_paper, tile_author, seed_class, train_mask, prior, target, tile_values, keep, swap = moved
    swapped = lax.ppermute(swap, "blk", [(i, i ^ 1) for i in range(blocks)])
    local = call(
        functools.partial(first_sum_kernel, authors), parts, [SMEM, SMEM] + [VMEM] * 4
    )(tile_paper, tile_count, tile_values, seed_class, train_mask, prior)
    both = shape((2, rows + META, columns), bf16)
    pairs = call(pair_kernel, (both,) * (blocks // 2 - 1), [VMEM] * 2)(keep, swapped)
    local, *pairs = lax.optimization_barrier((local, *pairs))
    held = [keep, swapped] + [
        lax.ppermute(one, "blk", [(i, i ^ (2 * k)) for i in range(blocks)])
        for k, one in enumerate(pairs, 1)
    ]
    summed = exchange(local)

    author_out = (shape((authors, classes), f32), parts)
    paper_out = (shape((papers, classes), f32), parts, shape((papers, classes), bf16))

    def across_pairs(value, k):
        return lax.ppermute(value, "blk", [(i, i ^ (2 * k)) for i in range(blocks)])

    def to_other(value):
        return lax.ppermute(value, "blk", [(i, i ^ 1) for i in range(blocks)])

    def balance(kernel, sent, local, count):
        here, there = {0: sent}, {}
        for step in range(count):
            if step == 0:
                moves = [(here, k, across_pairs(sent, k)) for k in range(1, blocks // 2)][:2]
            elif step == 1:
                moves = [(there, 0, to_other(sent))]
                moves += [(here, k, across_pairs(sent, k)) for k in range(3, blocks // 2)]
            else:
                ready = [k for k in here if k not in there]
                if step + 1 < count:
                    ready = ready[:2]
                moves = [(there, k, to_other(here[k])) for k in ready]
            summed = exchange(local)
            summed, *moved = lax.optimization_barrier((summed, *(one for _, _, one in moves)))
            for (place, k, _), one in zip(moves, moved):
                place[k] = one
            if step + 1 < count:
                local = call(balance_kernel, parts, [VMEM] * 3)(kernel, summed, target)
                local, sent, *moved = lax.optimization_barrier((local, sent, *here.values()))
                here = dict(zip(here, moved))
        order = range(blocks // 2)
        return summed, [here[k] for k in order] + [there[k] for k in order]

    def last_balance(kernel, local):
        for step in range(ITERS):
            summed = exchange(local)
            if step + 1 < ITERS:
                local = call(balance_kernel, parts, [VMEM] * 3)(kernel, summed, target)
        return summed

    for repeat in range(ROUNDS):
        if repeat == 0:
            own, local = call(
                functools.partial(first_author_kernel, rows), author_out, [VMEM] * (3 + len(held))
            )(summed, prior, target, *held)
            left = ITERS - 1
        else:
            own, local = call(
                functools.partial(author_kernel, rows, blocks),
                author_out,
                [VMEM] * (3 + blocks + len(held)),
            )(summed, prior, target, *kernels, *held)
            left = ITERS
        author_summed, kernels = balance(own, own, local, left)
        last = repeat + 1 == ROUNDS
        kernel, local, *half = call(
            functools.partial(paper_kernel, blocks),
            paper_out[:2] if last else paper_out,
            [SMEM, SMEM, SMEM] + [VMEM] * (4 + blocks),
        )(
            tile_paper, tile_author, tile_count, tile_values, author_summed, prior, target, *kernels
        )
        if last:
            summed = last_balance(kernel, local)
        else:
            summed, kernels = balance(kernel, half[0], local, ITERS)
    return call(
        functools.partial(final_kernel, rows),
        (shape((papers, classes), f32), shape((authors, classes), f32)),
        [VMEM] * 7,
        [
            pltpu.VMEM((papers, classes), f32),
            pltpu.VMEM((authors, classes), f32),
            pltpu.SemaphoreType.DMA((1 + papers // rows,)),
        ],
        (HBM, HBM),
    )(kernel, summed, own, author_summed, target, seed_class, train_mask)


def solution(mesh):
    placed = (
        P(("grp", "blk"), None, None),
        P(("grp", "blk")),
        P(("grp", "blk")),
        P(("grp", "blk")),
        P(("grp", "blk")),
        P(("grp", "blk")),
        P(),
        P(),
    )
    return jax.shard_map(
        on_device,
        mesh=mesh,
        in_specs=placed,
        out_specs=(P(("grp", "blk"), None), P(("grp", "blk"), None)),
        check_vma=False,
    )
```

```python
import functools

import jax
import jax.numpy as jnp
from jax import lax
from jax.experimental import pallas as pl
from jax.experimental.pallas import tpu as pltpu
from jax.sharding import PartitionSpec as P

AT_DEV = 2
ITERS = 4
ROUNDS = 2
LANES = 128
META = 16

keep_share = 0.8

AXES = ("grp", "blk")
VMEM = pl.BlockSpec(memory_space=pltpu.VMEM)
SMEM = pl.BlockSpec(memory_space=pltpu.SMEM)
HBM = pl.BlockSpec(memory_space=pltpu.HBM)


def call(kernel, out_shape, in_specs, scratch_shapes=(), out_specs=None):
    if out_specs is None:
        out_specs = jax.tree.map(lambda _: VMEM, out_shape)
    return pl.pallas_call(
        kernel,
        out_shape=out_shape,
        in_specs=in_specs,
        out_specs=out_specs,
        scratch_shapes=list(scratch_shapes),
        compiler_params=pltpu.CompilerParams(vmem_limit_bytes=48 * 1024 * 1024),
    )


def col_scale(parts_ref, target_ref):
    return target_ref[...] / jnp.sum(parts_ref[...], axis=0)


def row_scale(kernel, scale_cols):
    return 1.0 / jnp.sum(kernel * scale_cols, axis=1, keepdims=True)


def spread(value, parts_ref):
    parts_ref[...] = jnp.broadcast_to(value[None], parts_ref.shape)


def split(value):
    high = value.astype(jnp.bfloat16)
    return high, (value - high.astype(jnp.float32)).astype(jnp.bfloat16)


def scale_block(scale_cols):
    wide = jnp.broadcast_to(scale_cols, (LANES, scale_cols.shape[1])).T
    return jnp.concatenate(split(wide), axis=1)


def row_sums(half, block):
    sums = jnp.dot(half, block, preferred_element_type=jnp.float32)
    return sums[:, :LANES] + sums[:, LANES:]


def across(column, classes):
    return jnp.concatenate([column] * (classes // LANES), axis=1)


def dot_rows(left, right):
    return lax.dot_general(
        left, right, (((1,), (1,)), ((), ())), preferred_element_type=jnp.float32
    )


def code_lines(seed_class, train_mask, rows):
    code = jnp.where(train_mask[...] == 1, seed_class[...], -1).astype(jnp.float32)
    line = jnp.concatenate([code[i : i + 1] for i in range(code.shape[0])], axis=1)
    papers = line.shape[1]
    wide = jnp.broadcast_to(line, (8, papers))
    lines = []
    for start in range(0, papers, rows):
        lines.append((pltpu.roll(wide, papers - start, 1) if start else wide)[:1, :rows])
    return lines


def meta_line(meta, rows):
    count = -(-rows // LANES)
    return jnp.concatenate([meta[i : i + 1] for i in range(count)], axis=1)[:, :rows]


def code_columns(lines):
    rows = lines[0].shape[1]
    wide = jnp.concatenate(lines, axis=0)
    wide = jnp.pad(wide, ((0, -len(lines) % 8), (0, -rows % LANES)))
    columns = wide.T
    return [columns[:rows, i : i + 1] for i in range(len(lines))]


def seeds_of(line, classes):
    class_line = lax.broadcasted_iota(jnp.int32, (classes, line.shape[1]), 0)
    return jnp.where(class_line.astype(jnp.float32) == line, 1.0, 0.0).astype(jnp.bfloat16)


def pack_kernel(rows, tile_count, *refs):
    count = 7
    ins, places = refs[:count], refs[count : 2 * count]
    keep, swap, ready, arrived = refs[2 * count :]
    tile_paper, tile_author, seed_class, train_mask = places[:4]
    tiles = ins[-1]
    pairs = keep.shape[0]
    me = lax.axis_index("blk")
    pair, side = lax.div(me, 2), lax.rem(me, 2)
    moves = [
        pltpu.make_async_copy(source, place, ready.at[i])
        for i, (source, place) in enumerate(zip(ins, places))
    ]
    for copy in moves[:-1]:
        copy.start()
    outs = []
    copies = []
    for k in range(pairs):
        for way, (out, to) in enumerate(((keep, side), (swap, 1 - side))):
            slot = 2 * lax.bitwise_xor(pair, k) + to
            copy = pltpu.make_async_copy(
                tiles.at[slot], out.at[k, pl.ds(0, rows)], arrived.at[way, k]
            )
            copy.start()
            copies.append(copy)
            outs.append((out, k, slot))
    moves[-1].start()
    for copy in moves[:4]:
        copy.wait()
    line = lax.broadcasted_iota(jnp.int32, (META, LANES), 0)
    code_rows = -(-rows // LANES)
    blocks = []
    for codes in code_lines(seed_class, train_mask, rows):
        pad = jnp.full((1, code_rows * LANES - rows), -1.0, jnp.float32)
        codes = jnp.concatenate([codes, pad], axis=1)
        block = jnp.zeros((META, LANES), jnp.float32)
        for i in range(code_rows):
            block = jnp.where(line == i, codes[:, i * LANES : (i + 1) * LANES], block)
        blocks.append(block)
    for out, k, slot in outs:
        paper = tile_paper[slot]
        live = slot < tile_count[0]
        block = blocks[0]
        for i in range(1, len(blocks)):
            block = jnp.where(paper == i, blocks[i], block)
        for author in range(AT_DEV):
            chosen = jnp.where(live & (tile_author[slot] == author), 1.0, 0.0)
            block = jnp.where(line == code_rows + author, chosen, block)
        block = jnp.where(line == code_rows + AT_DEV, paper.astype(jnp.float32), block)
        out[k, rows:, :] = block.astype(jnp.bfloat16)
    for copy in moves[4:] + copies:
        copy.wait()


def pair_kernel(keep, swapped, *outs):
    for k, out in enumerate(outs, 1):
        out[0] = keep[k]
        out[1] = swapped[k]


def sources(count):
    me = lax.axis_index("blk")
    pair, side = lax.div(me, 2), lax.rem(me, 2)
    pairs = [2 * lax.bitwise_xor(pair, k) for k in range(count // 2)]
    return [other + side for other in pairs] + [other + 1 - side for other in pairs]


def slots_of(keep, swapped, *pairs):
    return [(keep, 0), *((ref, 0) for ref in pairs), (swapped, 0), *((ref, 1) for ref in pairs)]


def first_sum_kernel(
    authors, tile_paper, tile_count, tiles, seed_class, train_mask, class_prior, parts
):
    slots, rows, columns = tiles.shape
    classes = parts.shape[2]
    ones = jnp.ones((8, columns), jnp.bfloat16)
    total = authors * class_prior[...]
    for paper, codes in enumerate(code_lines(seed_class, train_mask, rows)):
        weight = jnp.zeros((rows, columns), jnp.float32)
        for slot in range(slots):
            chosen = (slot < tile_count[0]) & (tile_paper[slot] == paper)
            weight = weight + jnp.where(chosen, tiles[slot].astype(jnp.float32), 0.0)
        high, low = split(weight)
        high, low = split(dot_rows(ones, high) + dot_rows(ones, low))
        seeds = seeds_of(codes, classes)
        total = total + (dot_rows(high, seeds) + dot_rows(low, seeds))[:1]
    spread(total, parts)


def next_sum(kernel, summed, class_target, parts):
    scale_rows = row_scale(kernel, col_scale(summed, class_target))
    spread(jnp.sum(scale_rows * kernel, axis=0, keepdims=True), parts)


def first_author_kernel(rows, summed, class_prior, class_target, *rest):
    *held, full, parts = rest
    classes = full.shape[1]
    code_rows = -(-rows // LANES)
    totals = [jnp.zeros((classes, LANES), jnp.float32) for _ in range(AT_DEV)]
    for ref, place in slots_of(*held):
        meta = ref[place, rows:, :].astype(jnp.float32)
        seeds = seeds_of(meta_line(meta, rows), classes)
        parcel = jnp.dot(seeds, ref[place, :rows, :], preferred_element_type=jnp.float32)
        parcel = parcel.astype(jnp.bfloat16).astype(jnp.float32)
        for author in range(AT_DEV):
            chosen = meta[code_rows + author : code_rows + author + 1]
            totals[author] = totals[author] + parcel * chosen
    kernel = jnp.concatenate([total.T for total in totals], axis=0) + class_prior[...]
    full[...] = kernel
    next_sum(kernel, summed, class_target, parts)


def author_kernel(rows, blocks, summed, class_prior, class_target, *rest):
    *rest, full, parts = rest
    kernels, held = rest[:blocks], slots_of(*rest[blocks:])
    classes = full.shape[1]
    code_rows = -(-rows // LANES)
    metas = [ref[place, rows:, :].astype(jnp.float32) for ref, place in held]
    at = code_rows + AT_DEV
    papers = [jnp.max(meta[at : at + 1]).astype(jnp.int32) for meta in metas]
    scale_cols = col_scale(summed, class_target)
    block = scale_block(scale_cols)
    codes = code_columns([meta_line(meta, rows) for meta in metas])
    totals = [jnp.zeros((LANES, classes), jnp.float32) for _ in range(AT_DEV)]
    lane = lax.broadcasted_iota(jnp.int32, (rows, classes), 1).astype(jnp.float32)
    for shift, (ref, place) in enumerate(held):
        half = kernels[shift][pl.ds(pl.multiple_of(papers[shift] * rows, rows), rows), :]
        scale_rows = across(keep_share / row_sums(half, block), classes)
        share = half.astype(jnp.float32) * scale_cols * scale_rows
        labels = share + jnp.where(codes[shift] == lane, 1.0 - keep_share, 0.0)
        parcel = lax.dot_general(
            ref[place, :rows, :],
            labels.astype(jnp.bfloat16),
            (((0,), (0,)), ((), ())),
            preferred_element_type=jnp.float32,
        )
        parcel = parcel.astype(jnp.bfloat16).astype(jnp.float32)
        for author in range(AT_DEV):
            at = code_rows + author
            totals[author] = totals[author] + parcel * metas[shift][at : at + 1, :1]
    kernel = jnp.concatenate(totals, axis=0) + class_prior[...]
    full[...] = kernel
    spread(jnp.sum(kernel, axis=0, keepdims=True), parts)


def paper_kernel(
    blocks, tile_paper, tile_author, tile_count, tiles, summed, class_prior, class_target, *rest
):
    kernels, (full, parts, *half) = rest[:blocks], rest[blocks:]
    _, rows, columns = tiles.shape
    classes = full.shape[1]
    scale_cols = col_scale(summed, class_target)
    block = scale_block(scale_cols)
    slots = sources(blocks)
    wide = jnp.concatenate([tiles[slot] for slot in slots], axis=1)
    chosen = []
    for ref, slot in zip(kernels, slots):
        start = pl.multiple_of(tile_author[slot] * columns, columns)
        chosen.append(ref[pl.ds(start, columns), :])
    kernel = jnp.concatenate(chosen, axis=0)
    high, low = split(kernel)
    sums = row_sums(high, block) + jnp.dot(
        low, block[:, :LANES], preferred_element_type=jnp.float32
    )
    share = (kernel * scale_cols * across(1.0 / sums, classes)).astype(jnp.bfloat16)
    labels = [share[i * columns : (i + 1) * columns] for i in range(blocks)]
    column = jnp.zeros((1, classes), jnp.float32)
    for paper in range(full.shape[0] // rows):
        chosen = []
        for one, slot in zip(labels, slots):
            keep = (slot < tile_count[0]) & (tile_paper[slot] == paper)
            chosen.append(jnp.where(keep, one, jnp.zeros_like(one)))
        mass = jnp.dot(wide, jnp.concatenate(chosen, axis=0), preferred_element_type=jnp.float32)
        kernel = mass + class_prior[...]
        full[paper * rows : (paper + 1) * rows, :] = kernel
        for out in half:
            out[paper * rows : (paper + 1) * rows, :] = kernel.astype(jnp.bfloat16)
        column = column + jnp.sum(kernel, axis=0, keepdims=True)
    spread(column, parts)


def balance_kernel(kernel_ref, summed, class_target, parts):
    next_sum(kernel_ref[...], summed, class_target, parts)


def final_kernel(
    rows, kernel_ref, summed, own, author_summed, class_target, seed_class, train_mask,
    out, scores, out_made, scores_made, left,
):
    classes = out.shape[1]
    scaled = own[...] * col_scale(author_summed, class_target)
    scores_made[...] = scaled * (classes / jnp.sum(scaled, axis=1, keepdims=True))
    copies = [pltpu.make_async_copy(scores_made, scores, left.at[0])]
    copies[0].start()
    scale_cols = col_scale(summed, class_target)
    codes = code_columns(code_lines(seed_class, train_mask, rows))
    lane = lax.broadcasted_iota(jnp.int32, (rows, classes), 1).astype(jnp.float32)
    for paper, code in enumerate(codes):
        part = pl.ds(paper * rows, rows)
        scaled = kernel_ref[part, :] * scale_cols
        share = scaled * (1.0 / jnp.sum(scaled, axis=1, keepdims=True))
        updated = keep_share * share + jnp.where(code == lane, 1.0 - keep_share, 0.0)
        out_made[part, :] = classes * updated
        copies.append(pltpu.make_async_copy(out_made.at[part], out.at[part], left.at[paper + 1]))
        copies[-1].start()
    for copy in copies:
        copy.wait()


def in_hbm(value):
    return pltpu.with_memory_space_constraint(value, pltpu.HBM)


def exchange(parts):
    return lax.all_to_all(parts, AXES, split_axis=0, concat_axis=0, tiled=True)


def on_device(
    tile_values,
    tile_paper,
    tile_author,
    tile_count,
    seed_class,
    train_mask,
    class_prior,
    class_target,
):
    f32 = jnp.float32
    bf16 = jnp.bfloat16
    shape = jax.ShapeDtypeStruct
    slots, rows, columns = tile_values.shape
    classes = class_prior.shape[0]
    papers = seed_class.shape[0]
    authors = AT_DEV * columns
    paper_tiles = papers // rows
    devices = lax.axis_size(AXES)
    prior = class_prior.reshape(1, classes)
    target = class_target.reshape(1, classes)
    seed_class = seed_class.reshape(papers // LANES, LANES)
    train_mask = train_mask.reshape(papers // LANES, LANES)
    parts = shape((devices, 1, classes), f32)

    inputs = (
        tile_paper, tile_author, seed_class, train_mask, prior, target, tile_values,
    )
    places = (SMEM, SMEM, VMEM, VMEM, VMEM, VMEM, VMEM)
    blocks = lax.axis_size("blk")
    load = shape((blocks // 2, rows + META, columns), bf16)
    moved = call(
        functools.partial(pack_kernel, rows),
        tuple(shape(one.shape, one.dtype) for one in inputs) + (load, load),
        [SMEM] + [HBM] * len(inputs),
        [pltpu.SemaphoreType.DMA((len(inputs),)), pltpu.SemaphoreType.DMA((2, blocks // 2))],
        places + (VMEM, VMEM),
    )(tile_count, *(in_hbm(one) for one in inputs))
    tile_paper, tile_author, seed_class, train_mask, prior, target, tile_values, keep, swap = moved
    swapped = lax.ppermute(swap, "blk", [(i, i ^ 1) for i in range(blocks)])
    local = call(
        functools.partial(first_sum_kernel, authors), parts, [SMEM, SMEM] + [VMEM] * 4
    )(tile_paper, tile_count, tile_values, seed_class, train_mask, prior)
    both = shape((2, rows + META, columns), bf16)
    pairs = call(pair_kernel, (both,) * (blocks // 2 - 1), [VMEM] * 2)(keep, swapped)
    local, *pairs = lax.optimization_barrier((local, *pairs))
    held = [keep, swapped] + [
        lax.ppermute(one, "blk", [(i, i ^ (2 * k)) for i in range(blocks)])
        for k, one in enumerate(pairs, 1)
    ]
    summed = exchange(local)

    author_out = (shape((authors, classes), f32), parts)
    paper_out = (shape((papers, classes), f32), parts, shape((papers, classes), bf16))

    def across_pairs(value, k):
        return lax.ppermute(value, "blk", [(i, i ^ (2 * k)) for i in range(blocks)])

    def to_other(value):
        return lax.ppermute(value, "blk", [(i, i ^ 1) for i in range(blocks)])

    def balance(kernel, sent, local, count):
        here, there = {0: sent}, {}
        for step in range(count):
            if step == 0:
                moves = [(here, k, across_pairs(sent, k)) for k in (1, 2) if k < blocks // 2]
            elif step == 1:
                moves = [(there, 0, to_other(sent))]
                for k in range(3, blocks // 2):
                    got = across_pairs(here[1], 2) if k == 3 else across_pairs(sent, k)
                    moves.append((here, k, got))
            else:
                moves = [(there, k, to_other(here[k])) for k in here if k not in there]
            summed = exchange(local)
            summed, *moved = lax.optimization_barrier((summed, *(one for _, _, one in moves)))
            for (place, k, _), one in zip(moves, moved):
                place[k] = one
            if step + 1 < count:
                local = call(balance_kernel, parts, [VMEM] * 3)(kernel, summed, target)
                local, sent, *moved = lax.optimization_barrier((local, sent, *here.values()))
                here = dict(zip(here, moved))
        order = range(blocks // 2)
        return summed, [here[k] for k in order] + [there[k] for k in order]

    def last_balance(kernel, local):
        for step in range(ITERS):
            summed = exchange(local)
            if step + 1 < ITERS:
                local = call(balance_kernel, parts, [VMEM] * 3)(kernel, summed, target)
        return summed

    for repeat in range(ROUNDS):
        if repeat == 0:
            own, local = call(
                functools.partial(first_author_kernel, rows), author_out, [VMEM] * (3 + len(held))
            )(summed, prior, target, *held)
            left = ITERS - 1
        else:
            own, local = call(
                functools.partial(author_kernel, rows, blocks),
                author_out,
                [VMEM] * (3 + blocks + len(held)),
            )(summed, prior, target, *kernels, *held)
            left = ITERS
        author_summed, kernels = balance(own, own, local, left)
        last = repeat + 1 == ROUNDS
        kernel, local, *half = call(
            functools.partial(paper_kernel, blocks),
            paper_out[:2] if last else paper_out,
            [SMEM, SMEM, SMEM] + [VMEM] * (4 + blocks),
        )(
            tile_paper, tile_author, tile_count, tile_values, author_summed, prior, target, *kernels
        )
        if last:
            summed = last_balance(kernel, local)
        else:
            summed, kernels = balance(kernel, half[0], local, ITERS)
    return call(
        functools.partial(final_kernel, rows),
        (shape((papers, classes), f32), shape((authors, classes), f32)),
        [VMEM] * 7,
        [
            pltpu.VMEM((papers, classes), f32),
            pltpu.VMEM((authors, classes), f32),
            pltpu.SemaphoreType.DMA((1 + papers // rows,)),
        ],
        (HBM, HBM),
    )(kernel, summed, own, author_summed, target, seed_class, train_mask)


def solution(mesh):
    placed = (
        P(("grp", "blk"), None, None),
        P(("grp", "blk")),
        P(("grp", "blk")),
        P(("grp", "blk")),
        P(("grp", "blk")),
        P(("grp", "blk")),
        P(),
        P(),
    )
    return jax.shard_map(
        on_device,
        mesh=mesh,
        in_specs=placed,
        out_specs=(P(("grp", "blk"), None), P(("grp", "blk"), None)),
        check_vma=False,
    )
```

```python
import functools

import jax
import jax.numpy as jnp
from jax import lax
from jax.experimental import pallas as pl
from jax.experimental.pallas import tpu as pltpu
from jax.sharding import PartitionSpec as P

AT_DEV = 2
ITERS = 4
ROUNDS = 2
LANES = 128
META = 16

keep_share = 0.8

AXES = ("grp", "blk")
VMEM = pl.BlockSpec(memory_space=pltpu.VMEM)
SMEM = pl.BlockSpec(memory_space=pltpu.SMEM)
HBM = pl.BlockSpec(memory_space=pltpu.HBM)


def call(kernel, out_shape, in_specs, scratch_shapes=(), out_specs=None):
    if out_specs is None:
        out_specs = jax.tree.map(lambda _: VMEM, out_shape)
    return pl.pallas_call(
        kernel,
        out_shape=out_shape,
        in_specs=in_specs,
        out_specs=out_specs,
        scratch_shapes=list(scratch_shapes),
        compiler_params=pltpu.CompilerParams(vmem_limit_bytes=48 * 1024 * 1024),
    )


def col_scale(parts_ref, target_ref):
    return target_ref[...] / jnp.sum(parts_ref[...], axis=0)


def row_scale(kernel, scale_cols):
    return 1.0 / jnp.sum(kernel * scale_cols, axis=1, keepdims=True)


def spread(value, parts_ref):
    parts_ref[...] = jnp.broadcast_to(value[None], parts_ref.shape)


def code_lines(seed_class, train_mask, rows):
    code = jnp.where(train_mask[...] == 1, seed_class[...], -1).astype(jnp.float32)
    line = jnp.concatenate([code[i : i + 1] for i in range(code.shape[0])], axis=1)
    papers = line.shape[1]
    wide = jnp.broadcast_to(line, (8, papers))
    lines = []
    for start in range(0, papers, rows):
        lines.append((pltpu.roll(wide, papers - start, 1) if start else wide)[:1, :rows])
    return lines


def meta_line(meta, rows):
    count = -(-rows // LANES)
    return jnp.concatenate([meta[i : i + 1] for i in range(count)], axis=1)[:, :rows]


def code_columns(lines):
    rows = lines[0].shape[1]
    wide = jnp.concatenate(lines, axis=0)
    wide = jnp.pad(wide, ((0, -len(lines) % 8), (0, -rows % LANES)))
    columns = wide.T
    return [columns[:rows, i : i + 1] for i in range(len(lines))]


def seeds_of(line, classes):
    class_line = lax.broadcasted_iota(jnp.int32, (classes, line.shape[1]), 0)
    return jnp.where(class_line.astype(jnp.float32) == line, 1.0, 0.0).astype(jnp.bfloat16)


def pack_kernel(rows, tile_count, *refs):
    tiles, *refs = refs
    count = 6
    ins, places = refs[:count], refs[count : 2 * count]
    keep, swap, ready, arrived = refs[2 * count :]
    tile_paper, tile_author, seed_class, train_mask = places[:4]
    pairs = keep.shape[0]
    me = lax.axis_index("blk")
    pair, side = lax.div(me, 2), lax.rem(me, 2)
    moves = [
        pltpu.make_async_copy(source, place, ready.at[i])
        for i, (source, place) in enumerate(zip(ins, places))
    ]
    for copy in moves:
        copy.start()
    outs = []
    copies = []
    for k in range(pairs):
        for way, (out, to) in enumerate(((keep, side), (swap, 1 - side))):
            slot = 2 * lax.bitwise_xor(pair, k) + to
            copy = pltpu.make_async_copy(
                tiles.at[slot], out.at[k, pl.ds(0, rows)], arrived.at[way, k]
            )
            copy.start()
            copies.append(copy)
            outs.append((out, k, slot))
    for copy in moves[:4]:
        copy.wait()
    line = lax.broadcasted_iota(jnp.int32, (META, LANES), 0)
    code_rows = -(-rows // LANES)
    blocks = []
    for codes in code_lines(seed_class, train_mask, rows):
        pad = jnp.full((1, code_rows * LANES - rows), -1.0, jnp.float32)
        codes = jnp.concatenate([codes, pad], axis=1)
        block = jnp.zeros((META, LANES), jnp.float32)
        for i in range(code_rows):
            block = jnp.where(line == i, codes[:, i * LANES : (i + 1) * LANES], block)
        blocks.append(block)
    for out, k, slot in outs:
        paper = tile_paper[slot]
        live = slot < tile_count[0]
        block = blocks[0]
        for i in range(1, len(blocks)):
            block = jnp.where(paper == i, blocks[i], block)
        for author in range(AT_DEV):
            chosen = jnp.where(live & (tile_author[slot] == author), 1.0, 0.0)
            block = jnp.where(line == code_rows + author, chosen, block)
        block = jnp.where(line == code_rows + AT_DEV, paper.astype(jnp.float32), block)
        out[k, rows:, :] = block.astype(jnp.bfloat16)
    for copy in moves[4:] + copies:
        copy.wait()


def pair_kernel(keep, swapped, *outs):
    for k, out in enumerate(outs, 1):
        out[0] = keep[k]
        out[1] = swapped[k]


def sources(count):
    me = lax.axis_index("blk")
    pair, side = lax.div(me, 2), lax.rem(me, 2)
    pairs = [2 * lax.bitwise_xor(pair, k) for k in range(count // 2)]
    return [other + side for other in pairs] + [other + 1 - side for other in pairs]


def slots_of(keep, swapped, *pairs):
    return [(keep, 0), *((ref, 0) for ref in pairs), (swapped, 0), *((ref, 1) for ref in pairs)]


def first_sum_kernel(
    authors, rows, tile_paper, tile_count, keep, swap, seed_class, train_mask, class_prior, parts
):
    pairs, _, columns = keep.shape
    classes = parts.shape[2]
    slots = sources(2 * pairs)
    tiles = [ref[k, :rows, :].astype(jnp.float32) for ref in (keep, swap) for k in range(pairs)]
    lane = lax.broadcasted_iota(jnp.int32, (rows, classes), 1).astype(jnp.float32)
    total = authors * class_prior[...]
    for paper, code in enumerate(code_columns(code_lines(seed_class, train_mask, rows))):
        weight = jnp.zeros((rows, columns), jnp.float32)
        for slot, tile in zip(slots, tiles):
            chosen = (slot < tile_count[0]) & (tile_paper[slot] == paper)
            weight = weight + jnp.where(chosen, tile, 0.0)
        weight = jnp.sum(weight, axis=1, keepdims=True)
        seeds = jnp.where(code == lane, weight, 0.0)
        total = total + jnp.sum(seeds, axis=0, keepdims=True)
    spread(total, parts)


def next_sum(kernel, summed, class_target, parts):
    scale_rows = row_scale(kernel, col_scale(summed, class_target))
    spread(jnp.sum(scale_rows * kernel, axis=0, keepdims=True), parts)


def first_author_kernel(rows, summed, class_prior, class_target, *rest):
    *held, full, parts = rest
    classes = full.shape[1]
    code_rows = -(-rows // LANES)
    totals = [jnp.zeros((classes, LANES), jnp.float32) for _ in range(AT_DEV)]
    for ref, place in slots_of(*held):
        meta = ref[place, rows:, :].astype(jnp.float32)
        seeds = seeds_of(meta_line(meta, rows), classes)
        parcel = jnp.dot(seeds, ref[place, :rows, :], preferred_element_type=jnp.float32)
        parcel = parcel.astype(jnp.bfloat16).astype(jnp.float32)
        for author in range(AT_DEV):
            chosen = meta[code_rows + author : code_rows + author + 1]
            totals[author] = totals[author] + parcel * chosen
    kernel = jnp.concatenate([total.T for total in totals], axis=0) + class_prior[...]
    full[...] = kernel
    next_sum(kernel, summed, class_target, parts)


def author_kernel(rows, blocks, summed, class_prior, class_target, *rest):
    *rest, full, parts = rest
    kernels, held = rest[:blocks], slots_of(*rest[blocks:])
    classes = full.shape[1]
    code_rows = -(-rows // LANES)
    metas = [ref[place, rows:, :].astype(jnp.float32) for ref, place in held]
    at = code_rows + AT_DEV
    papers = [jnp.max(meta[at : at + 1]).astype(jnp.int32) for meta in metas]
    scale_cols = col_scale(summed, class_target)
    codes = code_columns([meta_line(meta, rows) for meta in metas])
    totals = [jnp.zeros((LANES, classes), jnp.float32) for _ in range(AT_DEV)]
    lane = lax.broadcasted_iota(jnp.int32, (rows, classes), 1).astype(jnp.float32)
    for shift, (ref, place) in enumerate(held):
        half = kernels[shift][pl.ds(pl.multiple_of(papers[shift] * rows, rows), rows), :]
        scaled = half.astype(jnp.float32) * scale_cols
        share = scaled * (keep_share / jnp.sum(scaled, axis=1, keepdims=True))
        labels = share + jnp.where(codes[shift] == lane, 1.0 - keep_share, 0.0)
        parcel = lax.dot_general(
            ref[place, :rows, :],
            labels.astype(jnp.bfloat16),
            (((0,), (0,)), ((), ())),
            preferred_element_type=jnp.float32,
        )
        parcel = parcel.astype(jnp.bfloat16).astype(jnp.float32)
        for author in range(AT_DEV):
            at = code_rows + author
            totals[author] = totals[author] + parcel * metas[shift][at : at + 1, :1]
    kernel = jnp.concatenate(totals, axis=0) + class_prior[...]
    full[...] = kernel
    spread(jnp.sum(kernel, axis=0, keepdims=True), parts)


def paper_kernel(
    blocks, rows, tile_paper, tile_author, tile_count, keep, swap, summed, class_prior,
    class_target, *rest,
):
    kernels, (full, parts, *half) = rest[:blocks], rest[blocks:]
    pairs, _, columns = keep.shape
    classes = full.shape[1]
    scale_cols = col_scale(summed, class_target)
    slots = sources(blocks)
    wide = [ref[k, :rows, :] for ref in (keep, swap) for k in range(pairs)]
    wide = jnp.concatenate(wide, axis=1)
    labels = []
    for ref, slot in zip(kernels, slots):
        start = pl.multiple_of(tile_author[slot] * columns, columns)
        scaled = ref[pl.ds(start, columns), :] * scale_cols
        share = scaled * (1.0 / jnp.sum(scaled, axis=1, keepdims=True))
        labels.append(share.astype(jnp.bfloat16))
    column = jnp.zeros((1, classes), jnp.float32)
    for paper in range(full.shape[0] // rows):
        chosen = []
        for one, slot in zip(labels, slots):
            mine = (slot < tile_count[0]) & (tile_paper[slot] == paper)
            chosen.append(jnp.where(mine, one, jnp.zeros_like(one)))
        mass = jnp.dot(wide, jnp.concatenate(chosen, axis=0), preferred_element_type=jnp.float32)
        kernel = mass + class_prior[...]
        full[paper * rows : (paper + 1) * rows, :] = kernel
        for out in half:
            out[paper * rows : (paper + 1) * rows, :] = kernel.astype(jnp.bfloat16)
        column = column + jnp.sum(kernel, axis=0, keepdims=True)
    spread(column, parts)


def balance_kernel(kernel_ref, summed, class_target, parts):
    next_sum(kernel_ref[...], summed, class_target, parts)


def final_kernel(
    rows, kernel_ref, summed, own, author_summed, class_target, seed_class, train_mask,
    out, scores, out_made, scores_made, left,
):
    classes = out.shape[1]
    scaled = own[...] * col_scale(author_summed, class_target)
    scores_made[...] = scaled * (classes / jnp.sum(scaled, axis=1, keepdims=True))
    copies = [pltpu.make_async_copy(scores_made, scores, left.at[0])]
    copies[0].start()
    scale_cols = col_scale(summed, class_target)
    codes = code_columns(code_lines(seed_class, train_mask, rows))
    lane = lax.broadcasted_iota(jnp.int32, (rows, classes), 1).astype(jnp.float32)
    for paper, code in enumerate(codes):
        part = pl.ds(paper * rows, rows)
        scaled = kernel_ref[part, :] * scale_cols
        share = scaled * (1.0 / jnp.sum(scaled, axis=1, keepdims=True))
        updated = keep_share * share + jnp.where(code == lane, 1.0 - keep_share, 0.0)
        out_made[part, :] = classes * updated
        copies.append(pltpu.make_async_copy(out_made.at[part], out.at[part], left.at[paper + 1]))
        copies[-1].start()
    for copy in copies:
        copy.wait()


def in_hbm(value):
    return pltpu.with_memory_space_constraint(value, pltpu.HBM)


def exchange(parts):
    return lax.all_to_all(parts, AXES, split_axis=0, concat_axis=0, tiled=True)


def on_device(
    tile_values,
    tile_paper,
    tile_author,
    tile_count,
    seed_class,
    train_mask,
    class_prior,
    class_target,
):
    f32 = jnp.float32
    bf16 = jnp.bfloat16
    shape = jax.ShapeDtypeStruct
    slots, rows, columns = tile_values.shape
    classes = class_prior.shape[0]
    papers = seed_class.shape[0]
    authors = AT_DEV * columns
    paper_tiles = papers // rows
    devices = lax.axis_size(AXES)
    prior = class_prior.reshape(1, classes)
    target = class_target.reshape(1, classes)
    seed_class = seed_class.reshape(papers // LANES, LANES)
    train_mask = train_mask.reshape(papers // LANES, LANES)
    parts = shape((devices, 1, classes), f32)

    inputs = (
        tile_paper, tile_author, seed_class, train_mask, prior, target,
    )
    places = (SMEM, SMEM, VMEM, VMEM, VMEM, VMEM)
    blocks = lax.axis_size("blk")
    load = shape((blocks // 2, rows + META, columns), bf16)
    moved = call(
        functools.partial(pack_kernel, rows),
        tuple(shape(one.shape, one.dtype) for one in inputs) + (load, load),
        [SMEM, HBM] + [HBM] * len(inputs),
        [pltpu.SemaphoreType.DMA((len(inputs),)), pltpu.SemaphoreType.DMA((2, blocks // 2))],
        places + (VMEM, VMEM),
    )(tile_count, in_hbm(tile_values), *(in_hbm(one) for one in inputs))
    tile_paper, tile_author, seed_class, train_mask, prior, target, keep, swap = moved
    swapped = lax.ppermute(swap, "blk", [(i, i ^ 1) for i in range(blocks)])
    local = call(
        functools.partial(first_sum_kernel, authors, rows), parts, [SMEM, SMEM] + [VMEM] * 5
    )(tile_paper, tile_count, keep, swap, seed_class, train_mask, prior)
    both = shape((2, rows + META, columns), bf16)
    pairs = call(pair_kernel, (both,) * (blocks // 2 - 1), [VMEM] * 2)(keep, swapped)
    local, *pairs = lax.optimization_barrier((local, *pairs))
    held = [keep, swapped] + [
        lax.ppermute(one, "blk", [(i, i ^ (2 * k)) for i in range(blocks)])
        for k, one in enumerate(pairs, 1)
    ]
    summed = exchange(local)

    author_out = (shape((authors, classes), f32), parts)
    paper_out = (shape((papers, classes), f32), parts, shape((papers, classes), bf16))

    def across_pairs(value, k):
        return lax.ppermute(value, "blk", [(i, i ^ (2 * k)) for i in range(blocks)])

    def to_other(value):
        return lax.ppermute(value, "blk", [(i, i ^ 1) for i in range(blocks)])

    def balance(kernel, sent, local, count):
        here, there = {0: sent}, {}
        for step in range(count):
            if step == 0:
                moves = [(here, k, across_pairs(sent, k)) for k in (1, 2) if k < blocks // 2]
            elif step == 1:
                moves = [(there, 0, to_other(sent))]
                for k in range(3, blocks // 2):
                    got = across_pairs(here[1], 2) if k == 3 else across_pairs(sent, k)
                    moves.append((here, k, got))
            else:
                moves = [(there, k, to_other(here[k])) for k in here if k not in there]
            summed = exchange(local)
            summed, *moved = lax.optimization_barrier((summed, *(one for _, _, one in moves)))
            for (place, k, _), one in zip(moves, moved):
                place[k] = one
            if step + 1 < count:
                local = call(balance_kernel, parts, [VMEM] * 3)(kernel, summed, target)
                local, sent, *moved = lax.optimization_barrier((local, sent, *here.values()))
                here = dict(zip(here, moved))
        order = range(blocks // 2)
        return summed, [here[k] for k in order] + [there[k] for k in order]

    def last_balance(kernel, local):
        for step in range(ITERS):
            summed = exchange(local)
            if step + 1 < ITERS:
                local = call(balance_kernel, parts, [VMEM] * 3)(kernel, summed, target)
        return summed

    for repeat in range(ROUNDS):
        if repeat == 0:
            own, local = call(
                functools.partial(first_author_kernel, rows), author_out, [VMEM] * (3 + len(held))
            )(summed, prior, target, *held)
            left = ITERS - 1
        else:
            own, local = call(
                functools.partial(author_kernel, rows, blocks),
                author_out,
                [VMEM] * (3 + blocks + len(held)),
            )(summed, prior, target, *kernels, *held)
            left = ITERS
        author_summed, kernels = balance(own, own, local, left)
        last = repeat + 1 == ROUNDS
        kernel, local, *half = call(
            functools.partial(paper_kernel, blocks, rows),
            paper_out[:2] if last else paper_out,
            [SMEM, SMEM, SMEM] + [VMEM] * (5 + blocks),
        )(
            tile_paper, tile_author, tile_count, keep, swap, author_summed, prior, target, *kernels
        )
        if last:
            summed = last_balance(kernel, local)
        else:
            summed, kernels = balance(kernel, half[0], local, ITERS)
    return call(
        functools.partial(final_kernel, rows),
        (shape((papers, classes), f32), shape((authors, classes), f32)),
        [VMEM] * 7,
        [
            pltpu.VMEM((papers, classes), f32),
            pltpu.VMEM((authors, classes), f32),
            pltpu.SemaphoreType.DMA((1 + papers // rows,)),
        ],
        (HBM, HBM),
    )(kernel, summed, own, author_summed, target, seed_class, train_mask)


def solution(mesh):
    placed = (
        P(("grp", "blk"), None, None),
        P(("grp", "blk")),
        P(("grp", "blk")),
        P(("grp", "blk")),
        P(("grp", "blk")),
        P(("grp", "blk")),
        P(),
        P(),
    )
    return jax.shard_map(
        on_device,
        mesh=mesh,
        in_specs=placed,
        out_specs=(P(("grp", "blk"), None), P(("grp", "blk"), None)),
        check_vma=False,
    )
```

```python
import functools

import jax
import jax.numpy as jnp
from jax import lax
from jax.experimental import pallas as pl
from jax.experimental.pallas import tpu as pltpu
from jax.sharding import PartitionSpec as P

AT_DEV = 2
ITERS = 4
ROUNDS = 2
LANES = 128
META = 16

keep_share = 0.8

AXES = ("grp", "blk")
VMEM = pl.BlockSpec(memory_space=pltpu.VMEM)
SMEM = pl.BlockSpec(memory_space=pltpu.SMEM)
HBM = pl.BlockSpec(memory_space=pltpu.HBM)


def call(kernel, out_shape, in_specs, scratch_shapes=(), out_specs=None):
    if out_specs is None:
        out_specs = jax.tree.map(lambda _: VMEM, out_shape)
    return pl.pallas_call(
        kernel,
        out_shape=out_shape,
        in_specs=in_specs,
        out_specs=out_specs,
        scratch_shapes=list(scratch_shapes),
        compiler_params=pltpu.CompilerParams(vmem_limit_bytes=48 * 1024 * 1024),
    )


def col_scale(parts_ref, target_ref):
    return target_ref[...] / jnp.sum(parts_ref[...], axis=0)


def row_scale(kernel, scale_cols):
    return 1.0 / jnp.sum(kernel * scale_cols, axis=1, keepdims=True)


def spread(value, parts_ref):
    parts_ref[...] = jnp.broadcast_to(value[None], parts_ref.shape)


def code_lines(seed_class, train_mask, rows):
    code = jnp.where(train_mask[...] == 1, seed_class[...], -1).astype(jnp.float32)
    line = jnp.concatenate([code[i : i + 1] for i in range(code.shape[0])], axis=1)
    papers = line.shape[1]
    wide = jnp.broadcast_to(line, (8, papers))
    lines = []
    for start in range(0, papers, rows):
        lines.append((pltpu.roll(wide, papers - start, 1) if start else wide)[:1, :rows])
    return lines


def meta_line(meta, rows):
    count = -(-rows // LANES)
    return jnp.concatenate([meta[i : i + 1] for i in range(count)], axis=1)[:, :rows]


def code_columns(lines):
    rows = lines[0].shape[1]
    wide = jnp.concatenate(lines, axis=0)
    wide = jnp.pad(wide, ((0, -len(lines) % 8), (0, -rows % LANES)))
    columns = wide.T
    return [columns[:rows, i : i + 1] for i in range(len(lines))]


def seeds_of(line, classes):
    class_line = lax.broadcasted_iota(jnp.int32, (classes, line.shape[1]), 0)
    return jnp.where(class_line.astype(jnp.float32) == line, 1.0, 0.0).astype(jnp.bfloat16)


def pack_kernel(rows, tile_count, *refs):
    tiles, *refs = refs
    count = 6
    ins, places = refs[:count], refs[count : 2 * count]
    keep, swap, ready, arrived = refs[2 * count :]
    tile_paper, tile_author, seed_class, train_mask = places[:4]
    pairs = keep.shape[0]
    me = lax.axis_index("blk")
    pair, side = lax.div(me, 2), lax.rem(me, 2)
    moves = [
        pltpu.make_async_copy(source, place, ready.at[i])
        for i, (source, place) in enumerate(zip(ins, places))
    ]
    for copy in moves:
        copy.start()
    outs = []
    copies = []
    for k in range(pairs):
        for way, (out, to) in enumerate(((keep, side), (swap, 1 - side))):
            slot = 2 * lax.bitwise_xor(pair, k) + to
            copy = pltpu.make_async_copy(
                tiles.at[slot], out.at[k, pl.ds(0, rows)], arrived.at[way, k]
            )
            copy.start()
            copies.append(copy)
            outs.append((out, k, slot))
    for copy in moves[:4]:
        copy.wait()
    line = lax.broadcasted_iota(jnp.int32, (META, LANES), 0)
    code_rows = -(-rows // LANES)
    blocks = []
    for codes in code_lines(seed_class, train_mask, rows):
        pad = jnp.full((1, code_rows * LANES - rows), -1.0, jnp.float32)
        codes = jnp.concatenate([codes, pad], axis=1)
        block = jnp.zeros((META, LANES), jnp.float32)
        for i in range(code_rows):
            block = jnp.where(line == i, codes[:, i * LANES : (i + 1) * LANES], block)
        blocks.append(block)
    for out, k, slot in outs:
        paper = tile_paper[slot]
        live = slot < tile_count[0]
        block = blocks[0]
        for i in range(1, len(blocks)):
            block = jnp.where(paper == i, blocks[i], block)
        for author in range(AT_DEV):
            chosen = jnp.where(live & (tile_author[slot] == author), 1.0, 0.0)
            block = jnp.where(line == code_rows + author, chosen, block)
        block = jnp.where(line == code_rows + AT_DEV, paper.astype(jnp.float32), block)
        out[k, rows:, :] = block.astype(jnp.bfloat16)
    for copy in moves[4:] + copies:
        copy.wait()


def pair_kernel(keep, swapped, *outs):
    for k, out in enumerate(outs, 1):
        out[0] = keep[k]
        out[1] = swapped[k]


def sources(count):
    me = lax.axis_index("blk")
    pair, side = lax.div(me, 2), lax.rem(me, 2)
    pairs = [2 * lax.bitwise_xor(pair, k) for k in range(count // 2)]
    return [other + side for other in pairs] + [other + 1 - side for other in pairs]


def slots_of(keep, swapped, *pairs):
    return [(keep, 0), *((ref, 0) for ref in pairs), (swapped, 0), *((ref, 1) for ref in pairs)]


def first_sum_kernel(
    authors, rows, tile_paper, tile_count, keep, swap, seed_class, train_mask, class_prior, parts
):
    pairs, _, columns = keep.shape
    classes = parts.shape[2]
    slots = sources(2 * pairs)
    tiles = [ref[k, :rows, :].astype(jnp.float32) for ref in (keep, swap) for k in range(pairs)]
    lane = lax.broadcasted_iota(jnp.int32, (rows, classes), 1).astype(jnp.float32)
    total = authors * class_prior[...]
    for paper, code in enumerate(code_columns(code_lines(seed_class, train_mask, rows))):
        weight = jnp.zeros((rows, columns), jnp.float32)
        for slot, tile in zip(slots, tiles):
            chosen = (slot < tile_count[0]) & (tile_paper[slot] == paper)
            weight = weight + jnp.where(chosen, tile, 0.0)
        weight = jnp.sum(weight, axis=1, keepdims=True)
        seeds = jnp.where(code == lane, weight, 0.0)
        total = total + jnp.sum(seeds, axis=0, keepdims=True)
    spread(total, parts)


def next_sum(kernel, summed, class_target, parts):
    scale_rows = row_scale(kernel, col_scale(summed, class_target))
    spread(jnp.sum(scale_rows * kernel, axis=0, keepdims=True), parts)


def first_author_kernel(rows, summed, class_prior, class_target, *rest):
    *held, full, parts = rest
    classes = full.shape[1]
    code_rows = -(-rows // LANES)
    totals = [jnp.zeros((classes, LANES), jnp.float32) for _ in range(AT_DEV)]
    for ref, place in slots_of(*held):
        meta = ref[place, rows:, :].astype(jnp.float32)
        seeds = seeds_of(meta_line(meta, rows), classes)
        parcel = jnp.dot(seeds, ref[place, :rows, :], preferred_element_type=jnp.float32)
        parcel = parcel.astype(jnp.bfloat16).astype(jnp.float32)
        for author in range(AT_DEV):
            chosen = meta[code_rows + author : code_rows + author + 1]
            totals[author] = totals[author] + parcel * chosen
    kernel = jnp.concatenate([total.T for total in totals], axis=0) + class_prior[...]
    full[...] = kernel
    next_sum(kernel, summed, class_target, parts)


def author_kernel(rows, blocks, summed, class_prior, class_target, *rest):
    *rest, full, parts = rest
    kernels, held = rest[:blocks], slots_of(*rest[blocks:])
    classes = full.shape[1]
    code_rows = -(-rows // LANES)
    metas = [ref[place, rows:, :].astype(jnp.float32) for ref, place in held]
    at = code_rows + AT_DEV
    papers = [jnp.max(meta[at : at + 1]).astype(jnp.int32) for meta in metas]
    scale_cols = col_scale(summed, class_target)
    codes = code_columns([meta_line(meta, rows) for meta in metas])
    totals = [jnp.zeros((LANES, classes), jnp.float32) for _ in range(AT_DEV)]
    lane = lax.broadcasted_iota(jnp.int32, (rows, classes), 1).astype(jnp.float32)
    for shift, (ref, place) in enumerate(held):
        half = kernels[shift][pl.ds(pl.multiple_of(papers[shift] * rows, rows), rows), :]
        scaled = half.astype(jnp.float32) * scale_cols
        share = scaled * (keep_share / jnp.sum(scaled, axis=1, keepdims=True))
        labels = share + jnp.where(codes[shift] == lane, 1.0 - keep_share, 0.0)
        parcel = lax.dot_general(
            ref[place, :rows, :],
            labels.astype(jnp.bfloat16),
            (((0,), (0,)), ((), ())),
            preferred_element_type=jnp.float32,
        )
        parcel = parcel.astype(jnp.bfloat16).astype(jnp.float32)
        for author in range(AT_DEV):
            at = code_rows + author
            totals[author] = totals[author] + parcel * metas[shift][at : at + 1, :1]
    kernel = jnp.concatenate(totals, axis=0) + class_prior[...]
    full[...] = kernel
    spread(jnp.sum(kernel, axis=0, keepdims=True), parts)


def paper_kernel(
    blocks, rows, tile_paper, tile_author, tile_count, keep, swap, summed, class_prior,
    class_target, *rest,
):
    kernels, (full, parts, *half) = rest[:blocks], rest[blocks:]
    pairs, _, columns = keep.shape
    classes = full.shape[1]
    scale_cols = col_scale(summed, class_target)
    slots = sources(blocks)
    wide = [ref[k, :rows, :] for ref in (keep, swap) for k in range(pairs)]
    wide = jnp.concatenate(wide, axis=1)
    labels = []
    for ref, slot in zip(kernels, slots):
        start = pl.multiple_of(tile_author[slot] * columns, columns)
        scaled = ref[pl.ds(start, columns), :] * scale_cols
        share = scaled * (1.0 / jnp.sum(scaled, axis=1, keepdims=True))
        labels.append(share.astype(jnp.bfloat16))
    column = jnp.zeros((1, classes), jnp.float32)
    for paper in range(full.shape[0] // rows):
        chosen = []
        for one, slot in zip(labels, slots):
            mine = (slot < tile_count[0]) & (tile_paper[slot] == paper)
            chosen.append(jnp.where(mine, one, jnp.zeros_like(one)))
        mass = jnp.dot(wide, jnp.concatenate(chosen, axis=0), preferred_element_type=jnp.float32)
        kernel = mass + class_prior[...]
        full[paper * rows : (paper + 1) * rows, :] = kernel
        for out in half:
            out[paper * rows : (paper + 1) * rows, :] = kernel.astype(jnp.bfloat16)
        column = column + jnp.sum(kernel, axis=0, keepdims=True)
    spread(column, parts)


def balance_kernel(*refs):
    *kernels, summed, class_target, parts = refs
    scale_cols = col_scale(summed, class_target)
    total = None
    for ref in kernels:
        kernel = ref[...].astype(jnp.float32)
        local = jnp.sum(row_scale(kernel, scale_cols) * kernel, axis=0, keepdims=True)
        total = local if total is None else total + local
    spread(total, parts)


def final_kernel(
    rows, kernel_ref, summed, own, author_summed, class_target, seed_class, train_mask,
    out, scores, out_made, scores_made, left,
):
    classes = out.shape[1]
    scaled = own[...] * col_scale(author_summed, class_target)
    scores_made[...] = scaled * (classes / jnp.sum(scaled, axis=1, keepdims=True))
    copies = [pltpu.make_async_copy(scores_made, scores, left.at[0])]
    copies[0].start()
    scale_cols = col_scale(summed, class_target)
    codes = code_columns(code_lines(seed_class, train_mask, rows))
    lane = lax.broadcasted_iota(jnp.int32, (rows, classes), 1).astype(jnp.float32)
    for paper, code in enumerate(codes):
        part = pl.ds(paper * rows, rows)
        scaled = kernel_ref[part, :] * scale_cols
        share = scaled * (1.0 / jnp.sum(scaled, axis=1, keepdims=True))
        updated = keep_share * share + jnp.where(code == lane, 1.0 - keep_share, 0.0)
        out_made[part, :] = classes * updated
        copies.append(pltpu.make_async_copy(out_made.at[part], out.at[part], left.at[paper + 1]))
        copies[-1].start()
    for copy in copies:
        copy.wait()


def in_hbm(value):
    return pltpu.with_memory_space_constraint(value, pltpu.HBM)


def exchange(parts):
    return lax.all_to_all(parts, AXES, split_axis=0, concat_axis=0, tiled=True)


def narrow_exchange(parts):
    groups, blocks = lax.axis_size("grp"), lax.axis_size("blk")
    sets = [
        [i * blocks + pair + side for i in range(groups) for side in range(2)]
        for pair in range(0, blocks, 2)
    ]
    return lax.all_to_all(
        parts, AXES, split_axis=0, concat_axis=0, axis_index_groups=sets, tiled=True
    )


def on_device(
    tile_values,
    tile_paper,
    tile_author,
    tile_count,
    seed_class,
    train_mask,
    class_prior,
    class_target,
):
    f32 = jnp.float32
    bf16 = jnp.bfloat16
    shape = jax.ShapeDtypeStruct
    slots, rows, columns = tile_values.shape
    classes = class_prior.shape[0]
    papers = seed_class.shape[0]
    authors = AT_DEV * columns
    paper_tiles = papers // rows
    devices = lax.axis_size(AXES)
    prior = class_prior.reshape(1, classes)
    target = class_target.reshape(1, classes)
    seed_class = seed_class.reshape(papers // LANES, LANES)
    train_mask = train_mask.reshape(papers // LANES, LANES)
    parts = shape((devices, 1, classes), f32)

    inputs = (
        tile_paper, tile_author, seed_class, train_mask, prior, target,
    )
    places = (SMEM, SMEM, VMEM, VMEM, VMEM, VMEM)
    blocks = lax.axis_size("blk")
    load = shape((blocks // 2, rows + META, columns), bf16)
    moved = call(
        functools.partial(pack_kernel, rows),
        tuple(shape(one.shape, one.dtype) for one in inputs) + (load, load),
        [SMEM, HBM] + [HBM] * len(inputs),
        [pltpu.SemaphoreType.DMA((len(inputs),)), pltpu.SemaphoreType.DMA((2, blocks // 2))],
        places + (VMEM, VMEM),
    )(tile_count, in_hbm(tile_values), *(in_hbm(one) for one in inputs))
    tile_paper, tile_author, seed_class, train_mask, prior, target, keep, swap = moved
    swapped = lax.ppermute(swap, "blk", [(i, i ^ 1) for i in range(blocks)])
    local = call(
        functools.partial(first_sum_kernel, authors, rows), parts, [SMEM, SMEM] + [VMEM] * 5
    )(tile_paper, tile_count, keep, swap, seed_class, train_mask, prior)
    both = shape((2, rows + META, columns), bf16)
    pairs = call(pair_kernel, (both,) * (blocks // 2 - 1), [VMEM] * 2)(keep, swapped)
    local, *pairs = lax.optimization_barrier((local, *pairs))
    held = [keep, swapped] + [
        lax.ppermute(one, "blk", [(i, i ^ (2 * k)) for i in range(blocks)])
        for k, one in enumerate(pairs, 1)
    ]
    summed = exchange(local)

    narrow = shape((2 * lax.axis_size("grp"), 1, classes), f32)
    author_out = (shape((authors, classes), f32), parts)
    paper_out = (shape((papers, classes), f32), parts, shape((papers, classes), bf16))

    def across_pairs(value, k):
        return lax.ppermute(value, "blk", [(i, i ^ (2 * k)) for i in range(blocks)])

    def to_other(value):
        return lax.ppermute(value, "blk", [(i, i ^ 1) for i in range(blocks)])

    def balance(kernel, sent, local, count):
        here, there = {0: sent}, {}
        for step in range(count):
            if step == 0:
                moves = [(here, k, across_pairs(sent, k)) for k in (1, 2) if k < blocks // 2]
            elif step == 1:
                moves = [(there, 0, to_other(sent))]
                for k in range(3, blocks // 2):
                    got = across_pairs(here[1], 2) if k == 3 else across_pairs(sent, k)
                    moves.append((here, k, got))
            else:
                moves = [(there, k, to_other(here[k])) for k in here if k not in there]
            summed = narrow_exchange(local) if step > 1 else exchange(local)
            summed, *moved = lax.optimization_barrier((summed, *(one for _, _, one in moves)))
            for (place, k, _), one in zip(moves, moved):
                place[k] = one
            if step + 1 < count:
                rest = [here[k] for k in range(blocks // 2)] if step > 0 else [kernel]
                local = call(
                    balance_kernel, narrow if step > 0 else parts, [VMEM] * (len(rest) + 2)
                )(*rest, summed, target)
                local, sent, *moved = lax.optimization_barrier((local, sent, *here.values()))
                here = dict(zip(here, moved))
        order = range(blocks // 2)
        return summed, [here[k] for k in order] + [there[k] for k in order]

    def last_balance(kernel, local):
        for step in range(ITERS):
            summed = exchange(local)
            if step + 1 < ITERS:
                local = call(balance_kernel, parts, [VMEM] * 3)(kernel, summed, target)
        return summed

    for repeat in range(ROUNDS):
        if repeat == 0:
            own, local = call(
                functools.partial(first_author_kernel, rows), author_out, [VMEM] * (3 + len(held))
            )(summed, prior, target, *held)
            left = ITERS - 1
        else:
            own, local = call(
                functools.partial(author_kernel, rows, blocks),
                author_out,
                [VMEM] * (3 + blocks + len(held)),
            )(summed, prior, target, *kernels, *held)
            left = ITERS
        author_summed, kernels = balance(own, own, local, left)
        last = repeat + 1 == ROUNDS
        kernel, local, *half = call(
            functools.partial(paper_kernel, blocks, rows),
            paper_out[:2] if last else paper_out,
            [SMEM, SMEM, SMEM] + [VMEM] * (5 + blocks),
        )(
            tile_paper, tile_author, tile_count, keep, swap, author_summed, prior, target, *kernels
        )
        if last:
            summed = last_balance(kernel, local)
        else:
            summed, kernels = balance(kernel, half[0], local, ITERS)
    return call(
        functools.partial(final_kernel, rows),
        (shape((papers, classes), f32), shape((authors, classes), f32)),
        [VMEM] * 7,
        [
            pltpu.VMEM((papers, classes), f32),
            pltpu.VMEM((authors, classes), f32),
            pltpu.SemaphoreType.DMA((1 + papers // rows,)),
        ],
        (HBM, HBM),
    )(kernel, summed, own, author_summed, target, seed_class, train_mask)


def solution(mesh):
    placed = (
        P(("grp", "blk"), None, None),
        P(("grp", "blk")),
        P(("grp", "blk")),
        P(("grp", "blk")),
        P(("grp", "blk")),
        P(("grp", "blk")),
        P(),
        P(),
    )
    return jax.shard_map(
        on_device,
        mesh=mesh,
        in_specs=placed,
        out_specs=(P(("grp", "blk"), None), P(("grp", "blk"), None)),
        check_vma=False,
    )
```

```python
import functools

import jax
import jax.numpy as jnp
from jax import lax
from jax.experimental import pallas as pl
from jax.experimental.pallas import tpu as pltpu
from jax.sharding import PartitionSpec as P

AT_DEV = 2
ITERS = 4
ROUNDS = 2
LANES = 128
META = 16

keep_share = 0.8

AXES = ("grp", "blk")
VMEM = pl.BlockSpec(memory_space=pltpu.VMEM)
SMEM = pl.BlockSpec(memory_space=pltpu.SMEM)
HBM = pl.BlockSpec(memory_space=pltpu.HBM)


def call(kernel, out_shape, in_specs, scratch_shapes=(), out_specs=None):
    if out_specs is None:
        out_specs = jax.tree.map(lambda _: VMEM, out_shape)
    return pl.pallas_call(
        kernel,
        out_shape=out_shape,
        in_specs=in_specs,
        out_specs=out_specs,
        scratch_shapes=list(scratch_shapes),
        compiler_params=pltpu.CompilerParams(vmem_limit_bytes=48 * 1024 * 1024),
    )


def col_scale(parts_ref, target_ref):
    return target_ref[...] / jnp.sum(parts_ref[...], axis=0)


def row_scale(kernel, scale_cols):
    return 1.0 / jnp.sum(kernel * scale_cols, axis=1, keepdims=True)


def spread(value, parts_ref):
    parts_ref[...] = jnp.broadcast_to(value[None], parts_ref.shape)


def code_lines(seed_class, train_mask, rows):
    code = jnp.where(train_mask[...] == 1, seed_class[...], -1).astype(jnp.float32)
    line = jnp.concatenate([code[i : i + 1] for i in range(code.shape[0])], axis=1)
    papers = line.shape[1]
    wide = jnp.broadcast_to(line, (8, papers))
    lines = []
    for start in range(0, papers, rows):
        lines.append((pltpu.roll(wide, papers - start, 1) if start else wide)[:1, :rows])
    return lines


def meta_line(meta, rows):
    count = -(-rows // LANES)
    return jnp.concatenate([meta[i : i + 1] for i in range(count)], axis=1)[:, :rows]


def code_columns(lines):
    rows = lines[0].shape[1]
    wide = jnp.concatenate(lines, axis=0)
    wide = jnp.pad(wide, ((0, -len(lines) % 8), (0, -rows % LANES)))
    columns = wide.T
    return [columns[:rows, i : i + 1] for i in range(len(lines))]


def code_column(line, classes):
    rows = line.shape[1]
    across = lax.broadcasted_iota(jnp.int32, (rows, rows), 1)
    eye = jnp.where(lax.broadcasted_iota(jnp.int32, (rows, rows), 0) == across, 1.0, 0.0)
    wide = jnp.broadcast_to(line, (LANES, rows)).astype(jnp.bfloat16)
    column = lax.dot_general(
        eye.astype(jnp.bfloat16),
        wide,
        (((1,), (1,)), ((), ())),
        preferred_element_type=jnp.float32,
    )
    return jnp.concatenate([column] * (classes // LANES), axis=1)


def seeds_of(line, classes):
    class_line = lax.broadcasted_iota(jnp.int32, (classes, line.shape[1]), 0)
    return jnp.where(class_line.astype(jnp.float32) == line, 1.0, 0.0).astype(jnp.bfloat16)


def pack_kernel(rows, tile_count, *refs):
    tiles, *refs = refs
    count = 6
    ins, places = refs[:count], refs[count : 2 * count]
    keep, swap, ready, arrived = refs[2 * count :]
    tile_paper, tile_author, seed_class, train_mask = places[:4]
    pairs = keep.shape[0]
    me = lax.axis_index("blk")
    pair, side = lax.div(me, 2), lax.rem(me, 2)
    moves = [
        pltpu.make_async_copy(source, place, ready.at[i])
        for i, (source, place) in enumerate(zip(ins, places))
    ]
    for copy in moves:
        copy.start()
    outs = []
    copies = []
    for k in range(pairs):
        for way, (out, to) in enumerate(((keep, side), (swap, 1 - side))):
            slot = 2 * lax.bitwise_xor(pair, k) + to
            copy = pltpu.make_async_copy(
                tiles.at[slot], out.at[k, pl.ds(0, rows)], arrived.at[way, k]
            )
            copy.start()
            copies.append(copy)
            outs.append((out, k, slot))
    for copy in moves[:4]:
        copy.wait()
    line = lax.broadcasted_iota(jnp.int32, (META, LANES), 0)
    code_rows = -(-rows // LANES)
    blocks = []
    for codes in code_lines(seed_class, train_mask, rows):
        pad = jnp.full((1, code_rows * LANES - rows), -1.0, jnp.float32)
        codes = jnp.concatenate([codes, pad], axis=1)
        block = jnp.zeros((META, LANES), jnp.float32)
        for i in range(code_rows):
            block = jnp.where(line == i, codes[:, i * LANES : (i + 1) * LANES], block)
        blocks.append(block)
    for out, k, slot in outs:
        paper = tile_paper[slot]
        live = slot < tile_count[0]
        block = blocks[0]
        for i in range(1, len(blocks)):
            block = jnp.where(paper == i, blocks[i], block)
        for author in range(AT_DEV):
            chosen = jnp.where(live & (tile_author[slot] == author), 1.0, 0.0)
            block = jnp.where(line == code_rows + author, chosen, block)
        block = jnp.where(line == code_rows + AT_DEV, paper.astype(jnp.float32), block)
        out[k, rows:, :] = block.astype(jnp.bfloat16)
    for copy in moves[4:] + copies:
        copy.wait()


def pair_kernel(keep, swapped, *outs):
    for k, out in enumerate(outs, 1):
        out[0] = keep[k]
        out[1] = swapped[k]


def sources(count):
    me = lax.axis_index("blk")
    pair, side = lax.div(me, 2), lax.rem(me, 2)
    pairs = [2 * lax.bitwise_xor(pair, k) for k in range(count // 2)]
    return [other + side for other in pairs] + [other + 1 - side for other in pairs]


def slots_of(keep, swapped, *pairs):
    return [(keep, 0), *((ref, 0) for ref in pairs), (swapped, 0), *((ref, 1) for ref in pairs)]


def first_sum_kernel(
    authors, rows, tile_paper, tile_count, keep, swap, seed_class, train_mask, class_prior, parts
):
    pairs, _, columns = keep.shape
    classes = parts.shape[2]
    slots = sources(2 * pairs)
    tiles = [ref[k, :rows, :].astype(jnp.float32) for ref in (keep, swap) for k in range(pairs)]
    lane = lax.broadcasted_iota(jnp.int32, (rows, classes), 1).astype(jnp.float32)
    total = authors * class_prior[...]
    for paper, code in enumerate(code_columns(code_lines(seed_class, train_mask, rows))):
        weight = jnp.zeros((rows, columns), jnp.float32)
        for slot, tile in zip(slots, tiles):
            chosen = (slot < tile_count[0]) & (tile_paper[slot] == paper)
            weight = weight + jnp.where(chosen, tile, 0.0)
        weight = jnp.sum(weight, axis=1, keepdims=True)
        seeds = jnp.where(code == lane, weight, 0.0)
        total = total + jnp.sum(seeds, axis=0, keepdims=True)
    spread(total, parts)


def next_sum(kernel, summed, class_target, parts):
    scale_rows = row_scale(kernel, col_scale(summed, class_target))
    spread(jnp.sum(scale_rows * kernel, axis=0, keepdims=True), parts)


def first_author_kernel(rows, summed, class_prior, class_target, *rest):
    *held, full, parts = rest
    classes = full.shape[1]
    code_rows = -(-rows // LANES)
    totals = [jnp.zeros((classes, LANES), jnp.float32) for _ in range(AT_DEV)]
    for ref, place in slots_of(*held):
        meta = ref[place, rows:, :].astype(jnp.float32)
        seeds = seeds_of(meta_line(meta, rows), classes)
        parcel = jnp.dot(seeds, ref[place, :rows, :], preferred_element_type=jnp.float32)
        parcel = parcel.astype(jnp.bfloat16).astype(jnp.float32)
        for author in range(AT_DEV):
            chosen = meta[code_rows + author : code_rows + author + 1]
            totals[author] = totals[author] + parcel * chosen
    kernel = jnp.concatenate([total.T for total in totals], axis=0) + class_prior[...]
    full[...] = kernel
    next_sum(kernel, summed, class_target, parts)


def author_kernel(rows, blocks, summed, class_prior, class_target, *rest):
    *rest, full, parts = rest
    kernels, held = rest[:blocks], slots_of(*rest[blocks:])
    classes = full.shape[1]
    code_rows = -(-rows // LANES)
    metas = [ref[place, rows:, :].astype(jnp.float32) for ref, place in held]
    at = code_rows + AT_DEV
    papers = [jnp.max(meta[at : at + 1]).astype(jnp.int32) for meta in metas]
    scale_cols = col_scale(summed, class_target)
    codes = code_columns([meta_line(meta, rows) for meta in metas])
    totals = [jnp.zeros((LANES, classes), jnp.float32) for _ in range(AT_DEV)]
    lane = lax.broadcasted_iota(jnp.int32, (rows, classes), 1).astype(jnp.float32)
    for shift, (ref, place) in enumerate(held):
        half = kernels[shift][pl.ds(pl.multiple_of(papers[shift] * rows, rows), rows), :]
        scaled = half.astype(jnp.float32) * scale_cols
        share = scaled * (keep_share / jnp.sum(scaled, axis=1, keepdims=True))
        labels = share + jnp.where(codes[shift] == lane, 1.0 - keep_share, 0.0)
        parcel = lax.dot_general(
            ref[place, :rows, :],
            labels.astype(jnp.bfloat16),
            (((0,), (0,)), ((), ())),
            preferred_element_type=jnp.float32,
        )
        parcel = parcel.astype(jnp.bfloat16).astype(jnp.float32)
        for author in range(AT_DEV):
            at = code_rows + author
            totals[author] = totals[author] + parcel * metas[shift][at : at + 1, :1]
    kernel = jnp.concatenate(totals, axis=0) + class_prior[...]
    full[...] = kernel
    spread(jnp.sum(kernel, axis=0, keepdims=True), parts)


def paper_kernel(
    blocks, rows, tile_paper, tile_author, tile_count, keep, swap, summed, class_prior,
    class_target, *rest,
):
    kernels, (full, parts, *half) = rest[:blocks], rest[blocks:]
    pairs, _, columns = keep.shape
    classes = full.shape[1]
    scale_cols = col_scale(summed, class_target)
    slots = sources(blocks)
    wide = [ref[k, :rows, :] for ref in (keep, swap) for k in range(pairs)]
    wide = jnp.concatenate(wide, axis=1)
    labels = []
    for ref, slot in zip(kernels, slots):
        start = pl.multiple_of(tile_author[slot] * columns, columns)
        scaled = ref[pl.ds(start, columns), :] * scale_cols
        share = scaled * (1.0 / jnp.sum(scaled, axis=1, keepdims=True))
        labels.append(share.astype(jnp.bfloat16))
    column = jnp.zeros((1, classes), jnp.float32)
    for paper in range(full.shape[0] // rows):
        chosen = []
        for one, slot in zip(labels, slots):
            mine = (slot < tile_count[0]) & (tile_paper[slot] == paper)
            chosen.append(jnp.where(mine, one, jnp.zeros_like(one)))
        mass = jnp.dot(wide, jnp.concatenate(chosen, axis=0), preferred_element_type=jnp.float32)
        kernel = mass + class_prior[...]
        full[paper * rows : (paper + 1) * rows, :] = kernel
        for out in half:
            out[paper * rows : (paper + 1) * rows, :] = kernel.astype(jnp.bfloat16)
        column = column + jnp.sum(kernel, axis=0, keepdims=True)
    spread(column, parts)


def balance_kernel(*refs):
    *kernels, summed, class_target, parts = refs
    scale_cols = col_scale(summed, class_target)
    total = None
    for ref in kernels:
        kernel = ref[...].astype(jnp.float32)
        local = jnp.sum(row_scale(kernel, scale_cols) * kernel, axis=0, keepdims=True)
        total = local if total is None else total + local
    spread(total, parts)


def final_kernel(
    rows, kernel_ref, summed, own, author_summed, class_target, seed_class, train_mask,
    out, scores, out_made, scores_made, left,
):
    classes = out.shape[1]
    scaled = own[...] * col_scale(author_summed, class_target)
    scores_made[...] = scaled * (classes / jnp.sum(scaled, axis=1, keepdims=True))
    copies = [pltpu.make_async_copy(scores_made, scores, left.at[0])]
    copies[0].start()
    scale_cols = col_scale(summed, class_target)
    lane = lax.broadcasted_iota(jnp.int32, (rows, classes), 1).astype(jnp.float32)
    for paper, line in enumerate(code_lines(seed_class, train_mask, rows)):
        code = code_column(line, classes)
        part = pl.ds(paper * rows, rows)
        scaled = kernel_ref[part, :] * scale_cols
        share = scaled * (1.0 / jnp.sum(scaled, axis=1, keepdims=True))
        updated = keep_share * share + jnp.where(code == lane, 1.0 - keep_share, 0.0)
        out_made[part, :] = classes * updated
        copies.append(pltpu.make_async_copy(out_made.at[part], out.at[part], left.at[paper + 1]))
        copies[-1].start()
    for copy in copies:
        copy.wait()


def in_hbm(value):
    return pltpu.with_memory_space_constraint(value, pltpu.HBM)


def exchange(parts):
    return lax.all_to_all(parts, AXES, split_axis=0, concat_axis=0, tiled=True)


def narrow_exchange(parts, sides):
    groups, blocks = lax.axis_size("grp"), lax.axis_size("blk")
    planes = sorted(range(groups), key=lambda i: abs(2 * i + 1 - groups))
    sets = [
        [i * blocks + first + side for i in planes for side in range(sides)]
        for first in range(0, blocks, sides)
    ]
    return lax.all_to_all(
        parts, AXES, split_axis=0, concat_axis=0, axis_index_groups=sets, tiled=True
    )


def on_device(
    tile_values,
    tile_paper,
    tile_author,
    tile_count,
    seed_class,
    train_mask,
    class_prior,
    class_target,
):
    f32 = jnp.float32
    bf16 = jnp.bfloat16
    shape = jax.ShapeDtypeStruct
    slots, rows, columns = tile_values.shape
    classes = class_prior.shape[0]
    papers = seed_class.shape[0]
    authors = AT_DEV * columns
    paper_tiles = papers // rows
    devices = lax.axis_size(AXES)
    prior = class_prior.reshape(1, classes)
    target = class_target.reshape(1, classes)
    seed_class = seed_class.reshape(papers // LANES, LANES)
    train_mask = train_mask.reshape(papers // LANES, LANES)
    parts = shape((devices, 1, classes), f32)

    inputs = (
        tile_paper, tile_author, seed_class, train_mask, prior, target,
    )
    places = (SMEM, SMEM, VMEM, VMEM, VMEM, VMEM)
    blocks = lax.axis_size("blk")
    load = shape((blocks // 2, rows + META, columns), bf16)
    moved = call(
        functools.partial(pack_kernel, rows),
        tuple(shape(one.shape, one.dtype) for one in inputs) + (load, load),
        [SMEM, HBM] + [HBM] * len(inputs),
        [pltpu.SemaphoreType.DMA((len(inputs),)), pltpu.SemaphoreType.DMA((2, blocks // 2))],
        places + (VMEM, VMEM),
    )(tile_count, in_hbm(tile_values), *(in_hbm(one) for one in inputs))
    tile_paper, tile_author, seed_class, train_mask, prior, target, keep, swap = moved
    swapped = lax.ppermute(swap, "blk", [(i, i ^ 1) for i in range(blocks)])
    local = call(
        functools.partial(first_sum_kernel, authors, rows), parts, [SMEM, SMEM] + [VMEM] * 5
    )(tile_paper, tile_count, keep, swap, seed_class, train_mask, prior)
    both = shape((2, rows + META, columns), bf16)
    pairs = call(pair_kernel, (both,) * (blocks // 2 - 1), [VMEM] * 2)(keep, swapped)
    local, *pairs = lax.optimization_barrier((local, *pairs))
    held = [keep, swapped] + [
        lax.ppermute(one, "blk", [(i, i ^ (2 * k)) for i in range(blocks)])
        for k, one in enumerate(pairs, 1)
    ]
    summed = exchange(local)

    author_out = (shape((authors, classes), f32), parts)
    paper_out = (shape((papers, classes), f32), parts, shape((papers, classes), bf16))

    def across_pairs(value, k):
        return lax.ppermute(value, "blk", [(i, i ^ (2 * k)) for i in range(blocks)])

    def to_other(value):
        return lax.ppermute(value, "blk", [(i, i ^ 1) for i in range(blocks)])

    def balance(kernel, sent, local, count):
        here, there = {0: sent}, {}
        sides = 0
        for step in range(count):
            if step == 0:
                moves = [(here, k, across_pairs(sent, k)) for k in (1, 2) if k < blocks // 2]
            elif step == 1:
                moves = [(there, 0, to_other(sent))]
                for k in range(3, blocks // 2):
                    got = across_pairs(here[1], 2) if k == 3 else across_pairs(sent, k)
                    moves.append((here, k, got))
            else:
                moves = [(there, k, to_other(here[k])) for k in here if k not in there]
            summed = narrow_exchange(local, sides) if sides else exchange(local)
            summed, *moved = lax.optimization_barrier((summed, *(one for _, _, one in moves)))
            for (place, k, _), one in zip(moves, moved):
                place[k] = one
            if step + 1 < count:
                added, size = [kernel], devices
                if step > 0:
                    added = list(here.values())
                    sides = 2
                    if step > 1:
                        added += list(there.values())
                        sides = 1
                    size = sides * lax.axis_size("grp")
                local = call(
                    balance_kernel, shape((size, 1, classes), f32), [VMEM] * (len(added) + 2)
                )(*added, summed, target)
                local, sent, *moved = lax.optimization_barrier((local, sent, *here.values()))
                here = dict(zip(here, moved))
        order = range(blocks // 2)
        return summed, [here[k] for k in order] + [there[k] for k in order]

    def last_balance(kernel, local):
        for step in range(ITERS):
            summed = exchange(local)
            if step + 1 < ITERS:
                local = call(balance_kernel, parts, [VMEM] * 3)(kernel, summed, target)
        return summed

    for repeat in range(ROUNDS):
        if repeat == 0:
            own, local = call(
                functools.partial(first_author_kernel, rows), author_out, [VMEM] * (3 + len(held))
            )(summed, prior, target, *held)
            left = ITERS - 1
        else:
            own, local = call(
                functools.partial(author_kernel, rows, blocks),
                author_out,
                [VMEM] * (3 + blocks + len(held)),
            )(summed, prior, target, *kernels, *held)
            left = ITERS
        author_summed, kernels = balance(own, own, local, left)
        last = repeat + 1 == ROUNDS
        kernel, local, *half = call(
            functools.partial(paper_kernel, blocks, rows),
            paper_out[:2] if last else paper_out,
            [SMEM, SMEM, SMEM] + [VMEM] * (5 + blocks),
        )(
            tile_paper, tile_author, tile_count, keep, swap, author_summed, prior, target, *kernels
        )
        if last:
            summed = last_balance(kernel, local)
        else:
            summed, kernels = balance(kernel, half[0], local, ITERS)
    return call(
        functools.partial(final_kernel, rows),
        (shape((papers, classes), f32), shape((authors, classes), f32)),
        [VMEM] * 7,
        [
            pltpu.VMEM((papers, classes), f32),
            pltpu.VMEM((authors, classes), f32),
            pltpu.SemaphoreType.DMA((1 + papers // rows,)),
        ],
        (HBM, HBM),
    )(kernel, summed, own, author_summed, target, seed_class, train_mask)


def solution(mesh):
    placed = (
        P(("grp", "blk"), None, None),
        P(("grp", "blk")),
        P(("grp", "blk")),
        P(("grp", "blk")),
        P(("grp", "blk")),
        P(("grp", "blk")),
        P(),
        P(),
    )
    return jax.shard_map(
        on_device,
        mesh=mesh,
        in_specs=placed,
        out_specs=(P(("grp", "blk"), None), P(("grp", "blk"), None)),
        check_vma=False,
    )
```

```python
import functools

import jax
import jax.numpy as jnp
from jax import lax
from jax.experimental import pallas as pl
from jax.experimental.pallas import tpu as pltpu
from jax.sharding import PartitionSpec as P

AT_DEV = 2
ITERS = 4
ROUNDS = 2
LANES = 128
META = 16

keep_share = 0.8

AXES = ("grp", "blk")
VMEM = pl.BlockSpec(memory_space=pltpu.VMEM)
SMEM = pl.BlockSpec(memory_space=pltpu.SMEM)
HBM = pl.BlockSpec(memory_space=pltpu.HBM)


def call(kernel, out_shape, in_specs, scratch_shapes=(), out_specs=None):
    if out_specs is None:
        out_specs = jax.tree.map(lambda _: VMEM, out_shape)
    return pl.pallas_call(
        kernel,
        out_shape=out_shape,
        in_specs=in_specs,
        out_specs=out_specs,
        scratch_shapes=list(scratch_shapes),
        compiler_params=pltpu.CompilerParams(vmem_limit_bytes=48 * 1024 * 1024),
    )


def col_scale(parts_ref, target_ref):
    return target_ref[...] / jnp.sum(parts_ref[...], axis=0)


def row_scale(kernel, scale_cols):
    return 1.0 / jnp.sum(kernel * scale_cols, axis=1, keepdims=True)


def spread(value, parts_ref):
    parts_ref[...] = jnp.broadcast_to(value[None], parts_ref.shape)


def code_lines(seed_class, train_mask, rows):
    code = jnp.where(train_mask[...] == 1, seed_class[...], -1).astype(jnp.float32)
    line = jnp.concatenate([code[i : i + 1] for i in range(code.shape[0])], axis=1)
    papers = line.shape[1]
    wide = jnp.broadcast_to(line, (8, papers))
    lines = []
    for start in range(0, papers, rows):
        lines.append((pltpu.roll(wide, papers - start, 1) if start else wide)[:1, :rows])
    return lines


def meta_line(meta, rows):
    count = -(-rows // LANES)
    return jnp.concatenate([meta[i : i + 1] for i in range(count)], axis=1)[:, :rows]


def code_columns(lines):
    rows = lines[0].shape[1]
    wide = jnp.concatenate(lines, axis=0)
    wide = jnp.pad(wide, ((0, -len(lines) % 8), (0, -rows % LANES)))
    columns = wide.T
    return [columns[:rows, i : i + 1] for i in range(len(lines))]


def code_column(line, classes):
    rows = line.shape[1]
    across = lax.broadcasted_iota(jnp.int32, (rows, rows), 1)
    eye = jnp.where(lax.broadcasted_iota(jnp.int32, (rows, rows), 0) == across, 1.0, 0.0)
    wide = jnp.broadcast_to(line, (LANES, rows)).astype(jnp.bfloat16)
    column = lax.dot_general(
        eye.astype(jnp.bfloat16),
        wide,
        (((1,), (1,)), ((), ())),
        preferred_element_type=jnp.float32,
    )
    return jnp.concatenate([column] * (classes // LANES), axis=1)


def seeds_of(line, classes):
    class_line = lax.broadcasted_iota(jnp.int32, (classes, line.shape[1]), 0)
    return jnp.where(class_line.astype(jnp.float32) == line, 1.0, 0.0).astype(jnp.bfloat16)


def pack_kernel(rows, tile_count, *refs):
    tiles, *refs = refs
    count = 6
    ins, places = refs[:count], refs[count : 2 * count]
    keep, swap, ready, arrived = refs[2 * count :]
    tile_paper, tile_author, seed_class, train_mask = places[:4]
    pairs = keep.shape[0]
    me = lax.axis_index("blk")
    pair, side = lax.div(me, 2), lax.rem(me, 2)
    moves = [
        pltpu.make_async_copy(source, place, ready.at[i])
        for i, (source, place) in enumerate(zip(ins, places))
    ]
    for copy in moves:
        copy.start()
    outs = []
    copies = []
    for k in range(pairs):
        for way, (out, to) in enumerate(((keep, side), (swap, 1 - side))):
            slot = 2 * lax.bitwise_xor(pair, k) + to
            copy = pltpu.make_async_copy(
                tiles.at[slot], out.at[k, pl.ds(0, rows)], arrived.at[way, k]
            )
            copy.start()
            copies.append(copy)
            outs.append((out, k, slot))
    for copy in moves[:4]:
        copy.wait()
    line = lax.broadcasted_iota(jnp.int32, (META, LANES), 0)
    code_rows = -(-rows // LANES)
    blocks = []
    for codes in code_lines(seed_class, train_mask, rows):
        pad = jnp.full((1, code_rows * LANES - rows), -1.0, jnp.float32)
        codes = jnp.concatenate([codes, pad], axis=1)
        block = jnp.zeros((META, LANES), jnp.float32)
        for i in range(code_rows):
            block = jnp.where(line == i, codes[:, i * LANES : (i + 1) * LANES], block)
        blocks.append(block)
    for out, k, slot in outs:
        paper = tile_paper[slot]
        live = slot < tile_count[0]
        block = blocks[0]
        for i in range(1, len(blocks)):
            block = jnp.where(paper == i, blocks[i], block)
        for author in range(AT_DEV):
            chosen = jnp.where(live & (tile_author[slot] == author), 1.0, 0.0)
            block = jnp.where(line == code_rows + author, chosen, block)
        block = jnp.where(line == code_rows + AT_DEV, paper.astype(jnp.float32), block)
        out[k, rows:, :] = block.astype(jnp.bfloat16)
    for copy in moves[4:] + copies:
        copy.wait()


def pair_kernel(keep, swapped, *outs):
    for k, out in enumerate(outs, 1):
        out[0] = keep[k]
        out[1] = swapped[k]


def sources(count):
    me = lax.axis_index("blk")
    pair, side = lax.div(me, 2), lax.rem(me, 2)
    pairs = [2 * lax.bitwise_xor(pair, k) for k in range(count // 2)]
    return [other + side for other in pairs] + [other + 1 - side for other in pairs]


def slots_of(keep, swapped, *pairs):
    return [(keep, 0), *((ref, 0) for ref in pairs), (swapped, 0), *((ref, 1) for ref in pairs)]


def first_sum_kernel(
    authors, rows, tile_paper, tile_count, keep, swap, seed_class, train_mask, class_prior, parts
):
    pairs, _, columns = keep.shape
    classes = parts.shape[2]
    slots = sources(2 * pairs)
    tiles = [ref[k, :rows, :].astype(jnp.float32) for ref in (keep, swap) for k in range(pairs)]
    lane = lax.broadcasted_iota(jnp.int32, (rows, classes), 1).astype(jnp.float32)
    total = authors * class_prior[...]
    for paper, code in enumerate(code_columns(code_lines(seed_class, train_mask, rows))):
        weight = jnp.zeros((rows, columns), jnp.float32)
        for slot, tile in zip(slots, tiles):
            chosen = (slot < tile_count[0]) & (tile_paper[slot] == paper)
            weight = weight + jnp.where(chosen, tile, 0.0)
        weight = jnp.sum(weight, axis=1, keepdims=True)
        seeds = jnp.where(code == lane, weight, 0.0)
        total = total + jnp.sum(seeds, axis=0, keepdims=True)
    spread(total, parts)


def next_sum(kernel, summed, class_target, parts):
    scale_rows = row_scale(kernel, col_scale(summed, class_target))
    spread(jnp.sum(scale_rows * kernel, axis=0, keepdims=True), parts)


def first_author_kernel(rows, summed, class_prior, class_target, *rest):
    *held, full, parts = rest
    classes = full.shape[1]
    code_rows = -(-rows // LANES)
    totals = [jnp.zeros((classes, LANES), jnp.float32) for _ in range(AT_DEV)]
    for ref, place in slots_of(*held):
        meta = ref[place, rows:, :].astype(jnp.float32)
        seeds = seeds_of(meta_line(meta, rows), classes)
        parcel = jnp.dot(seeds, ref[place, :rows, :], preferred_element_type=jnp.float32)
        parcel = parcel.astype(jnp.bfloat16).astype(jnp.float32)
        for author in range(AT_DEV):
            chosen = meta[code_rows + author : code_rows + author + 1]
            totals[author] = totals[author] + parcel * chosen
    kernel = jnp.concatenate([total.T for total in totals], axis=0) + class_prior[...]
    full[...] = kernel
    next_sum(kernel, summed, class_target, parts)


def author_kernel(rows, blocks, summed, class_prior, class_target, *rest):
    *rest, full, parts = rest
    kernels, held = rest[:blocks], slots_of(*rest[blocks:])
    classes = full.shape[1]
    code_rows = -(-rows // LANES)
    metas = [ref[place, rows:, :].astype(jnp.float32) for ref, place in held]
    at = code_rows + AT_DEV
    papers = [jnp.max(meta[at : at + 1]).astype(jnp.int32) for meta in metas]
    scale_cols = col_scale(summed, class_target)
    codes = code_columns([meta_line(meta, rows) for meta in metas])
    totals = [jnp.zeros((LANES, classes), jnp.float32) for _ in range(AT_DEV)]
    lane = lax.broadcasted_iota(jnp.int32, (rows, classes), 1).astype(jnp.float32)
    for shift, (ref, place) in enumerate(held):
        half = kernels[shift][pl.ds(pl.multiple_of(papers[shift] * rows, rows), rows), :]
        scaled = half.astype(jnp.float32) * scale_cols
        share = scaled * (keep_share / jnp.sum(scaled, axis=1, keepdims=True))
        labels = share + jnp.where(codes[shift] == lane, 1.0 - keep_share, 0.0)
        parcel = lax.dot_general(
            ref[place, :rows, :],
            labels.astype(jnp.bfloat16),
            (((0,), (0,)), ((), ())),
            preferred_element_type=jnp.float32,
        )
        parcel = parcel.astype(jnp.bfloat16).astype(jnp.float32)
        for author in range(AT_DEV):
            at = code_rows + author
            totals[author] = totals[author] + parcel * metas[shift][at : at + 1, :1]
    kernel = jnp.concatenate(totals, axis=0) + class_prior[...]
    full[...] = kernel
    spread(jnp.sum(kernel, axis=0, keepdims=True), parts)


def paper_kernel(
    blocks, rows, tile_paper, tile_author, tile_count, keep, swap, summed, class_prior,
    class_target, *rest,
):
    kernels, (full, parts, *half) = rest[:blocks], rest[blocks:]
    pairs, _, columns = keep.shape
    classes = full.shape[1]
    scale_cols = col_scale(summed, class_target)
    slots = sources(blocks)
    wide = [ref[k, :rows, :] for ref in (keep, swap) for k in range(pairs)]
    wide = jnp.concatenate(wide, axis=1)
    labels = []
    for ref, slot in zip(kernels, slots):
        start = pl.multiple_of(tile_author[slot] * columns, columns)
        scaled = ref[pl.ds(start, columns), :] * scale_cols
        share = scaled * (1.0 / jnp.sum(scaled, axis=1, keepdims=True))
        labels.append(share.astype(jnp.bfloat16))
    column = jnp.zeros((1, classes), jnp.float32)
    for paper in range(full.shape[0] // rows):
        chosen = []
        for one, slot in zip(labels, slots):
            mine = (slot < tile_count[0]) & (tile_paper[slot] == paper)
            chosen.append(jnp.where(mine, one, jnp.zeros_like(one)))
        mass = jnp.dot(wide, jnp.concatenate(chosen, axis=0), preferred_element_type=jnp.float32)
        kernel = mass + class_prior[...]
        full[paper * rows : (paper + 1) * rows, :] = kernel
        for out in half:
            out[paper * rows : (paper + 1) * rows, :] = kernel.astype(jnp.bfloat16)
        column = column + jnp.sum(kernel, axis=0, keepdims=True)
    spread(column, parts)


def balance_kernel(*refs):
    *kernels, summed, class_target, parts = refs
    scale_cols = col_scale(summed, class_target)
    total = None
    for ref in kernels:
        kernel = ref[...].astype(jnp.float32)
        local = jnp.sum(row_scale(kernel, scale_cols) * kernel, axis=0, keepdims=True)
        total = local if total is None else total + local
    spread(total, parts)


def final_kernel(
    rows, kernel_ref, summed, own, author_summed, class_target, seed_class, train_mask,
    out, scores, out_made, scores_made, left,
):
    classes = out.shape[1]
    scaled = own[...] * col_scale(author_summed, class_target)
    scores_made[...] = scaled * (classes / jnp.sum(scaled, axis=1, keepdims=True))
    copies = [pltpu.make_async_copy(scores_made, scores, left.at[0])]
    copies[0].start()
    scale_cols = col_scale(summed, class_target)
    lane = lax.broadcasted_iota(jnp.int32, (rows, classes), 1).astype(jnp.float32)
    for paper, line in enumerate(code_lines(seed_class, train_mask, rows)):
        code = code_column(line, classes)
        part = pl.ds(paper * rows, rows)
        scaled = kernel_ref[part, :] * scale_cols
        share = scaled * (1.0 / jnp.sum(scaled, axis=1, keepdims=True))
        updated = keep_share * share + jnp.where(code == lane, 1.0 - keep_share, 0.0)
        out_made[part, :] = classes * updated
        copies.append(pltpu.make_async_copy(out_made.at[part], out.at[part], left.at[paper + 1]))
        copies[-1].start()
    for copy in copies:
        copy.wait()


def in_hbm(value):
    return pltpu.with_memory_space_constraint(value, pltpu.HBM)


def exchange(parts):
    return lax.all_to_all(parts, AXES, split_axis=0, concat_axis=0, tiled=True)


def narrow_exchange(parts, sides):
    groups, blocks = lax.axis_size("grp"), lax.axis_size("blk")
    planes = sorted(reversed(range(groups)), key=lambda i: abs(2 * i + 1 - groups))
    sets = [
        [i * blocks + first + side for i in planes for side in reversed(range(sides))]
        for first in range(0, blocks, sides)
    ]
    return lax.all_to_all(
        parts, AXES, split_axis=0, concat_axis=0, axis_index_groups=sets, tiled=True
    )


def on_device(
    tile_values,
    tile_paper,
    tile_author,
    tile_count,
    seed_class,
    train_mask,
    class_prior,
    class_target,
):
    f32 = jnp.float32
    bf16 = jnp.bfloat16
    shape = jax.ShapeDtypeStruct
    slots, rows, columns = tile_values.shape
    classes = class_prior.shape[0]
    papers = seed_class.shape[0]
    authors = AT_DEV * columns
    paper_tiles = papers // rows
    devices = lax.axis_size(AXES)
    prior = class_prior.reshape(1, classes)
    target = class_target.reshape(1, classes)
    seed_class = seed_class.reshape(papers // LANES, LANES)
    train_mask = train_mask.reshape(papers // LANES, LANES)
    parts = shape((devices, 1, classes), f32)

    inputs = (
        tile_paper, tile_author, seed_class, train_mask, prior, target,
    )
    places = (SMEM, SMEM, VMEM, VMEM, VMEM, VMEM)
    blocks = lax.axis_size("blk")
    load = shape((blocks // 2, rows + META, columns), bf16)
    moved = call(
        functools.partial(pack_kernel, rows),
        tuple(shape(one.shape, one.dtype) for one in inputs) + (load, load),
        [SMEM, HBM] + [HBM] * len(inputs),
        [pltpu.SemaphoreType.DMA((len(inputs),)), pltpu.SemaphoreType.DMA((2, blocks // 2))],
        places + (VMEM, VMEM),
    )(tile_count, in_hbm(tile_values), *(in_hbm(one) for one in inputs))
    tile_paper, tile_author, seed_class, train_mask, prior, target, keep, swap = moved
    swapped = lax.ppermute(swap, "blk", [(i, i ^ 1) for i in range(blocks)])
    local = call(
        functools.partial(first_sum_kernel, authors, rows), parts, [SMEM, SMEM] + [VMEM] * 5
    )(tile_paper, tile_count, keep, swap, seed_class, train_mask, prior)
    both = shape((2, rows + META, columns), bf16)
    pairs = call(pair_kernel, (both,) * (blocks // 2 - 1), [VMEM] * 2)(keep, swapped)
    local, *pairs = lax.optimization_barrier((local, *pairs))
    held = [keep, swapped] + [
        lax.ppermute(one, "blk", [(i, i ^ (2 * k)) for i in range(blocks)])
        for k, one in enumerate(pairs, 1)
    ]
    summed = exchange(local)

    author_out = (shape((authors, classes), f32), parts)
    paper_out = (shape((papers, classes), f32), parts, shape((papers, classes), bf16))

    def across_pairs(value, k):
        return lax.ppermute(value, "blk", [(i, i ^ (2 * k)) for i in range(blocks)])

    def to_other(value):
        return lax.ppermute(value, "blk", [(i, i ^ 1) for i in range(blocks)])

    def balance(kernel, sent, local, count):
        here, there = {0: sent}, {}
        sides = 0
        for step in range(count):
            if step == 0:
                moves = [(here, k, across_pairs(sent, k)) for k in (1, 2) if k < blocks // 2]
            elif step == 1:
                moves = [(there, 0, to_other(sent))]
                for k in range(3, blocks // 2):
                    got = across_pairs(here[1], 2) if k == 3 else across_pairs(sent, k)
                    moves.append((here, k, got))
            else:
                moves = [(there, k, to_other(here[k])) for k in here if k not in there]
            summed = narrow_exchange(local, sides) if sides else exchange(local)
            summed, *moved = lax.optimization_barrier((summed, *(one for _, _, one in moves)))
            for (place, k, _), one in zip(moves, moved):
                place[k] = one
            if step + 1 < count:
                added, size = [kernel], devices
                if step > 0:
                    added = list(here.values())
                    sides = 2
                    if step > 1:
                        added += list(there.values())
                        sides = 1
                    size = sides * lax.axis_size("grp")
                local = call(
                    balance_kernel, shape((size, 1, classes), f32), [VMEM] * (len(added) + 2)
                )(*added, summed, target)
                local, sent, *moved = lax.optimization_barrier((local, sent, *here.values()))
                here = dict(zip(here, moved))
        order = range(blocks // 2)
        return summed, [here[k] for k in order] + [there[k] for k in order]

    def last_balance(kernel, local):
        for step in range(ITERS):
            summed = exchange(local)
            if step + 1 < ITERS:
                local = call(balance_kernel, parts, [VMEM] * 3)(kernel, summed, target)
        return summed

    for repeat in range(ROUNDS):
        if repeat == 0:
            own, local = call(
                functools.partial(first_author_kernel, rows), author_out, [VMEM] * (3 + len(held))
            )(summed, prior, target, *held)
            left = ITERS - 1
        else:
            own, local = call(
                functools.partial(author_kernel, rows, blocks),
                author_out,
                [VMEM] * (3 + blocks + len(held)),
            )(summed, prior, target, *kernels, *held)
            left = ITERS
        author_summed, kernels = balance(own, own, local, left)
        last = repeat + 1 == ROUNDS
        kernel, local, *half = call(
            functools.partial(paper_kernel, blocks, rows),
            paper_out[:2] if last else paper_out,
            [SMEM, SMEM, SMEM] + [VMEM] * (5 + blocks),
        )(
            tile_paper, tile_author, tile_count, keep, swap, author_summed, prior, target, *kernels
        )
        if last:
            summed = last_balance(kernel, local)
        else:
            summed, kernels = balance(kernel, half[0], local, ITERS)
    return call(
        functools.partial(final_kernel, rows),
        (shape((papers, classes), f32), shape((authors, classes), f32)),
        [VMEM] * 7,
        [
            pltpu.VMEM((papers, classes), f32),
            pltpu.VMEM((authors, classes), f32),
            pltpu.SemaphoreType.DMA((1 + papers // rows,)),
        ],
        (HBM, HBM),
    )(kernel, summed, own, author_summed, target, seed_class, train_mask)


def solution(mesh):
    placed = (
        P(("grp", "blk"), None, None),
        P(("grp", "blk")),
        P(("grp", "blk")),
        P(("grp", "blk")),
        P(("grp", "blk")),
        P(("grp", "blk")),
        P(),
        P(),
    )
    return jax.shard_map(
        on_device,
        mesh=mesh,
        in_specs=placed,
        out_specs=(P(("grp", "blk"), None), P(("grp", "blk"), None)),
        check_vma=False,
    )
```

```python
import functools

import jax
import jax.numpy as jnp
from jax import lax
from jax.experimental import pallas as pl
from jax.experimental.pallas import tpu as pltpu
from jax.sharding import PartitionSpec as P

AT_DEV = 2
ITERS = 4
ROUNDS = 2
LANES = 128
META = 16

keep_share = 0.8

AXES = ("grp", "blk")
VMEM = pl.BlockSpec(memory_space=pltpu.VMEM)
SMEM = pl.BlockSpec(memory_space=pltpu.SMEM)
HBM = pl.BlockSpec(memory_space=pltpu.HBM)


def call(kernel, out_shape, in_specs, scratch_shapes=(), out_specs=None):
    if out_specs is None:
        out_specs = jax.tree.map(lambda _: VMEM, out_shape)
    return pl.pallas_call(
        kernel,
        out_shape=out_shape,
        in_specs=in_specs,
        out_specs=out_specs,
        scratch_shapes=list(scratch_shapes),
        compiler_params=pltpu.CompilerParams(vmem_limit_bytes=48 * 1024 * 1024),
    )


def col_scale(parts_ref, target_ref):
    return target_ref[...] / jnp.sum(parts_ref[...], axis=0)


def row_scale(kernel, scale_cols):
    return 1.0 / jnp.sum(kernel * scale_cols, axis=1, keepdims=True)


def spread(value, parts_ref):
    parts_ref[...] = jnp.broadcast_to(value[None], parts_ref.shape)


def code_lines(seed_class, train_mask, rows):
    code = jnp.where(train_mask[...] == 1, seed_class[...], -1).astype(jnp.float32)
    line = jnp.concatenate([code[i : i + 1] for i in range(code.shape[0])], axis=1)
    papers = line.shape[1]
    wide = jnp.broadcast_to(line, (8, papers))
    lines = []
    for start in range(0, papers, rows):
        lines.append((pltpu.roll(wide, papers - start, 1) if start else wide)[:1, :rows])
    return lines


def meta_line(meta, rows):
    count = -(-rows // LANES)
    return jnp.concatenate([meta[i : i + 1] for i in range(count)], axis=1)[:, :rows]


def code_columns(lines):
    rows = lines[0].shape[1]
    wide = jnp.concatenate(lines, axis=0)
    wide = jnp.pad(wide, ((0, -len(lines) % 8), (0, -rows % LANES)))
    columns = wide.T
    return [columns[:rows, i : i + 1] for i in range(len(lines))]


def code_column(line, classes):
    rows = line.shape[1]
    across = lax.broadcasted_iota(jnp.int32, (rows, rows), 1)
    eye = jnp.where(lax.broadcasted_iota(jnp.int32, (rows, rows), 0) == across, 1.0, 0.0)
    wide = jnp.broadcast_to(line, (LANES, rows)).astype(jnp.bfloat16)
    column = lax.dot_general(
        eye.astype(jnp.bfloat16),
        wide,
        (((1,), (1,)), ((), ())),
        preferred_element_type=jnp.float32,
    )
    return jnp.concatenate([column] * (classes // LANES), axis=1)


def seeds_of(line, classes):
    class_line = lax.broadcasted_iota(jnp.int32, (classes, line.shape[1]), 0)
    return jnp.where(class_line.astype(jnp.float32) == line, 1.0, 0.0).astype(jnp.bfloat16)


def pack_kernel(rows, tile_count, *refs):
    tiles, *refs = refs
    count = 6
    ins, places = refs[:count], refs[count : 2 * count]
    keep, swap, ready, arrived = refs[2 * count :]
    tile_paper, tile_author, seed_class, train_mask = places[:4]
    pairs = keep.shape[0]
    me = lax.axis_index("blk")
    pair, side = lax.div(me, 2), lax.rem(me, 2)
    moves = [
        pltpu.make_async_copy(source, place, ready.at[i])
        for i, (source, place) in enumerate(zip(ins, places))
    ]
    for copy in moves:
        copy.start()
    outs = []
    copies = []
    for k in range(pairs):
        for way, (out, to) in enumerate(((keep, side), (swap, 1 - side))):
            slot = 2 * lax.bitwise_xor(pair, k) + to
            copy = pltpu.make_async_copy(
                tiles.at[slot], out.at[k, pl.ds(0, rows)], arrived.at[way, k]
            )
            copy.start()
            copies.append(copy)
            outs.append((out, k, slot))
    for copy in moves[:4]:
        copy.wait()
    line = lax.broadcasted_iota(jnp.int32, (META, LANES), 0)
    code_rows = -(-rows // LANES)
    blocks = []
    for codes in code_lines(seed_class, train_mask, rows):
        pad = jnp.full((1, code_rows * LANES - rows), -1.0, jnp.float32)
        codes = jnp.concatenate([codes, pad], axis=1)
        block = jnp.zeros((META, LANES), jnp.float32)
        for i in range(code_rows):
            block = jnp.where(line == i, codes[:, i * LANES : (i + 1) * LANES], block)
        blocks.append(block)
    for out, k, slot in outs:
        paper = tile_paper[slot]
        live = slot < tile_count[0]
        block = blocks[0]
        for i in range(1, len(blocks)):
            block = jnp.where(paper == i, blocks[i], block)
        for author in range(AT_DEV):
            chosen = jnp.where(live & (tile_author[slot] == author), 1.0, 0.0)
            block = jnp.where(line == code_rows + author, chosen, block)
        block = jnp.where(line == code_rows + AT_DEV, paper.astype(jnp.float32), block)
        out[k, rows:, :] = block.astype(jnp.bfloat16)
    for copy in moves[4:] + copies:
        copy.wait()


def pair_kernel(keep, swapped, *outs):
    for k, out in enumerate(outs, 1):
        out[0] = keep[k]
        out[1] = swapped[k]


def sources(count):
    me = lax.axis_index("blk")
    pair, side = lax.div(me, 2), lax.rem(me, 2)
    pairs = [2 * lax.bitwise_xor(pair, k) for k in range(count // 2)]
    return [other + side for other in pairs] + [other + 1 - side for other in pairs]


def slots_of(keep, swapped, *pairs):
    return [(keep, 0), *((ref, 0) for ref in pairs), (swapped, 0), *((ref, 1) for ref in pairs)]


def first_sum_kernel(
    authors, rows, tile_paper, tile_count, keep, swap, seed_class, train_mask, class_prior, parts
):
    pairs, _, columns = keep.shape
    classes = parts.shape[2]
    slots = sources(2 * pairs)
    tiles = [ref[k, :rows, :].astype(jnp.float32) for ref in (keep, swap) for k in range(pairs)]
    lane = lax.broadcasted_iota(jnp.int32, (rows, classes), 1).astype(jnp.float32)
    total = authors * class_prior[...]
    for paper, code in enumerate(code_columns(code_lines(seed_class, train_mask, rows))):
        weight = jnp.zeros((rows, columns), jnp.float32)
        for slot, tile in zip(slots, tiles):
            chosen = (slot < tile_count[0]) & (tile_paper[slot] == paper)
            weight = weight + jnp.where(chosen, tile, 0.0)
        weight = jnp.sum(weight, axis=1, keepdims=True)
        seeds = jnp.where(code == lane, weight, 0.0)
        total = total + jnp.sum(seeds, axis=0, keepdims=True)
    spread(total, parts)


def next_sum(kernel, summed, class_target, parts):
    scale_rows = row_scale(kernel, col_scale(summed, class_target))
    spread(jnp.sum(scale_rows * kernel, axis=0, keepdims=True), parts)


def first_author_kernel(rows, summed, class_prior, class_target, *rest):
    *held, full, parts = rest
    classes = full.shape[1]
    code_rows = -(-rows // LANES)
    totals = [jnp.zeros((classes, LANES), jnp.float32) for _ in range(AT_DEV)]
    for ref, place in slots_of(*held):
        meta = ref[place, rows:, :].astype(jnp.float32)
        seeds = seeds_of(meta_line(meta, rows), classes)
        parcel = jnp.dot(seeds, ref[place, :rows, :], preferred_element_type=jnp.float32)
        parcel = parcel.astype(jnp.bfloat16).astype(jnp.float32)
        for author in range(AT_DEV):
            chosen = meta[code_rows + author : code_rows + author + 1]
            totals[author] = totals[author] + parcel * chosen
    kernel = jnp.concatenate([total.T for total in totals], axis=0) + class_prior[...]
    full[...] = kernel
    next_sum(kernel, summed, class_target, parts)


def author_kernel(rows, blocks, summed, class_prior, class_target, *rest):
    *rest, full, parts = rest
    kernels, held = rest[:blocks], slots_of(*rest[blocks:])
    classes = full.shape[1]
    code_rows = -(-rows // LANES)
    metas = [ref[place, rows:, :].astype(jnp.float32) for ref, place in held]
    at = code_rows + AT_DEV
    papers = [jnp.max(meta[at : at + 1]).astype(jnp.int32) for meta in metas]
    scale_cols = col_scale(summed, class_target)
    codes = code_columns([meta_line(meta, rows) for meta in metas])
    totals = [jnp.zeros((LANES, classes), jnp.float32) for _ in range(AT_DEV)]
    lane = lax.broadcasted_iota(jnp.int32, (rows, classes), 1).astype(jnp.float32)
    for shift, (ref, place) in enumerate(held):
        half = kernels[shift][pl.ds(pl.multiple_of(papers[shift] * rows, rows), rows), :]
        scaled = half.astype(jnp.float32) * scale_cols
        share = scaled * (keep_share / jnp.sum(scaled, axis=1, keepdims=True))
        labels = share + jnp.where(codes[shift] == lane, 1.0 - keep_share, 0.0)
        parcel = lax.dot_general(
            ref[place, :rows, :],
            labels.astype(jnp.bfloat16),
            (((0,), (0,)), ((), ())),
            preferred_element_type=jnp.float32,
        )
        parcel = parcel.astype(jnp.bfloat16).astype(jnp.float32)
        for author in range(AT_DEV):
            at = code_rows + author
            totals[author] = totals[author] + parcel * metas[shift][at : at + 1, :1]
    kernel = jnp.concatenate(totals, axis=0) + class_prior[...]
    full[...] = kernel
    spread(jnp.sum(kernel, axis=0, keepdims=True), parts)


def paper_kernel(
    blocks, rows, tile_paper, tile_author, tile_count, keep, swap, summed, class_prior,
    class_target, *rest,
):
    kernels, (full, parts, *half) = rest[:blocks], rest[blocks:]
    pairs, _, columns = keep.shape
    classes = full.shape[1]
    scale_cols = col_scale(summed, class_target)
    slots = sources(blocks)
    wide = [ref[k, :rows, :] for ref in (keep, swap) for k in range(pairs)]
    wide = jnp.concatenate(wide, axis=1)
    labels = []
    for ref, slot in zip(kernels, slots):
        start = pl.multiple_of(tile_author[slot] * columns, columns)
        scaled = ref[pl.ds(start, columns), :] * scale_cols
        share = scaled * (1.0 / jnp.sum(scaled, axis=1, keepdims=True))
        labels.append(share.astype(jnp.bfloat16))
    column = jnp.zeros((1, classes), jnp.float32)
    for paper in range(full.shape[0] // rows):
        chosen = []
        for one, slot in zip(labels, slots):
            mine = (slot < tile_count[0]) & (tile_paper[slot] == paper)
            chosen.append(jnp.where(mine, one, jnp.zeros_like(one)))
        mass = jnp.dot(wide, jnp.concatenate(chosen, axis=0), preferred_element_type=jnp.float32)
        kernel = mass + class_prior[...]
        full[paper * rows : (paper + 1) * rows, :] = kernel
        for out in half:
            out[paper * rows : (paper + 1) * rows, :] = kernel.astype(jnp.bfloat16)
        column = column + jnp.sum(kernel, axis=0, keepdims=True)
    spread(column, parts)


def balance_kernel(*refs):
    *kernels, summed, class_target, parts = refs
    scale_cols = col_scale(summed, class_target)
    total = None
    for ref in kernels:
        kernel = ref[...].astype(jnp.float32)
        local = jnp.sum(row_scale(kernel, scale_cols) * kernel, axis=0, keepdims=True)
        total = local if total is None else total + local
    spread(total, parts)


def final_kernel(
    rows, kernel_ref, summed, own, author_summed, class_target, seed_class, train_mask,
    out, scores, out_made, scores_made, left,
):
    classes = out.shape[1]
    scaled = own[...] * col_scale(author_summed, class_target)
    scores_made[...] = scaled * (classes / jnp.sum(scaled, axis=1, keepdims=True))
    copies = [pltpu.make_async_copy(scores_made, scores, left.at[0])]
    copies[0].start()
    scale_cols = col_scale(summed, class_target)
    lane = lax.broadcasted_iota(jnp.int32, (rows, classes), 1).astype(jnp.float32)
    for paper, line in enumerate(code_lines(seed_class, train_mask, rows)):
        code = code_column(line, classes)
        part = pl.ds(paper * rows, rows)
        scaled = kernel_ref[part, :] * scale_cols
        share = scaled * (1.0 / jnp.sum(scaled, axis=1, keepdims=True))
        updated = keep_share * share + jnp.where(code == lane, 1.0 - keep_share, 0.0)
        out_made[part, :] = classes * updated
        copies.append(pltpu.make_async_copy(out_made.at[part], out.at[part], left.at[paper + 1]))
        copies[-1].start()
    for copy in copies:
        copy.wait()


def in_hbm(value):
    return pltpu.with_memory_space_constraint(value, pltpu.HBM)


def exchange(parts):
    return lax.all_to_all(parts, AXES, split_axis=0, concat_axis=0, tiled=True)


def narrow_exchange(parts, sides, upwards):
    groups, blocks = lax.axis_size("grp"), lax.axis_size("blk")
    planes = range(groups)
    if not upwards:
        planes = sorted(planes, key=lambda i: abs(2 * i + 1 - groups))
    sets = [
        [i * blocks + first + side for i in planes for side in range(sides)]
        for first in range(0, blocks, sides)
    ]
    return lax.all_to_all(
        parts, AXES, split_axis=0, concat_axis=0, axis_index_groups=sets, tiled=True
    )


def on_device(
    tile_values,
    tile_paper,
    tile_author,
    tile_count,
    seed_class,
    train_mask,
    class_prior,
    class_target,
):
    f32 = jnp.float32
    bf16 = jnp.bfloat16
    shape = jax.ShapeDtypeStruct
    slots, rows, columns = tile_values.shape
    classes = class_prior.shape[0]
    papers = seed_class.shape[0]
    authors = AT_DEV * columns
    paper_tiles = papers // rows
    devices = lax.axis_size(AXES)
    prior = class_prior.reshape(1, classes)
    target = class_target.reshape(1, classes)
    seed_class = seed_class.reshape(papers // LANES, LANES)
    train_mask = train_mask.reshape(papers // LANES, LANES)
    parts = shape((devices, 1, classes), f32)

    inputs = (
        tile_paper, tile_author, seed_class, train_mask, prior, target,
    )
    places = (SMEM, SMEM, VMEM, VMEM, VMEM, VMEM)
    blocks = lax.axis_size("blk")
    load = shape((blocks // 2, rows + META, columns), bf16)
    moved = call(
        functools.partial(pack_kernel, rows),
        tuple(shape(one.shape, one.dtype) for one in inputs) + (load, load),
        [SMEM, HBM] + [HBM] * len(inputs),
        [pltpu.SemaphoreType.DMA((len(inputs),)), pltpu.SemaphoreType.DMA((2, blocks // 2))],
        places + (VMEM, VMEM),
    )(tile_count, in_hbm(tile_values), *(in_hbm(one) for one in inputs))
    tile_paper, tile_author, seed_class, train_mask, prior, target, keep, swap = moved
    swapped = lax.ppermute(swap, "blk", [(i, i ^ 1) for i in range(blocks)])
    local = call(
        functools.partial(first_sum_kernel, authors, rows), parts, [SMEM, SMEM] + [VMEM] * 5
    )(tile_paper, tile_count, keep, swap, seed_class, train_mask, prior)
    both = shape((2, rows + META, columns), bf16)
    pairs = call(pair_kernel, (both,) * (blocks // 2 - 1), [VMEM] * 2)(keep, swapped)
    local, *pairs = lax.optimization_barrier((local, *pairs))
    held = [keep, swapped] + [
        lax.ppermute(one, "blk", [(i, i ^ (2 * k)) for i in range(blocks)])
        for k, one in enumerate(pairs, 1)
    ]
    summed = exchange(local)

    author_out = (shape((authors, classes), f32), parts)
    paper_out = (shape((papers, classes), f32), parts, shape((papers, classes), bf16))

    def across_pairs(value, k):
        return lax.ppermute(value, "blk", [(i, i ^ (2 * k)) for i in range(blocks)])

    def to_other(value):
        return lax.ppermute(value, "blk", [(i, i ^ 1) for i in range(blocks)])

    def balance(kernel, sent, local, count, widest):
        here, there = {0: sent}, {}
        sides = 0
        for step in range(count):
            if step == 0:
                moves = [(here, k, across_pairs(sent, k)) for k in (1, 2) if k < blocks // 2]
            elif step == 1:
                moves = [(there, 0, to_other(sent))]
                for k in range(3, blocks // 2):
                    got = across_pairs(here[1], 2) if k == 3 else across_pairs(sent, k)
                    moves.append((here, k, got))
            else:
                moves = [(there, k, to_other(here[k])) for k in here if k not in there]
            if sides:
                summed = narrow_exchange(local, sides, step + 1 == count and sides == 2)
            else:
                summed = exchange(local)
            summed, *moved = lax.optimization_barrier((summed, *(one for _, _, one in moves)))
            for (place, k, _), one in zip(moves, moved):
                place[k] = one
            if step + 1 < count:
                added, size = [kernel], devices
                if step > 0:
                    added = list(here.values())
                    sides = 2
                    if step > 1 and widest:
                        added += list(there.values())
                        sides = 1
                    size = sides * lax.axis_size("grp")
                local = call(
                    balance_kernel, shape((size, 1, classes), f32), [VMEM] * (len(added) + 2)
                )(*added, summed, target)
                local, sent, *moved = lax.optimization_barrier((local, sent, *here.values()))
                here = dict(zip(here, moved))
        order = range(blocks // 2)
        return summed, [here[k] for k in order] + [there[k] for k in order]

    def last_balance(kernel, local):
        for step in range(ITERS):
            summed = exchange(local)
            if step + 1 < ITERS:
                local = call(balance_kernel, parts, [VMEM] * 3)(kernel, summed, target)
        return summed

    for repeat in range(ROUNDS):
        if repeat == 0:
            own, local = call(
                functools.partial(first_author_kernel, rows), author_out, [VMEM] * (3 + len(held))
            )(summed, prior, target, *held)
            left = ITERS - 1
        else:
            own, local = call(
                functools.partial(author_kernel, rows, blocks),
                author_out,
                [VMEM] * (3 + blocks + len(held)),
            )(summed, prior, target, *kernels, *held)
            left = ITERS
        author_summed, kernels = balance(own, own, local, left, True)
        last = repeat + 1 == ROUNDS
        kernel, local, *half = call(
            functools.partial(paper_kernel, blocks, rows),
            paper_out[:2] if last else paper_out,
            [SMEM, SMEM, SMEM] + [VMEM] * (5 + blocks),
        )(
            tile_paper, tile_author, tile_count, keep, swap, author_summed, prior, target, *kernels
        )
        if last:
            summed = last_balance(kernel, local)
        else:
            summed, kernels = balance(kernel, half[0], local, ITERS, False)
    return call(
        functools.partial(final_kernel, rows),
        (shape((papers, classes), f32), shape((authors, classes), f32)),
        [VMEM] * 7,
        [
            pltpu.VMEM((papers, classes), f32),
            pltpu.VMEM((authors, classes), f32),
            pltpu.SemaphoreType.DMA((1 + papers // rows,)),
        ],
        (HBM, HBM),
    )(kernel, summed, own, author_summed, target, seed_class, train_mask)


def solution(mesh):
    placed = (
        P(("grp", "blk"), None, None),
        P(("grp", "blk")),
        P(("grp", "blk")),
        P(("grp", "blk")),
        P(("grp", "blk")),
        P(("grp", "blk")),
        P(),
        P(),
    )
    return jax.shard_map(
        on_device,
        mesh=mesh,
        in_specs=placed,
        out_specs=(P(("grp", "blk"), None), P(("grp", "blk"), None)),
        check_vma=False,
    )
```

```python
import functools

import jax
import jax.numpy as jnp
from jax import lax
from jax.experimental import pallas as pl
from jax.experimental.pallas import tpu as pltpu
from jax.sharding import PartitionSpec as P

AT_DEV = 2
ITERS = 4
ROUNDS = 2
LANES = 128
META = 16

keep_share = 0.8

AXES = ("grp", "blk")
VMEM = pl.BlockSpec(memory_space=pltpu.VMEM)
SMEM = pl.BlockSpec(memory_space=pltpu.SMEM)
HBM = pl.BlockSpec(memory_space=pltpu.HBM)


def call(kernel, out_shape, in_specs, scratch_shapes=(), out_specs=None):
    if out_specs is None:
        out_specs = jax.tree.map(lambda _: VMEM, out_shape)
    return pl.pallas_call(
        kernel,
        out_shape=out_shape,
        in_specs=in_specs,
        out_specs=out_specs,
        scratch_shapes=list(scratch_shapes),
        compiler_params=pltpu.CompilerParams(vmem_limit_bytes=48 * 1024 * 1024),
    )


def col_scale(parts_ref, target_ref):
    return target_ref[...] / jnp.sum(parts_ref[...], axis=0)


def row_scale(kernel, scale_cols):
    return 1.0 / jnp.sum(kernel * scale_cols, axis=1, keepdims=True)


def spread(value, parts_ref):
    parts_ref[...] = jnp.broadcast_to(value[None], parts_ref.shape)


def code_lines(seed_class, train_mask, rows):
    code = jnp.where(train_mask[...] == 1, seed_class[...], -1).astype(jnp.float32)
    line = jnp.concatenate([code[i : i + 1] for i in range(code.shape[0])], axis=1)
    papers = line.shape[1]
    wide = jnp.broadcast_to(line, (8, papers))
    lines = []
    for start in range(0, papers, rows):
        lines.append((pltpu.roll(wide, papers - start, 1) if start else wide)[:1, :rows])
    return lines


def meta_line(meta, rows):
    count = -(-rows // LANES)
    return jnp.concatenate([meta[i : i + 1] for i in range(count)], axis=1)[:, :rows]


def code_columns(lines):
    rows = lines[0].shape[1]
    wide = jnp.concatenate(lines, axis=0)
    wide = jnp.pad(wide, ((0, -len(lines) % 8), (0, -rows % LANES)))
    columns = wide.T
    return [columns[:rows, i : i + 1] for i in range(len(lines))]


def code_column(line, classes):
    rows = line.shape[1]
    across = lax.broadcasted_iota(jnp.int32, (rows, rows), 1)
    eye = jnp.where(lax.broadcasted_iota(jnp.int32, (rows, rows), 0) == across, 1.0, 0.0)
    wide = jnp.broadcast_to(line, (LANES, rows)).astype(jnp.bfloat16)
    column = lax.dot_general(
        eye.astype(jnp.bfloat16),
        wide,
        (((1,), (1,)), ((), ())),
        preferred_element_type=jnp.float32,
    )
    return jnp.concatenate([column] * (classes // LANES), axis=1)


def seeds_of(line, classes):
    class_line = lax.broadcasted_iota(jnp.int32, (classes, line.shape[1]), 0)
    return jnp.where(class_line.astype(jnp.float32) == line, 1.0, 0.0).astype(jnp.bfloat16)


def pack_kernel(rows, tile_count, *refs):
    tiles, *refs = refs
    count = 6
    ins, places = refs[:count], refs[count : 2 * count]
    keep, swap, ready, arrived = refs[2 * count :]
    tile_paper, tile_author, seed_class, train_mask = places[:4]
    pairs = keep.shape[0]
    me = lax.axis_index("blk")
    pair, side = lax.div(me, 2), lax.rem(me, 2)
    moves = [
        pltpu.make_async_copy(source, place, ready.at[i])
        for i, (source, place) in enumerate(zip(ins, places))
    ]
    for copy in moves:
        copy.start()
    outs = []
    copies = []
    for way, (out, to) in enumerate(((keep, side), (swap, 1 - side))):
        for k, other in enumerate(pair_order(pairs, to)):
            slot = 2 * lax.bitwise_xor(pair, other) + to
            copy = pltpu.make_async_copy(
                tiles.at[slot], out.at[k, pl.ds(0, rows)], arrived.at[way, k]
            )
            copy.start()
            copies.append(copy)
            outs.append((out, k, slot))
    for copy in moves[:4]:
        copy.wait()
    line = lax.broadcasted_iota(jnp.int32, (META, LANES), 0)
    code_rows = -(-rows // LANES)
    blocks = []
    for codes in code_lines(seed_class, train_mask, rows):
        pad = jnp.full((1, code_rows * LANES - rows), -1.0, jnp.float32)
        codes = jnp.concatenate([codes, pad], axis=1)
        block = jnp.zeros((META, LANES), jnp.float32)
        for i in range(code_rows):
            block = jnp.where(line == i, codes[:, i * LANES : (i + 1) * LANES], block)
        blocks.append(block)
    for out, k, slot in outs:
        paper = tile_paper[slot]
        live = slot < tile_count[0]
        block = blocks[0]
        for i in range(1, len(blocks)):
            block = jnp.where(paper == i, blocks[i], block)
        for author in range(AT_DEV):
            chosen = jnp.where(live & (tile_author[slot] == author), 1.0, 0.0)
            block = jnp.where(line == code_rows + author, chosen, block)
        block = jnp.where(line == code_rows + AT_DEV, paper.astype(jnp.float32), block)
        out[k, rows:, :] = block.astype(jnp.bfloat16)
    for copy in moves[4:] + copies:
        copy.wait()


def join_kernel(one, two, out):
    out[0] = one[...]
    out[1] = two[...]


def pair_kernel(keep, swapped, *outs):
    for k, out in enumerate(outs, 1):
        out[0] = keep[k]
        out[1] = swapped[k]


def pair_order(pairs, side):
    return [0, 1 + side, 2 - side, 3] if pairs == 4 else list(range(pairs))


def turned(pairs):
    return [0, 2, 1, 3] if pairs == 4 else list(range(pairs))


def sources(count):
    me = lax.axis_index("blk")
    pair, side = lax.div(me, 2), lax.rem(me, 2)
    pairs = [2 * lax.bitwise_xor(pair, k) for k in pair_order(count // 2, side)]
    return [other + side for other in pairs] + [other + 1 - side for other in pairs]


def own_tiles(keep, swap, rows):
    pairs = keep.shape[0]
    kept = [keep[k, :rows, :] for k in range(pairs)]
    return kept + [swap[k, :rows, :] for k in turned(pairs)]


def views(refs, places):
    return [refs[i] if place is None else refs[i].at[place] for i, place in places]


def slots_of(keep, swapped, *pairs):
    return [(keep, 0), *((ref, 0) for ref in pairs), (swapped, 0), *((ref, 1) for ref in pairs)]


def first_sum_kernel(
    authors, rows, tile_paper, tile_count, keep, swap, seed_class, train_mask, class_prior, parts
):
    pairs, _, columns = keep.shape
    classes = parts.shape[2]
    slots = sources(2 * pairs)
    tiles = [tile.astype(jnp.float32) for tile in own_tiles(keep, swap, rows)]
    lane = lax.broadcasted_iota(jnp.int32, (rows, classes), 1).astype(jnp.float32)
    total = authors * class_prior[...]
    for paper, code in enumerate(code_columns(code_lines(seed_class, train_mask, rows))):
        weight = jnp.zeros((rows, columns), jnp.float32)
        for slot, tile in zip(slots, tiles):
            chosen = (slot < tile_count[0]) & (tile_paper[slot] == paper)
            weight = weight + jnp.where(chosen, tile, 0.0)
        weight = jnp.sum(weight, axis=1, keepdims=True)
        seeds = jnp.where(code == lane, weight, 0.0)
        total = total + jnp.sum(seeds, axis=0, keepdims=True)
    spread(total, parts)


def next_sum(kernel, summed, class_target, parts):
    scale_rows = row_scale(kernel, col_scale(summed, class_target))
    spread(jnp.sum(scale_rows * kernel, axis=0, keepdims=True), parts)


def first_author_kernel(rows, summed, class_prior, class_target, *rest):
    *held, full, parts = rest
    classes = full.shape[1]
    code_rows = -(-rows // LANES)
    totals = [jnp.zeros((classes, LANES), jnp.float32) for _ in range(AT_DEV)]
    for ref, place in slots_of(*held):
        meta = ref[place, rows:, :].astype(jnp.float32)
        seeds = seeds_of(meta_line(meta, rows), classes)
        parcel = jnp.dot(seeds, ref[place, :rows, :], preferred_element_type=jnp.float32)
        parcel = parcel.astype(jnp.bfloat16).astype(jnp.float32)
        for author in range(AT_DEV):
            chosen = meta[code_rows + author : code_rows + author + 1]
            totals[author] = totals[author] + parcel * chosen
    kernel = jnp.concatenate([total.T for total in totals], axis=0) + class_prior[...]
    full[...] = kernel
    next_sum(kernel, summed, class_target, parts)


def author_kernel(rows, places, summed, class_prior, class_target, *rest):
    *rest, full, parts = rest
    count = 1 + max(i for i, _ in places)
    kernels, held = views(rest, places), slots_of(*rest[count:])
    classes = full.shape[1]
    code_rows = -(-rows // LANES)
    metas = [ref[place, rows:, :].astype(jnp.float32) for ref, place in held]
    at = code_rows + AT_DEV
    papers = [jnp.max(meta[at : at + 1]).astype(jnp.int32) for meta in metas]
    scale_cols = col_scale(summed, class_target)
    codes = code_columns([meta_line(meta, rows) for meta in metas])
    totals = [jnp.zeros((LANES, classes), jnp.float32) for _ in range(AT_DEV)]
    lane = lax.broadcasted_iota(jnp.int32, (rows, classes), 1).astype(jnp.float32)
    for shift, (ref, place) in enumerate(held):
        half = kernels[shift][pl.ds(pl.multiple_of(papers[shift] * rows, rows), rows), :]
        scaled = half.astype(jnp.float32) * scale_cols
        share = scaled * (keep_share / jnp.sum(scaled, axis=1, keepdims=True))
        labels = share + jnp.where(codes[shift] == lane, 1.0 - keep_share, 0.0)
        parcel = lax.dot_general(
            ref[place, :rows, :],
            labels.astype(jnp.bfloat16),
            (((0,), (0,)), ((), ())),
            preferred_element_type=jnp.float32,
        )
        parcel = parcel.astype(jnp.bfloat16).astype(jnp.float32)
        for author in range(AT_DEV):
            at = code_rows + author
            totals[author] = totals[author] + parcel * metas[shift][at : at + 1, :1]
    kernel = jnp.concatenate(totals, axis=0) + class_prior[...]
    full[...] = kernel
    spread(jnp.sum(kernel, axis=0, keepdims=True), parts)


def paper_kernel(
    places, rows, tile_paper, tile_author, tile_count, keep, swap, summed, class_prior,
    class_target, *rest,
):
    kernels, (full, parts, *half) = views(rest, places), rest[1 + max(i for i, _ in places) :]
    columns = keep.shape[2]
    classes = full.shape[1]
    scale_cols = col_scale(summed, class_target)
    slots = sources(len(kernels))
    wide = jnp.concatenate(own_tiles(keep, swap, rows), axis=1)
    labels = []
    for ref, slot in zip(kernels, slots):
        start = pl.multiple_of(tile_author[slot] * columns, columns)
        scaled = ref[pl.ds(start, columns), :] * scale_cols
        share = scaled * (1.0 / jnp.sum(scaled, axis=1, keepdims=True))
        labels.append(share.astype(jnp.bfloat16))
    column = jnp.zeros((1, classes), jnp.float32)
    for paper in range(full.shape[0] // rows):
        chosen = []
        for one, slot in zip(labels, slots):
            mine = (slot < tile_count[0]) & (tile_paper[slot] == paper)
            chosen.append(jnp.where(mine, one, jnp.zeros_like(one)))
        mass = jnp.dot(wide, jnp.concatenate(chosen, axis=0), preferred_element_type=jnp.float32)
        kernel = mass + class_prior[...]
        full[paper * rows : (paper + 1) * rows, :] = kernel
        for out in half:
            out[paper * rows : (paper + 1) * rows, :] = kernel.astype(jnp.bfloat16)
        column = column + jnp.sum(kernel, axis=0, keepdims=True)
    spread(column, parts)


def balance_kernel(*refs):
    *kernels, summed, class_target, parts = refs
    scale_cols = col_scale(summed, class_target)
    total = None
    refs = [(ref, i) for ref in kernels for i in range(ref.shape[0] if ref.ndim == 3 else 1)]
    for ref, i in refs:
        kernel = (ref[i] if ref.ndim == 3 else ref[...]).astype(jnp.float32)
        local = jnp.sum(row_scale(kernel, scale_cols) * kernel, axis=0, keepdims=True)
        total = local if total is None else total + local
    spread(total, parts)


def final_kernel(
    rows, kernel_ref, summed, own, author_summed, class_target, seed_class, train_mask,
    out, scores, out_made, scores_made, left,
):
    classes = out.shape[1]
    scaled = own[...] * col_scale(author_summed, class_target)
    scores_made[...] = scaled * (classes / jnp.sum(scaled, axis=1, keepdims=True))
    copies = [pltpu.make_async_copy(scores_made, scores, left.at[0])]
    copies[0].start()
    scale_cols = col_scale(summed, class_target)
    lane = lax.broadcasted_iota(jnp.int32, (rows, classes), 1).astype(jnp.float32)
    for paper, line in enumerate(code_lines(seed_class, train_mask, rows)):
        code = code_column(line, classes)
        part = pl.ds(paper * rows, rows)
        scaled = kernel_ref[part, :] * scale_cols
        share = scaled * (1.0 / jnp.sum(scaled, axis=1, keepdims=True))
        updated = keep_share * share + jnp.where(code == lane, 1.0 - keep_share, 0.0)
        out_made[part, :] = classes * updated
        copies.append(pltpu.make_async_copy(out_made.at[part], out.at[part], left.at[paper + 1]))
        copies[-1].start()
    for copy in copies:
        copy.wait()


def in_hbm(value):
    return pltpu.with_memory_space_constraint(value, pltpu.HBM)


def exchange(parts):
    return lax.all_to_all(parts, AXES, split_axis=0, concat_axis=0, tiled=True)


def narrow_exchange(parts, sides, upwards):
    groups, blocks = lax.axis_size("grp"), lax.axis_size("blk")
    planes = range(groups)
    if not upwards:
        planes = sorted(planes, key=lambda i: abs(2 * i + 1 - groups))
    sets = [
        [i * blocks + first + side for i in planes for side in range(sides)]
        for first in range(0, blocks, sides)
    ]
    return lax.all_to_all(
        parts, AXES, split_axis=0, concat_axis=0, axis_index_groups=sets, tiled=True
    )


def on_device(
    tile_values,
    tile_paper,
    tile_author,
    tile_count,
    seed_class,
    train_mask,
    class_prior,
    class_target,
):
    f32 = jnp.float32
    bf16 = jnp.bfloat16
    shape = jax.ShapeDtypeStruct
    slots, rows, columns = tile_values.shape
    classes = class_prior.shape[0]
    papers = seed_class.shape[0]
    authors = AT_DEV * columns
    paper_tiles = papers // rows
    devices = lax.axis_size(AXES)
    prior = class_prior.reshape(1, classes)
    target = class_target.reshape(1, classes)
    seed_class = seed_class.reshape(papers // LANES, LANES)
    train_mask = train_mask.reshape(papers // LANES, LANES)
    parts = shape((devices, 1, classes), f32)

    inputs = (
        tile_paper, tile_author, seed_class, train_mask, prior, target,
    )
    places = (SMEM, SMEM, VMEM, VMEM, VMEM, VMEM)
    blocks = lax.axis_size("blk")
    load = shape((blocks // 2, rows + META, columns), bf16)
    moved = call(
        functools.partial(pack_kernel, rows),
        tuple(shape(one.shape, one.dtype) for one in inputs) + (load, load),
        [SMEM, HBM] + [HBM] * len(inputs),
        [pltpu.SemaphoreType.DMA((len(inputs),)), pltpu.SemaphoreType.DMA((2, blocks // 2))],
        places + (VMEM, VMEM),
    )(tile_count, in_hbm(tile_values), *(in_hbm(one) for one in inputs))
    tile_paper, tile_author, seed_class, train_mask, prior, target, keep, swap = moved
    swapped = lax.ppermute(swap, "blk", [(i, i ^ 1) for i in range(blocks)])
    local = call(
        functools.partial(first_sum_kernel, authors, rows), parts, [SMEM, SMEM] + [VMEM] * 5
    )(tile_paper, tile_count, keep, swap, seed_class, train_mask, prior)
    both = shape((2, rows + META, columns), bf16)
    pairs = call(pair_kernel, (both,) * (blocks // 2 - 1), [VMEM] * 2)(keep, swapped)
    local, *pairs = lax.optimization_barrier((local, *pairs))
    count = blocks // 2

    def across_pairs(value, even, odd):
        hops = [2 * odd if i % 2 else 2 * even for i in range(blocks)]
        return lax.ppermute(value, "blk", [(i, i ^ hop) for i, hop in enumerate(hops)])

    def to_other(value):
        return lax.ppermute(value, "blk", [(i, i ^ 1) for i in range(blocks)])

    ways = list(zip(pair_order(count, 0), pair_order(count, 1)))
    held = [keep, swapped] + [across_pairs(one, *way) for one, way in zip(pairs, ways[1:])]
    summed = exchange(local)

    author_out = (shape((authors, classes), f32), parts)
    paper_out = (shape((papers, classes), f32), parts, shape((papers, classes), bf16))

    four = count == 4
    places = [(i, None) for i in range(blocks)]
    if four:
        places = [(0, None), (1, None), (2, 0), (2, 1)]
        places += [(3 + places[k][0], places[k][1]) for k in turned(count)]

    def balance(kernel, sent, local, steps, widest):
        here, there, joined = [sent], [], None
        sides = 0
        for step in range(steps):
            moves = []
            if step == 0:
                moves = [(sent, *way) for way in ways[1 : 2 if four else 3]]
            elif step == 1:
                moves = [(joined, *ways[2])] if four else [(sent, *way) for way in ways[3:]]
            moves = [across_pairs(*move) for move in moves]
            others = [] if step == 0 else [sent] if step == 1 else here[len(there) :]
            others = [to_other(one) for one in others]
            if sides:
                summed = narrow_exchange(local, sides, step + 1 == steps and sides == 2)
            else:
                summed = exchange(local)
            summed, *moved = lax.optimization_barrier((summed, *moves, *others))
            here += moved[: len(moves)]
            there += moved[len(moves) :]
            if step + 1 < steps:
                added, size = [kernel], devices
                if step > 0:
                    added = list(here)
                    sides = 2
                    if step > 1 and widest:
                        added += there
                        sides = 1
                    size = sides * lax.axis_size("grp")
                local = call(
                    balance_kernel, shape((size, 1, classes), f32), [VMEM] * (len(added) + 2)
                )(*added, summed, target)
                joined = sent
                if four and step == 0:
                    joined = call(join_kernel, shape((2, *sent.shape), sent.dtype), [VMEM] * 2)(*here)
                local, sent, joined, *here = lax.optimization_barrier((local, sent, joined, *here))
        return summed, here + there

    def last_balance(kernel, local):
        for step in range(ITERS):
            summed = exchange(local)
            if step + 1 < ITERS:
                local = call(balance_kernel, parts, [VMEM] * 3)(kernel, summed, target)
        return summed

    for repeat in range(ROUNDS):
        if repeat == 0:
            own, local = call(
                functools.partial(first_author_kernel, rows), author_out, [VMEM] * (3 + len(held))
            )(summed, prior, target, *held)
            left = ITERS - 1
        else:
            own, local = call(
                functools.partial(author_kernel, rows, places),
                author_out,
                [VMEM] * (3 + len(kernels) + len(held)),
            )(summed, prior, target, *kernels, *held)
            left = ITERS
        author_summed, kernels = balance(own, own, local, left, True)
        last = repeat + 1 == ROUNDS
        kernel, local, *half = call(
            functools.partial(paper_kernel, places, rows),
            paper_out[:2] if last else paper_out,
            [SMEM, SMEM, SMEM] + [VMEM] * (5 + len(kernels)),
        )(
            tile_paper, tile_author, tile_count, keep, swap, author_summed, prior, target, *kernels
        )
        if last:
            summed = last_balance(kernel, local)
        else:
            summed, kernels = balance(kernel, half[0], local, ITERS, False)
    return call(
        functools.partial(final_kernel, rows),
        (shape((papers, classes), f32), shape((authors, classes), f32)),
        [VMEM] * 7,
        [
            pltpu.VMEM((papers, classes), f32),
            pltpu.VMEM((authors, classes), f32),
            pltpu.SemaphoreType.DMA((1 + papers // rows,)),
        ],
        (HBM, HBM),
    )(kernel, summed, own, author_summed, target, seed_class, train_mask)


def solution(mesh):
    placed = (
        P(("grp", "blk"), None, None),
        P(("grp", "blk")),
        P(("grp", "blk")),
        P(("grp", "blk")),
        P(("grp", "blk")),
        P(("grp", "blk")),
        P(),
        P(),
    )
    return jax.shard_map(
        on_device,
        mesh=mesh,
        in_specs=placed,
        out_specs=(P(("grp", "blk"), None), P(("grp", "blk"), None)),
        check_vma=False,
    )
```

```python
import functools

import jax
import jax.numpy as jnp
from jax import lax
from jax.experimental import pallas as pl
from jax.experimental.pallas import tpu as pltpu
from jax.sharding import PartitionSpec as P

AT_DEV = 2
ITERS = 4
ROUNDS = 2
LANES = 128
META = 16

keep_share = 0.8

AXES = ("grp", "blk")
VMEM = pl.BlockSpec(memory_space=pltpu.VMEM)
SMEM = pl.BlockSpec(memory_space=pltpu.SMEM)
HBM = pl.BlockSpec(memory_space=pltpu.HBM)


def call(kernel, out_shape, in_specs, scratch_shapes=(), out_specs=None):
    if out_specs is None:
        out_specs = jax.tree.map(lambda _: VMEM, out_shape)
    return pl.pallas_call(
        kernel,
        out_shape=out_shape,
        in_specs=in_specs,
        out_specs=out_specs,
        scratch_shapes=list(scratch_shapes),
        compiler_params=pltpu.CompilerParams(vmem_limit_bytes=48 * 1024 * 1024),
    )


def col_scale(parts_ref, target_ref):
    return target_ref[...] / jnp.sum(parts_ref[...], axis=0)


def row_scale(kernel, scale_cols):
    return 1.0 / jnp.sum(kernel * scale_cols, axis=1, keepdims=True)


def spread(value, parts_ref):
    parts_ref[...] = jnp.broadcast_to(value[None], parts_ref.shape)


def code_lines(seed_class, train_mask, rows):
    code = jnp.where(train_mask[...] == 1, seed_class[...], -1).astype(jnp.float32)
    line = jnp.concatenate([code[i : i + 1] for i in range(code.shape[0])], axis=1)
    papers = line.shape[1]
    wide = jnp.broadcast_to(line, (8, papers))
    lines = []
    for start in range(0, papers, rows):
        lines.append((pltpu.roll(wide, papers - start, 1) if start else wide)[:1, :rows])
    return lines


def meta_line(meta, rows):
    count = -(-rows // LANES)
    return jnp.concatenate([meta[i : i + 1] for i in range(count)], axis=1)[:, :rows]


def code_columns(lines):
    rows = lines[0].shape[1]
    wide = jnp.concatenate(lines, axis=0)
    wide = jnp.pad(wide, ((0, -len(lines) % 8), (0, -rows % LANES)))
    columns = wide.T
    return [columns[:rows, i : i + 1] for i in range(len(lines))]


def code_column(line, classes):
    rows = line.shape[1]
    across = lax.broadcasted_iota(jnp.int32, (rows, rows), 1)
    eye = jnp.where(lax.broadcasted_iota(jnp.int32, (rows, rows), 0) == across, 1.0, 0.0)
    wide = jnp.broadcast_to(line, (LANES, rows)).astype(jnp.bfloat16)
    column = lax.dot_general(
        eye.astype(jnp.bfloat16),
        wide,
        (((1,), (1,)), ((), ())),
        preferred_element_type=jnp.float32,
    )
    return jnp.concatenate([column] * (classes // LANES), axis=1)


def seeds_of(line, classes):
    class_line = lax.broadcasted_iota(jnp.int32, (classes, line.shape[1]), 0)
    return jnp.where(class_line.astype(jnp.float32) == line, 1.0, 0.0).astype(jnp.bfloat16)


def pack_kernel(rows, tile_count, *refs):
    tiles, *refs = refs
    count = 6
    ins, places = refs[:count], refs[count : 2 * count]
    keep, swap, ready, arrived = refs[2 * count :]
    tile_paper, tile_author, seed_class, train_mask = places[:4]
    pairs = keep.shape[0]
    me = lax.axis_index("blk")
    pair, side = lax.div(me, 2), lax.rem(me, 2)
    moves = [
        pltpu.make_async_copy(source, place, ready.at[i])
        for i, (source, place) in enumerate(zip(ins, places))
    ]
    for copy in moves:
        copy.start()
    outs = []
    copies = []
    for way, (out, to) in enumerate(((keep, side), (swap, 1 - side))):
        for k, other in enumerate(pair_order(pairs, to)):
            slot = 2 * lax.bitwise_xor(pair, other) + to
            copy = pltpu.make_async_copy(
                tiles.at[slot], out.at[k, pl.ds(0, rows)], arrived.at[way, k]
            )
            copy.start()
            copies.append(copy)
            outs.append((out, k, slot))
    for copy in moves[:4]:
        copy.wait()
    line = lax.broadcasted_iota(jnp.int32, (META, LANES), 0)
    code_rows = -(-rows // LANES)
    blocks = []
    for codes in code_lines(seed_class, train_mask, rows):
        pad = jnp.full((1, code_rows * LANES - rows), -1.0, jnp.float32)
        codes = jnp.concatenate([codes, pad], axis=1)
        block = jnp.zeros((META, LANES), jnp.float32)
        for i in range(code_rows):
            block = jnp.where(line == i, codes[:, i * LANES : (i + 1) * LANES], block)
        blocks.append(block)
    for out, k, slot in outs:
        paper = tile_paper[slot]
        live = slot < tile_count[0]
        block = blocks[0]
        for i in range(1, len(blocks)):
            block = jnp.where(paper == i, blocks[i], block)
        for author in range(AT_DEV):
            chosen = jnp.where(live & (tile_author[slot] == author), 1.0, 0.0)
            block = jnp.where(line == code_rows + author, chosen, block)
        block = jnp.where(line == code_rows + AT_DEV, paper.astype(jnp.float32), block)
        out[k, rows:, :] = block.astype(jnp.bfloat16)
    for copy in moves[4:] + copies:
        copy.wait()


def join_kernel(one, two, out):
    out[0] = one[...]
    out[1] = two[...]


def pair_kernel(keep, swapped, *outs):
    for k, out in enumerate(outs, 1):
        out[0] = keep[k]
        out[1] = swapped[k]


def pair_order(pairs, side):
    return [0, 1 + side, 2 - side, 3] if pairs == 4 else list(range(pairs))


def turned(pairs):
    return [0, 2, 1, 3] if pairs == 4 else list(range(pairs))


def sources(count):
    me = lax.axis_index("blk")
    pair, side = lax.div(me, 2), lax.rem(me, 2)
    pairs = [2 * lax.bitwise_xor(pair, k) for k in pair_order(count // 2, side)]
    return [other + side for other in pairs] + [other + 1 - side for other in pairs]


def own_tiles(keep, swap, rows):
    pairs = keep.shape[0]
    kept = [keep[k, :rows, :] for k in range(pairs)]
    return kept + [swap[k, :rows, :] for k in turned(pairs)]


def views(refs, places):
    return [refs[i] if place is None else refs[i].at[place] for i, place in places]


def slots_of(keep, swapped, *pairs):
    return [(keep, 0), *((ref, 0) for ref in pairs), (swapped, 0), *((ref, 1) for ref in pairs)]


def first_sum_kernel(
    authors, rows, tile_paper, tile_count, keep, swap, seed_class, train_mask, class_prior, parts
):
    pairs, _, columns = keep.shape
    classes = parts.shape[2]
    slots = sources(2 * pairs)
    tiles = [tile.astype(jnp.float32) for tile in own_tiles(keep, swap, rows)]
    lane = lax.broadcasted_iota(jnp.int32, (rows, classes), 1).astype(jnp.float32)
    total = authors * class_prior[...]
    for paper, code in enumerate(code_columns(code_lines(seed_class, train_mask, rows))):
        weight = jnp.zeros((rows, columns), jnp.float32)
        for slot, tile in zip(slots, tiles):
            chosen = (slot < tile_count[0]) & (tile_paper[slot] == paper)
            weight = weight + jnp.where(chosen, tile, 0.0)
        weight = jnp.sum(weight, axis=1, keepdims=True)
        seeds = jnp.where(code == lane, weight, 0.0)
        total = total + jnp.sum(seeds, axis=0, keepdims=True)
    spread(total, parts)


def next_sum(kernel, summed, class_target, parts):
    scale_rows = row_scale(kernel, col_scale(summed, class_target))
    spread(jnp.sum(scale_rows * kernel, axis=0, keepdims=True), parts)


def first_author_kernel(rows, summed, class_prior, class_target, *rest):
    *held, full, parts = rest
    classes = full.shape[1]
    code_rows = -(-rows // LANES)
    totals = [jnp.zeros((classes, LANES), jnp.float32) for _ in range(AT_DEV)]
    for ref, place in slots_of(*held):
        meta = ref[place, rows:, :].astype(jnp.float32)
        seeds = seeds_of(meta_line(meta, rows), classes)
        parcel = jnp.dot(seeds, ref[place, :rows, :], preferred_element_type=jnp.float32)
        parcel = parcel.astype(jnp.bfloat16).astype(jnp.float32)
        for author in range(AT_DEV):
            chosen = meta[code_rows + author : code_rows + author + 1]
            totals[author] = totals[author] + parcel * chosen
    kernel = jnp.concatenate([total.T for total in totals], axis=0) + class_prior[...]
    full[...] = kernel
    next_sum(kernel, summed, class_target, parts)


def author_kernel(rows, places, summed, class_prior, class_target, *rest):
    *rest, full, parts = rest
    count = 1 + max(i for i, _ in places)
    kernels, held = views(rest, places), slots_of(*rest[count:])
    classes = full.shape[1]
    code_rows = -(-rows // LANES)
    metas = [ref[place, rows:, :].astype(jnp.float32) for ref, place in held]
    at = code_rows + AT_DEV
    papers = [jnp.max(meta[at : at + 1]).astype(jnp.int32) for meta in metas]
    scale_cols = col_scale(summed, class_target)
    codes = code_columns([meta_line(meta, rows) for meta in metas])
    totals = [jnp.zeros((LANES, classes), jnp.float32) for _ in range(AT_DEV)]
    lane = lax.broadcasted_iota(jnp.int32, (rows, classes), 1).astype(jnp.float32)
    for shift, (ref, place) in enumerate(held):
        half = kernels[shift][pl.ds(pl.multiple_of(papers[shift] * rows, rows), rows), :]
        scaled = half.astype(jnp.float32) * scale_cols
        share = scaled * (keep_share / jnp.sum(scaled, axis=1, keepdims=True))
        labels = jnp.where(codes[shift] == lane, share + (1.0 - keep_share), share)
        parcel = lax.dot_general(
            ref[place, :rows, :],
            labels.astype(jnp.bfloat16),
            (((0,), (0,)), ((), ())),
            preferred_element_type=jnp.float32,
        )
        parcel = parcel.astype(jnp.bfloat16).astype(jnp.float32)
        for author in range(AT_DEV):
            at = code_rows + author
            totals[author] = totals[author] + parcel * metas[shift][at : at + 1, :1]
    kernel = jnp.concatenate(totals, axis=0) + class_prior[...]
    full[...] = kernel
    spread(jnp.sum(kernel, axis=0, keepdims=True), parts)


def paper_kernel(
    places, rows, tile_paper, tile_author, tile_count, keep, swap, summed, class_prior,
    class_target, *rest,
):
    kernels, (full, parts, *half) = views(rest, places), rest[1 + max(i for i, _ in places) :]
    columns = keep.shape[2]
    classes = full.shape[1]
    scale_cols = col_scale(summed, class_target)
    slots = sources(len(kernels))
    wide = jnp.concatenate(own_tiles(keep, swap, rows), axis=1)
    labels = []
    for ref, slot in zip(kernels, slots):
        start = pl.multiple_of(tile_author[slot] * columns, columns)
        scaled = ref[pl.ds(start, columns), :] * scale_cols
        share = scaled * (1.0 / jnp.sum(scaled, axis=1, keepdims=True))
        labels.append(share.astype(jnp.bfloat16))
    column = jnp.zeros((1, classes), jnp.float32)
    for paper in range(full.shape[0] // rows):
        chosen = []
        for one, slot in zip(labels, slots):
            mine = (slot < tile_count[0]) & (tile_paper[slot] == paper)
            chosen.append(jnp.where(mine, one, jnp.zeros_like(one)))
        mass = jnp.dot(wide, jnp.concatenate(chosen, axis=0), preferred_element_type=jnp.float32)
        kernel = mass + class_prior[...]
        full[paper * rows : (paper + 1) * rows, :] = kernel
        for out in half:
            out[paper * rows : (paper + 1) * rows, :] = kernel.astype(jnp.bfloat16)
        column = column + jnp.sum(kernel, axis=0, keepdims=True)
    spread(column, parts)


def balance_kernel(*refs):
    *kernels, summed, class_target, parts = refs
    scale_cols = col_scale(summed, class_target)
    total = None
    refs = [(ref, i) for ref in kernels for i in range(ref.shape[0] if ref.ndim == 3 else 1)]
    for ref, i in refs:
        kernel = (ref[i] if ref.ndim == 3 else ref[...]).astype(jnp.float32)
        local = jnp.sum(row_scale(kernel, scale_cols) * kernel, axis=0, keepdims=True)
        total = local if total is None else total + local
    spread(total, parts)


def final_kernel(
    rows, kernel_ref, summed, own, author_summed, class_target, seed_class, train_mask,
    out, scores, out_made, scores_made, left,
):
    classes = out.shape[1]
    scaled = own[...] * col_scale(author_summed, class_target)
    scores_made[...] = scaled * (classes / jnp.sum(scaled, axis=1, keepdims=True))
    copies = [pltpu.make_async_copy(scores_made, scores, left.at[0])]
    copies[0].start()
    scale_cols = col_scale(summed, class_target)
    lane = lax.broadcasted_iota(jnp.int32, (rows, classes), 1).astype(jnp.float32)
    for paper, line in enumerate(code_lines(seed_class, train_mask, rows)):
        code = code_column(line, classes)
        part = pl.ds(paper * rows, rows)
        scaled = kernel_ref[part, :] * scale_cols
        share = scaled * (1.0 / jnp.sum(scaled, axis=1, keepdims=True))
        updated = keep_share * share + jnp.where(code == lane, 1.0 - keep_share, 0.0)
        out_made[part, :] = classes * updated
        copies.append(pltpu.make_async_copy(out_made.at[part], out.at[part], left.at[paper + 1]))
        copies[-1].start()
    for copy in copies:
        copy.wait()


def in_hbm(value):
    return pltpu.with_memory_space_constraint(value, pltpu.HBM)


def exchange(parts):
    return lax.all_to_all(parts, AXES, split_axis=0, concat_axis=0, tiled=True)


def narrow_exchange(parts, sides, upwards):
    groups, blocks = lax.axis_size("grp"), lax.axis_size("blk")
    planes = range(groups)
    if not upwards:
        planes = sorted(planes, key=lambda i: abs(2 * i + 1 - groups))
    sets = [
        [i * blocks + first + side for i in planes for side in reversed(range(sides))]
        for first in range(0, blocks, sides)
    ]
    return lax.all_to_all(
        parts, AXES, split_axis=0, concat_axis=0, axis_index_groups=sets, tiled=True
    )


def on_device(
    tile_values,
    tile_paper,
    tile_author,
    tile_count,
    seed_class,
    train_mask,
    class_prior,
    class_target,
):
    f32 = jnp.float32
    bf16 = jnp.bfloat16
    shape = jax.ShapeDtypeStruct
    slots, rows, columns = tile_values.shape
    classes = class_prior.shape[0]
    papers = seed_class.shape[0]
    authors = AT_DEV * columns
    paper_tiles = papers // rows
    devices = lax.axis_size(AXES)
    prior = class_prior.reshape(1, classes)
    target = class_target.reshape(1, classes)
    seed_class = seed_class.reshape(papers // LANES, LANES)
    train_mask = train_mask.reshape(papers // LANES, LANES)
    parts = shape((devices, 1, classes), f32)

    inputs = (
        tile_paper, tile_author, seed_class, train_mask, prior, target,
    )
    places = (SMEM, SMEM, VMEM, VMEM, VMEM, VMEM)
    blocks = lax.axis_size("blk")
    load = shape((blocks // 2, rows + META, columns), bf16)
    moved = call(
        functools.partial(pack_kernel, rows),
        tuple(shape(one.shape, one.dtype) for one in inputs) + (load, load),
        [SMEM, HBM] + [HBM] * len(inputs),
        [pltpu.SemaphoreType.DMA((len(inputs),)), pltpu.SemaphoreType.DMA((2, blocks // 2))],
        places + (VMEM, VMEM),
    )(tile_count, in_hbm(tile_values), *(in_hbm(one) for one in inputs))
    tile_paper, tile_author, seed_class, train_mask, prior, target, keep, swap = moved
    swapped = lax.ppermute(swap, "blk", [(i, i ^ 1) for i in range(blocks)])
    local = call(
        functools.partial(first_sum_kernel, authors, rows), parts, [SMEM, SMEM] + [VMEM] * 5
    )(tile_paper, tile_count, keep, swap, seed_class, train_mask, prior)
    both = shape((2, rows + META, columns), bf16)
    pairs = call(pair_kernel, (both,) * (blocks // 2 - 1), [VMEM] * 2)(keep, swapped)
    local, *pairs = lax.optimization_barrier((local, *pairs))
    count = blocks // 2

    def across_pairs(value, even, odd):
        hops = [2 * odd if i % 2 else 2 * even for i in range(blocks)]
        return lax.ppermute(value, "blk", [(i, i ^ hop) for i, hop in enumerate(hops)])

    def to_other(value):
        return lax.ppermute(value, "blk", [(i, i ^ 1) for i in range(blocks)])

    ways = list(zip(pair_order(count, 0), pair_order(count, 1)))
    held = [keep, swapped] + [across_pairs(one, *way) for one, way in zip(pairs, ways[1:])]
    summed = exchange(local)

    author_out = (shape((authors, classes), f32), parts)
    paper_out = (shape((papers, classes), f32), parts, shape((papers, classes), bf16))

    four = count == 4
    places = [(i, None) for i in range(blocks)]
    if four:
        places = [(0, None), (1, None), (2, 0), (2, 1)]
        places += [(3 + places[k][0], places[k][1]) for k in turned(count)]

    def balance(kernel, sent, local, steps, widest):
        here, there, joined = [sent], [], None
        sides = 0
        for step in range(steps):
            moves = []
            if step == 0:
                moves = [(sent, *way) for way in ways[1 : 2 if four else 3]]
            elif step == 1:
                moves = [(joined, *ways[2])] if four else [(sent, *way) for way in ways[3:]]
            moves = [across_pairs(*move) for move in moves]
            others = [] if step == 0 else [sent] if step == 1 else here[len(there) :]
            others = [to_other(one) for one in others]
            if sides:
                summed = narrow_exchange(local, sides, step + 1 == steps and sides == 2)
            else:
                summed = exchange(local)
            summed, *moved = lax.optimization_barrier((summed, *moves, *others))
            here += moved[: len(moves)]
            there += moved[len(moves) :]
            if step + 1 < steps:
                added, size = [kernel], devices
                if step > 0:
                    added = list(here)
                    sides = 2
                    if step > 1 and widest:
                        added += there
                        sides = 1
                    size = sides * lax.axis_size("grp")
                local = call(
                    balance_kernel, shape((size, 1, classes), f32), [VMEM] * (len(added) + 2)
                )(*added, summed, target)
                joined = sent
                if four and step == 0:
                    joined = call(join_kernel, shape((2, *sent.shape), sent.dtype), [VMEM] * 2)(*here)
                local, sent, joined, *here = lax.optimization_barrier((local, sent, joined, *here))
        return summed, here + there

    def last_balance(kernel, local):
        for step in range(ITERS):
            summed = exchange(local)
            if step + 1 < ITERS:
                local = call(balance_kernel, parts, [VMEM] * 3)(kernel, summed, target)
        return summed

    for repeat in range(ROUNDS):
        if repeat == 0:
            own, local = call(
                functools.partial(first_author_kernel, rows), author_out, [VMEM] * (3 + len(held))
            )(summed, prior, target, *held)
            left = ITERS - 1
        else:
            own, local = call(
                functools.partial(author_kernel, rows, places),
                author_out,
                [VMEM] * (3 + len(kernels) + len(held)),
            )(summed, prior, target, *kernels, *held)
            left = ITERS
        author_summed, kernels = balance(own, own, local, left, True)
        last = repeat + 1 == ROUNDS
        kernel, local, *half = call(
            functools.partial(paper_kernel, places, rows),
            paper_out[:2] if last else paper_out,
            [SMEM, SMEM, SMEM] + [VMEM] * (5 + len(kernels)),
        )(
            tile_paper, tile_author, tile_count, keep, swap, author_summed, prior, target, *kernels
        )
        if last:
            summed = last_balance(kernel, local)
        else:
            summed, kernels = balance(kernel, half[0], local, ITERS, False)
    return call(
        functools.partial(final_kernel, rows),
        (shape((papers, classes), f32), shape((authors, classes), f32)),
        [VMEM] * 7,
        [
            pltpu.VMEM((papers, classes), f32),
            pltpu.VMEM((authors, classes), f32),
            pltpu.SemaphoreType.DMA((1 + papers // rows,)),
        ],
        (HBM, HBM),
    )(kernel, summed, own, author_summed, target, seed_class, train_mask)


def solution(mesh):
    placed = (
        P(("grp", "blk"), None, None),
        P(("grp", "blk")),
        P(("grp", "blk")),
        P(("grp", "blk")),
        P(("grp", "blk")),
        P(("grp", "blk")),
        P(),
        P(),
    )
    return jax.shard_map(
        on_device,
        mesh=mesh,
        in_specs=placed,
        out_specs=(P(("grp", "blk"), None), P(("grp", "blk"), None)),
        check_vma=False,
    )
```

```python
import functools

import jax
import jax.numpy as jnp
from jax import lax
from jax.experimental import pallas as pl
from jax.experimental.pallas import tpu as pltpu
from jax.sharding import PartitionSpec as P

AT_DEV = 2
ITERS = 4
ROUNDS = 2
LANES = 128
META = 16

keep_share = 0.8

AXES = ("grp", "blk")
VMEM = pl.BlockSpec(memory_space=pltpu.VMEM)
SMEM = pl.BlockSpec(memory_space=pltpu.SMEM)
HBM = pl.BlockSpec(memory_space=pltpu.HBM)


def call(kernel, out_shape, in_specs, scratch_shapes=(), out_specs=None):
    if out_specs is None:
        out_specs = jax.tree.map(lambda _: VMEM, out_shape)
    return pl.pallas_call(
        kernel,
        out_shape=out_shape,
        in_specs=in_specs,
        out_specs=out_specs,
        scratch_shapes=list(scratch_shapes),
        compiler_params=pltpu.CompilerParams(vmem_limit_bytes=48 * 1024 * 1024),
    )


def col_scale(parts_ref, target_ref):
    return target_ref[...] / jnp.sum(parts_ref[...], axis=0)


def row_scale(kernel, scale_cols):
    return 1.0 / jnp.sum(kernel * scale_cols, axis=1, keepdims=True)


def spread(value, parts_ref):
    parts_ref[...] = jnp.broadcast_to(value[None], parts_ref.shape)


def code_lines(seed_class, train_mask, rows):
    code = jnp.where(train_mask[...] == 1, seed_class[...], -1).astype(jnp.float32)
    line = jnp.concatenate([code[i : i + 1] for i in range(code.shape[0])], axis=1)
    papers = line.shape[1]
    wide = jnp.broadcast_to(line, (8, papers))
    lines = []
    for start in range(0, papers, rows):
        lines.append((pltpu.roll(wide, papers - start, 1) if start else wide)[:1, :rows])
    return lines


def meta_line(meta, rows):
    count = -(-rows // LANES)
    return jnp.concatenate([meta[i : i + 1] for i in range(count)], axis=1)[:, :rows]


def code_columns(lines):
    rows = lines[0].shape[1]
    wide = jnp.concatenate(lines, axis=0)
    wide = jnp.pad(wide, ((0, -len(lines) % 8), (0, -rows % LANES)))
    columns = wide.T
    return [columns[:rows, i : i + 1] for i in range(len(lines))]


def code_column(line, classes):
    rows = line.shape[1]
    across = lax.broadcasted_iota(jnp.int32, (rows, rows), 1)
    eye = jnp.where(lax.broadcasted_iota(jnp.int32, (rows, rows), 0) == across, 1.0, 0.0)
    wide = jnp.broadcast_to(line, (LANES, rows)).astype(jnp.bfloat16)
    column = lax.dot_general(
        eye.astype(jnp.bfloat16),
        wide,
        (((1,), (1,)), ((), ())),
        preferred_element_type=jnp.float32,
    )
    return jnp.concatenate([column] * (classes // LANES), axis=1)


def seeds_of(line, classes):
    class_line = lax.broadcasted_iota(jnp.int32, (classes, line.shape[1]), 0)
    return jnp.where(class_line.astype(jnp.float32) == line, 1.0, 0.0).astype(jnp.bfloat16)


def pack_kernel(rows, tile_count, *refs):
    tiles, *refs = refs
    count = 6
    ins, places = refs[:count], refs[count : 2 * count]
    keep, swap, ready, arrived = refs[2 * count :]
    tile_paper, tile_author, seed_class, train_mask = places[:4]
    pairs = keep.shape[0]
    me = lax.axis_index("blk")
    pair, side = lax.div(me, 2), lax.rem(me, 2)
    moves = [
        pltpu.make_async_copy(source, place, ready.at[i])
        for i, (source, place) in enumerate(zip(ins, places))
    ]
    for copy in moves:
        copy.start()
    outs = []
    copies = []
    for way, (out, to) in enumerate(((keep, side), (swap, 1 - side))):
        for k, other in enumerate(pair_order(pairs, to)):
            slot = 2 * lax.bitwise_xor(pair, other) + to
            copy = pltpu.make_async_copy(
                tiles.at[slot], out.at[k, pl.ds(0, rows)], arrived.at[way, k]
            )
            copy.start()
            copies.append(copy)
            outs.append((out, k, slot))
    for copy in moves[:4]:
        copy.wait()
    line = lax.broadcasted_iota(jnp.int32, (META, LANES), 0)
    code_rows = -(-rows // LANES)
    blocks = []
    for codes in code_lines(seed_class, train_mask, rows):
        pad = jnp.full((1, code_rows * LANES - rows), -1.0, jnp.float32)
        codes = jnp.concatenate([codes, pad], axis=1)
        block = jnp.zeros((META, LANES), jnp.float32)
        for i in range(code_rows):
            block = jnp.where(line == i, codes[:, i * LANES : (i + 1) * LANES], block)
        blocks.append(block)
    for out, k, slot in outs:
        paper = tile_paper[slot]
        live = slot < tile_count[0]
        block = blocks[0]
        for i in range(1, len(blocks)):
            block = jnp.where(paper == i, blocks[i], block)
        for author in range(AT_DEV):
            chosen = jnp.where(live & (tile_author[slot] == author), 1.0, 0.0)
            block = jnp.where(line == code_rows + author, chosen, block)
        block = jnp.where(line == code_rows + AT_DEV, paper.astype(jnp.float32), block)
        out[k, rows:, :] = block.astype(jnp.bfloat16)
    for copy in moves[4:] + copies:
        copy.wait()


def join_kernel(one, two, out):
    out[0] = one[...]
    out[1] = two[...]


def pair_kernel(keep, swapped, *outs):
    for k, out in enumerate(outs, 1):
        out[0] = keep[k]
        out[1] = swapped[k]


def pair_order(pairs, side):
    return [0, 1 + side, 2 - side, 3] if pairs == 4 else list(range(pairs))


def turned(pairs):
    return [0, 2, 1, 3] if pairs == 4 else list(range(pairs))


def sources(count):
    me = lax.axis_index("blk")
    pair, side = lax.div(me, 2), lax.rem(me, 2)
    pairs = [2 * lax.bitwise_xor(pair, k) for k in pair_order(count // 2, side)]
    return [other + side for other in pairs] + [other + 1 - side for other in pairs]


def own_tiles(keep, swap, rows):
    pairs = keep.shape[0]
    kept = [keep[k, :rows, :] for k in range(pairs)]
    return kept + [swap[k, :rows, :] for k in turned(pairs)]


def views(refs, places):
    return [refs[i] if place is None else refs[i].at[place] for i, place in places]


def slots_of(keep, swapped, *pairs):
    return [(keep, 0), *((ref, 0) for ref in pairs), (swapped, 0), *((ref, 1) for ref in pairs)]


def first_sum_kernel(
    authors, rows, tile_paper, tile_count, keep, swap, seed_class, train_mask, class_prior, parts
):
    pairs, _, columns = keep.shape
    classes = parts.shape[2]
    slots = sources(2 * pairs)
    tiles = [tile.astype(jnp.float32) for tile in own_tiles(keep, swap, rows)]
    lane = lax.broadcasted_iota(jnp.int32, (rows, classes), 1).astype(jnp.float32)
    total = authors * class_prior[...]
    for paper, code in enumerate(code_columns(code_lines(seed_class, train_mask, rows))):
        weight = jnp.zeros((rows, columns), jnp.float32)
        for slot, tile in zip(slots, tiles):
            chosen = (slot < tile_count[0]) & (tile_paper[slot] == paper)
            weight = weight + jnp.where(chosen, tile, 0.0)
        weight = jnp.sum(weight, axis=1, keepdims=True)
        seeds = jnp.where(code == lane, weight, 0.0)
        total = total + jnp.sum(seeds, axis=0, keepdims=True)
    spread(total, parts)


def next_sum(kernel, summed, class_target, parts):
    scale_rows = row_scale(kernel, col_scale(summed, class_target))
    spread(jnp.sum(scale_rows * kernel, axis=0, keepdims=True), parts)


def first_author_kernel(rows, summed, class_prior, class_target, *rest):
    *held, full, parts = rest
    classes = full.shape[1]
    code_rows = -(-rows // LANES)
    totals = [jnp.zeros((classes, LANES), jnp.float32) for _ in range(AT_DEV)]
    for ref, place in slots_of(*held):
        meta = ref[place, rows:, :].astype(jnp.float32)
        seeds = seeds_of(meta_line(meta, rows), classes)
        parcel = jnp.dot(seeds, ref[place, :rows, :], preferred_element_type=jnp.float32)
        parcel = parcel.astype(jnp.bfloat16).astype(jnp.float32)
        for author in range(AT_DEV):
            chosen = meta[code_rows + author : code_rows + author + 1]
            totals[author] = totals[author] + parcel * chosen
    kernel = jnp.concatenate([total.T for total in totals], axis=0) + class_prior[...]
    full[...] = kernel
    next_sum(kernel, summed, class_target, parts)


def author_kernel(rows, places, summed, class_prior, class_target, *rest):
    *rest, full, parts = rest
    count = 1 + max(i for i, _ in places)
    kernels, held = views(rest, places), slots_of(*rest[count:])
    classes = full.shape[1]
    code_rows = -(-rows // LANES)
    metas = [ref[place, rows:, :].astype(jnp.float32) for ref, place in held]
    at = code_rows + AT_DEV
    papers = [jnp.max(meta[at : at + 1]).astype(jnp.int32) for meta in metas]
    scale_cols = col_scale(summed, class_target)
    codes = code_columns([meta_line(meta, rows) for meta in metas])
    totals = [jnp.zeros((LANES, classes), jnp.float32) for _ in range(AT_DEV)]
    lane = lax.broadcasted_iota(jnp.int32, (rows, classes), 1).astype(jnp.float32)
    for shift, (ref, place) in enumerate(held):
        half = kernels[shift][pl.ds(pl.multiple_of(papers[shift] * rows, rows), rows), :]
        scaled = half.astype(jnp.float32) * scale_cols
        share = scaled * (keep_share / jnp.sum(scaled, axis=1, keepdims=True))
        labels = jnp.where(codes[shift] == lane, share + (1.0 - keep_share), share)
        parcel = lax.dot_general(
            ref[place, :rows, :],
            labels.astype(jnp.bfloat16),
            (((0,), (0,)), ((), ())),
            preferred_element_type=jnp.float32,
        )
        parcel = parcel.astype(jnp.bfloat16).astype(jnp.float32)
        for author in range(AT_DEV):
            at = code_rows + author
            totals[author] = totals[author] + parcel * metas[shift][at : at + 1, :1]
    kernel = jnp.concatenate(totals, axis=0) + class_prior[...]
    full[...] = kernel
    spread(jnp.sum(kernel, axis=0, keepdims=True), parts)


def paper_kernel(
    places, rows, tile_paper, tile_author, tile_count, keep, swap, summed, class_prior,
    class_target, *rest,
):
    kernels, (full, parts, half) = views(rest, places), rest[1 + max(i for i, _ in places) :]
    columns = keep.shape[2]
    classes = full.shape[1]
    scale_cols = col_scale(summed, class_target)
    slots = sources(len(kernels))
    wide = jnp.concatenate(own_tiles(keep, swap, rows), axis=1)
    labels = []
    for ref, slot in zip(kernels, slots):
        start = pl.multiple_of(tile_author[slot] * columns, columns)
        scaled = ref[pl.ds(start, columns), :] * scale_cols
        share = scaled * (1.0 / jnp.sum(scaled, axis=1, keepdims=True))
        labels.append(share.astype(jnp.bfloat16))
    column = jnp.zeros((1, classes), jnp.float32)
    for paper in range(full.shape[0] // rows):
        chosen = []
        for one, slot in zip(labels, slots):
            mine = (slot < tile_count[0]) & (tile_paper[slot] == paper)
            chosen.append(jnp.where(mine, one, jnp.zeros_like(one)))
        mass = jnp.dot(wide, jnp.concatenate(chosen, axis=0), preferred_element_type=jnp.float32)
        kernel = mass + class_prior[...]
        full[paper * rows : (paper + 1) * rows, :] = kernel
        half[paper * rows : (paper + 1) * rows, :] = kernel.astype(jnp.bfloat16)
        column = column + jnp.sum(kernel, axis=0, keepdims=True)
    spread(column, parts)


def balance_kernel(*refs):
    *kernels, summed, class_target, parts = refs
    scale_cols = col_scale(summed, class_target)
    total = None
    refs = [(ref, i) for ref in kernels for i in range(ref.shape[0] if ref.ndim == 3 else 1)]
    for ref, i in refs:
        kernel = (ref[i] if ref.ndim == 3 else ref[...]).astype(jnp.float32)
        local = jnp.sum(row_scale(kernel, scale_cols) * kernel, axis=0, keepdims=True)
        total = local if total is None else total + local
    spread(total, parts)


def final_kernel(
    rows, kernel_ref, summed, own, author_summed, class_target, seed_class, train_mask,
    out, scores, out_made, scores_made, left,
):
    classes = out.shape[1]
    scaled = own[...] * col_scale(author_summed, class_target)
    scores_made[...] = scaled * (classes / jnp.sum(scaled, axis=1, keepdims=True))
    copies = [pltpu.make_async_copy(scores_made, scores, left.at[0])]
    copies[0].start()
    scale_cols = col_scale(summed, class_target)
    lane = lax.broadcasted_iota(jnp.int32, (rows, classes), 1).astype(jnp.float32)
    for paper, line in enumerate(code_lines(seed_class, train_mask, rows)):
        code = code_column(line, classes)
        part = pl.ds(paper * rows, rows)
        scaled = kernel_ref[part, :] * scale_cols
        share = scaled * (1.0 / jnp.sum(scaled, axis=1, keepdims=True))
        updated = keep_share * share + jnp.where(code == lane, 1.0 - keep_share, 0.0)
        out_made[part, :] = classes * updated
        copies.append(pltpu.make_async_copy(out_made.at[part], out.at[part], left.at[paper + 1]))
        copies[-1].start()
    for copy in copies:
        copy.wait()


def in_hbm(value):
    return pltpu.with_memory_space_constraint(value, pltpu.HBM)


def exchange(parts):
    return lax.all_to_all(parts, AXES, split_axis=0, concat_axis=0, tiled=True)


def narrow_exchange(parts, sides, upwards):
    groups, blocks = lax.axis_size("grp"), lax.axis_size("blk")
    planes = range(groups)
    if not upwards:
        planes = sorted(planes, key=lambda i: abs(2 * i + 1 - groups))
    sets = [
        [i * blocks + first + side for i in planes for side in reversed(range(sides))]
        for first in range(0, blocks, sides)
    ]
    return lax.all_to_all(
        parts, AXES, split_axis=0, concat_axis=0, axis_index_groups=sets, tiled=True
    )


def on_device(
    tile_values,
    tile_paper,
    tile_author,
    tile_count,
    seed_class,
    train_mask,
    class_prior,
    class_target,
):
    f32 = jnp.float32
    bf16 = jnp.bfloat16
    shape = jax.ShapeDtypeStruct
    slots, rows, columns = tile_values.shape
    classes = class_prior.shape[0]
    papers = seed_class.shape[0]
    authors = AT_DEV * columns
    paper_tiles = papers // rows
    devices = lax.axis_size(AXES)
    prior = class_prior.reshape(1, classes)
    target = class_target.reshape(1, classes)
    seed_class = seed_class.reshape(papers // LANES, LANES)
    train_mask = train_mask.reshape(papers // LANES, LANES)
    parts = shape((devices, 1, classes), f32)

    inputs = (
        tile_paper, tile_author, seed_class, train_mask, prior, target,
    )
    places = (SMEM, SMEM, VMEM, VMEM, VMEM, VMEM)
    blocks = lax.axis_size("blk")
    load = shape((blocks // 2, rows + META, columns), bf16)
    moved = call(
        functools.partial(pack_kernel, rows),
        tuple(shape(one.shape, one.dtype) for one in inputs) + (load, load),
        [SMEM, HBM] + [HBM] * len(inputs),
        [pltpu.SemaphoreType.DMA((len(inputs),)), pltpu.SemaphoreType.DMA((2, blocks // 2))],
        places + (VMEM, VMEM),
    )(tile_count, in_hbm(tile_values), *(in_hbm(one) for one in inputs))
    tile_paper, tile_author, seed_class, train_mask, prior, target, keep, swap = moved
    swapped = lax.ppermute(swap, "blk", [(i, i ^ 1) for i in range(blocks)])
    local = call(
        functools.partial(first_sum_kernel, authors, rows), parts, [SMEM, SMEM] + [VMEM] * 5
    )(tile_paper, tile_count, keep, swap, seed_class, train_mask, prior)
    both = shape((2, rows + META, columns), bf16)
    pairs = call(pair_kernel, (both,) * (blocks // 2 - 1), [VMEM] * 2)(keep, swapped)
    local, *pairs = lax.optimization_barrier((local, *pairs))
    count = blocks // 2

    def across_pairs(value, even, odd):
        hops = [2 * odd if i % 2 else 2 * even for i in range(blocks)]
        return lax.ppermute(value, "blk", [(i, i ^ hop) for i, hop in enumerate(hops)])

    def to_other(value):
        return lax.ppermute(value, "blk", [(i, i ^ 1) for i in range(blocks)])

    ways = list(zip(pair_order(count, 0), pair_order(count, 1)))
    held = [keep, swapped] + [across_pairs(one, *way) for one, way in zip(pairs, ways[1:])]
    summed = exchange(local)

    author_out = (shape((authors, classes), f32), parts)
    paper_out = (shape((papers, classes), f32), parts, shape((papers, classes), bf16))

    four = count == 4
    places = [(i, None) for i in range(blocks)]
    if four:
        places = [(0, None), (1, None), (2, 0), (2, 1)]
        places += [(3 + places[k][0], places[k][1]) for k in turned(count)]

    def balance(kernel, sent, local, steps, widest=False, last=False):
        here, there, joined = [sent], [], None
        sides = 0
        for step in range(steps):
            moves = []
            if step == 0:
                moves = [(sent, *way) for way in ways[1 : 2 if four else 3]]
            elif step == 1:
                moves = [(joined, *ways[2])] if four else [(sent, *way) for way in ways[3:]]
            moves = [across_pairs(*move) for move in moves]
            others = [] if step == 0 else [sent] if step == 1 else here[len(there) :]
            others = [] if last else [to_other(one) for one in others]
            if sides:
                upwards = step + 1 == steps and sides == 2 and not last
                summed = narrow_exchange(local, sides, upwards)
            else:
                summed = exchange(local)
            summed, *moved = lax.optimization_barrier((summed, *moves, *others))
            here += moved[: len(moves)]
            there += moved[len(moves) :]
            if step + 1 < steps:
                added, size = [kernel], devices
                if step > 0:
                    added = list(here)
                    sides = 2
                    if step > 1 and widest:
                        added += there
                        sides = 1
                    size = sides * lax.axis_size("grp")
                local = call(
                    balance_kernel, shape((size, 1, classes), f32), [VMEM] * (len(added) + 2)
                )(*added, summed, target)
                joined = sent
                if four and step == 0:
                    joined = call(join_kernel, shape((2, *sent.shape), sent.dtype), [VMEM] * 2)(*here)
                local, sent, joined, *here = lax.optimization_barrier((local, sent, joined, *here))
        return summed, here + there

    for repeat in range(ROUNDS):
        if repeat == 0:
            own, local = call(
                functools.partial(first_author_kernel, rows), author_out, [VMEM] * (3 + len(held))
            )(summed, prior, target, *held)
            left = ITERS - 1
        else:
            own, local = call(
                functools.partial(author_kernel, rows, places),
                author_out,
                [VMEM] * (3 + len(kernels) + len(held)),
            )(summed, prior, target, *kernels, *held)
            left = ITERS
        author_summed, kernels = balance(own, own, local, left, widest=True)
        last = repeat + 1 == ROUNDS
        kernel, local, half = call(
            functools.partial(paper_kernel, places, rows),
            paper_out,
            [SMEM, SMEM, SMEM] + [VMEM] * (5 + len(kernels)),
        )(
            tile_paper, tile_author, tile_count, keep, swap, author_summed, prior, target, *kernels
        )
        summed, kernels = balance(kernel, half, local, ITERS, last=last)
    return call(
        functools.partial(final_kernel, rows),
        (shape((papers, classes), f32), shape((authors, classes), f32)),
        [VMEM] * 7,
        [
            pltpu.VMEM((papers, classes), f32),
            pltpu.VMEM((authors, classes), f32),
            pltpu.SemaphoreType.DMA((1 + papers // rows,)),
        ],
        (HBM, HBM),
    )(kernel, summed, own, author_summed, target, seed_class, train_mask)


def solution(mesh):
    placed = (
        P(("grp", "blk"), None, None),
        P(("grp", "blk")),
        P(("grp", "blk")),
        P(("grp", "blk")),
        P(("grp", "blk")),
        P(("grp", "blk")),
        P(),
        P(),
    )
    return jax.shard_map(
        on_device,
        mesh=mesh,
        in_specs=placed,
        out_specs=(P(("grp", "blk"), None), P(("grp", "blk"), None)),
        check_vma=False,
    )
```

```python
import functools

import jax
import jax.numpy as jnp
from jax import lax
from jax.experimental import pallas as pl
from jax.experimental.pallas import tpu as pltpu
from jax.sharding import PartitionSpec as P

AT_DEV = 2
ITERS = 4
ROUNDS = 2
LANES = 128
META = 16

keep_share = 0.8

AXES = ("grp", "blk")
VMEM = pl.BlockSpec(memory_space=pltpu.VMEM)
SMEM = pl.BlockSpec(memory_space=pltpu.SMEM)
HBM = pl.BlockSpec(memory_space=pltpu.HBM)


def call(kernel, out_shape, in_specs, scratch_shapes=(), out_specs=None):
    if out_specs is None:
        out_specs = jax.tree.map(lambda _: VMEM, out_shape)
    return pl.pallas_call(
        kernel,
        out_shape=out_shape,
        in_specs=in_specs,
        out_specs=out_specs,
        scratch_shapes=list(scratch_shapes),
        compiler_params=pltpu.CompilerParams(vmem_limit_bytes=48 * 1024 * 1024),
    )


def col_scale(parts_ref, target_ref):
    return target_ref[...] / jnp.sum(parts_ref[...], axis=0)


def row_scale(kernel, scale_cols):
    return 1.0 / jnp.sum(kernel * scale_cols, axis=1, keepdims=True)


def spread(value, parts_ref):
    parts_ref[...] = jnp.broadcast_to(value[None], parts_ref.shape)


def code_lines(seed_class, train_mask, rows):
    code = jnp.where(train_mask[...] == 1, seed_class[...], -1).astype(jnp.float32)
    line = jnp.concatenate([code[i : i + 1] for i in range(code.shape[0])], axis=1)
    papers = line.shape[1]
    wide = jnp.broadcast_to(line, (8, papers))
    lines = []
    for start in range(0, papers, rows):
        lines.append((pltpu.roll(wide, papers - start, 1) if start else wide)[:1, :rows])
    return lines


def meta_line(meta, rows):
    count = -(-rows // LANES)
    return jnp.concatenate([meta[i : i + 1] for i in range(count)], axis=1)[:, :rows]


def code_columns(lines):
    rows = lines[0].shape[1]
    wide = jnp.concatenate(lines, axis=0)
    wide = jnp.pad(wide, ((0, -len(lines) % 8), (0, -rows % LANES)))
    columns = wide.T
    return [columns[:rows, i : i + 1] for i in range(len(lines))]


def code_column(line, classes):
    rows = line.shape[1]
    across = lax.broadcasted_iota(jnp.int32, (rows, rows), 1)
    eye = jnp.where(lax.broadcasted_iota(jnp.int32, (rows, rows), 0) == across, 1.0, 0.0)
    wide = jnp.broadcast_to(line, (LANES, rows)).astype(jnp.bfloat16)
    column = lax.dot_general(
        eye.astype(jnp.bfloat16),
        wide,
        (((1,), (1,)), ((), ())),
        preferred_element_type=jnp.float32,
    )
    return jnp.concatenate([column] * (classes // LANES), axis=1)


def seeds_of(line, classes):
    class_line = lax.broadcasted_iota(jnp.int32, (classes, line.shape[1]), 0)
    return jnp.where(class_line.astype(jnp.float32) == line, 1.0, 0.0).astype(jnp.bfloat16)


def pack_kernel(rows, tile_count, *refs):
    tiles, *refs = refs
    count = 6
    ins, places = refs[:count], refs[count : 2 * count]
    keep, swap, ready, arrived = refs[2 * count :]
    tile_paper, tile_author, seed_class, train_mask = places[:4]
    pairs = keep.shape[0]
    me = lax.axis_index("blk")
    pair, side = lax.div(me, 2), lax.rem(me, 2)
    moves = [
        pltpu.make_async_copy(source, place, ready.at[i])
        for i, (source, place) in enumerate(zip(ins, places))
    ]
    for copy in moves:
        copy.start()
    outs = []
    copies = []
    for way, (out, to) in enumerate(((keep, side), (swap, 1 - side))):
        for k, other in enumerate(pair_order(pairs, to)):
            slot = 2 * lax.bitwise_xor(pair, other) + to
            copy = pltpu.make_async_copy(
                tiles.at[slot], out.at[k, pl.ds(0, rows)], arrived.at[way, k]
            )
            copy.start()
            copies.append(copy)
            outs.append((out, k, slot))
    for copy in moves[:4]:
        copy.wait()
    line = lax.broadcasted_iota(jnp.int32, (META, LANES), 0)
    code_rows = -(-rows // LANES)
    blocks = []
    for codes in code_lines(seed_class, train_mask, rows):
        pad = jnp.full((1, code_rows * LANES - rows), -1.0, jnp.float32)
        codes = jnp.concatenate([codes, pad], axis=1)
        block = jnp.zeros((META, LANES), jnp.float32)
        for i in range(code_rows):
            block = jnp.where(line == i, codes[:, i * LANES : (i + 1) * LANES], block)
        blocks.append(block)
    for out, k, slot in outs:
        paper = tile_paper[slot]
        live = slot < tile_count[0]
        block = blocks[0]
        for i in range(1, len(blocks)):
            block = jnp.where(paper == i, blocks[i], block)
        for author in range(AT_DEV):
            chosen = jnp.where(live & (tile_author[slot] == author), 1.0, 0.0)
            block = jnp.where(line == code_rows + author, chosen, block)
        block = jnp.where(line == code_rows + AT_DEV, paper.astype(jnp.float32), block)
        out[k, rows:, :] = block.astype(jnp.bfloat16)
    for copy in moves[4:] + copies:
        copy.wait()


def pieces(refs):
    return [(ref, i) for ref in refs for i in range(ref.shape[0] if ref.ndim == 3 else 1)]


def piece(ref, i):
    return ref[i] if ref.ndim == 3 else ref[...]


def join_kernel(*refs):
    *ins, out = refs
    for place, one in enumerate(pieces(ins)):
        out[place] = piece(*one)


def pair_kernel(keep, swapped, *outs):
    for k, out in enumerate(outs, 1):
        out[0] = keep[k]
        out[1] = swapped[k]


def pair_order(pairs, side):
    return [0, 1 + side, 2 - side, 3] if pairs == 4 else list(range(pairs))


def turned(pairs):
    return [0, 2, 1, 3] if pairs == 4 else list(range(pairs))


def sources(count):
    me = lax.axis_index("blk")
    pair, side = lax.div(me, 2), lax.rem(me, 2)
    pairs = [2 * lax.bitwise_xor(pair, k) for k in pair_order(count // 2, side)]
    return [other + side for other in pairs] + [other + 1 - side for other in pairs]


def own_tiles(keep, swap, rows):
    pairs = keep.shape[0]
    kept = [keep[k, :rows, :] for k in range(pairs)]
    return kept + [swap[k, :rows, :] for k in turned(pairs)]


def views(refs, places):
    return [refs[i] if place is None else refs[i].at[place] for i, place in places]


def slots_of(keep, swapped, *pairs):
    return [(keep, 0), *((ref, 0) for ref in pairs), (swapped, 0), *((ref, 1) for ref in pairs)]


def first_sum_kernel(
    authors, rows, tile_paper, tile_count, keep, swap, seed_class, train_mask, class_prior, parts
):
    pairs, _, columns = keep.shape
    classes = parts.shape[2]
    slots = sources(2 * pairs)
    tiles = [tile.astype(jnp.float32) for tile in own_tiles(keep, swap, rows)]
    lane = lax.broadcasted_iota(jnp.int32, (rows, classes), 1).astype(jnp.float32)
    total = authors * class_prior[...]
    for paper, code in enumerate(code_columns(code_lines(seed_class, train_mask, rows))):
        weight = jnp.zeros((rows, columns), jnp.float32)
        for slot, tile in zip(slots, tiles):
            chosen = (slot < tile_count[0]) & (tile_paper[slot] == paper)
            weight = weight + jnp.where(chosen, tile, 0.0)
        weight = jnp.sum(weight, axis=1, keepdims=True)
        seeds = jnp.where(code == lane, weight, 0.0)
        total = total + jnp.sum(seeds, axis=0, keepdims=True)
    spread(total, parts)


def next_sum(kernel, summed, class_target, parts):
    scale_rows = row_scale(kernel, col_scale(summed, class_target))
    spread(jnp.sum(scale_rows * kernel, axis=0, keepdims=True), parts)


def first_author_kernel(rows, summed, class_prior, class_target, *rest):
    *held, full, parts = rest
    classes = full.shape[1]
    code_rows = -(-rows // LANES)
    totals = [jnp.zeros((classes, LANES), jnp.float32) for _ in range(AT_DEV)]
    for ref, place in slots_of(*held):
        meta = ref[place, rows:, :].astype(jnp.float32)
        seeds = seeds_of(meta_line(meta, rows), classes)
        parcel = jnp.dot(seeds, ref[place, :rows, :], preferred_element_type=jnp.float32)
        parcel = parcel.astype(jnp.bfloat16).astype(jnp.float32)
        for author in range(AT_DEV):
            chosen = meta[code_rows + author : code_rows + author + 1]
            totals[author] = totals[author] + parcel * chosen
    kernel = jnp.concatenate([total.T for total in totals], axis=0) + class_prior[...]
    full[...] = kernel
    next_sum(kernel, summed, class_target, parts)


def author_kernel(rows, places, summed, class_prior, class_target, *rest):
    *rest, full, parts = rest
    count = 1 + max(i for i, _ in places)
    kernels, held = views(rest, places), slots_of(*rest[count:])
    classes = full.shape[1]
    code_rows = -(-rows // LANES)
    metas = [ref[place, rows:, :].astype(jnp.float32) for ref, place in held]
    at = code_rows + AT_DEV
    papers = [jnp.max(meta[at : at + 1]).astype(jnp.int32) for meta in metas]
    scale_cols = col_scale(summed, class_target)
    codes = code_columns([meta_line(meta, rows) for meta in metas])
    totals = [jnp.zeros((LANES, classes), jnp.float32) for _ in range(AT_DEV)]
    lane = lax.broadcasted_iota(jnp.int32, (rows, classes), 1).astype(jnp.float32)
    for shift, (ref, place) in enumerate(held):
        half = kernels[shift][pl.ds(pl.multiple_of(papers[shift] * rows, rows), rows), :]
        scaled = half.astype(jnp.float32) * scale_cols
        share = scaled * (keep_share / jnp.sum(scaled, axis=1, keepdims=True))
        labels = jnp.where(codes[shift] == lane, share + (1.0 - keep_share), share)
        parcel = lax.dot_general(
            ref[place, :rows, :],
            labels.astype(jnp.bfloat16),
            (((0,), (0,)), ((), ())),
            preferred_element_type=jnp.float32,
        )
        parcel = parcel.astype(jnp.bfloat16).astype(jnp.float32)
        for author in range(AT_DEV):
            at = code_rows + author
            totals[author] = totals[author] + parcel * metas[shift][at : at + 1, :1]
    kernel = jnp.concatenate(totals, axis=0) + class_prior[...]
    full[...] = kernel
    spread(jnp.sum(kernel, axis=0, keepdims=True), parts)


def paper_kernel(
    places, rows, tile_paper, tile_author, tile_count, keep, swap, summed, class_prior,
    class_target, *rest,
):
    kernels, (full, parts, *half) = views(rest, places), rest[1 + max(i for i, _ in places) :]
    columns = keep.shape[2]
    classes = full.shape[1]
    scale_cols = col_scale(summed, class_target)
    slots = sources(len(kernels))
    wide = jnp.concatenate(own_tiles(keep, swap, rows), axis=1)
    labels = []
    for ref, slot in zip(kernels, slots):
        start = pl.multiple_of(tile_author[slot] * columns, columns)
        scaled = ref[pl.ds(start, columns), :] * scale_cols
        share = scaled * (1.0 / jnp.sum(scaled, axis=1, keepdims=True))
        labels.append(share.astype(jnp.bfloat16))
    column = jnp.zeros((1, classes), jnp.float32)
    for paper in range(full.shape[0] // rows):
        chosen = []
        for one, slot in zip(labels, slots):
            mine = (slot < tile_count[0]) & (tile_paper[slot] == paper)
            chosen.append(jnp.where(mine, one, jnp.zeros_like(one)))
        mass = jnp.dot(wide, jnp.concatenate(chosen, axis=0), preferred_element_type=jnp.float32)
        kernel = mass + class_prior[...]
        full[paper * rows : (paper + 1) * rows, :] = kernel
        for out in half:
            out[paper * rows : (paper + 1) * rows, :] = kernel.astype(jnp.bfloat16)
        column = column + jnp.sum(kernel, axis=0, keepdims=True)
    spread(column, parts)


def balance_kernel(*refs):
    *kernels, summed, class_target, parts = refs
    scale_cols = col_scale(summed, class_target)
    total = None
    for one in pieces(kernels):
        kernel = piece(*one).astype(jnp.float32)
        local = jnp.sum(row_scale(kernel, scale_cols) * kernel, axis=0, keepdims=True)
        total = local if total is None else total + local
    spread(total, parts)


def final_kernel(
    rows, kernel_ref, summed, own, author_summed, class_target, seed_class, train_mask,
    out, scores, out_made, scores_made, left,
):
    classes = out.shape[1]
    scaled = own[...] * col_scale(author_summed, class_target)
    scores_made[...] = scaled * (classes / jnp.sum(scaled, axis=1, keepdims=True))
    copies = [pltpu.make_async_copy(scores_made, scores, left.at[0])]
    copies[0].start()
    scale_cols = col_scale(summed, class_target)
    lane = lax.broadcasted_iota(jnp.int32, (rows, classes), 1).astype(jnp.float32)
    for paper, line in enumerate(code_lines(seed_class, train_mask, rows)):
        code = code_column(line, classes)
        part = pl.ds(paper * rows, rows)
        scaled = kernel_ref[part, :] * scale_cols
        share = scaled * (1.0 / jnp.sum(scaled, axis=1, keepdims=True))
        updated = keep_share * share + jnp.where(code == lane, 1.0 - keep_share, 0.0)
        out_made[part, :] = classes * updated
        copies.append(pltpu.make_async_copy(out_made.at[part], out.at[part], left.at[paper + 1]))
        copies[-1].start()
    for copy in copies:
        copy.wait()


def in_hbm(value):
    return pltpu.with_memory_space_constraint(value, pltpu.HBM)


def exchange(parts):
    return lax.all_to_all(parts, AXES, split_axis=0, concat_axis=0, tiled=True)


def narrow_exchange(parts, sides, upwards):
    groups, blocks = lax.axis_size("grp"), lax.axis_size("blk")
    planes = range(groups)
    if not upwards:
        planes = sorted(planes, key=lambda i: abs(2 * i + 1 - groups))
    sets = [
        [i * blocks + first + side for i in planes for side in reversed(range(sides))]
        for first in range(0, blocks, sides)
    ]
    return lax.all_to_all(
        parts, AXES, split_axis=0, concat_axis=0, axis_index_groups=sets, tiled=True
    )


def on_device(
    tile_values,
    tile_paper,
    tile_author,
    tile_count,
    seed_class,
    train_mask,
    class_prior,
    class_target,
):
    f32 = jnp.float32
    bf16 = jnp.bfloat16
    shape = jax.ShapeDtypeStruct
    slots, rows, columns = tile_values.shape
    classes = class_prior.shape[0]
    papers = seed_class.shape[0]
    authors = AT_DEV * columns
    paper_tiles = papers // rows
    devices = lax.axis_size(AXES)
    prior = class_prior.reshape(1, classes)
    target = class_target.reshape(1, classes)
    seed_class = seed_class.reshape(papers // LANES, LANES)
    train_mask = train_mask.reshape(papers // LANES, LANES)
    parts = shape((devices, 1, classes), f32)

    inputs = (
        tile_paper, tile_author, seed_class, train_mask, prior, target,
    )
    places = (SMEM, SMEM, VMEM, VMEM, VMEM, VMEM)
    blocks = lax.axis_size("blk")
    load = shape((blocks // 2, rows + META, columns), bf16)
    moved = call(
        functools.partial(pack_kernel, rows),
        tuple(shape(one.shape, one.dtype) for one in inputs) + (load, load),
        [SMEM, HBM] + [HBM] * len(inputs),
        [pltpu.SemaphoreType.DMA((len(inputs),)), pltpu.SemaphoreType.DMA((2, blocks // 2))],
        places + (VMEM, VMEM),
    )(tile_count, in_hbm(tile_values), *(in_hbm(one) for one in inputs))
    tile_paper, tile_author, seed_class, train_mask, prior, target, keep, swap = moved
    swapped = lax.ppermute(swap, "blk", [(i, i ^ 1) for i in range(blocks)])
    local = call(
        functools.partial(first_sum_kernel, authors, rows), parts, [SMEM, SMEM] + [VMEM] * 5
    )(tile_paper, tile_count, keep, swap, seed_class, train_mask, prior)
    both = shape((2, rows + META, columns), bf16)
    pairs = call(pair_kernel, (both,) * (blocks // 2 - 1), [VMEM] * 2)(keep, swapped)
    local, *pairs = lax.optimization_barrier((local, *pairs))
    count = blocks // 2

    def across_pairs(value, even, odd):
        hops = [2 * odd if i % 2 else 2 * even for i in range(blocks)]
        return lax.ppermute(value, "blk", [(i, i ^ hop) for i, hop in enumerate(hops)])

    def to_other(value):
        return lax.ppermute(value, "blk", [(i, i ^ 1) for i in range(blocks)])

    ways = list(zip(pair_order(count, 0), pair_order(count, 1)))
    held = [keep, swapped] + [across_pairs(one, *way) for one, way in zip(pairs, ways[1:])]
    summed = exchange(local)

    author_out = (shape((authors, classes), f32), parts)
    paper_out = (shape((papers, classes), f32), parts, shape((papers, classes), bf16))

    four = count == 4
    places = [(i, None) for i in range(blocks)]
    if four:
        places = [(0, None), (1, None), (2, 0), (2, 1)]
        places += [(3, k) for k in turned(count)]

    def balance(kernel, sent, local, steps, widest):
        here, there, joined = [sent], [], None
        sides = 0
        for step in range(steps):
            moves = []
            if step == 0:
                moves = [(sent, *way) for way in ways[1 : 2 if four else 3]]
            elif step == 1:
                moves = [(joined, *ways[2])] if four else [(sent, *way) for way in ways[3:]]
            moves = [across_pairs(*move) for move in moves]
            others = [] if step == 0 else [sent] if step == 1 else here[len(there) :]
            if four:
                others = [joined] if step == 2 else []
            others = [to_other(one) for one in others]
            if sides:
                summed = narrow_exchange(local, sides, step + 1 == steps and sides == 2)
            else:
                summed = exchange(local)
            summed, *moved = lax.optimization_barrier((summed, *moves, *others))
            here += moved[: len(moves)]
            there += moved[len(moves) :]
            if step + 1 < steps:
                added, size = [kernel], devices
                if step > 0:
                    added = list(here)
                    sides = 2
                    if step > 1 and widest:
                        added += there
                        sides = 1
                    size = sides * lax.axis_size("grp")
                local = call(
                    balance_kernel, shape((size, 1, classes), f32), [VMEM] * (len(added) + 2)
                )(*added, summed, target)
                joined = sent
                if four and step < 2:
                    joined = call(
                        join_kernel, shape((2 * step + 2, *sent.shape), sent.dtype), [VMEM] * len(here)
                    )(*here)
                local, sent, joined, *here = lax.optimization_barrier((local, sent, joined, *here))
        return summed, here + there

    def last_balance(kernel, local):
        for step in range(ITERS):
            summed = exchange(local)
            if step + 1 < ITERS:
                local = call(balance_kernel, parts, [VMEM] * 3)(kernel, summed, target)
        return summed

    for repeat in range(ROUNDS):
        if repeat == 0:
            own, local = call(
                functools.partial(first_author_kernel, rows), author_out, [VMEM] * (3 + len(held))
            )(summed, prior, target, *held)
            left = ITERS - 1
        else:
            own, local = call(
                functools.partial(author_kernel, rows, places),
                author_out,
                [VMEM] * (3 + len(kernels) + len(held)),
            )(summed, prior, target, *kernels, *held)
            left = ITERS
        author_summed, kernels = balance(own, own, local, left, True)
        last = repeat + 1 == ROUNDS
        kernel, local, *half = call(
            functools.partial(paper_kernel, places, rows),
            paper_out[:2] if last else paper_out,
            [SMEM, SMEM, SMEM] + [VMEM] * (5 + len(kernels)),
        )(
            tile_paper, tile_author, tile_count, keep, swap, author_summed, prior, target, *kernels
        )
        if last:
            summed = last_balance(kernel, local)
        else:
            summed, kernels = balance(kernel, half[0], local, ITERS, False)
    return call(
        functools.partial(final_kernel, rows),
        (shape((papers, classes), f32), shape((authors, classes), f32)),
        [VMEM] * 7,
        [
            pltpu.VMEM((papers, classes), f32),
            pltpu.VMEM((authors, classes), f32),
            pltpu.SemaphoreType.DMA((1 + papers // rows,)),
        ],
        (HBM, HBM),
    )(kernel, summed, own, author_summed, target, seed_class, train_mask)


def solution(mesh):
    placed = (
        P(("grp", "blk"), None, None),
        P(("grp", "blk")),
        P(("grp", "blk")),
        P(("grp", "blk")),
        P(("grp", "blk")),
        P(("grp", "blk")),
        P(),
        P(),
    )
    return jax.shard_map(
        on_device,
        mesh=mesh,
        in_specs=placed,
        out_specs=(P(("grp", "blk"), None), P(("grp", "blk"), None)),
        check_vma=False,
    )
```

```python
import functools

import jax
import jax.numpy as jnp
from jax import lax
from jax.experimental import pallas as pl
from jax.experimental.pallas import tpu as pltpu
from jax.sharding import PartitionSpec as P

AT_DEV = 2
ITERS = 4
ROUNDS = 2
LANES = 128
META = 16

keep_share = 0.8

AXES = ("grp", "blk")
VMEM = pl.BlockSpec(memory_space=pltpu.VMEM)
SMEM = pl.BlockSpec(memory_space=pltpu.SMEM)
HBM = pl.BlockSpec(memory_space=pltpu.HBM)


def call(kernel, out_shape, in_specs, scratch_shapes=(), out_specs=None):
    if out_specs is None:
        out_specs = jax.tree.map(lambda _: VMEM, out_shape)
    return pl.pallas_call(
        kernel,
        out_shape=out_shape,
        in_specs=in_specs,
        out_specs=out_specs,
        scratch_shapes=list(scratch_shapes),
        compiler_params=pltpu.CompilerParams(vmem_limit_bytes=48 * 1024 * 1024),
    )


def col_scale(parts_ref, target_ref):
    return target_ref[...] / jnp.sum(parts_ref[...], axis=0)


def row_scale(kernel, scale_cols):
    return 1.0 / jnp.sum(kernel * scale_cols, axis=1, keepdims=True)


def spread(value, parts_ref):
    parts_ref[...] = jnp.broadcast_to(value[None], parts_ref.shape)


def code_lines(seed_class, train_mask, rows):
    code = jnp.where(train_mask[...] == 1, seed_class[...], -1).astype(jnp.float32)
    line = jnp.concatenate([code[i : i + 1] for i in range(code.shape[0])], axis=1)
    papers = line.shape[1]
    wide = jnp.broadcast_to(line, (8, papers))
    lines = []
    for start in range(0, papers, rows):
        lines.append((pltpu.roll(wide, papers - start, 1) if start else wide)[:1, :rows])
    return lines


def meta_line(meta, rows):
    count = -(-rows // LANES)
    return jnp.concatenate([meta[i : i + 1] for i in range(count)], axis=1)[:, :rows]


def code_columns(lines):
    rows = lines[0].shape[1]
    wide = jnp.concatenate(lines, axis=0)
    wide = jnp.pad(wide, ((0, -len(lines) % 8), (0, -rows % LANES)))
    columns = wide.T
    return [columns[:rows, i : i + 1] for i in range(len(lines))]


def code_column(line, classes):
    rows = line.shape[1]
    across = lax.broadcasted_iota(jnp.int32, (rows, rows), 1)
    eye = jnp.where(lax.broadcasted_iota(jnp.int32, (rows, rows), 0) == across, 1.0, 0.0)
    wide = jnp.broadcast_to(line, (LANES, rows)).astype(jnp.bfloat16)
    column = lax.dot_general(
        eye.astype(jnp.bfloat16),
        wide,
        (((1,), (1,)), ((), ())),
        preferred_element_type=jnp.float32,
    )
    return jnp.concatenate([column] * (classes // LANES), axis=1)


def seeds_of(line, classes):
    class_line = lax.broadcasted_iota(jnp.int32, (classes, line.shape[1]), 0)
    return jnp.where(class_line.astype(jnp.float32) == line, 1.0, 0.0).astype(jnp.bfloat16)


def pack_kernel(rows, tile_count, *refs):
    tiles, *refs = refs
    count = 6
    ins, places = refs[:count], refs[count : 2 * count]
    keep, swap, ready, arrived = refs[2 * count :]
    tile_paper, tile_author, seed_class, train_mask = places[:4]
    pairs = keep.shape[0]
    me = lax.axis_index("blk")
    pair, side = lax.div(me, 2), lax.rem(me, 2)
    moves = [
        pltpu.make_async_copy(source, place, ready.at[i])
        for i, (source, place) in enumerate(zip(ins, places))
    ]
    for copy in moves:
        copy.start()
    outs = []
    copies = []
    for way, (out, to) in enumerate(((keep, side), (swap, 1 - side))):
        for k, other in enumerate(pair_order(pairs, to)):
            slot = 2 * lax.bitwise_xor(pair, other) + to
            copy = pltpu.make_async_copy(
                tiles.at[slot], out.at[k, pl.ds(0, rows)], arrived.at[way, k]
            )
            copy.start()
            copies.append(copy)
            outs.append((out, k, slot))
    for copy in moves[:4]:
        copy.wait()
    line = lax.broadcasted_iota(jnp.int32, (META, LANES), 0)
    code_rows = -(-rows // LANES)
    blocks = []
    for codes in code_lines(seed_class, train_mask, rows):
        pad = jnp.full((1, code_rows * LANES - rows), -1.0, jnp.float32)
        codes = jnp.concatenate([codes, pad], axis=1)
        block = jnp.zeros((META, LANES), jnp.float32)
        for i in range(code_rows):
            block = jnp.where(line == i, codes[:, i * LANES : (i + 1) * LANES], block)
        blocks.append(block)
    for out, k, slot in outs:
        paper = tile_paper[slot]
        live = slot < tile_count[0]
        block = blocks[0]
        for i in range(1, len(blocks)):
            block = jnp.where(paper == i, blocks[i], block)
        for author in range(AT_DEV):
            chosen = jnp.where(live & (tile_author[slot] == author), 1.0, 0.0)
            block = jnp.where(line == code_rows + author, chosen, block)
        block = jnp.where(line == code_rows + AT_DEV, paper.astype(jnp.float32), block)
        out[k, rows:, :] = block.astype(jnp.bfloat16)
    for copy in moves[4:] + copies:
        copy.wait()


def pieces(refs):
    return [(ref, i) for ref in refs for i in range(ref.shape[0] if ref.ndim == 3 else 1)]


def piece(ref, i):
    return ref[i] if ref.ndim == 3 else ref[...]


def join_kernel(*refs):
    *ins, out = refs
    for place, one in enumerate(pieces(ins)):
        out[place] = piece(*one)


def pair_kernel(keep, swapped, *outs):
    for k, out in enumerate(outs, 1):
        out[0] = keep[k]
        out[1] = swapped[k]


def pair_order(pairs, side):
    return [0, 1 + side, 2 - side, 3] if pairs == 4 else list(range(pairs))


def turned(pairs):
    return [0, 2, 1, 3] if pairs == 4 else list(range(pairs))


def sources(count):
    me = lax.axis_index("blk")
    pair, side = lax.div(me, 2), lax.rem(me, 2)
    pairs = [2 * lax.bitwise_xor(pair, k) for k in pair_order(count // 2, side)]
    return [other + side for other in pairs] + [other + 1 - side for other in pairs]


def own_tiles(keep, swap, rows):
    pairs = keep.shape[0]
    kept = [keep[k, :rows, :] for k in range(pairs)]
    return kept + [swap[k, :rows, :] for k in turned(pairs)]


def views(refs, places):
    return [refs[i] if place is None else refs[i].at[place] for i, place in places]


def slots_of(keep, swapped, *pairs):
    return [(keep, 0), *((ref, 0) for ref in pairs), (swapped, 0), *((ref, 1) for ref in pairs)]


def first_sum_kernel(
    authors, rows, tile_paper, tile_count, keep, swap, seed_class, train_mask, class_prior, parts
):
    pairs, _, columns = keep.shape
    classes = parts.shape[2]
    slots = sources(2 * pairs)
    tiles = [tile.astype(jnp.float32) for tile in own_tiles(keep, swap, rows)]
    lane = lax.broadcasted_iota(jnp.int32, (rows, classes), 1).astype(jnp.float32)
    total = authors * class_prior[...]
    for paper, code in enumerate(code_columns(code_lines(seed_class, train_mask, rows))):
        weight = jnp.zeros((rows, columns), jnp.float32)
        for slot, tile in zip(slots, tiles):
            chosen = (slot < tile_count[0]) & (tile_paper[slot] == paper)
            weight = weight + jnp.where(chosen, tile, 0.0)
        weight = jnp.sum(weight, axis=1, keepdims=True)
        seeds = jnp.where(code == lane, weight, 0.0)
        total = total + jnp.sum(seeds, axis=0, keepdims=True)
    spread(total, parts)


def next_sum(kernel, summed, class_target, parts):
    scale_rows = row_scale(kernel, col_scale(summed, class_target))
    spread(jnp.sum(scale_rows * kernel, axis=0, keepdims=True), parts)


def first_author_kernel(rows, summed, class_prior, class_target, *rest):
    *held, full, parts = rest
    classes = full.shape[1]
    code_rows = -(-rows // LANES)
    totals = [jnp.zeros((classes, LANES), jnp.float32) for _ in range(AT_DEV)]
    for ref, place in slots_of(*held):
        meta = ref[place, rows:, :].astype(jnp.float32)
        seeds = seeds_of(meta_line(meta, rows), classes)
        parcel = jnp.dot(seeds, ref[place, :rows, :], preferred_element_type=jnp.float32)
        parcel = parcel.astype(jnp.bfloat16).astype(jnp.float32)
        for author in range(AT_DEV):
            chosen = meta[code_rows + author : code_rows + author + 1]
            totals[author] = totals[author] + parcel * chosen
    kernel = jnp.concatenate([total.T for total in totals], axis=0) + class_prior[...]
    full[...] = kernel
    next_sum(kernel, summed, class_target, parts)


def author_kernel(rows, places, summed, class_prior, class_target, *rest):
    *rest, full, parts = rest
    count = 1 + max(i for i, _ in places)
    kernels, held = views(rest, places), slots_of(*rest[count:])
    classes = full.shape[1]
    code_rows = -(-rows // LANES)
    metas = [ref[place, rows:, :].astype(jnp.float32) for ref, place in held]
    at = code_rows + AT_DEV
    papers = [jnp.max(meta[at : at + 1]).astype(jnp.int32) for meta in metas]
    scale_cols = col_scale(summed, class_target)
    codes = code_columns([meta_line(meta, rows) for meta in metas])
    totals = [jnp.zeros((LANES, classes), jnp.float32) for _ in range(AT_DEV)]
    lane = lax.broadcasted_iota(jnp.int32, (rows, classes), 1).astype(jnp.float32)
    for shift, (ref, place) in enumerate(held):
        half = kernels[shift][pl.ds(pl.multiple_of(papers[shift] * rows, rows), rows), :]
        scaled = half.astype(jnp.float32) * scale_cols
        share = scaled * (keep_share / jnp.sum(scaled, axis=1, keepdims=True))
        labels = jnp.where(codes[shift] == lane, share + (1.0 - keep_share), share)
        parcel = lax.dot_general(
            ref[place, :rows, :],
            labels.astype(jnp.bfloat16),
            (((0,), (0,)), ((), ())),
            preferred_element_type=jnp.float32,
        )
        parcel = parcel.astype(jnp.bfloat16).astype(jnp.float32)
        for author in range(AT_DEV):
            at = code_rows + author
            totals[author] = totals[author] + parcel * metas[shift][at : at + 1, :1]
    kernel = jnp.concatenate(totals, axis=0) + class_prior[...]
    full[...] = kernel
    spread(jnp.sum(kernel, axis=0, keepdims=True), parts)


def paper_kernel(
    places, rows, tile_paper, tile_author, tile_count, keep, swap, summed, class_prior,
    class_target, *rest,
):
    kernels, (full, parts, *half) = views(rest, places), rest[1 + max(i for i, _ in places) :]
    columns = keep.shape[2]
    classes = full.shape[1]
    scale_cols = col_scale(summed, class_target)
    slots = sources(len(kernels))
    wide = jnp.concatenate(own_tiles(keep, swap, rows), axis=1)
    labels = []
    for ref, slot in zip(kernels, slots):
        start = pl.multiple_of(tile_author[slot] * columns, columns)
        scaled = ref[pl.ds(start, columns), :] * scale_cols
        share = scaled * (1.0 / jnp.sum(scaled, axis=1, keepdims=True))
        labels.append(share.astype(jnp.bfloat16))
    column = jnp.zeros((1, classes), jnp.float32)
    for paper in range(full.shape[0] // rows):
        chosen = []
        for one, slot in zip(labels, slots):
            mine = (slot < tile_count[0]) & (tile_paper[slot] == paper)
            chosen.append(jnp.where(mine, one, jnp.zeros_like(one)))
        mass = jnp.dot(wide, jnp.concatenate(chosen, axis=0), preferred_element_type=jnp.float32)
        kernel = mass + class_prior[...]
        full[paper * rows : (paper + 1) * rows, :] = kernel
        for out in half:
            out[paper * rows : (paper + 1) * rows, :] = kernel.astype(jnp.bfloat16)
        column = column + jnp.sum(kernel, axis=0, keepdims=True)
    spread(column, parts)


def balance_kernel(*refs):
    *kernels, summed, class_target, parts = refs
    scale_cols = col_scale(summed, class_target)
    total = None
    for one in pieces(kernels):
        kernel = piece(*one).astype(jnp.float32)
        local = jnp.sum(row_scale(kernel, scale_cols) * kernel, axis=0, keepdims=True)
        total = local if total is None else total + local
    spread(total, parts)


def final_kernel(
    rows, kernel_ref, summed, own, author_summed, class_target, seed_class, train_mask,
    out, scores, out_made, scores_made, left,
):
    classes = out.shape[1]
    scaled = own[...] * col_scale(author_summed, class_target)
    scores_made[...] = scaled * (classes / jnp.sum(scaled, axis=1, keepdims=True))
    copies = [pltpu.make_async_copy(scores_made, scores, left.at[0])]
    copies[0].start()
    scale_cols = col_scale(summed, class_target)
    lane = lax.broadcasted_iota(jnp.int32, (rows, classes), 1).astype(jnp.float32)
    for paper, line in enumerate(code_lines(seed_class, train_mask, rows)):
        code = code_column(line, classes)
        part = pl.ds(paper * rows, rows)
        scaled = kernel_ref[part, :] * scale_cols
        share = scaled * (1.0 / jnp.sum(scaled, axis=1, keepdims=True))
        updated = keep_share * share + jnp.where(code == lane, 1.0 - keep_share, 0.0)
        out_made[part, :] = classes * updated
        copies.append(pltpu.make_async_copy(out_made.at[part], out.at[part], left.at[paper + 1]))
        copies[-1].start()
    for copy in copies:
        copy.wait()


def in_hbm(value):
    return pltpu.with_memory_space_constraint(value, pltpu.HBM)


def exchange(parts):
    return lax.all_to_all(parts, AXES, split_axis=0, concat_axis=0, tiled=True)


def narrow_exchange(parts, corners, upwards):
    groups, blocks = lax.axis_size("grp"), lax.axis_size("blk")
    planes = range(groups)
    if not upwards:
        planes = sorted(planes, key=lambda i: abs(2 * i + 1 - groups))
    sets = [[i * blocks + corner for i in planes for corner in one] for one in corners]
    return lax.all_to_all(
        parts, AXES, split_axis=0, concat_axis=0, axis_index_groups=sets, tiled=True
    )


def on_device(
    tile_values,
    tile_paper,
    tile_author,
    tile_count,
    seed_class,
    train_mask,
    class_prior,
    class_target,
):
    f32 = jnp.float32
    bf16 = jnp.bfloat16
    shape = jax.ShapeDtypeStruct
    slots, rows, columns = tile_values.shape
    classes = class_prior.shape[0]
    papers = seed_class.shape[0]
    authors = AT_DEV * columns
    paper_tiles = papers // rows
    devices = lax.axis_size(AXES)
    prior = class_prior.reshape(1, classes)
    target = class_target.reshape(1, classes)
    seed_class = seed_class.reshape(papers // LANES, LANES)
    train_mask = train_mask.reshape(papers // LANES, LANES)
    parts = shape((devices, 1, classes), f32)

    inputs = (
        tile_paper, tile_author, seed_class, train_mask, prior, target,
    )
    places = (SMEM, SMEM, VMEM, VMEM, VMEM, VMEM)
    blocks = lax.axis_size("blk")
    load = shape((blocks // 2, rows + META, columns), bf16)
    moved = call(
        functools.partial(pack_kernel, rows),
        tuple(shape(one.shape, one.dtype) for one in inputs) + (load, load),
        [SMEM, HBM] + [HBM] * len(inputs),
        [pltpu.SemaphoreType.DMA((len(inputs),)), pltpu.SemaphoreType.DMA((2, blocks // 2))],
        places + (VMEM, VMEM),
    )(tile_count, in_hbm(tile_values), *(in_hbm(one) for one in inputs))
    tile_paper, tile_author, seed_class, train_mask, prior, target, keep, swap = moved
    swapped = lax.ppermute(swap, "blk", [(i, i ^ 1) for i in range(blocks)])
    local = call(
        functools.partial(first_sum_kernel, authors, rows), parts, [SMEM, SMEM] + [VMEM] * 5
    )(tile_paper, tile_count, keep, swap, seed_class, train_mask, prior)
    both = shape((2, rows + META, columns), bf16)
    pairs = call(pair_kernel, (both,) * (blocks // 2 - 1), [VMEM] * 2)(keep, swapped)
    local, *pairs = lax.optimization_barrier((local, *pairs))
    count = blocks // 2

    def across_pairs(value, even, odd):
        hops = [2 * odd if i % 2 else 2 * even for i in range(blocks)]
        return lax.ppermute(value, "blk", [(i, i ^ hop) for i, hop in enumerate(hops)])

    def to_other(value):
        return lax.ppermute(value, "blk", [(i, i ^ 1) for i in range(blocks)])

    ways = list(zip(pair_order(count, 0), pair_order(count, 1)))
    held = [keep, swapped] + [across_pairs(one, *way) for one, way in zip(pairs, ways[1:])]
    summed = exchange(local)

    author_out = (shape((authors, classes), f32), parts)
    paper_out = (shape((papers, classes), f32), parts, shape((papers, classes), bf16))

    four = count == 4
    places = [(i, None) for i in range(blocks)]
    if four:
        places = [(0, None), (1, None), (2, 0), (2, 1)]
        places += [(3, k) for k in turned(count)]

    alone = [[i] for i in range(blocks)]
    in_pair = [[i + 1, i] for i in range(0, blocks, 2)]
    in_cross = [[1, 3, 0, 4], [7, 5, 6, 2]]

    def balance(kernel, sent, local, steps, widest):
        here, there, joined = [sent], [], None
        corners = None
        for step in range(steps):
            moves = []
            if step == 0:
                moves = [(sent, *way) for way in ways[1 : 2 if four else 3]]
            elif step == 1:
                moves = [(joined, *ways[2])] if four else [(sent, *way) for way in ways[3:]]
            moves = [across_pairs(*move) for move in moves]
            others = [] if step == 0 else [sent] if step == 1 else here[len(there) :]
            if four:
                others = [joined] if step == 2 else []
            others = [to_other(one) for one in others]
            if corners:
                upwards = step + 1 == steps and corners == in_pair
                summed = narrow_exchange(local, corners, upwards)
            else:
                summed = exchange(local)
            summed, *moved = lax.optimization_barrier((summed, *moves, *others))
            here += moved[: len(moves)]
            there += moved[len(moves) :]
            if step + 1 < steps:
                added, size = [kernel], devices
                if step > 0 or four:
                    added = list(here)
                    corners = in_pair if step > 0 else in_cross
                    if step > 1 and widest:
                        added += there
                        corners = alone
                    size = len(corners[0]) * lax.axis_size("grp")
                local = call(
                    balance_kernel, shape((size, 1, classes), f32), [VMEM] * (len(added) + 2)
                )(*added, summed, target)
                joined = sent
                if four and step < 2:
                    joined = call(
                        join_kernel, shape((2 * step + 2, *sent.shape), sent.dtype), [VMEM] * len(here)
                    )(*here)
                local, sent, joined, *here = lax.optimization_barrier((local, sent, joined, *here))
        return summed, here + there

    def last_balance(kernel, local):
        for step in range(ITERS):
            summed = exchange(local)
            if step + 1 < ITERS:
                local = call(balance_kernel, parts, [VMEM] * 3)(kernel, summed, target)
        return summed

    for repeat in range(ROUNDS):
        if repeat == 0:
            own, local = call(
                functools.partial(first_author_kernel, rows), author_out, [VMEM] * (3 + len(held))
            )(summed, prior, target, *held)
            left = ITERS - 1
        else:
            own, local = call(
                functools.partial(author_kernel, rows, places),
                author_out,
                [VMEM] * (3 + len(kernels) + len(held)),
            )(summed, prior, target, *kernels, *held)
            left = ITERS
        author_summed, kernels = balance(own, own, local, left, True)
        last = repeat + 1 == ROUNDS
        kernel, local, *half = call(
            functools.partial(paper_kernel, places, rows),
            paper_out[:2] if last else paper_out,
            [SMEM, SMEM, SMEM] + [VMEM] * (5 + len(kernels)),
        )(
            tile_paper, tile_author, tile_count, keep, swap, author_summed, prior, target, *kernels
        )
        if last:
            summed = last_balance(kernel, local)
        else:
            summed, kernels = balance(kernel, half[0], local, ITERS, False)
    return call(
        functools.partial(final_kernel, rows),
        (shape((papers, classes), f32), shape((authors, classes), f32)),
        [VMEM] * 7,
        [
            pltpu.VMEM((papers, classes), f32),
            pltpu.VMEM((authors, classes), f32),
            pltpu.SemaphoreType.DMA((1 + papers // rows,)),
        ],
        (HBM, HBM),
    )(kernel, summed, own, author_summed, target, seed_class, train_mask)


def solution(mesh):
    placed = (
        P(("grp", "blk"), None, None),
        P(("grp", "blk")),
        P(("grp", "blk")),
        P(("grp", "blk")),
        P(("grp", "blk")),
        P(("grp", "blk")),
        P(),
        P(),
    )
    return jax.shard_map(
        on_device,
        mesh=mesh,
        in_specs=placed,
        out_specs=(P(("grp", "blk"), None), P(("grp", "blk"), None)),
        check_vma=False,
    )
```

```python
import functools

import jax
import jax.numpy as jnp
from jax import lax
from jax.experimental import pallas as pl
from jax.experimental.pallas import tpu as pltpu
from jax.sharding import PartitionSpec as P

AT_DEV = 2
ITERS = 4
ROUNDS = 2
LANES = 128
META = 16

keep_share = 0.8

AXES = ("grp", "blk")
VMEM = pl.BlockSpec(memory_space=pltpu.VMEM)
SMEM = pl.BlockSpec(memory_space=pltpu.SMEM)
HBM = pl.BlockSpec(memory_space=pltpu.HBM)


def call(kernel, out_shape, in_specs, scratch_shapes=(), out_specs=None):
    if out_specs is None:
        out_specs = jax.tree.map(lambda _: VMEM, out_shape)
    room = 20 if lax.axis_size("blk") <= 8 else 48
    return pl.pallas_call(
        kernel,
        out_shape=out_shape,
        in_specs=in_specs,
        out_specs=out_specs,
        scratch_shapes=list(scratch_shapes),
        compiler_params=pltpu.CompilerParams(vmem_limit_bytes=room * 1024 * 1024),
    )


def col_scale(parts_ref, target_ref):
    return target_ref[...] / jnp.sum(parts_ref[...], axis=0)


def row_scale(kernel, scale_cols):
    return 1.0 / jnp.sum(kernel * scale_cols, axis=1, keepdims=True)


def spread(value, parts_ref):
    parts_ref[...] = jnp.broadcast_to(value[None], parts_ref.shape)


def code_lines(seed_class, train_mask, rows):
    code = jnp.where(train_mask[...] == 1, seed_class[...], -1).astype(jnp.float32)
    line = jnp.concatenate([code[i : i + 1] for i in range(code.shape[0])], axis=1)
    papers = line.shape[1]
    wide = jnp.broadcast_to(line, (8, papers))
    lines = []
    for start in range(0, papers, rows):
        lines.append((pltpu.roll(wide, papers - start, 1) if start else wide)[:1, :rows])
    return lines


def meta_line(meta, rows):
    count = -(-rows // LANES)
    return jnp.concatenate([meta[i : i + 1] for i in range(count)], axis=1)[:, :rows]


def code_columns(lines):
    rows = lines[0].shape[1]
    wide = jnp.concatenate(lines, axis=0)
    wide = jnp.pad(wide, ((0, -len(lines) % 8), (0, -rows % LANES)))
    columns = wide.T
    return [columns[:rows, i : i + 1] for i in range(len(lines))]


def code_column(line, classes):
    rows = line.shape[1]
    across = lax.broadcasted_iota(jnp.int32, (rows, rows), 1)
    eye = jnp.where(lax.broadcasted_iota(jnp.int32, (rows, rows), 0) == across, 1.0, 0.0)
    wide = jnp.broadcast_to(line, (LANES, rows)).astype(jnp.bfloat16)
    column = lax.dot_general(
        eye.astype(jnp.bfloat16),
        wide,
        (((1,), (1,)), ((), ())),
        preferred_element_type=jnp.float32,
    )
    return jnp.concatenate([column] * (classes // LANES), axis=1)


def seeds_of(line, classes):
    class_line = lax.broadcasted_iota(jnp.int32, (classes, line.shape[1]), 0)
    return jnp.where(class_line.astype(jnp.float32) == line, 1.0, 0.0).astype(jnp.bfloat16)


def pack_kernel(rows, tile_count, *refs):
    tiles, *refs = refs
    count = 6
    ins, places = refs[:count], refs[count : 2 * count]
    keep, swap, ready, arrived = refs[2 * count :]
    tile_paper, tile_author, seed_class, train_mask = places[:4]
    pairs = keep.shape[0]
    me = lax.axis_index("blk")
    pair, side = lax.div(me, 2), lax.rem(me, 2)
    moves = [
        pltpu.make_async_copy(source, place, ready.at[i])
        for i, (source, place) in enumerate(zip(ins, places))
    ]
    for copy in moves:
        copy.start()
    outs = []
    copies = []
    for way, (out, to) in enumerate(((keep, side), (swap, 1 - side))):
        for k, other in enumerate(pair_order(pairs, to)):
            slot = 2 * lax.bitwise_xor(pair, other) + to
            copy = pltpu.make_async_copy(
                tiles.at[slot], out.at[k, pl.ds(0, rows)], arrived.at[way, k]
            )
            copy.start()
            copies.append(copy)
            outs.append((out, k, slot))
    for copy in moves[:4]:
        copy.wait()
    line = lax.broadcasted_iota(jnp.int32, (META, LANES), 0)
    code_rows = -(-rows // LANES)
    blocks = []
    for codes in code_lines(seed_class, train_mask, rows):
        pad = jnp.full((1, code_rows * LANES - rows), -1.0, jnp.float32)
        codes = jnp.concatenate([codes, pad], axis=1)
        block = jnp.zeros((META, LANES), jnp.float32)
        for i in range(code_rows):
            block = jnp.where(line == i, codes[:, i * LANES : (i + 1) * LANES], block)
        blocks.append(block)
    for out, k, slot in outs:
        paper = tile_paper[slot]
        live = slot < tile_count[0]
        block = blocks[0]
        for i in range(1, len(blocks)):
            block = jnp.where(paper == i, blocks[i], block)
        for author in range(AT_DEV):
            chosen = jnp.where(live & (tile_author[slot] == author), 1.0, 0.0)
            block = jnp.where(line == code_rows + author, chosen, block)
        block = jnp.where(line == code_rows + AT_DEV, paper.astype(jnp.float32), block)
        out[k, rows:, :] = block.astype(jnp.bfloat16)
    for copy in moves[4:] + copies:
        copy.wait()


def pieces(refs):
    return [(ref, i) for ref in refs for i in range(ref.shape[0] if ref.ndim == 3 else 1)]


def piece(ref, i):
    return ref[i] if ref.ndim == 3 else ref[...]


def join_kernel(*refs):
    *ins, out = refs
    for place, one in enumerate(pieces(ins)):
        out[place] = piece(*one)


def pair_kernel(keep, swapped, *outs):
    for k, out in enumerate(outs, 1):
        out[0] = keep[k]
        out[1] = swapped[k]


def pair_order(pairs, side):
    return [0, 1 + side, 2 - side, 3] if pairs == 4 else list(range(pairs))


def turned(pairs):
    return [0, 2, 1, 3] if pairs == 4 else list(range(pairs))


def sources(count):
    me = lax.axis_index("blk")
    pair, side = lax.div(me, 2), lax.rem(me, 2)
    pairs = [2 * lax.bitwise_xor(pair, k) for k in pair_order(count // 2, side)]
    return [other + side for other in pairs] + [other + 1 - side for other in pairs]


def own_tiles(keep, swap, rows):
    pairs = keep.shape[0]
    kept = [keep[k, :rows, :] for k in range(pairs)]
    return kept + [swap[k, :rows, :] for k in turned(pairs)]


def views(refs, places):
    return [refs[i] if place is None else refs[i].at[place] for i, place in places]


def slots_of(keep, swapped, *pairs):
    return [(keep, 0), *((ref, 0) for ref in pairs), (swapped, 0), *((ref, 1) for ref in pairs)]


def first_sum_kernel(
    authors, rows, tile_paper, tile_count, keep, swap, seed_class, train_mask, class_prior, parts
):
    pairs, _, columns = keep.shape
    classes = parts.shape[2]
    slots = sources(2 * pairs)
    tiles = [tile.astype(jnp.float32) for tile in own_tiles(keep, swap, rows)]
    lane = lax.broadcasted_iota(jnp.int32, (rows, classes), 1).astype(jnp.float32)
    total = authors * class_prior[...]
    for paper, code in enumerate(code_columns(code_lines(seed_class, train_mask, rows))):
        weight = jnp.zeros((rows, columns), jnp.float32)
        for slot, tile in zip(slots, tiles):
            chosen = (slot < tile_count[0]) & (tile_paper[slot] == paper)
            weight = weight + jnp.where(chosen, tile, 0.0)
        weight = jnp.sum(weight, axis=1, keepdims=True)
        seeds = jnp.where(code == lane, weight, 0.0)
        total = total + jnp.sum(seeds, axis=0, keepdims=True)
    spread(total, parts)


def next_sum(kernel, summed, class_target, parts):
    scale_rows = row_scale(kernel, col_scale(summed, class_target))
    spread(jnp.sum(scale_rows * kernel, axis=0, keepdims=True), parts)


def first_author_kernel(rows, summed, class_prior, class_target, *rest):
    *held, full, parts = rest
    classes = full.shape[1]
    code_rows = -(-rows // LANES)
    totals = [jnp.zeros((classes, LANES), jnp.float32) for _ in range(AT_DEV)]
    for ref, place in slots_of(*held):
        meta = ref[place, rows:, :].astype(jnp.float32)
        seeds = seeds_of(meta_line(meta, rows), classes)
        parcel = jnp.dot(seeds, ref[place, :rows, :], preferred_element_type=jnp.float32)
        parcel = parcel.astype(jnp.bfloat16).astype(jnp.float32)
        for author in range(AT_DEV):
            chosen = meta[code_rows + author : code_rows + author + 1]
            totals[author] = totals[author] + parcel * chosen
    kernel = jnp.concatenate([total.T for total in totals], axis=0) + class_prior[...]
    full[...] = kernel
    next_sum(kernel, summed, class_target, parts)


def author_kernel(rows, places, summed, class_prior, class_target, *rest):
    *rest, full, parts = rest
    count = 1 + max(i for i, _ in places)
    kernels, held = views(rest, places), slots_of(*rest[count:])
    classes = full.shape[1]
    code_rows = -(-rows // LANES)
    metas = [ref[place, rows:, :].astype(jnp.float32) for ref, place in held]
    at = code_rows + AT_DEV
    papers = [jnp.max(meta[at : at + 1]).astype(jnp.int32) for meta in metas]
    scale_cols = col_scale(summed, class_target)
    codes = code_columns([meta_line(meta, rows) for meta in metas])
    totals = [jnp.zeros((LANES, classes), jnp.float32) for _ in range(AT_DEV)]
    lane = lax.broadcasted_iota(jnp.int32, (rows, classes), 1).astype(jnp.float32)
    for shift, (ref, place) in enumerate(held):
        half = kernels[shift][pl.ds(pl.multiple_of(papers[shift] * rows, rows), rows), :]
        scaled = half.astype(jnp.float32) * scale_cols
        share = scaled * (keep_share / jnp.sum(scaled, axis=1, keepdims=True))
        labels = jnp.where(codes[shift] == lane, share + (1.0 - keep_share), share)
        parcel = lax.dot_general(
            ref[place, :rows, :],
            labels.astype(jnp.bfloat16),
            (((0,), (0,)), ((), ())),
            preferred_element_type=jnp.float32,
        )
        parcel = parcel.astype(jnp.bfloat16).astype(jnp.float32)
        for author in range(AT_DEV):
            at = code_rows + author
            totals[author] = totals[author] + parcel * metas[shift][at : at + 1, :1]
    kernel = jnp.concatenate(totals, axis=0) + class_prior[...]
    full[...] = kernel
    spread(jnp.sum(kernel, axis=0, keepdims=True), parts)


def paper_kernel(
    places, rows, tile_paper, tile_author, tile_count, keep, swap, summed, class_prior,
    class_target, *rest,
):
    kernels, (full, parts) = views(rest, places), rest[1 + max(i for i, _ in places) :]
    columns = keep.shape[2]
    classes = full.shape[1]
    scale_cols = col_scale(summed, class_target)
    slots = sources(len(kernels))
    wide = jnp.concatenate(own_tiles(keep, swap, rows), axis=1)
    labels = []
    for ref, slot in zip(kernels, slots):
        start = pl.multiple_of(tile_author[slot] * columns, columns)
        scaled = ref[pl.ds(start, columns), :] * scale_cols
        share = scaled * (1.0 / jnp.sum(scaled, axis=1, keepdims=True))
        labels.append(share.astype(jnp.bfloat16))
    column = jnp.zeros((1, classes), jnp.float32)
    for paper in range(full.shape[0] // rows):
        chosen = []
        for one, slot in zip(labels, slots):
            mine = (slot < tile_count[0]) & (tile_paper[slot] == paper)
            chosen.append(jnp.where(mine, one, jnp.zeros_like(one)))
        mass = jnp.dot(wide, jnp.concatenate(chosen, axis=0), preferred_element_type=jnp.float32)
        kernel = mass + class_prior[...]
        full[paper * rows : (paper + 1) * rows, :] = kernel
        column = column + jnp.sum(kernel, axis=0, keepdims=True)
    spread(column, parts)


def balance_kernel(*refs):
    *kernels, summed, class_target, parts = refs
    scale_cols = col_scale(summed, class_target)
    total = None
    for one in pieces(kernels):
        kernel = piece(*one).astype(jnp.float32)
        local = jnp.sum(row_scale(kernel, scale_cols) * kernel, axis=0, keepdims=True)
        total = local if total is None else total + local
    spread(total, parts)


def final_kernel(
    rows, kernel_ref, summed, own, author_summed, class_target, seed_class, train_mask,
    out, scores, out_made, scores_made, left,
):
    classes = out.shape[1]
    scaled = own[...] * col_scale(author_summed, class_target)
    scores_made[...] = scaled * (classes / jnp.sum(scaled, axis=1, keepdims=True))
    copies = [pltpu.make_async_copy(scores_made, scores, left.at[0])]
    copies[0].start()
    scale_cols = col_scale(summed, class_target)
    lane = lax.broadcasted_iota(jnp.int32, (rows, classes), 1).astype(jnp.float32)
    for paper, line in enumerate(code_lines(seed_class, train_mask, rows)):
        code = code_column(line, classes)
        part = pl.ds(paper * rows, rows)
        scaled = kernel_ref[part, :] * scale_cols
        share = scaled * (1.0 / jnp.sum(scaled, axis=1, keepdims=True))
        updated = keep_share * share + jnp.where(code == lane, 1.0 - keep_share, 0.0)
        out_made[part, :] = classes * updated
        copies.append(pltpu.make_async_copy(out_made.at[part], out.at[part], left.at[paper + 1]))
        copies[-1].start()
    for copy in copies:
        copy.wait()


def in_hbm(value):
    return pltpu.with_memory_space_constraint(value, pltpu.HBM)


def exchange(parts):
    return lax.all_to_all(parts, AXES, split_axis=0, concat_axis=0, tiled=True)


def narrow_exchange(parts, sides, upwards):
    groups, blocks = lax.axis_size("grp"), lax.axis_size("blk")
    planes = range(groups)
    if not upwards:
        planes = sorted(planes, key=lambda i: abs(2 * i + 1 - groups))
    sets = [
        [i * blocks + first + side for i in planes for side in reversed(range(sides))]
        for first in range(0, blocks, sides)
    ]
    return lax.all_to_all(
        parts, AXES, split_axis=0, concat_axis=0, axis_index_groups=sets, tiled=True
    )


def on_device(
    tile_values,
    tile_paper,
    tile_author,
    tile_count,
    seed_class,
    train_mask,
    class_prior,
    class_target,
):
    f32 = jnp.float32
    bf16 = jnp.bfloat16
    shape = jax.ShapeDtypeStruct
    slots, rows, columns = tile_values.shape
    classes = class_prior.shape[0]
    papers = seed_class.shape[0]
    authors = AT_DEV * columns
    paper_tiles = papers // rows
    devices = lax.axis_size(AXES)
    prior = class_prior.reshape(1, classes)
    target = class_target.reshape(1, classes)
    seed_class = seed_class.reshape(papers // LANES, LANES)
    train_mask = train_mask.reshape(papers // LANES, LANES)
    parts = shape((devices, 1, classes), f32)

    inputs = (
        tile_paper, tile_author, seed_class, train_mask, prior, target,
    )
    places = (SMEM, SMEM, VMEM, VMEM, VMEM, VMEM)
    blocks = lax.axis_size("blk")
    load = shape((blocks // 2, rows + META, columns), bf16)
    moved = call(
        functools.partial(pack_kernel, rows),
        tuple(shape(one.shape, one.dtype) for one in inputs) + (load, load),
        [SMEM, HBM] + [HBM] * len(inputs),
        [pltpu.SemaphoreType.DMA((len(inputs),)), pltpu.SemaphoreType.DMA((2, blocks // 2))],
        places + (VMEM, VMEM),
    )(tile_count, in_hbm(tile_values), *(in_hbm(one) for one in inputs))
    tile_paper, tile_author, seed_class, train_mask, prior, target, keep, swap = moved
    swapped = lax.ppermute(swap, "blk", [(i, i ^ 1) for i in range(blocks)])
    local = call(
        functools.partial(first_sum_kernel, authors, rows), parts, [SMEM, SMEM] + [VMEM] * 5
    )(tile_paper, tile_count, keep, swap, seed_class, train_mask, prior)
    both = shape((2, rows + META, columns), bf16)
    pairs = call(pair_kernel, (both,) * (blocks // 2 - 1), [VMEM] * 2)(keep, swapped)
    local, *pairs = lax.optimization_barrier((local, *pairs))
    count = blocks // 2

    def across_pairs(value, even, odd):
        hops = [2 * odd if i % 2 else 2 * even for i in range(blocks)]
        return lax.ppermute(value, "blk", [(i, i ^ hop) for i, hop in enumerate(hops)])

    def to_other(value):
        return lax.ppermute(value, "blk", [(i, i ^ 1) for i in range(blocks)])

    ways = list(zip(pair_order(count, 0), pair_order(count, 1)))
    held = [keep, swapped] + [across_pairs(one, *way) for one, way in zip(pairs, ways[1:])]
    summed = exchange(local)

    author_out = (shape((authors, classes), f32), parts)
    paper_out = (shape((papers, classes), f32), parts)

    four = count == 4
    places = [(i, None) for i in range(blocks)]
    if four:
        places = [(0, None), (1, None), (2, 0), (2, 1)]
        places += [(3, k) for k in turned(count)]
    paper_places = [(i, None) for i in range(count)]
    paper_places += [(count, k) if four else (count + k, None) for k in turned(count)]

    def balance(kernel, local, steps, authors):
        sent = kernel
        here, there, joined = [sent], [], None
        full = 1 if authors or not four else 2
        sides = 0
        for step in range(steps):
            moves = []
            if step == 0:
                moves = [(sent, *way) for way in ways[1 : 2 if four else 3]]
            elif step == 1:
                moves = [(sent, *way) for way in ways[3:]]
                if four:
                    moves = [(joined if authors else sent, *ways[2])]
            elif step == full:
                moves = [(here[1], *ways[2])]
            moves = [across_pairs(*move) for move in moves]
            others = [] if step == 0 else [sent] if step == 1 else here[len(there) :]
            if four:
                others = [joined] if step == full + 1 else []
            others = [to_other(one) for one in others]
            if sides:
                summed = narrow_exchange(local, sides, step + 1 == steps and sides == 2)
            else:
                summed = exchange(local)
            summed, *moved = lax.optimization_barrier((summed, *moves, *others))
            here += moved[: len(moves)]
            there += moved[len(moves) :]
            if step + 1 < steps:
                added, size = [kernel], devices
                if step >= full:
                    added = list(here)
                    sides = 2
                    if step > 1 and authors:
                        added += there
                        sides = 1
                    size = sides * lax.axis_size("grp")
                local = call(
                    balance_kernel, shape((size, 1, classes), f32), [VMEM] * (len(added) + 2)
                )(*added, summed, target)
                joined = sent
                if four and (step == full or authors and step == 0):
                    size = 4 if step == full else 2
                    joined = call(
                        join_kernel, shape((size, *sent.shape), sent.dtype), [VMEM] * len(here)
                    )(*here)
                local, sent, joined, *here = lax.optimization_barrier((local, sent, joined, *here))
        return summed, here + there

    def last_balance(kernel, local):
        for step in range(ITERS):
            summed = exchange(local)
            if step + 1 < ITERS:
                local = call(balance_kernel, parts, [VMEM] * 3)(kernel, summed, target)
        return summed

    for repeat in range(ROUNDS):
        if repeat == 0:
            own, local = call(
                functools.partial(first_author_kernel, rows), author_out, [VMEM] * (3 + len(held))
            )(summed, prior, target, *held)
            left = ITERS - 1
        else:
            own, local = call(
                functools.partial(author_kernel, rows, paper_places),
                author_out,
                [VMEM] * (3 + len(kernels) + len(held)),
            )(summed, prior, target, *kernels, *held)
            left = ITERS
        author_summed, kernels = balance(own, local, left, True)
        last = repeat + 1 == ROUNDS
        kernel, local = call(
            functools.partial(paper_kernel, places, rows),
            paper_out,
            [SMEM, SMEM, SMEM] + [VMEM] * (5 + len(kernels)),
        )(
            tile_paper, tile_author, tile_count, keep, swap, author_summed, prior, target, *kernels
        )
        if last:
            summed = last_balance(kernel, local)
        else:
            summed, kernels = balance(kernel, local, ITERS, False)
    return call(
        functools.partial(final_kernel, rows),
        (shape((papers, classes), f32), shape((authors, classes), f32)),
        [VMEM] * 7,
        [
            pltpu.VMEM((papers, classes), f32),
            pltpu.VMEM((authors, classes), f32),
            pltpu.SemaphoreType.DMA((1 + papers // rows,)),
        ],
        (HBM, HBM),
    )(kernel, summed, own, author_summed, target, seed_class, train_mask)


def solution(mesh):
    placed = (
        P(("grp", "blk"), None, None),
        P(("grp", "blk")),
        P(("grp", "blk")),
        P(("grp", "blk")),
        P(("grp", "blk")),
        P(("grp", "blk")),
        P(),
        P(),
    )
    return jax.shard_map(
        on_device,
        mesh=mesh,
        in_specs=placed,
        out_specs=(P(("grp", "blk"), None), P(("grp", "blk"), None)),
        check_vma=False,
    )
```

```python
import functools

import jax
import jax.numpy as jnp
from jax import lax
from jax.experimental import pallas as pl
from jax.experimental.pallas import tpu as pltpu
from jax.sharding import PartitionSpec as P

AT_DEV = 2
ITERS = 4
ROUNDS = 2
LANES = 128
META = 16

keep_share = 0.8

AXES = ("grp", "blk")
VMEM = pl.BlockSpec(memory_space=pltpu.VMEM)
SMEM = pl.BlockSpec(memory_space=pltpu.SMEM)
HBM = pl.BlockSpec(memory_space=pltpu.HBM)


def call(kernel, out_shape, in_specs, scratch_shapes=(), out_specs=None):
    if out_specs is None:
        out_specs = jax.tree.map(lambda _: VMEM, out_shape)
    room = 20 if lax.axis_size("blk") <= 8 else 48
    return pl.pallas_call(
        kernel,
        out_shape=out_shape,
        in_specs=in_specs,
        out_specs=out_specs,
        scratch_shapes=list(scratch_shapes),
        compiler_params=pltpu.CompilerParams(vmem_limit_bytes=room * 1024 * 1024),
    )


def col_scale(parts_ref, target_ref):
    return target_ref[...] / jnp.sum(parts_ref[...], axis=0)


def row_scale(kernel, scale_cols):
    return 1.0 / jnp.sum(kernel * scale_cols, axis=1, keepdims=True)


def spread(value, parts_ref):
    parts_ref[...] = jnp.broadcast_to(value[None], parts_ref.shape)


def code_lines(seed_class, train_mask, rows):
    code = jnp.where(train_mask[...] == 1, seed_class[...], -1).astype(jnp.float32)
    line = jnp.concatenate([code[i : i + 1] for i in range(code.shape[0])], axis=1)
    papers = line.shape[1]
    wide = jnp.broadcast_to(line, (8, papers))
    lines = []
    for start in range(0, papers, rows):
        lines.append((pltpu.roll(wide, papers - start, 1) if start else wide)[:1, :rows])
    return lines


def meta_line(meta, rows):
    count = -(-rows // LANES)
    return jnp.concatenate([meta[i : i + 1] for i in range(count)], axis=1)[:, :rows]


def code_columns(lines):
    rows = lines[0].shape[1]
    wide = jnp.concatenate(lines, axis=0)
    wide = jnp.pad(wide, ((0, -len(lines) % 8), (0, -rows % LANES)))
    columns = wide.T
    return [columns[:rows, i : i + 1] for i in range(len(lines))]


def code_column(line, classes):
    rows = line.shape[1]
    across = lax.broadcasted_iota(jnp.int32, (rows, rows), 1)
    eye = jnp.where(lax.broadcasted_iota(jnp.int32, (rows, rows), 0) == across, 1.0, 0.0)
    wide = jnp.broadcast_to(line, (LANES, rows)).astype(jnp.bfloat16)
    column = lax.dot_general(
        eye.astype(jnp.bfloat16),
        wide,
        (((1,), (1,)), ((), ())),
        preferred_element_type=jnp.float32,
    )
    return jnp.concatenate([column] * (classes // LANES), axis=1)


def seeds_of(line, classes):
    class_line = lax.broadcasted_iota(jnp.int32, (classes, line.shape[1]), 0)
    return jnp.where(class_line.astype(jnp.float32) == line, 1.0, 0.0).astype(jnp.bfloat16)


def pack_kernel(rows, tile_count, *refs):
    tiles, *refs = refs
    count = 6
    ins, places = refs[:count], refs[count : 2 * count]
    keep, swap, ready, arrived = refs[2 * count :]
    tile_paper, tile_author, seed_class, train_mask = places[:4]
    pairs = keep.shape[0]
    me = lax.axis_index("blk")
    pair, side = lax.div(me, 2), lax.rem(me, 2)
    moves = [
        pltpu.make_async_copy(source, place, ready.at[i])
        for i, (source, place) in enumerate(zip(ins, places))
    ]
    for copy in moves:
        copy.start()
    outs = []
    copies = []
    for way, (out, to) in enumerate(((keep, side), (swap, 1 - side))):
        for k, other in enumerate(pair_order(pairs, to)):
            slot = 2 * lax.bitwise_xor(pair, other) + to
            copy = pltpu.make_async_copy(
                tiles.at[slot], out.at[k, pl.ds(0, rows)], arrived.at[way, k]
            )
            copy.start()
            copies.append(copy)
            outs.append((out, k, slot))
    for copy in moves[:4]:
        copy.wait()
    line = lax.broadcasted_iota(jnp.int32, (META, LANES), 0)
    code_rows = -(-rows // LANES)
    blocks = []
    for codes in code_lines(seed_class, train_mask, rows):
        pad = jnp.full((1, code_rows * LANES - rows), -1.0, jnp.float32)
        codes = jnp.concatenate([codes, pad], axis=1)
        block = jnp.zeros((META, LANES), jnp.float32)
        for i in range(code_rows):
            block = jnp.where(line == i, codes[:, i * LANES : (i + 1) * LANES], block)
        blocks.append(block)
    for out, k, slot in outs:
        paper = tile_paper[slot]
        live = slot < tile_count[0]
        block = blocks[0]
        for i in range(1, len(blocks)):
            block = jnp.where(paper == i, blocks[i], block)
        for author in range(AT_DEV):
            chosen = jnp.where(live & (tile_author[slot] == author), 1.0, 0.0)
            block = jnp.where(line == code_rows + author, chosen, block)
        block = jnp.where(line == code_rows + AT_DEV, paper.astype(jnp.float32), block)
        out[k, rows:, :] = block.astype(jnp.bfloat16)
    for copy in moves[4:] + copies:
        copy.wait()


def pieces(refs):
    return [(ref, i) for ref in refs for i in range(ref.shape[0] if ref.ndim == 3 else 1)]


def piece(ref, i):
    return ref[i] if ref.ndim == 3 else ref[...]


def join_kernel(*refs):
    *ins, out = refs
    for place, one in enumerate(pieces(ins)):
        out[place] = piece(*one)


def pair_kernel(keep, swapped, *outs):
    for k, out in enumerate(outs, 1):
        out[0] = keep[k]
        out[1] = swapped[k]


def pair_order(pairs, side):
    return [0, 1 + side, 2 - side, 3] if pairs == 4 else list(range(pairs))


def turned(pairs):
    return [0, 2, 1, 3] if pairs == 4 else list(range(pairs))


def sources(count):
    me = lax.axis_index("blk")
    pair, side = lax.div(me, 2), lax.rem(me, 2)
    pairs = [2 * lax.bitwise_xor(pair, k) for k in pair_order(count // 2, side)]
    return [other + side for other in pairs] + [other + 1 - side for other in pairs]


def own_tiles(keep, swap, rows):
    pairs = keep.shape[0]
    kept = [keep[k, :rows, :] for k in range(pairs)]
    return kept + [swap[k, :rows, :] for k in turned(pairs)]


def views(refs, places):
    return [refs[i] if place is None else refs[i].at[place] for i, place in places]


def slots_of(keep, swapped, *pairs):
    return [(keep, 0), *((ref, 0) for ref in pairs), (swapped, 0), *((ref, 1) for ref in pairs)]


def first_sum_kernel(
    authors, rows, tile_paper, tile_count, keep, swap, seed_class, train_mask, class_prior, parts
):
    pairs, _, columns = keep.shape
    classes = parts.shape[2]
    slots = sources(2 * pairs)
    tiles = [tile.astype(jnp.float32) for tile in own_tiles(keep, swap, rows)]
    lane = lax.broadcasted_iota(jnp.int32, (rows, classes), 1).astype(jnp.float32)
    total = authors * class_prior[...]
    for paper, code in enumerate(code_columns(code_lines(seed_class, train_mask, rows))):
        weight = jnp.zeros((rows, columns), jnp.float32)
        for slot, tile in zip(slots, tiles):
            chosen = (slot < tile_count[0]) & (tile_paper[slot] == paper)
            weight = weight + jnp.where(chosen, tile, 0.0)
        weight = jnp.sum(weight, axis=1, keepdims=True)
        seeds = jnp.where(code == lane, weight, 0.0)
        total = total + jnp.sum(seeds, axis=0, keepdims=True)
    spread(total, parts)


def next_sum(kernel, summed, class_target, parts):
    scale_rows = row_scale(kernel, col_scale(summed, class_target))
    spread(jnp.sum(scale_rows * kernel, axis=0, keepdims=True), parts)


def first_author_kernel(rows, summed, class_prior, class_target, *rest):
    *held, full, parts = rest
    classes = full.shape[1]
    code_rows = -(-rows // LANES)
    totals = [jnp.zeros((classes, LANES), jnp.float32) for _ in range(AT_DEV)]
    for ref, place in slots_of(*held):
        meta = ref[place, rows:, :].astype(jnp.float32)
        seeds = seeds_of(meta_line(meta, rows), classes)
        parcel = jnp.dot(seeds, ref[place, :rows, :], preferred_element_type=jnp.float32)
        parcel = parcel.astype(jnp.bfloat16).astype(jnp.float32)
        for author in range(AT_DEV):
            chosen = meta[code_rows + author : code_rows + author + 1]
            totals[author] = totals[author] + parcel * chosen
    kernel = jnp.concatenate([total.T for total in totals], axis=0) + class_prior[...]
    full[...] = kernel
    next_sum(kernel, summed, class_target, parts)


def author_kernel(rows, places, summed, class_prior, class_target, *rest):
    *rest, full, parts = rest
    count = 1 + max(i for i, _ in places)
    kernels, held = views(rest, places), slots_of(*rest[count:])
    classes = full.shape[1]
    code_rows = -(-rows // LANES)
    metas = [ref[place, rows:, :].astype(jnp.float32) for ref, place in held]
    at = code_rows + AT_DEV
    papers = [jnp.max(meta[at : at + 1]).astype(jnp.int32) for meta in metas]
    scale_cols = col_scale(summed, class_target)
    codes = code_columns([meta_line(meta, rows) for meta in metas])
    totals = [jnp.zeros((LANES, classes), jnp.float32) for _ in range(AT_DEV)]
    lane = lax.broadcasted_iota(jnp.int32, (rows, classes), 1).astype(jnp.float32)
    for shift, (ref, place) in enumerate(held):
        half = kernels[shift][pl.ds(pl.multiple_of(papers[shift] * rows, rows), rows), :]
        scaled = half.astype(jnp.float32) * scale_cols
        share = scaled * (keep_share / jnp.sum(scaled, axis=1, keepdims=True))
        labels = jnp.where(codes[shift] == lane, share + (1.0 - keep_share), share)
        parcel = lax.dot_general(
            ref[place, :rows, :],
            labels.astype(jnp.bfloat16),
            (((0,), (0,)), ((), ())),
            preferred_element_type=jnp.float32,
        )
        parcel = parcel.astype(jnp.bfloat16).astype(jnp.float32)
        for author in range(AT_DEV):
            at = code_rows + author
            totals[author] = totals[author] + parcel * metas[shift][at : at + 1, :1]
    kernel = jnp.concatenate(totals, axis=0) + class_prior[...]
    full[...] = kernel
    spread(jnp.sum(kernel, axis=0, keepdims=True), parts)


def paper_kernel(
    places, rows, tile_paper, tile_author, tile_count, keep, swap, summed, class_prior,
    class_target, *rest,
):
    kernels, (full, parts, *half) = views(rest, places), rest[1 + max(i for i, _ in places) :]
    columns = keep.shape[2]
    classes = full.shape[1]
    scale_cols = col_scale(summed, class_target)
    slots = sources(len(kernels))
    wide = jnp.concatenate(own_tiles(keep, swap, rows), axis=1)
    labels = []
    for ref, slot in zip(kernels, slots):
        start = pl.multiple_of(tile_author[slot] * columns, columns)
        scaled = ref[pl.ds(start, columns), :] * scale_cols
        share = scaled * (1.0 / jnp.sum(scaled, axis=1, keepdims=True))
        labels.append(share.astype(jnp.bfloat16))
    column = jnp.zeros((1, classes), jnp.float32)
    for paper in range(full.shape[0] // rows):
        chosen = []
        for one, slot in zip(labels, slots):
            mine = (slot < tile_count[0]) & (tile_paper[slot] == paper)
            chosen.append(jnp.where(mine, one, jnp.zeros_like(one)))
        mass = jnp.dot(wide, jnp.concatenate(chosen, axis=0), preferred_element_type=jnp.float32)
        kernel = mass + class_prior[...]
        full[paper * rows : (paper + 1) * rows, :] = kernel
        for out in half:
            out[paper * rows : (paper + 1) * rows, :] = kernel.astype(jnp.bfloat16)
        column = column + jnp.sum(kernel, axis=0, keepdims=True)
    spread(column, parts)


def balance_kernel(*refs):
    *kernels, summed, class_target, parts = refs
    scale_cols = col_scale(summed, class_target)
    total = None
    for one in pieces(kernels):
        kernel = piece(*one).astype(jnp.float32)
        local = jnp.sum(row_scale(kernel, scale_cols) * kernel, axis=0, keepdims=True)
        total = local if total is None else total + local
    spread(total, parts)


def final_kernel(
    rows, kernel_ref, summed, own, author_summed, class_target, seed_class, train_mask,
    out, scores, out_made, scores_made, left,
):
    classes = out.shape[1]
    scaled = own[...] * col_scale(author_summed, class_target)
    scores_made[...] = scaled * (classes / jnp.sum(scaled, axis=1, keepdims=True))
    copies = [pltpu.make_async_copy(scores_made, scores, left.at[0])]
    copies[0].start()
    scale_cols = col_scale(summed, class_target)
    lane = lax.broadcasted_iota(jnp.int32, (rows, classes), 1).astype(jnp.float32)
    for paper, line in enumerate(code_lines(seed_class, train_mask, rows)):
        code = code_column(line, classes)
        part = pl.ds(paper * rows, rows)
        scaled = kernel_ref[part, :] * scale_cols
        share = scaled * (1.0 / jnp.sum(scaled, axis=1, keepdims=True))
        updated = keep_share * share + jnp.where(code == lane, 1.0 - keep_share, 0.0)
        out_made[part, :] = classes * updated
        copies.append(pltpu.make_async_copy(out_made.at[part], out.at[part], left.at[paper + 1]))
        copies[-1].start()
    for copy in copies:
        copy.wait()


def in_hbm(value):
    return pltpu.with_memory_space_constraint(value, pltpu.HBM)


def exchange(parts):
    return lax.all_to_all(parts, AXES, split_axis=0, concat_axis=0, tiled=True)


def narrow_exchange(parts, corners, upwards):
    groups, blocks = lax.axis_size("grp"), lax.axis_size("blk")
    planes = range(groups)
    if not upwards:
        planes = sorted(planes, key=lambda i: abs(2 * i + 1 - groups))
    sets = [[i * blocks + corner for i in planes for corner in one] for one in corners]
    return lax.all_to_all(
        parts, AXES, split_axis=0, concat_axis=0, axis_index_groups=sets, tiled=True
    )


def on_device(
    tile_values,
    tile_paper,
    tile_author,
    tile_count,
    seed_class,
    train_mask,
    class_prior,
    class_target,
):
    f32 = jnp.float32
    bf16 = jnp.bfloat16
    shape = jax.ShapeDtypeStruct
    slots, rows, columns = tile_values.shape
    classes = class_prior.shape[0]
    papers = seed_class.shape[0]
    authors = AT_DEV * columns
    paper_tiles = papers // rows
    devices = lax.axis_size(AXES)
    prior = class_prior.reshape(1, classes)
    target = class_target.reshape(1, classes)
    seed_class = seed_class.reshape(papers // LANES, LANES)
    train_mask = train_mask.reshape(papers // LANES, LANES)
    parts = shape((devices, 1, classes), f32)

    inputs = (
        tile_paper, tile_author, seed_class, train_mask, prior, target,
    )
    places = (SMEM, SMEM, VMEM, VMEM, VMEM, VMEM)
    blocks = lax.axis_size("blk")
    load = shape((blocks // 2, rows + META, columns), bf16)
    moved = call(
        functools.partial(pack_kernel, rows),
        tuple(shape(one.shape, one.dtype) for one in inputs) + (load, load),
        [SMEM, HBM] + [HBM] * len(inputs),
        [pltpu.SemaphoreType.DMA((len(inputs),)), pltpu.SemaphoreType.DMA((2, blocks // 2))],
        places + (VMEM, VMEM),
    )(tile_count, in_hbm(tile_values), *(in_hbm(one) for one in inputs))
    tile_paper, tile_author, seed_class, train_mask, prior, target, keep, swap = moved
    swapped = lax.ppermute(swap, "blk", [(i, i ^ 1) for i in range(blocks)])
    local = call(
        functools.partial(first_sum_kernel, authors, rows), parts, [SMEM, SMEM] + [VMEM] * 5
    )(tile_paper, tile_count, keep, swap, seed_class, train_mask, prior)
    both = shape((2, rows + META, columns), bf16)
    pairs = call(pair_kernel, (both,) * (blocks // 2 - 1), [VMEM] * 2)(keep, swapped)
    local, *pairs = lax.optimization_barrier((local, *pairs))
    count = blocks // 2

    def across_pairs(value, even, odd):
        hops = [2 * odd if i % 2 else 2 * even for i in range(blocks)]
        return lax.ppermute(value, "blk", [(i, i ^ hop) for i, hop in enumerate(hops)])

    def to_other(value):
        return lax.ppermute(value, "blk", [(i, i ^ 1) for i in range(blocks)])

    ways = list(zip(pair_order(count, 0), pair_order(count, 1)))
    held = [keep, swapped] + [across_pairs(one, *way) for one, way in zip(pairs, ways[1:])]
    summed = exchange(local)

    author_out = (shape((authors, classes), f32), parts)
    paper_out = (shape((papers, classes), f32), parts, shape((papers, classes), bf16))

    four = count == 4
    places = [(i, None) for i in range(blocks)]
    if four:
        places = [(0, None), (1, None), (2, 0), (2, 1)]
        places += [(3, k) for k in turned(count)]

    alone = [[i] for i in range(blocks)]
    in_pair = [[i + 1, i] for i in range(0, blocks, 2)]
    in_cross = [[1, 3, 0, 4], [7, 5, 6, 2]]

    def balance(kernel, sent, local, steps, widest):
        here, there, joined = [sent], [], None
        corners = None
        for step in range(steps):
            moves = []
            if step == 0:
                moves = [(sent, *way) for way in ways[1 : 2 if four else 3]]
            elif step == 1:
                moves = [(joined, *ways[2])] if four else [(sent, *way) for way in ways[3:]]
            moves = [across_pairs(*move) for move in moves]
            others = [] if step == 0 else [sent] if step == 1 else here[len(there) :]
            if four:
                others = [joined] if step == 2 else []
            others = [to_other(one) for one in others]
            if corners:
                upwards = step + 1 == steps and corners == in_pair
                summed = narrow_exchange(local, corners, upwards)
            else:
                summed = exchange(local)
            summed, *moved = lax.optimization_barrier((summed, *moves, *others))
            here += moved[: len(moves)]
            there += moved[len(moves) :]
            if step + 1 < steps:
                added, size = [kernel], devices
                if step > 0 or four and widest:
                    added = list(here)
                    corners = in_pair if step > 0 else in_cross
                    if step > 1 and widest:
                        added += there
                        corners = alone
                    size = len(corners[0]) * lax.axis_size("grp")
                local = call(
                    balance_kernel, shape((size, 1, classes), f32), [VMEM] * (len(added) + 2)
                )(*added, summed, target)
                joined = sent
                if four and step < 2:
                    joined = call(
                        join_kernel, shape((2 * step + 2, *sent.shape), sent.dtype), [VMEM] * len(here)
                    )(*here)
                local, sent, joined, *here = lax.optimization_barrier((local, sent, joined, *here))
        return summed, here + there

    def last_balance(kernel, local):
        for step in range(ITERS):
            summed = exchange(local)
            if step + 1 < ITERS:
                local = call(balance_kernel, parts, [VMEM] * 3)(kernel, summed, target)
        return summed

    for repeat in range(ROUNDS):
        if repeat == 0:
            own, local = call(
                functools.partial(first_author_kernel, rows), author_out, [VMEM] * (3 + len(held))
            )(summed, prior, target, *held)
            left = ITERS - 1
        else:
            own, local = call(
                functools.partial(author_kernel, rows, places),
                author_out,
                [VMEM] * (3 + len(kernels) + len(held)),
            )(summed, prior, target, *kernels, *held)
            left = ITERS
        author_summed, kernels = balance(own, own, local, left, True)
        last = repeat + 1 == ROUNDS
        kernel, local, *half = call(
            functools.partial(paper_kernel, places, rows),
            paper_out[:2] if last else paper_out,
            [SMEM, SMEM, SMEM] + [VMEM] * (5 + len(kernels)),
        )(
            tile_paper, tile_author, tile_count, keep, swap, author_summed, prior, target, *kernels
        )
        if last:
            summed = last_balance(kernel, local)
        else:
            summed, kernels = balance(kernel, half[0], local, ITERS, False)
    return call(
        functools.partial(final_kernel, rows),
        (shape((papers, classes), f32), shape((authors, classes), f32)),
        [VMEM] * 7,
        [
            pltpu.VMEM((papers, classes), f32),
            pltpu.VMEM((authors, classes), f32),
            pltpu.SemaphoreType.DMA((1 + papers // rows,)),
        ],
        (HBM, HBM),
    )(kernel, summed, own, author_summed, target, seed_class, train_mask)


def solution(mesh):
    placed = (
        P(("grp", "blk"), None, None),
        P(("grp", "blk")),
        P(("grp", "blk")),
        P(("grp", "blk")),
        P(("grp", "blk")),
        P(("grp", "blk")),
        P(),
        P(),
    )
    return jax.shard_map(
        on_device,
        mesh=mesh,
        in_specs=placed,
        out_specs=(P(("grp", "blk"), None), P(("grp", "blk"), None)),
        check_vma=False,
    )
```

```python
import functools

import jax
import jax.numpy as jnp
from jax import lax
from jax.experimental import pallas as pl
from jax.experimental.pallas import tpu as pltpu
from jax.sharding import PartitionSpec as P

AT_DEV = 2
ITERS = 4
ROUNDS = 2
LANES = 128
META = 16

keep_share = 0.8

AXES = ("grp", "blk")
VMEM = pl.BlockSpec(memory_space=pltpu.VMEM)
SMEM = pl.BlockSpec(memory_space=pltpu.SMEM)
HBM = pl.BlockSpec(memory_space=pltpu.HBM)


def call(kernel, out_shape, in_specs, scratch_shapes=(), out_specs=None):
    if out_specs is None:
        out_specs = jax.tree.map(lambda _: VMEM, out_shape)
    return pl.pallas_call(
        kernel,
        out_shape=out_shape,
        in_specs=in_specs,
        out_specs=out_specs,
        scratch_shapes=list(scratch_shapes),
        compiler_params=pltpu.CompilerParams(vmem_limit_bytes=48 * 1024 * 1024),
    )


def col_scale(parts_ref, target_ref):
    return target_ref[...] / jnp.sum(parts_ref[...], axis=0)


def row_scale(kernel, scale_cols):
    return 1.0 / jnp.sum(kernel * scale_cols, axis=1, keepdims=True)


def spread(value, parts_ref):
    parts_ref[...] = jnp.broadcast_to(value[None], parts_ref.shape)


def code_lines(seed_class, train_mask, rows):
    code = jnp.where(train_mask[...] == 1, seed_class[...], -1).astype(jnp.float32)
    line = jnp.concatenate([code[i : i + 1] for i in range(code.shape[0])], axis=1)
    papers = line.shape[1]
    wide = jnp.broadcast_to(line, (8, papers))
    lines = []
    for start in range(0, papers, rows):
        lines.append((pltpu.roll(wide, papers - start, 1) if start else wide)[:1, :rows])
    return lines


def meta_line(meta, rows):
    count = -(-rows // LANES)
    return jnp.concatenate([meta[i : i + 1] for i in range(count)], axis=1)[:, :rows]


def code_columns(lines):
    rows = lines[0].shape[1]
    wide = jnp.concatenate(lines, axis=0)
    wide = jnp.pad(wide, ((0, -len(lines) % 8), (0, -rows % LANES)))
    columns = wide.T
    return [columns[:rows, i : i + 1] for i in range(len(lines))]


def code_column(line, classes):
    rows = line.shape[1]
    across = lax.broadcasted_iota(jnp.int32, (rows, rows), 1)
    eye = jnp.where(lax.broadcasted_iota(jnp.int32, (rows, rows), 0) == across, 1.0, 0.0)
    wide = jnp.broadcast_to(line, (LANES, rows)).astype(jnp.bfloat16)
    column = lax.dot_general(
        eye.astype(jnp.bfloat16),
        wide,
        (((1,), (1,)), ((), ())),
        preferred_element_type=jnp.float32,
    )
    return jnp.concatenate([column] * (classes // LANES), axis=1)


def seeds_of(line, classes):
    class_line = lax.broadcasted_iota(jnp.int32, (classes, line.shape[1]), 0)
    return jnp.where(class_line.astype(jnp.float32) == line, 1.0, 0.0).astype(jnp.bfloat16)


def pack_kernel(rows, tile_count, *refs):
    tiles, *refs = refs
    count = 6
    ins, places = refs[:count], refs[count : 2 * count]
    keep, swap, ready, arrived = refs[2 * count :]
    tile_paper, tile_author, seed_class, train_mask = places[:4]
    pairs = keep.shape[0]
    me = lax.axis_index("blk")
    pair, side = lax.div(me, 2), lax.rem(me, 2)
    moves = [
        pltpu.make_async_copy(source, place, ready.at[i])
        for i, (source, place) in enumerate(zip(ins, places))
    ]
    for copy in moves:
        copy.start()
    outs = []
    copies = []
    for way, (out, to) in enumerate(((keep, side), (swap, 1 - side))):
        for k, other in enumerate(pair_order(pairs, to)):
            slot = 2 * lax.bitwise_xor(pair, other) + to
            copy = pltpu.make_async_copy(
                tiles.at[slot], out.at[k, pl.ds(0, rows)], arrived.at[way, k]
            )
            copy.start()
            copies.append(copy)
            outs.append((out, k, slot))
    for copy in moves[:4]:
        copy.wait()
    line = lax.broadcasted_iota(jnp.int32, (META, LANES), 0)
    code_rows = -(-rows // LANES)
    blocks = []
    for codes in code_lines(seed_class, train_mask, rows):
        pad = jnp.full((1, code_rows * LANES - rows), -1.0, jnp.float32)
        codes = jnp.concatenate([codes, pad], axis=1)
        block = jnp.zeros((META, LANES), jnp.float32)
        for i in range(code_rows):
            block = jnp.where(line == i, codes[:, i * LANES : (i + 1) * LANES], block)
        blocks.append(block)
    for out, k, slot in outs:
        paper = tile_paper[slot]
        live = slot < tile_count[0]
        block = blocks[0]
        for i in range(1, len(blocks)):
            block = jnp.where(paper == i, blocks[i], block)
        for author in range(AT_DEV):
            chosen = jnp.where(live & (tile_author[slot] == author), 1.0, 0.0)
            block = jnp.where(line == code_rows + author, chosen, block)
        block = jnp.where(line == code_rows + AT_DEV, paper.astype(jnp.float32), block)
        out[k, rows:, :] = block.astype(jnp.bfloat16)
    for copy in moves[4:] + copies:
        copy.wait()


def pieces(refs):
    return [(ref, i) for ref in refs for i in range(ref.shape[0] if ref.ndim == 3 else 1)]


def piece(ref, i):
    return ref[i] if ref.ndim == 3 else ref[...]


def join_kernel(*refs):
    *ins, out = refs
    for place, one in enumerate(pieces(ins)):
        out[place] = piece(*one)


def pair_kernel(keep, swapped, *outs):
    for k, out in enumerate(outs, 1):
        out[0] = keep[k]
        out[1] = swapped[k]


def pair_order(pairs, side):
    return [0, 1 + side, 2 - side, 3] if pairs == 4 else list(range(pairs))


def turned(pairs):
    return [0, 2, 1, 3] if pairs == 4 else list(range(pairs))


def sources(count):
    me = lax.axis_index("blk")
    pair, side = lax.div(me, 2), lax.rem(me, 2)
    pairs = [2 * lax.bitwise_xor(pair, k) for k in pair_order(count // 2, side)]
    return [other + side for other in pairs] + [other + 1 - side for other in pairs]


def own_tiles(keep, swap, rows):
    pairs = keep.shape[0]
    kept = [keep[k, :rows, :] for k in range(pairs)]
    return kept + [swap[k, :rows, :] for k in turned(pairs)]


def views(refs, places):
    return [refs[i] if place is None else refs[i].at[place] for i, place in places]


def slots_of(keep, swapped, *pairs):
    return [(keep, 0), *((ref, 0) for ref in pairs), (swapped, 0), *((ref, 1) for ref in pairs)]


def first_sum_kernel(
    authors, rows, tile_paper, tile_count, keep, swap, seed_class, train_mask, class_prior, parts
):
    pairs, _, columns = keep.shape
    classes = parts.shape[2]
    slots = sources(2 * pairs)
    tiles = [tile.astype(jnp.float32) for tile in own_tiles(keep, swap, rows)]
    lane = lax.broadcasted_iota(jnp.int32, (rows, classes), 1).astype(jnp.float32)
    total = authors * class_prior[...]
    for paper, code in enumerate(code_columns(code_lines(seed_class, train_mask, rows))):
        weight = jnp.zeros((rows, columns), jnp.float32)
        for slot, tile in zip(slots, tiles):
            chosen = (slot < tile_count[0]) & (tile_paper[slot] == paper)
            weight = weight + jnp.where(chosen, tile, 0.0)
        weight = jnp.sum(weight, axis=1, keepdims=True)
        seeds = jnp.where(code == lane, weight, 0.0)
        total = total + jnp.sum(seeds, axis=0, keepdims=True)
    spread(total, parts)


def next_sum(kernel, summed, class_target, parts):
    scale_rows = row_scale(kernel, col_scale(summed, class_target))
    spread(jnp.sum(scale_rows * kernel, axis=0, keepdims=True), parts)


def first_author_kernel(rows, summed, class_prior, class_target, *rest):
    *held, full, parts = rest
    classes = full.shape[1]
    code_rows = -(-rows // LANES)
    totals = [jnp.zeros((classes, LANES), jnp.float32) for _ in range(AT_DEV)]
    for ref, place in slots_of(*held):
        meta = ref[place, rows:, :].astype(jnp.float32)
        seeds = seeds_of(meta_line(meta, rows), classes)
        parcel = jnp.dot(seeds, ref[place, :rows, :], preferred_element_type=jnp.float32)
        parcel = parcel.astype(jnp.bfloat16).astype(jnp.float32)
        for author in range(AT_DEV):
            chosen = meta[code_rows + author : code_rows + author + 1]
            totals[author] = totals[author] + parcel * chosen
    kernel = jnp.concatenate([total.T for total in totals], axis=0) + class_prior[...]
    full[...] = kernel
    next_sum(kernel, summed, class_target, parts)


def author_kernel(rows, places, summed, class_prior, class_target, *rest):
    *rest, full, parts = rest
    count = 1 + max(i for i, _ in places)
    kernels, held = views(rest, places), slots_of(*rest[count:])
    classes = full.shape[1]
    code_rows = -(-rows // LANES)
    metas = [ref[place, rows:, :].astype(jnp.float32) for ref, place in held]
    at = code_rows + AT_DEV
    papers = [jnp.max(meta[at : at + 1]).astype(jnp.int32) for meta in metas]
    scale_cols = col_scale(summed, class_target)
    codes = code_columns([meta_line(meta, rows) for meta in metas])
    totals = [jnp.zeros((LANES, classes), jnp.float32) for _ in range(AT_DEV)]
    lane = lax.broadcasted_iota(jnp.int32, (rows, classes), 1).astype(jnp.float32)
    for shift, (ref, place) in enumerate(held):
        half = kernels[shift][pl.ds(pl.multiple_of(papers[shift] * rows, rows), rows), :]
        scaled = half.astype(jnp.float32) * scale_cols
        share = scaled * (keep_share / jnp.sum(scaled, axis=1, keepdims=True))
        labels = jnp.where(codes[shift] == lane, share + (1.0 - keep_share), share)
        parcel = lax.dot_general(
            ref[place, :rows, :],
            labels.astype(jnp.bfloat16),
            (((0,), (0,)), ((), ())),
            preferred_element_type=jnp.float32,
        )
        parcel = parcel.astype(jnp.bfloat16).astype(jnp.float32)
        for author in range(AT_DEV):
            at = code_rows + author
            totals[author] = totals[author] + parcel * metas[shift][at : at + 1, :1]
    kernel = jnp.concatenate(totals, axis=0) + class_prior[...]
    full[...] = kernel
    spread(jnp.sum(kernel, axis=0, keepdims=True), parts)


def paper_kernel(
    places, rows, tile_paper, tile_author, tile_count, keep, swap, summed, class_prior,
    class_target, *rest,
):
    kernels, (full, parts, *half) = views(rest, places), rest[1 + max(i for i, _ in places) :]
    columns = keep.shape[2]
    classes = full.shape[1]
    scale_cols = col_scale(summed, class_target)
    slots = sources(len(kernels))
    wide = jnp.concatenate(own_tiles(keep, swap, rows), axis=1)
    labels = []
    for ref, slot in zip(kernels, slots):
        start = pl.multiple_of(tile_author[slot] * columns, columns)
        scaled = ref[pl.ds(start, columns), :] * scale_cols
        share = scaled * (1.0 / jnp.sum(scaled, axis=1, keepdims=True))
        labels.append(share.astype(jnp.bfloat16))
    column = jnp.zeros((1, classes), jnp.float32)
    for paper in range(full.shape[0] // rows):
        chosen = []
        for one, slot in zip(labels, slots):
            mine = (slot < tile_count[0]) & (tile_paper[slot] == paper)
            chosen.append(jnp.where(mine, one, jnp.zeros_like(one)))
        mass = jnp.dot(wide, jnp.concatenate(chosen, axis=0), preferred_element_type=jnp.float32)
        kernel = mass + class_prior[...]
        full[paper * rows : (paper + 1) * rows, :] = kernel
        for out in half:
            out[paper * rows : (paper + 1) * rows, :] = kernel.astype(jnp.bfloat16)
        column = column + jnp.sum(kernel, axis=0, keepdims=True)
    spread(column, parts)


def balance_kernel(*refs):
    *kernels, summed, class_target, parts = refs
    scale_cols = col_scale(summed, class_target)
    total = None
    for one in pieces(kernels):
        kernel = piece(*one).astype(jnp.float32)
        local = jnp.sum(row_scale(kernel, scale_cols) * kernel, axis=0, keepdims=True)
        total = local if total is None else total + local
    spread(total, parts)


def final_kernel(
    rows, kernel_ref, summed, own, author_summed, class_target, seed_class, train_mask,
    out, scores, out_made, scores_made, left,
):
    classes = out.shape[1]
    scaled = own[...] * col_scale(author_summed, class_target)
    scores_made[...] = scaled * (classes / jnp.sum(scaled, axis=1, keepdims=True))
    copies = [pltpu.make_async_copy(scores_made, scores, left.at[0])]
    copies[0].start()
    scale_cols = col_scale(summed, class_target)
    lane = lax.broadcasted_iota(jnp.int32, (rows, classes), 1).astype(jnp.float32)
    for paper, line in enumerate(code_lines(seed_class, train_mask, rows)):
        code = code_column(line, classes)
        part = pl.ds(paper * rows, rows)
        scaled = kernel_ref[part, :] * scale_cols
        share = scaled * (1.0 / jnp.sum(scaled, axis=1, keepdims=True))
        updated = keep_share * share + jnp.where(code == lane, 1.0 - keep_share, 0.0)
        out_made[part, :] = classes * updated
        copies.append(pltpu.make_async_copy(out_made.at[part], out.at[part], left.at[paper + 1]))
        copies[-1].start()
    for copy in copies:
        copy.wait()


def in_hbm(value):
    return pltpu.with_memory_space_constraint(value, pltpu.HBM)


def exchange(parts):
    return lax.all_to_all(parts, AXES, split_axis=0, concat_axis=0, tiled=True)


def narrow_exchange(parts, sides, upwards):
    groups, blocks = lax.axis_size("grp"), lax.axis_size("blk")
    planes = range(groups)
    if not upwards:
        planes = sorted(planes, key=lambda i: abs(2 * i + 1 - groups))
    sets = [
        [i * blocks + first + side for i in planes for side in reversed(range(sides))]
        for first in range(0, blocks, sides)
    ]
    return lax.all_to_all(
        parts, AXES, split_axis=0, concat_axis=0, axis_index_groups=sets, tiled=True
    )


def on_device(
    tile_values,
    tile_paper,
    tile_author,
    tile_count,
    seed_class,
    train_mask,
    class_prior,
    class_target,
):
    f32 = jnp.float32
    bf16 = jnp.bfloat16
    shape = jax.ShapeDtypeStruct
    slots, rows, columns = tile_values.shape
    classes = class_prior.shape[0]
    papers = seed_class.shape[0]
    authors = AT_DEV * columns
    paper_tiles = papers // rows
    devices = lax.axis_size(AXES)
    prior = class_prior.reshape(1, classes)
    target = class_target.reshape(1, classes)
    seed_class = seed_class.reshape(papers // LANES, LANES)
    train_mask = train_mask.reshape(papers // LANES, LANES)
    parts = shape((devices, 1, classes), f32)

    inputs = (
        tile_paper, tile_author, seed_class, train_mask, prior, target,
    )
    places = (SMEM, SMEM, VMEM, VMEM, VMEM, VMEM)
    blocks = lax.axis_size("blk")
    load = shape((blocks // 2, rows + META, columns), bf16)
    moved = call(
        functools.partial(pack_kernel, rows),
        tuple(shape(one.shape, one.dtype) for one in inputs) + (load, load),
        [SMEM, HBM] + [HBM] * len(inputs),
        [pltpu.SemaphoreType.DMA((len(inputs),)), pltpu.SemaphoreType.DMA((2, blocks // 2))],
        places + (VMEM, VMEM),
    )(tile_count, in_hbm(tile_values), *(in_hbm(one) for one in inputs))
    tile_paper, tile_author, seed_class, train_mask, prior, target, keep, swap = moved
    swapped = lax.ppermute(swap, "blk", [(i, i ^ 1) for i in range(blocks)])
    local = call(
        functools.partial(first_sum_kernel, authors, rows), parts, [SMEM, SMEM] + [VMEM] * 5
    )(tile_paper, tile_count, keep, swap, seed_class, train_mask, prior)
    both = shape((2, rows + META, columns), bf16)
    pairs = call(pair_kernel, (both,) * (blocks // 2 - 1), [VMEM] * 2)(keep, swapped)
    local, *pairs = lax.optimization_barrier((local, *pairs))
    count = blocks // 2

    def across_pairs(value, even, odd):
        hops = [2 * odd if i % 2 else 2 * even for i in range(blocks)]
        return lax.ppermute(value, "blk", [(i, i ^ hop) for i, hop in enumerate(hops)])

    def to_other(value):
        return lax.ppermute(value, "blk", [(i, i ^ 1) for i in range(blocks)])

    ways = list(zip(pair_order(count, 0), pair_order(count, 1)))
    held = [keep, swapped] + [across_pairs(one, *way) for one, way in zip(pairs, ways[1:])]
    summed = exchange(local)

    author_out = (shape((authors, classes), f32), parts)
    paper_out = (shape((papers, classes), f32), parts, shape((papers, classes), bf16))

    four = count == 4
    places = [(i, None) for i in range(blocks)]
    if four:
        places = [(0, None), (1, None), (2, 0), (2, 1)]
        places += [(3, k) for k in turned(count)]

    def balance(kernel, sent, local, steps, widest):
        here, there, joined = [sent], [], None
        sides = 0
        for step in range(steps):
            moves = []
            if step == 0:
                moves = [(sent, *way) for way in ways[1 : 2 if four else 3]]
            elif step == 1:
                moves = [(joined, *ways[2])] if four else [(sent, *way) for way in ways[3:]]
            moves = [across_pairs(*move) for move in moves]
            others = [] if step == 0 else [sent] if step == 1 else here[len(there) :]
            if four:
                others = [joined] if step == 2 else []
            others = [to_other(one) for one in others]
            if sides:
                summed = narrow_exchange(local, sides, step + 1 == steps and sides == 2)
            else:
                summed = exchange(local)
            summed, *moved = lax.optimization_barrier((summed, *moves, *others))
            here += moved[: len(moves)]
            there += moved[len(moves) :]
            if step + 1 < steps:
                added, size = [kernel], devices
                if step > 0:
                    added = list(here)
                    sides = 2
                    if step > 1 and widest:
                        added += there
                        sides = 1
                    size = sides * lax.axis_size("grp")
                joined = sent
                if four and step < 2:
                    joined = call(
                        join_kernel, shape((2 * step + 2, *sent.shape), sent.dtype), [VMEM] * len(here)
                    )(*here)
                    joined, summed = lax.optimization_barrier((joined, summed))
                local = call(
                    balance_kernel, shape((size, 1, classes), f32), [VMEM] * (len(added) + 2)
                )(*added, summed, target)
                if four:
                    local, sent, *here = lax.optimization_barrier((local, sent, *here))
                else:
                    local, sent, joined, *here = lax.optimization_barrier((local, sent, joined, *here))
        return summed, here + there

    def last_balance(kernel, local):
        for step in range(ITERS):
            summed = exchange(local)
            if step + 1 < ITERS:
                local = call(balance_kernel, parts, [VMEM] * 3)(kernel, summed, target)
        return summed

    for repeat in range(ROUNDS):
        if repeat == 0:
            own, local = call(
                functools.partial(first_author_kernel, rows), author_out, [VMEM] * (3 + len(held))
            )(summed, prior, target, *held)
            left = ITERS - 1
        else:
            own, local = call(
                functools.partial(author_kernel, rows, places),
                author_out,
                [VMEM] * (3 + len(kernels) + len(held)),
            )(summed, prior, target, *kernels, *held)
            left = ITERS
        author_summed, kernels = balance(own, own, local, left, True)
        last = repeat + 1 == ROUNDS
        kernel, local, *half = call(
            functools.partial(paper_kernel, places, rows),
            paper_out[:2] if last else paper_out,
            [SMEM, SMEM, SMEM] + [VMEM] * (5 + len(kernels)),
        )(
            tile_paper, tile_author, tile_count, keep, swap, author_summed, prior, target, *kernels
        )
        if last:
            summed = last_balance(kernel, local)
        else:
            summed, kernels = balance(kernel, half[0], local, ITERS, False)
    return call(
        functools.partial(final_kernel, rows),
        (shape((papers, classes), f32), shape((authors, classes), f32)),
        [VMEM] * 7,
        [
            pltpu.VMEM((papers, classes), f32),
            pltpu.VMEM((authors, classes), f32),
            pltpu.SemaphoreType.DMA((1 + papers // rows,)),
        ],
        (HBM, HBM),
    )(kernel, summed, own, author_summed, target, seed_class, train_mask)


def solution(mesh):
    placed = (
        P(("grp", "blk"), None, None),
        P(("grp", "blk")),
        P(("grp", "blk")),
        P(("grp", "blk")),
        P(("grp", "blk")),
        P(("grp", "blk")),
        P(),
        P(),
    )
    return jax.shard_map(
        on_device,
        mesh=mesh,
        in_specs=placed,
        out_specs=(P(("grp", "blk"), None), P(("grp", "blk"), None)),
        check_vma=False,
    )
```

```python
import functools

import jax
import jax.numpy as jnp
from jax import lax
from jax.experimental import pallas as pl
from jax.experimental.pallas import tpu as pltpu
from jax.sharding import PartitionSpec as P

AT_DEV = 2
ITERS = 4
ROUNDS = 2
LANES = 128
META = 16

keep_share = 0.8

AXES = ("grp", "blk")
VMEM = pl.BlockSpec(memory_space=pltpu.VMEM)
SMEM = pl.BlockSpec(memory_space=pltpu.SMEM)
HBM = pl.BlockSpec(memory_space=pltpu.HBM)


def call(kernel, out_shape, in_specs, scratch_shapes=(), out_specs=None):
    if out_specs is None:
        out_specs = jax.tree.map(lambda _: VMEM, out_shape)
    return pl.pallas_call(
        kernel,
        out_shape=out_shape,
        in_specs=in_specs,
        out_specs=out_specs,
        scratch_shapes=list(scratch_shapes),
        compiler_params=pltpu.CompilerParams(vmem_limit_bytes=48 * 1024 * 1024),
    )


def col_scale(parts_ref, target_ref):
    return target_ref[...] / jnp.sum(parts_ref[...], axis=0)


def row_scale(kernel, scale_cols):
    return 1.0 / jnp.sum(kernel * scale_cols, axis=1, keepdims=True)


def spread(value, parts_ref):
    parts_ref[...] = jnp.broadcast_to(value[None], parts_ref.shape)


def code_lines(seed_class, train_mask, rows):
    code = jnp.where(train_mask[...] == 1, seed_class[...], -1).astype(jnp.float32)
    line = jnp.concatenate([code[i : i + 1] for i in range(code.shape[0])], axis=1)
    papers = line.shape[1]
    wide = jnp.broadcast_to(line, (8, papers))
    lines = []
    for start in range(0, papers, rows):
        lines.append((pltpu.roll(wide, papers - start, 1) if start else wide)[:1, :rows])
    return lines


def meta_line(meta, rows):
    count = -(-rows // LANES)
    return jnp.concatenate([meta[i : i + 1] for i in range(count)], axis=1)[:, :rows]


def code_columns(lines):
    rows = lines[0].shape[1]
    wide = jnp.concatenate(lines, axis=0)
    wide = jnp.pad(wide, ((0, -len(lines) % 8), (0, -rows % LANES)))
    columns = wide.T
    return [columns[:rows, i : i + 1] for i in range(len(lines))]


def code_column(line, classes):
    rows = line.shape[1]
    across = lax.broadcasted_iota(jnp.int32, (rows, rows), 1)
    eye = jnp.where(lax.broadcasted_iota(jnp.int32, (rows, rows), 0) == across, 1.0, 0.0)
    wide = jnp.broadcast_to(line, (LANES, rows)).astype(jnp.bfloat16)
    column = lax.dot_general(
        eye.astype(jnp.bfloat16),
        wide,
        (((1,), (1,)), ((), ())),
        preferred_element_type=jnp.float32,
    )
    return jnp.concatenate([column] * (classes // LANES), axis=1)


def seeds_of(line, classes):
    class_line = lax.broadcasted_iota(jnp.int32, (classes, line.shape[1]), 0)
    return jnp.where(class_line.astype(jnp.float32) == line, 1.0, 0.0).astype(jnp.bfloat16)


def pack_kernel(rows, tile_count, *refs):
    tiles, *refs = refs
    count = 6
    ins, places = refs[:count], refs[count : 2 * count]
    keep, swap, ready, arrived = refs[2 * count :]
    tile_paper, tile_author, seed_class, train_mask = places[:4]
    pairs = keep.shape[0]
    me = lax.axis_index("blk")
    pair, side = lax.div(me, 2), lax.rem(me, 2)
    moves = [
        pltpu.make_async_copy(source, place, ready.at[i])
        for i, (source, place) in enumerate(zip(ins, places))
    ]
    for copy in moves:
        copy.start()
    outs = []
    copies = []
    for way, (out, to) in enumerate(((keep, side), (swap, 1 - side))):
        for k, other in enumerate(pair_order(pairs, to)):
            slot = 2 * lax.bitwise_xor(pair, other) + to
            copy = pltpu.make_async_copy(
                tiles.at[slot], out.at[k, pl.ds(0, rows)], arrived.at[way, k]
            )
            copy.start()
            copies.append(copy)
            outs.append((out, k, slot))
    for copy in moves[:4]:
        copy.wait()
    line = lax.broadcasted_iota(jnp.int32, (META, LANES), 0)
    code_rows = -(-rows // LANES)
    blocks = []
    for codes in code_lines(seed_class, train_mask, rows):
        pad = jnp.full((1, code_rows * LANES - rows), -1.0, jnp.float32)
        codes = jnp.concatenate([codes, pad], axis=1)
        block = jnp.zeros((META, LANES), jnp.float32)
        for i in range(code_rows):
            block = jnp.where(line == i, codes[:, i * LANES : (i + 1) * LANES], block)
        blocks.append(block)
    for out, k, slot in outs:
        paper = tile_paper[slot]
        live = slot < tile_count[0]
        block = blocks[0]
        for i in range(1, len(blocks)):
            block = jnp.where(paper == i, blocks[i], block)
        for author in range(AT_DEV):
            chosen = jnp.where(live & (tile_author[slot] == author), 1.0, 0.0)
            block = jnp.where(line == code_rows + author, chosen, block)
        block = jnp.where(line == code_rows + AT_DEV, paper.astype(jnp.float32), block)
        out[k, rows:, :] = block.astype(jnp.bfloat16)
    for copy in moves[4:] + copies:
        copy.wait()


def pieces(refs):
    return [(ref, i) for ref in refs for i in range(ref.shape[0] if ref.ndim == 3 else 1)]


def piece(ref, i):
    return ref[i] if ref.ndim == 3 else ref[...]


def join_kernel(*refs):
    *ins, out = refs
    for place, one in enumerate(pieces(ins)):
        out[place] = piece(*one)


def pair_kernel(keep, swapped, *outs):
    for k, out in enumerate(outs, 1):
        out[0] = keep[k]
        out[1] = swapped[k]


def pair_order(pairs, side):
    return [0, 1 + side, 2 - side, 3] if pairs == 4 else list(range(pairs))


def turned(pairs):
    return [0, 2, 1, 3] if pairs == 4 else list(range(pairs))


def sources(count):
    me = lax.axis_index("blk")
    pair, side = lax.div(me, 2), lax.rem(me, 2)
    pairs = [2 * lax.bitwise_xor(pair, k) for k in pair_order(count // 2, side)]
    return [other + side for other in pairs] + [other + 1 - side for other in pairs]


def own_tiles(keep, swap, rows):
    pairs = keep.shape[0]
    kept = [keep[k, :rows, :] for k in range(pairs)]
    return kept + [swap[k, :rows, :] for k in turned(pairs)]


def views(refs, places):
    return [refs[i] if place is None else refs[i].at[place] for i, place in places]


def slots_of(keep, swapped, *pairs):
    return [(keep, 0), *((ref, 0) for ref in pairs), (swapped, 0), *((ref, 1) for ref in pairs)]


def first_sum_kernel(
    authors, rows, tile_paper, tile_count, keep, swap, seed_class, train_mask, class_prior, parts
):
    pairs, _, columns = keep.shape
    classes = parts.shape[2]
    slots = sources(2 * pairs)
    tiles = [tile.astype(jnp.float32) for tile in own_tiles(keep, swap, rows)]
    lane = lax.broadcasted_iota(jnp.int32, (rows, classes), 1).astype(jnp.float32)
    total = authors * class_prior[...]
    for paper, code in enumerate(code_columns(code_lines(seed_class, train_mask, rows))):
        weight = jnp.zeros((rows, columns), jnp.float32)
        for slot, tile in zip(slots, tiles):
            chosen = (slot < tile_count[0]) & (tile_paper[slot] == paper)
            weight = weight + jnp.where(chosen, tile, 0.0)
        weight = jnp.sum(weight, axis=1, keepdims=True)
        seeds = jnp.where(code == lane, weight, 0.0)
        total = total + jnp.sum(seeds, axis=0, keepdims=True)
    spread(total, parts)


def next_sum(kernel, summed, class_target, parts):
    scale_rows = row_scale(kernel, col_scale(summed, class_target))
    spread(jnp.sum(scale_rows * kernel, axis=0, keepdims=True), parts)


def first_author_kernel(rows, summed, class_prior, class_target, *rest):
    *held, full, parts = rest
    classes = full.shape[1]
    code_rows = -(-rows // LANES)
    totals = [jnp.zeros((classes, LANES), jnp.float32) for _ in range(AT_DEV)]
    for ref, place in slots_of(*held):
        meta = ref[place, rows:, :].astype(jnp.float32)
        seeds = seeds_of(meta_line(meta, rows), classes)
        parcel = jnp.dot(seeds, ref[place, :rows, :], preferred_element_type=jnp.float32)
        parcel = parcel.astype(jnp.bfloat16).astype(jnp.float32)
        for author in range(AT_DEV):
            chosen = meta[code_rows + author : code_rows + author + 1]
            totals[author] = totals[author] + parcel * chosen
    kernel = jnp.concatenate([total.T for total in totals], axis=0) + class_prior[...]
    full[...] = kernel
    next_sum(kernel, summed, class_target, parts)


def author_kernel(rows, places, summed, class_prior, class_target, *rest):
    *rest, full, parts = rest
    count = 1 + max(i for i, _ in places)
    kernels, held = views(rest, places), slots_of(*rest[count:])
    classes = full.shape[1]
    code_rows = -(-rows // LANES)
    metas = [ref[place, rows:, :].astype(jnp.float32) for ref, place in held]
    at = code_rows + AT_DEV
    papers = [jnp.max(meta[at : at + 1]).astype(jnp.int32) for meta in metas]
    scale_cols = col_scale(summed, class_target)
    codes = code_columns([meta_line(meta, rows) for meta in metas])
    totals = [jnp.zeros((LANES, classes), jnp.float32) for _ in range(AT_DEV)]
    lane = lax.broadcasted_iota(jnp.int32, (rows, classes), 1).astype(jnp.float32)
    for shift, (ref, place) in enumerate(held):
        half = kernels[shift][pl.ds(pl.multiple_of(papers[shift] * rows, rows), rows), :]
        scaled = half.astype(jnp.float32) * scale_cols
        share = scaled * (keep_share / jnp.sum(scaled, axis=1, keepdims=True))
        labels = jnp.where(codes[shift] == lane, share + (1.0 - keep_share), share)
        parcel = lax.dot_general(
            ref[place, :rows, :],
            labels.astype(jnp.bfloat16),
            (((0,), (0,)), ((), ())),
            preferred_element_type=jnp.float32,
        )
        parcel = parcel.astype(jnp.bfloat16).astype(jnp.float32)
        for author in range(AT_DEV):
            at = code_rows + author
            totals[author] = totals[author] + parcel * metas[shift][at : at + 1, :1]
    kernel = jnp.concatenate(totals, axis=0) + class_prior[...]
    full[...] = kernel
    spread(jnp.sum(kernel, axis=0, keepdims=True), parts)


def paper_kernel(
    places, rows, tile_paper, tile_author, tile_count, keep, swap, summed, class_prior,
    class_target, *rest,
):
    kernels, (full, parts, *half) = views(rest, places), rest[1 + max(i for i, _ in places) :]
    columns = keep.shape[2]
    classes = full.shape[1]
    scale_cols = col_scale(summed, class_target)
    slots = sources(len(kernels))
    wide = jnp.concatenate(own_tiles(keep, swap, rows), axis=1)
    labels = []
    for ref, slot in zip(kernels, slots):
        start = pl.multiple_of(tile_author[slot] * columns, columns)
        scaled = ref[pl.ds(start, columns), :] * scale_cols
        share = scaled * (1.0 / jnp.sum(scaled, axis=1, keepdims=True))
        labels.append(share.astype(jnp.bfloat16))
    column = jnp.zeros((1, classes), jnp.float32)
    for paper in range(full.shape[0] // rows):
        chosen = []
        for one, slot in zip(labels, slots):
            mine = (slot < tile_count[0]) & (tile_paper[slot] == paper)
            chosen.append(jnp.where(mine, one, jnp.zeros_like(one)))
        mass = jnp.dot(wide, jnp.concatenate(chosen, axis=0), preferred_element_type=jnp.float32)
        kernel = mass + class_prior[...]
        full[paper * rows : (paper + 1) * rows, :] = kernel
        for out in half:
            out[paper * rows : (paper + 1) * rows, :] = kernel.astype(jnp.bfloat16)
        column = column + jnp.sum(kernel, axis=0, keepdims=True)
    spread(column, parts)


def balance_kernel(*refs):
    *kernels, summed, class_target, parts = refs
    scale_cols = col_scale(summed, class_target)
    total = None
    for one in pieces(kernels):
        kernel = piece(*one).astype(jnp.float32)
        local = jnp.sum(row_scale(kernel, scale_cols) * kernel, axis=0, keepdims=True)
        total = local if total is None else total + local
    spread(total, parts)


def final_kernel(
    rows, kernel_ref, summed, own, author_summed, class_target, seed_class, train_mask,
    out, scores, out_made, scores_made, left,
):
    classes = out.shape[1]
    scaled = own[...] * col_scale(author_summed, class_target)
    scores_made[...] = scaled * (classes / jnp.sum(scaled, axis=1, keepdims=True))
    copies = [pltpu.make_async_copy(scores_made, scores, left.at[0])]
    copies[0].start()
    scale_cols = col_scale(summed, class_target)
    lane = lax.broadcasted_iota(jnp.int32, (rows, classes), 1).astype(jnp.float32)
    for paper, line in enumerate(code_lines(seed_class, train_mask, rows)):
        code = code_column(line, classes)
        part = pl.ds(paper * rows, rows)
        scaled = kernel_ref[part, :] * scale_cols
        share = scaled * (1.0 / jnp.sum(scaled, axis=1, keepdims=True))
        updated = keep_share * share + jnp.where(code == lane, 1.0 - keep_share, 0.0)
        out_made[part, :] = classes * updated
        copies.append(pltpu.make_async_copy(out_made.at[part], out.at[part], left.at[paper + 1]))
        copies[-1].start()
    for copy in copies:
        copy.wait()


def in_hbm(value):
    return pltpu.with_memory_space_constraint(value, pltpu.HBM)


def exchange(parts):
    return lax.all_to_all(parts, AXES, split_axis=0, concat_axis=0, tiled=True)


def narrow_exchange(parts, sides, upwards):
    groups, blocks = lax.axis_size("grp"), lax.axis_size("blk")
    planes = range(groups)
    if not upwards:
        planes = sorted(planes, key=lambda i: abs(2 * i + 1 - groups))
    sets = [
        [i * blocks + first + side for i in planes for side in reversed(range(sides))]
        for first in range(0, blocks, sides)
    ]
    return lax.all_to_all(
        parts, AXES, split_axis=0, concat_axis=0, axis_index_groups=sets, tiled=True
    )


def on_device(
    tile_values,
    tile_paper,
    tile_author,
    tile_count,
    seed_class,
    train_mask,
    class_prior,
    class_target,
):
    f32 = jnp.float32
    bf16 = jnp.bfloat16
    shape = jax.ShapeDtypeStruct
    slots, rows, columns = tile_values.shape
    classes = class_prior.shape[0]
    papers = seed_class.shape[0]
    authors = AT_DEV * columns
    paper_tiles = papers // rows
    devices = lax.axis_size(AXES)
    prior = class_prior.reshape(1, classes)
    target = class_target.reshape(1, classes)
    seed_class = seed_class.reshape(papers // LANES, LANES)
    train_mask = train_mask.reshape(papers // LANES, LANES)
    parts = shape((devices, 1, classes), f32)

    inputs = (
        tile_paper, tile_author, seed_class, train_mask, prior, target,
    )
    places = (SMEM, SMEM, VMEM, VMEM, VMEM, VMEM)
    blocks = lax.axis_size("blk")
    load = shape((blocks // 2, rows + META, columns), bf16)
    moved = call(
        functools.partial(pack_kernel, rows),
        tuple(shape(one.shape, one.dtype) for one in inputs) + (load, load),
        [SMEM, HBM] + [HBM] * len(inputs),
        [pltpu.SemaphoreType.DMA((len(inputs),)), pltpu.SemaphoreType.DMA((2, blocks // 2))],
        places + (VMEM, VMEM),
    )(tile_count, in_hbm(tile_values), *(in_hbm(one) for one in inputs))
    tile_paper, tile_author, seed_class, train_mask, prior, target, keep, swap = moved
    swapped = lax.ppermute(swap, "blk", [(i, i ^ 1) for i in range(blocks)])
    local = call(
        functools.partial(first_sum_kernel, authors, rows), parts, [SMEM, SMEM] + [VMEM] * 5
    )(tile_paper, tile_count, keep, swap, seed_class, train_mask, prior)
    both = shape((2, rows + META, columns), bf16)
    pairs = call(pair_kernel, (both,) * (blocks // 2 - 1), [VMEM] * 2)(keep, swapped)
    local, *pairs = lax.optimization_barrier((local, *pairs))
    count = blocks // 2

    def across_pairs(value, even, odd):
        hops = [2 * odd if i % 2 else 2 * even for i in range(blocks)]
        return lax.ppermute(value, "blk", [(i, i ^ hop) for i, hop in enumerate(hops)])

    def to_other(value):
        return lax.ppermute(value, "blk", [(i, i ^ 1) for i in range(blocks)])

    ways = list(zip(pair_order(count, 0), pair_order(count, 1)))
    held = [keep, swapped] + [across_pairs(one, *way) for one, way in zip(pairs, ways[1:])]
    summed = exchange(local)

    author_out = (shape((authors, classes), f32), parts)
    paper_out = (shape((papers, classes), f32), parts, shape((papers, classes), bf16))

    four = count == 4
    places = [(i, None) for i in range(blocks)]
    if four:
        places = [(0, None), (1, None), (2, 0), (2, 1)]
        places += [(3, k) for k in turned(count)]

    def balance(kernel, sent, local, steps, calm):
        here, there, joined = [sent], [], None
        sides = 0
        for step in range(steps):
            moves = []
            if step == 0:
                moves = [(sent, *way) for way in ways[1 : 2 if four else 3]]
            elif step == 1:
                moves = [(joined, *ways[2])] if four else [(sent, *way) for way in ways[3:]]
            moves = [across_pairs(*move) for move in moves]
            others = [] if step == 0 else [sent] if step == 1 else here[len(there) :]
            if four:
                others = [joined] if step == 2 else []
            others = [to_other(one) for one in others]
            if sides:
                summed = narrow_exchange(local, sides, step + 1 == steps and not calm)
            else:
                summed = exchange(local)
            summed, *moved = lax.optimization_barrier((summed, *moves, *others))
            here += moved[: len(moves)]
            there += moved[len(moves) :]
            if step + 1 < steps:
                added, size = [kernel], devices
                if step > 0:
                    added = list(here)
                    sides = 2
                    size = sides * lax.axis_size("grp")
                joined = sent
                if four and step < 2:
                    joined = call(
                        join_kernel, shape((2 * step + 2, *sent.shape), sent.dtype), [VMEM] * len(here)
                    )(*here)
                    joined, summed = lax.optimization_barrier((joined, summed))
                local = call(
                    balance_kernel, shape((size, 1, classes), f32), [VMEM] * (len(added) + 2)
                )(*added, summed, target)
                if four:
                    local, sent, *here = lax.optimization_barrier((local, sent, *here))
                else:
                    local, sent, joined, *here = lax.optimization_barrier((local, sent, joined, *here))
        return summed, here + there

    def last_balance(kernel, local):
        for step in range(ITERS):
            summed = exchange(local)
            if step + 1 < ITERS:
                local = call(balance_kernel, parts, [VMEM] * 3)(kernel, summed, target)
        return summed

    for repeat in range(ROUNDS):
        if repeat == 0:
            own, local = call(
                functools.partial(first_author_kernel, rows), author_out, [VMEM] * (3 + len(held))
            )(summed, prior, target, *held)
            left = ITERS - 1
        else:
            own, local = call(
                functools.partial(author_kernel, rows, places),
                author_out,
                [VMEM] * (3 + len(kernels) + len(held)),
            )(summed, prior, target, *kernels, *held)
            left = ITERS
        author_summed, kernels = balance(own, own, local, left, repeat + 1 == ROUNDS)
        last = repeat + 1 == ROUNDS
        kernel, local, *half = call(
            functools.partial(paper_kernel, places, rows),
            paper_out[:2] if last else paper_out,
            [SMEM, SMEM, SMEM] + [VMEM] * (5 + len(kernels)),
        )(
            tile_paper, tile_author, tile_count, keep, swap, author_summed, prior, target, *kernels
        )
        if last:
            summed = last_balance(kernel, local)
        else:
            summed, kernels = balance(kernel, half[0], local, ITERS, False)
    return call(
        functools.partial(final_kernel, rows),
        (shape((papers, classes), f32), shape((authors, classes), f32)),
        [VMEM] * 7,
        [
            pltpu.VMEM((papers, classes), f32),
            pltpu.VMEM((authors, classes), f32),
            pltpu.SemaphoreType.DMA((1 + papers // rows,)),
        ],
        (HBM, HBM),
    )(kernel, summed, own, author_summed, target, seed_class, train_mask)


def solution(mesh):
    placed = (
        P(("grp", "blk"), None, None),
        P(("grp", "blk")),
        P(("grp", "blk")),
        P(("grp", "blk")),
        P(("grp", "blk")),
        P(("grp", "blk")),
        P(),
        P(),
    )
    return jax.shard_map(
        on_device,
        mesh=mesh,
        in_specs=placed,
        out_specs=(P(("grp", "blk"), None), P(("grp", "blk"), None)),
        check_vma=False,
    )
```

```python
import functools

import jax
import jax.numpy as jnp
from jax import lax
from jax.experimental import pallas as pl
from jax.experimental.pallas import tpu as pltpu
from jax.sharding import PartitionSpec as P

AT_DEV = 2
ITERS = 4
ROUNDS = 2
LANES = 128
META = 16

keep_share = 0.8

AXES = ("grp", "blk")
VMEM = pl.BlockSpec(memory_space=pltpu.VMEM)
SMEM = pl.BlockSpec(memory_space=pltpu.SMEM)
HBM = pl.BlockSpec(memory_space=pltpu.HBM)


def call(kernel, out_shape, in_specs, scratch_shapes=(), out_specs=None):
    if out_specs is None:
        out_specs = jax.tree.map(lambda _: VMEM, out_shape)
    return pl.pallas_call(
        kernel,
        out_shape=out_shape,
        in_specs=in_specs,
        out_specs=out_specs,
        scratch_shapes=list(scratch_shapes),
        compiler_params=pltpu.CompilerParams(vmem_limit_bytes=48 * 1024 * 1024),
    )


def col_scale(parts_ref, target_ref):
    return target_ref[...] / jnp.sum(parts_ref[...], axis=0)


def row_scale(kernel, scale_cols):
    return 1.0 / jnp.sum(kernel * scale_cols, axis=1, keepdims=True)


def spread(value, parts_ref):
    parts_ref[...] = jnp.broadcast_to(value[None], parts_ref.shape)


def code_lines(seed_class, train_mask, rows):
    code = jnp.where(train_mask[...] == 1, seed_class[...], -1).astype(jnp.float32)
    line = jnp.concatenate([code[i : i + 1] for i in range(code.shape[0])], axis=1)
    papers = line.shape[1]
    wide = jnp.broadcast_to(line, (8, papers))
    lines = []
    for start in range(0, papers, rows):
        lines.append((pltpu.roll(wide, papers - start, 1) if start else wide)[:1, :rows])
    return lines


def meta_line(meta, rows):
    count = -(-rows // LANES)
    return jnp.concatenate([meta[i : i + 1] for i in range(count)], axis=1)[:, :rows]


def code_columns(lines):
    rows = lines[0].shape[1]
    wide = jnp.concatenate(lines, axis=0)
    wide = jnp.pad(wide, ((0, -len(lines) % 8), (0, -rows % LANES)))
    columns = wide.T
    return [columns[:rows, i : i + 1] for i in range(len(lines))]


def code_column(line, classes):
    rows = line.shape[1]
    across = lax.broadcasted_iota(jnp.int32, (rows, rows), 1)
    eye = jnp.where(lax.broadcasted_iota(jnp.int32, (rows, rows), 0) == across, 1.0, 0.0)
    wide = jnp.broadcast_to(line, (LANES, rows)).astype(jnp.bfloat16)
    column = lax.dot_general(
        eye.astype(jnp.bfloat16),
        wide,
        (((1,), (1,)), ((), ())),
        preferred_element_type=jnp.float32,
    )
    return jnp.concatenate([column] * (classes // LANES), axis=1)


def seeds_of(line, classes):
    class_line = lax.broadcasted_iota(jnp.int32, (classes, line.shape[1]), 0)
    return jnp.where(class_line.astype(jnp.float32) == line, 1.0, 0.0).astype(jnp.bfloat16)


def pack_kernel(rows, tile_count, *refs):
    tiles, *refs = refs
    count = 6
    ins, places = refs[:count], refs[count : 2 * count]
    keep, swap, ready, arrived = refs[2 * count :]
    tile_paper, tile_author, seed_class, train_mask = places[:4]
    pairs = keep.shape[0]
    me = lax.axis_index("blk")
    pair, side = lax.div(me, 2), lax.rem(me, 2)
    moves = [
        pltpu.make_async_copy(source, place, ready.at[i])
        for i, (source, place) in enumerate(zip(ins, places))
    ]
    for copy in moves:
        copy.start()
    outs = []
    copies = []
    for way, (out, to) in enumerate(((keep, side), (swap, 1 - side))):
        for k, other in enumerate(pair_order(pairs, to)):
            slot = 2 * lax.bitwise_xor(pair, other) + to
            copy = pltpu.make_async_copy(
                tiles.at[slot], out.at[k, pl.ds(0, rows)], arrived.at[way, k]
            )
            copy.start()
            copies.append(copy)
            outs.append((out, k, slot))
    for copy in moves[:4]:
        copy.wait()
    line = lax.broadcasted_iota(jnp.int32, (META, LANES), 0)
    code_rows = -(-rows // LANES)
    blocks = []
    for codes in code_lines(seed_class, train_mask, rows):
        pad = jnp.full((1, code_rows * LANES - rows), -1.0, jnp.float32)
        codes = jnp.concatenate([codes, pad], axis=1)
        block = jnp.zeros((META, LANES), jnp.float32)
        for i in range(code_rows):
            block = jnp.where(line == i, codes[:, i * LANES : (i + 1) * LANES], block)
        blocks.append(block)
    for out, k, slot in outs:
        paper = tile_paper[slot]
        live = slot < tile_count[0]
        block = blocks[0]
        for i in range(1, len(blocks)):
            block = jnp.where(paper == i, blocks[i], block)
        for author in range(AT_DEV):
            chosen = jnp.where(live & (tile_author[slot] == author), 1.0, 0.0)
            block = jnp.where(line == code_rows + author, chosen, block)
        block = jnp.where(line == code_rows + AT_DEV, paper.astype(jnp.float32), block)
        out[k, rows:, :] = block.astype(jnp.bfloat16)
    for copy in moves[4:] + copies:
        copy.wait()


def pieces(refs):
    return [(ref, i) for ref in refs for i in range(ref.shape[0] if ref.ndim == 3 else 1)]


def piece(ref, i):
    return ref[i] if ref.ndim == 3 else ref[...]


def join_kernel(*refs):
    *ins, out = refs
    for place, one in enumerate(pieces(ins)):
        out[place] = piece(*one)


def pair_kernel(keep, swapped, *outs):
    for k, out in enumerate(outs, 1):
        out[0] = keep[k]
        out[1] = swapped[k]


def pair_order(pairs, side):
    return [0, 1 + side, 2 - side, 3] if pairs == 4 else list(range(pairs))


def turned(pairs):
    return [0, 2, 1, 3] if pairs == 4 else list(range(pairs))


def sources(count):
    me = lax.axis_index("blk")
    pair, side = lax.div(me, 2), lax.rem(me, 2)
    pairs = [2 * lax.bitwise_xor(pair, k) for k in pair_order(count // 2, side)]
    return [other + side for other in pairs] + [other + 1 - side for other in pairs]


def own_tiles(keep, swap, rows):
    pairs = keep.shape[0]
    kept = [keep[k, :rows, :] for k in range(pairs)]
    return kept + [swap[k, :rows, :] for k in turned(pairs)]


def views(refs, places):
    return [refs[i] if place is None else refs[i].at[place] for i, place in places]


def slots_of(keep, swapped, *pairs):
    return [(keep, 0), *((ref, 0) for ref in pairs), (swapped, 0), *((ref, 1) for ref in pairs)]


def first_sum_kernel(
    authors, rows, tile_paper, tile_count, keep, swap, seed_class, train_mask, class_prior, parts
):
    pairs, _, columns = keep.shape
    classes = parts.shape[2]
    slots = sources(2 * pairs)
    tiles = [tile.astype(jnp.float32) for tile in own_tiles(keep, swap, rows)]
    lane = lax.broadcasted_iota(jnp.int32, (rows, classes), 1).astype(jnp.float32)
    total = authors * class_prior[...]
    for paper, code in enumerate(code_columns(code_lines(seed_class, train_mask, rows))):
        weight = jnp.zeros((rows, columns), jnp.float32)
        for slot, tile in zip(slots, tiles):
            chosen = (slot < tile_count[0]) & (tile_paper[slot] == paper)
            weight = weight + jnp.where(chosen, tile, 0.0)
        weight = jnp.sum(weight, axis=1, keepdims=True)
        seeds = jnp.where(code == lane, weight, 0.0)
        total = total + jnp.sum(seeds, axis=0, keepdims=True)
    spread(total, parts)


def next_sum(kernel, summed, class_target, parts):
    scale_rows = row_scale(kernel, col_scale(summed, class_target))
    spread(jnp.sum(scale_rows * kernel, axis=0, keepdims=True), parts)


def first_author_kernel(rows, summed, class_prior, class_target, *rest):
    *held, full, parts = rest
    classes = full.shape[1]
    code_rows = -(-rows // LANES)
    totals = [jnp.zeros((classes, LANES), jnp.float32) for _ in range(AT_DEV)]
    for ref, place in slots_of(*held):
        meta = ref[place, rows:, :].astype(jnp.float32)
        seeds = seeds_of(meta_line(meta, rows), classes)
        parcel = jnp.dot(seeds, ref[place, :rows, :], preferred_element_type=jnp.float32)
        parcel = parcel.astype(jnp.bfloat16).astype(jnp.float32)
        for author in range(AT_DEV):
            chosen = meta[code_rows + author : code_rows + author + 1]
            totals[author] = totals[author] + parcel * chosen
    kernel = jnp.concatenate([total.T for total in totals], axis=0) + class_prior[...]
    full[...] = kernel
    next_sum(kernel, summed, class_target, parts)


def author_kernel(rows, places, summed, class_prior, class_target, *rest):
    *rest, full, parts = rest
    count = 1 + max(i for i, _ in places)
    kernels, held = views(rest, places), slots_of(*rest[count:])
    classes = full.shape[1]
    code_rows = -(-rows // LANES)
    metas = [ref[place, rows:, :].astype(jnp.float32) for ref, place in held]
    at = code_rows + AT_DEV
    papers = [jnp.max(meta[at : at + 1]).astype(jnp.int32) for meta in metas]
    scale_cols = col_scale(summed, class_target)
    codes = code_columns([meta_line(meta, rows) for meta in metas])
    totals = [jnp.zeros((LANES, classes), jnp.float32) for _ in range(AT_DEV)]
    lane = lax.broadcasted_iota(jnp.int32, (rows, classes), 1).astype(jnp.float32)
    for shift, (ref, place) in enumerate(held):
        half = kernels[shift][pl.ds(pl.multiple_of(papers[shift] * rows, rows), rows), :]
        scaled = half.astype(jnp.float32) * scale_cols
        share = scaled * (keep_share / jnp.sum(scaled, axis=1, keepdims=True))
        labels = jnp.where(codes[shift] == lane, share + (1.0 - keep_share), share)
        parcel = lax.dot_general(
            ref[place, :rows, :],
            labels.astype(jnp.bfloat16),
            (((0,), (0,)), ((), ())),
            preferred_element_type=jnp.float32,
        )
        parcel = parcel.astype(jnp.bfloat16).astype(jnp.float32)
        for author in range(AT_DEV):
            at = code_rows + author
            totals[author] = totals[author] + parcel * metas[shift][at : at + 1, :1]
    kernel = jnp.concatenate(totals, axis=0) + class_prior[...]
    full[...] = kernel
    spread(jnp.sum(kernel, axis=0, keepdims=True), parts)


def paper_kernel(
    places, rows, tile_paper, tile_author, tile_count, keep, swap, summed, class_prior,
    class_target, *rest,
):
    kernels, (full, parts, *half) = views(rest, places), rest[1 + max(i for i, _ in places) :]
    columns = keep.shape[2]
    classes = full.shape[1]
    scale_cols = col_scale(summed, class_target)
    slots = sources(len(kernels))
    wide = jnp.concatenate(own_tiles(keep, swap, rows), axis=1)
    labels = []
    for ref, slot in zip(kernels, slots):
        start = pl.multiple_of(tile_author[slot] * columns, columns)
        scaled = ref[pl.ds(start, columns), :] * scale_cols
        share = scaled * (1.0 / jnp.sum(scaled, axis=1, keepdims=True))
        labels.append(share.astype(jnp.bfloat16))
    column = jnp.zeros((1, classes), jnp.float32)
    for paper in range(full.shape[0] // rows):
        chosen = []
        for one, slot in zip(labels, slots):
            mine = (slot < tile_count[0]) & (tile_paper[slot] == paper)
            chosen.append(jnp.where(mine, one, jnp.zeros_like(one)))
        mass = jnp.dot(wide, jnp.concatenate(chosen, axis=0), preferred_element_type=jnp.float32)
        kernel = mass + class_prior[...]
        full[paper * rows : (paper + 1) * rows, :] = kernel
        for out in half:
            out[paper * rows : (paper + 1) * rows, :] = kernel.astype(jnp.bfloat16)
        column = column + jnp.sum(kernel, axis=0, keepdims=True)
    spread(column, parts)


def balance_kernel(*refs):
    *kernels, summed, class_target, parts = refs
    scale_cols = col_scale(summed, class_target)
    total = None
    for one in pieces(kernels):
        kernel = piece(*one).astype(jnp.float32)
        local = jnp.sum(row_scale(kernel, scale_cols) * kernel, axis=0, keepdims=True)
        total = local if total is None else total + local
    spread(total, parts)


def final_kernel(
    rows, kernel_ref, summed, own, author_summed, class_target, seed_class, train_mask,
    out, scores, out_made, scores_made, left,
):
    classes = out.shape[1]
    scaled = own[...] * col_scale(author_summed, class_target)
    scores_made[...] = scaled * (classes / jnp.sum(scaled, axis=1, keepdims=True))
    copies = [pltpu.make_async_copy(scores_made, scores, left.at[0])]
    copies[0].start()
    scale_cols = col_scale(summed, class_target)
    lane = lax.broadcasted_iota(jnp.int32, (rows, classes), 1).astype(jnp.float32)
    for paper, line in enumerate(code_lines(seed_class, train_mask, rows)):
        code = code_column(line, classes)
        part = pl.ds(paper * rows, rows)
        scaled = kernel_ref[part, :] * scale_cols
        share = scaled * (1.0 / jnp.sum(scaled, axis=1, keepdims=True))
        updated = keep_share * share + jnp.where(code == lane, 1.0 - keep_share, 0.0)
        out_made[part, :] = classes * updated
        copies.append(pltpu.make_async_copy(out_made.at[part], out.at[part], left.at[paper + 1]))
        copies[-1].start()
    for copy in copies:
        copy.wait()


def in_hbm(value):
    return pltpu.with_memory_space_constraint(value, pltpu.HBM)


def exchange(parts):
    return lax.all_to_all(parts, AXES, split_axis=0, concat_axis=0, tiled=True)


def narrow_exchange(parts, sides, upwards):
    groups, blocks = lax.axis_size("grp"), lax.axis_size("blk")
    planes = [1, 0, *range(2, groups)]
    if not upwards:
        planes = sorted(planes, key=lambda i: abs(2 * i + 1 - groups))
    sets = [
        [i * blocks + first + side for i in planes for side in reversed(range(sides))]
        for first in range(0, blocks, sides)
    ]
    return lax.all_to_all(
        parts, AXES, split_axis=0, concat_axis=0, axis_index_groups=sets, tiled=True
    )


def on_device(
    tile_values,
    tile_paper,
    tile_author,
    tile_count,
    seed_class,
    train_mask,
    class_prior,
    class_target,
):
    f32 = jnp.float32
    bf16 = jnp.bfloat16
    shape = jax.ShapeDtypeStruct
    slots, rows, columns = tile_values.shape
    classes = class_prior.shape[0]
    papers = seed_class.shape[0]
    authors = AT_DEV * columns
    paper_tiles = papers // rows
    devices = lax.axis_size(AXES)
    prior = class_prior.reshape(1, classes)
    target = class_target.reshape(1, classes)
    seed_class = seed_class.reshape(papers // LANES, LANES)
    train_mask = train_mask.reshape(papers // LANES, LANES)
    parts = shape((devices, 1, classes), f32)

    inputs = (
        tile_paper, tile_author, seed_class, train_mask, prior, target,
    )
    places = (SMEM, SMEM, VMEM, VMEM, VMEM, VMEM)
    blocks = lax.axis_size("blk")
    load = shape((blocks // 2, rows + META, columns), bf16)
    moved = call(
        functools.partial(pack_kernel, rows),
        tuple(shape(one.shape, one.dtype) for one in inputs) + (load, load),
        [SMEM, HBM] + [HBM] * len(inputs),
        [pltpu.SemaphoreType.DMA((len(inputs),)), pltpu.SemaphoreType.DMA((2, blocks // 2))],
        places + (VMEM, VMEM),
    )(tile_count, in_hbm(tile_values), *(in_hbm(one) for one in inputs))
    tile_paper, tile_author, seed_class, train_mask, prior, target, keep, swap = moved
    swapped = lax.ppermute(swap, "blk", [(i, i ^ 1) for i in range(blocks)])
    local = call(
        functools.partial(first_sum_kernel, authors, rows), parts, [SMEM, SMEM] + [VMEM] * 5
    )(tile_paper, tile_count, keep, swap, seed_class, train_mask, prior)
    both = shape((2, rows + META, columns), bf16)
    pairs = call(pair_kernel, (both,) * (blocks // 2 - 1), [VMEM] * 2)(keep, swapped)
    local, *pairs = lax.optimization_barrier((local, *pairs))
    count = blocks // 2

    def across_pairs(value, even, odd):
        hops = [2 * odd if i % 2 else 2 * even for i in range(blocks)]
        return lax.ppermute(value, "blk", [(i, i ^ hop) for i, hop in enumerate(hops)])

    def to_other(value):
        return lax.ppermute(value, "blk", [(i, i ^ 1) for i in range(blocks)])

    ways = list(zip(pair_order(count, 0), pair_order(count, 1)))
    held = [keep, swapped] + [across_pairs(one, *way) for one, way in zip(pairs, ways[1:])]
    summed = exchange(local)

    author_out = (shape((authors, classes), f32), parts)
    paper_out = (shape((papers, classes), f32), parts, shape((papers, classes), bf16))

    four = count == 4
    places = [(i, None) for i in range(blocks)]
    if four:
        places = [(0, None), (1, None), (2, 0), (2, 1)]
        places += [(3, k) for k in turned(count)]

    def balance(kernel, sent, local, steps, widest):
        here, there, joined = [sent], [], None
        sides = 0
        for step in range(steps):
            moves = []
            if step == 0:
                moves = [(sent, *way) for way in ways[1 : 2 if four else 3]]
            elif step == 1:
                moves = [(joined, *ways[2])] if four else [(sent, *way) for way in ways[3:]]
            moves = [across_pairs(*move) for move in moves]
            others = [] if step == 0 else [sent] if step == 1 else here[len(there) :]
            if four:
                others = [joined] if step == 2 else []
            others = [to_other(one) for one in others]
            if sides:
                summed = narrow_exchange(local, sides, step + 1 == steps and sides == 2)
            else:
                summed = exchange(local)
            summed, *moved = lax.optimization_barrier((summed, *moves, *others))
            here += moved[: len(moves)]
            there += moved[len(moves) :]
            if step + 1 < steps:
                added, size = [kernel], devices
                if step > 0:
                    added = list(here)
                    sides = 2
                    if step > 1 and widest:
                        added += there
                        sides = 1
                    size = sides * lax.axis_size("grp")
                joined = sent
                if four and step < 2:
                    joined = call(
                        join_kernel, shape((2 * step + 2, *sent.shape), sent.dtype), [VMEM] * len(here)
                    )(*here)
                    joined, summed = lax.optimization_barrier((joined, summed))
                local = call(
                    balance_kernel, shape((size, 1, classes), f32), [VMEM] * (len(added) + 2)
                )(*added, summed, target)
                if four:
                    local, sent, *here = lax.optimization_barrier((local, sent, *here))
                else:
                    local, sent, joined, *here = lax.optimization_barrier((local, sent, joined, *here))
        return summed, here + there

    def last_balance(kernel, local):
        for step in range(ITERS):
            summed = exchange(local)
            if step + 1 < ITERS:
                local = call(balance_kernel, parts, [VMEM] * 3)(kernel, summed, target)
        return summed

    for repeat in range(ROUNDS):
        if repeat == 0:
            own, local = call(
                functools.partial(first_author_kernel, rows), author_out, [VMEM] * (3 + len(held))
            )(summed, prior, target, *held)
            left = ITERS - 1
        else:
            own, local = call(
                functools.partial(author_kernel, rows, places),
                author_out,
                [VMEM] * (3 + len(kernels) + len(held)),
            )(summed, prior, target, *kernels, *held)
            left = ITERS
        author_summed, kernels = balance(own, own, local, left, True)
        last = repeat + 1 == ROUNDS
        kernel, local, *half = call(
            functools.partial(paper_kernel, places, rows),
            paper_out[:2] if last else paper_out,
            [SMEM, SMEM, SMEM] + [VMEM] * (5 + len(kernels)),
        )(
            tile_paper, tile_author, tile_count, keep, swap, author_summed, prior, target, *kernels
        )
        if last:
            summed = last_balance(kernel, local)
        else:
            summed, kernels = balance(kernel, half[0], local, ITERS, False)
    return call(
        functools.partial(final_kernel, rows),
        (shape((papers, classes), f32), shape((authors, classes), f32)),
        [VMEM] * 7,
        [
            pltpu.VMEM((papers, classes), f32),
            pltpu.VMEM((authors, classes), f32),
            pltpu.SemaphoreType.DMA((1 + papers // rows,)),
        ],
        (HBM, HBM),
    )(kernel, summed, own, author_summed, target, seed_class, train_mask)


def solution(mesh):
    placed = (
        P(("grp", "blk"), None, None),
        P(("grp", "blk")),
        P(("grp", "blk")),
        P(("grp", "blk")),
        P(("grp", "blk")),
        P(("grp", "blk")),
        P(),
        P(),
    )
    return jax.shard_map(
        on_device,
        mesh=mesh,
        in_specs=placed,
        out_specs=(P(("grp", "blk"), None), P(("grp", "blk"), None)),
        check_vma=False,
    )
```
